32 devices in a mesh: grp: 2 (over x), row: 4 (over z), col: 4 (over y, core).
Axes of the slice: x: 2, y: 2, z: 4, core: 2. Of those that a mesh axis runs over, the one named last changes fastest.
Arguments:
- right_side: float32 [2, 16, 12288], P(None, None, 'row'), may hold values from -6 to 6
- near_tiles: bfloat16 [2, 256, 256, 256], P(None, ('grp', 'row', 'col')), may hold values from -0.078125 to 0.078125
- tile_pairs: int32 [256], P(('grp', 'row', 'col')), may hold values from 0 to 59, as said below
- tile_count: int32 [32], P(('grp', 'row', 'col')), may hold values from 1 to 8, as said below
- panel_expansions: bfloat16 [2, 12288, 441], P(None, 'row'), may hold values from -0.125 to 0.125
- leaf_of_panel: int32 [4, 3072], P('row'), may hold values from 0 to 23, never falling along the last dimension, each value on 1 to 256 neighbouring positions
- far_pick: int32 [4, 4, 2], replicated, may hold values from 0 to 23, as said below
- far_target: int32 [4, 8], P('row'), may hold values from 0 to 23
- far_offset: int32 [4, 8], P('row'), may hold values from 0 to 3
- translations: bfloat16 [4, 2, 441, 441], replicated, may hold values from -0.375 to 0.375
Outputs:
- solution: float32 [2, 16, 12288], P(None, None, 'row')
The draws below stay inside these ranges and needn't reach their ends.
Inputs may be any that keep to these rules, and one draw needn't show every extreme that they name: `tile_pairs`: within one device's 8 slots the codes are distinct, and over the live slots of all devices with the same row index they are distinct too. `tile_count`: some device has all 8 slots live. far_pick[d, r] holds 2 distinct leaves.
All inputs are finite; a program needn't handle non-finite values.
Results may differ from the reference program's by a relative error of at most 0.0016.
Values may be sent and summed in bfloat16 or wider, within the bound.
No kernel may reach another device: no remote copies, remote signals or barrier semaphores. Data moves between devices by JAX's collectives and lax.ppermute only.
A program may use at most 64 MiB of HBM per device.

```python
import math
import jax
import jax.numpy as jnp
import numpy as np
from jax import lax

TILE = 256
COEFS = 441
FIELDS = 16
BLK_DEV = 12
REACH = 2
SLOT_DEV = 8
SEND = 2
OFFSETS = 4
LEAF_DEV = 24
PAN_DEV = 3072
PANELS = 12288
BLOCKS = 48
TILES = 256
ITEMS = 8
N_GRP = 2
N_ROW = 4
N_COL = 4


def live_counts(key):
    device_count = N_GRP * N_ROW * N_COL
    group_count = N_GRP * N_COL
    code_count = BLK_DEV * (2 * REACH + 1)
    upper = min(SLOT_DEV, (code_count - SLOT_DEV) // (group_count - 1))
    counts = jax.random.randint(jax.random.fold_in(key, 11), (device_count,), 1, upper + 1)
    busiest = jax.random.randint(jax.random.fold_in(key, 12), (), 0, device_count)
    counts = jnp.where(jnp.arange(device_count) == busiest, SLOT_DEV, counts)
    return counts.astype(jnp.int32)


def draw_tile_count(key, part):
    return live_counts(key)


def draw_tile_pairs(key, part):
    group_count = N_GRP * N_COL
    code_count = BLK_DEV * (2 * REACH + 1)
    counts = live_counts(key).reshape(N_GRP, N_ROW, N_COL).transpose(1, 0, 2).reshape(N_ROW, group_count)
    starts = jnp.cumsum(counts, axis=1) - counts
    row_keys = jax.random.split(jax.random.fold_in(key, 13), N_ROW)

    def one_row(row_key):
        return jax.random.permutation(row_key, code_count)
    orders = jax.vmap(one_row)(row_keys)
    positions = (starts[:, :, None] + jnp.arange(SLOT_DEV, dtype=jnp.int32)[None, None, :]) % code_count
    codes = jnp.take_along_axis(orders, positions.reshape(N_ROW, -1), axis=1)
    codes = codes.reshape(N_ROW, N_GRP, N_COL, SLOT_DEV).transpose(1, 0, 2, 3)
    return codes.reshape(-1).astype(jnp.int32)


def draw_far_pick(key, part):
    pair_keys = jax.random.split(key, N_ROW * N_ROW)

    def one_pair(pair_key):
        return jax.random.permutation(pair_key, LEAF_DEV)[:SEND]
    return jax.vmap(one_pair)(pair_keys).reshape(N_ROW, N_ROW, SEND).astype(jnp.int32)


def plant(drawn, stream_key, low, high):
    spot = [jax.random.randint(jax.random.fold_in(stream_key, axis), (), 0, length) for axis, length in enumerate(drawn.shape)]
    main_axis = drawn.shape.index(max(drawn.shape))
    next_to = spot[:main_axis] + [(spot[main_axis] + 1) % drawn.shape[main_axis]] + spot[main_axis + 1:]
    return drawn.at[tuple(spot)].set(low).at[tuple(next_to)].set(high)


def block_scale(stream_key, shape, shards, smallest, top_value):
    level, own = 1.0, jax.random.fold_in(stream_key, 6)
    for dim, blocks in shards:
        heights = jnp.exp(jax.random.uniform(jax.random.fold_in(own, dim), (blocks,), jnp.float32, smallest / len(shards), top_value / len(shards)))
        level = level * jnp.repeat(heights, shape[dim] // blocks).reshape([-1 if axis == dim else 1 for axis in range(len(shape))])
    return level


def profile(count, total, reach, lean):
    portions = [(1 << 20) // math.isqrt(standing ** lean) + 1 for standing in range(2, count + 1)]
    spare, holding = total - reach - (count - 1), [1] * (count - 1)
    while spare > 0:
        free = [i for i in range(count - 1) if holding[i] < reach]
        mass, remaining = sum([portions[i] for i in free]), spare
        for i in free:
            addition = min(reach - holding[i], max(1, remaining * portions[i] // mass), spare)
            holding[i] = holding[i] + addition
            spare = spare - addition
    return np.array([reach] + holding)


def ragged(key, count, total, reach, slope):
    if count == 2:
        one = jax.random.randint(key, (), max(1, total - reach), min(reach, total - 1) + 1)
        return jnp.stack([one, total - one])
    lengths = jnp.asarray(profile(count, total, reach, slope), jnp.int32)
    couples = (count - 1) // 2
    donor, receiver = lengths[1:1 + 2 * couples:2], lengths[2:2 + 2 * couples:2]
    margin = jnp.minimum(donor - 1, reach - receiver)
    passed = jax.random.randint(jax.random.fold_in(key, 1), (couples,), 0, 1 << 20) % (margin + 1)
    lengths = lengths.at[1:1 + 2 * couples:2].set(donor - passed).at[2:2 + 2 * couples:2].set(receiver + passed)
    return lengths[jax.random.permutation(jax.random.fold_in(key, 2), count)]


def scatter_about(own_key, shape, deviation, reach, cuts=(), held_as=jnp.bfloat16):
    drawn = deviation * jax.random.normal(own_key, shape, jnp.float32)
    if cuts:
        drawn = drawn * block_scale(own_key, shape, cuts, -0.22, 0.18)
    return jnp.clip(drawn, -reach, reach).astype(held_as)


def setup_inputs(seed: int = 0) -> dict:
    seeds = jax.random.split(jax.random.key(seed), 11)
    right_side = scatter_about(seeds[0], (2, FIELDS, PANELS), 1.0, 6.0, ((2, 4),), jnp.float32)
    near_tiles = scatter_about(seeds[1], (2, TILES, TILE, TILE), (4 * TILE * (2 * REACH + 1)) ** -0.5, 0.078125, ((1, 32),))
    tile_pairs = draw_tile_pairs(jax.random.fold_in(seeds[10], 71), 0)
    tile_count = draw_tile_count(jax.random.fold_in(seeds[10], 71), 0)
    panel_expansions = scatter_about(seeds[4], (2, PANELS, COEFS), (4 * COEFS) ** -0.5, 0.125, ((1, 4),))
    leaf_of_panel = jax.vmap(lambda own: jnp.searchsorted(jnp.cumsum(ragged(own, LEAF_DEV, PAN_DEV, 2 * PAN_DEV // LEAF_DEV, 1)), jnp.arange(PAN_DEV), side="right"))(jax.random.split(seeds[5], N_ROW)).reshape((N_ROW, PAN_DEV)).astype(jnp.int32)
    far_pick = draw_far_pick(jax.random.fold_in(seeds[10], 71), 0)
    far_target = plant(jax.random.randint(seeds[7], (N_ROW, ITEMS), 0, LEAF_DEV), jax.random.fold_in(seeds[7], 1), 0, LEAF_DEV - 1).astype(jnp.int32)
    far_offset = plant(jax.random.randint(seeds[8], (N_ROW, ITEMS), 0, OFFSETS), jax.random.fold_in(seeds[8], 1), 0, OFFSETS - 1).astype(jnp.int32)
    translations = scatter_about(seeds[9], (OFFSETS, 2, COEFS, COEFS), (2 * COEFS * ITEMS // LEAF_DEV) ** -0.5, 0.375)
    return {"right_side": right_side, "near_tiles": near_tiles, "tile_pairs": tile_pairs, "tile_count": tile_count, "panel_expansions": panel_expansions, "leaf_of_panel": leaf_of_panel, "far_pick": far_pick, "far_target": far_target, "far_offset": far_offset, "translations": translations}


EPSILON = 1e-06
HIGHEST = lax.Precision.HIGHEST

def complex_mix(products):
    return jnp.stack([products[0, 0] - products[1, 1], products[0, 1] + products[1, 0]])

def near_field(vector_low, near_tiles, tile_pairs, tile_count):
    blocks = vector_low.astype(jnp.float32).reshape(2, FIELDS, BLOCKS, TILE)
    span_count = 2 * REACH + 1
    device_count = N_GRP * N_ROW * N_COL

    def visit(totals, device):
        row_index = device // N_COL % N_ROW
        pair_codes = lax.dynamic_slice_in_dim(tile_pairs, device * SLOT_DEV, SLOT_DEV)
        tile_block = lax.dynamic_slice_in_dim(near_tiles, device * SLOT_DEV, SLOT_DEV, 1).astype(jnp.float32)
        target = row_index * BLK_DEV + pair_codes // span_count
        source = (target + pair_codes % span_count - REACH) % BLOCKS
        source_rows = jnp.take(blocks, source, axis=2)
        values = complex_mix(jnp.einsum('xstj,ytij->xysti', source_rows, tile_block, precision=HIGHEST))
        live_mask = (jnp.arange(SLOT_DEV, dtype=jnp.int32) < tile_count[device]).astype(jnp.float32)
        values = values * live_mask[None, None, :, None]
        return (totals.at[:, :, target, :].add(values), None)
    initial = jnp.zeros((2, FIELDS, BLOCKS, TILE), jnp.float32)
    totals, unused = lax.scan(visit, initial, jnp.arange(device_count, dtype=jnp.int32))
    return totals.reshape(2, FIELDS, PANELS)

def far_field(vector_low, panel_expansions, leaf_of_panel, far_pick, far_target, far_offset, translations):
    leaf_ids = jnp.arange(LEAF_DEV, dtype=jnp.int32)
    vector_rows = vector_low.reshape(2, FIELDS, N_ROW, PAN_DEV).transpose(2, 0, 1, 3)
    expansion_rows = panel_expansions.reshape(2, N_ROW, PAN_DEV, COEFS).transpose(1, 0, 2, 3)
    translate_wide = translations.astype(jnp.float32)

    def outgoing(operands):
        vector_part, expansion_part, leaf_part = operands
        member = (leaf_part[None, :] == leaf_ids[:, None]).astype(jnp.float32)
        weighted = member[None, None] * vector_part.astype(jnp.float32)[:, :, None, :]
        multipoles = complex_mix(jnp.einsum('xslp,ypk->xyslk', weighted, expansion_part.astype(jnp.float32), precision=HIGHEST))
        return lax.optimization_barrier(multipoles.astype(jnp.bfloat16))
    multipoles = lax.map(outgoing, (vector_rows, expansion_rows, leaf_of_panel))
    flat_leaves = multipoles.transpose(0, 3, 1, 2, 4).reshape(N_ROW * LEAF_DEV, 2, FIELDS, COEFS)
    row_ids = jnp.arange(N_ROW, dtype=jnp.int32)
    slot_ids = jnp.arange(OFFSETS * LEAF_DEV, dtype=jnp.int32)

    def incoming(operands):
        pick_codes, targets, offsets, expansion_part, leaf_part = operands
        chosen = (row_ids[:, None] * LEAF_DEV + pick_codes).reshape(-1)
        item_rows = jnp.take(flat_leaves, chosen, axis=0).astype(jnp.float32)
        selector = (slot_ids[:, None] == (offsets * LEAF_DEV + targets)[None, :]).astype(jnp.float32)
        gathered = jnp.einsum('ai,ixsk->xsak', selector, item_rows, precision=HIGHEST)
        gathered = lax.optimization_barrier(gathered.astype(jnp.bfloat16)).astype(jnp.float32)
        gathered = gathered.reshape(2, FIELDS, OFFSETS, LEAF_DEV, COEFS)
        local_field = complex_mix(jnp.einsum('xsolk,oykj->xyslj', gathered, translate_wide, precision=HIGHEST))
        local_field = lax.optimization_barrier(local_field.astype(jnp.bfloat16)).astype(jnp.float32)
        member = (leaf_part[:, None] == leaf_ids[None, :]).astype(jnp.float32)
        spread = jnp.einsum('pl,xslk->xspk', member, local_field, precision=HIGHEST)
        return complex_mix(jnp.einsum('xspk,ypk->xysp', spread, expansion_part.astype(jnp.float32), precision=HIGHEST))
    result = lax.map(incoming, (far_pick, far_target, far_offset, expansion_rows, leaf_of_panel))
    return result.transpose(1, 2, 0, 3).reshape(2, FIELDS, PANELS)

def inner_product(left, right):
    real_part = lax.optimization_barrier(jnp.sum(left[0] * right[0] + left[1] * right[1], axis=-1))
    imag_part = lax.optimization_barrier(jnp.sum(left[0] * right[1] - left[1] * right[0], axis=-1))
    return jnp.stack([real_part, imag_part])

def scaled_vector(coeff, vector):
    real_coeff = coeff[0][:, None]
    imag_coeff = coeff[1][:, None]
    return jnp.stack([real_coeff * vector[0] - imag_coeff * vector[1], real_coeff * vector[1] + imag_coeff * vector[0]])

def complex_times(left, right):
    return jnp.stack([left[0] * right[0] - left[1] * right[1], left[0] * right[1] + left[1] * right[0]])

def conjugate(value):
    return jnp.stack([value[0], -value[1]])

def small_solve(beta_norm, h_first, h_sub, h_upper, h_middle, h_last):
    radius = jnp.sqrt(h_first[0] * h_first[0] + h_first[1] * h_first[1] + h_sub * h_sub)
    cosine = h_first / radius
    sine_one = h_sub / radius
    upper_row = complex_times(conjugate(cosine), h_upper) + sine_one * h_middle
    lower_row = complex_times(cosine, h_middle) - sine_one * h_upper
    radius_two = jnp.sqrt(lower_row[0] * lower_row[0] + lower_row[1] * lower_row[1] + h_last * h_last)
    cosine_two = lower_row / radius_two
    goal_top = conjugate(cosine) * beta_norm
    goal_mid = -sine_one * beta_norm
    weight_two = conjugate(cosine_two) * (goal_mid / radius_two)
    weight_one = (goal_top - complex_times(upper_row, weight_two)) / radius
    return (weight_one, weight_two)

def reference(right_side, near_tiles, tile_pairs, tile_count, panel_expansions, leaf_of_panel, far_pick, far_target, far_offset, translations):

    def apply_operator(vector):
        vector_low = lax.optimization_barrier(vector.astype(jnp.bfloat16))
        near_image = near_field(vector_low, near_tiles, tile_pairs, tile_count)
        far_image = far_field(vector_low, panel_expansions, leaf_of_panel, far_pick, far_target, far_offset, translations)
        return 0.5 * vector + near_image + far_image
    beta_norm = jnp.sqrt(lax.optimization_barrier(jnp.sum(right_side * right_side, axis=(0, 2))) + EPSILON)
    first_basis = right_side / beta_norm[None, :, None]
    image_one = apply_operator(first_basis)
    h_first = inner_product(first_basis, image_one)
    residue = image_one - scaled_vector(h_first, first_basis)
    h_sub = jnp.sqrt(lax.optimization_barrier(jnp.sum(residue * residue, axis=(0, 2))) + EPSILON)
    second_basis = residue / h_sub[None, :, None]
    image_two = apply_operator(second_basis)
    h_upper = inner_product(first_basis, image_two)
    h_middle = inner_product(second_basis, image_two)
    remainder = image_two - scaled_vector(h_upper, first_basis) - scaled_vector(h_middle, second_basis)
    h_last = jnp.sqrt(lax.optimization_barrier(jnp.sum(remainder * remainder, axis=(0, 2))) + EPSILON)
    weight_one, weight_two = small_solve(beta_norm, h_first, h_sub, h_upper, h_middle, h_last)
    return scaled_vector(weight_one, first_basis) + scaled_vector(weight_two, second_basis)
```

```python
import functools

import jax
import jax.numpy as jnp
from jax import lax
from jax.experimental import pallas as pl
from jax.experimental.pallas import tpu as pltpu
from jax.sharding import PartitionSpec as P

REACH = 2
SPAN = 2 * REACH + 1
LANES = 128
EPSILON = 1e-06
GROUP = ("grp", "col")
EVERY = ("grp", "row", "col")

F32 = jnp.float32
BF16 = jnp.bfloat16
SMEM = pl.BlockSpec(memory_space=pltpu.SMEM)
VMEM = pl.BlockSpec(memory_space=pltpu.VMEM)
ANY = pl.BlockSpec(memory_space=pl.ANY)


def dot_nn(left, right):
    return lax.dot_general(left, right, (((1,), (0,)), ((), ())), preferred_element_type=F32)


def dot_nt(left, right):
    return lax.dot_general(left, right, (((1,), (1,)), ((), ())), preferred_element_type=F32)


def mixed(real_side, imag_side, fields):
    real_part = real_side[:fields] - imag_side[fields:]
    imag_part = real_side[fields:] + imag_side[:fields]
    return jnp.concatenate([real_part, imag_part], axis=0)


def complex_dot(dot, rows, real_matrix, imag_matrix, fields):
    if rows.dtype == F32:
        high = rows.astype(BF16)
        rest = (rows - high.astype(F32)).astype(BF16)
        both = jnp.concatenate([high, rest], axis=0)
        real_side = dot(both, real_matrix)
        imag_side = dot(both, imag_matrix)
        real_side = real_side[: 2 * fields] + real_side[2 * fields :]
        imag_side = imag_side[: 2 * fields] + imag_side[2 * fields :]
    else:
        real_side = dot(rows, real_matrix)
        imag_side = dot(rows, imag_matrix)
    return mixed(real_side, imag_side, fields)


def lower_bound(leaf_ref, value, count):
    def halve(_, bounds):
        low, high = bounds
        middle = lax.div(low + high, 2)
        below = leaf_ref[0, jnp.minimum(middle, count - 1)] < value
        go_up = jnp.logical_and(below, low < high)
        return (jnp.where(go_up, middle + 1, low), jnp.where(go_up, high, jnp.minimum(middle, high)))

    low, _ = lax.fori_loop(0, count.bit_length(), halve, (jnp.int32(0), jnp.int32(count)))
    return low


def leaf_window(leaf_ref, leaf, count, width):
    start = lower_bound(leaf_ref, leaf, count)
    end = lower_bound(leaf_ref, leaf + 1, count)
    unit = jnp.minimum(lax.div(start, LANES), count // LANES - width)
    return start, end, unit


def window_mask(start, end, unit, rows, width):
    lane = lax.broadcasted_iota(jnp.int32, (rows, width * LANES), 1) + unit * LANES
    return jnp.logical_and(lane >= start, lane < end)


def multi_kernel(fields, items, width, pick_ref, leaf_ref, low_ref, exp_ref, out_ref, buf, sem):
    count = leaf_ref.shape[1]
    windows, copies = [], []
    for i in range(items):
        start, end, unit = leaf_window(leaf_ref, pick_ref[i], count, width)
        first = pl.multiple_of(unit * LANES, LANES)
        copy = pltpu.make_async_copy(
            exp_ref.at[:, pl.ds(first, width * LANES), :], buf.at[i], sem.at[i]
        )
        copy.start()
        windows.append((start, end, unit))
        copies.append(copy)
    for i in range(items):
        start, end, unit = windows[i]
        if len(low_ref.shape) == 2:
            first = pl.multiple_of(unit * LANES, LANES)
            rows = low_ref[:, pl.ds(first, width * LANES)]
        else:
            rows = jnp.concatenate([low_ref[unit + k] for k in range(width)], axis=-1)
        mask = window_mask(start, end, unit, 2 * fields, width)
        kept = jnp.where(mask, rows.astype(F32), 0.0).astype(rows.dtype)
        copies[i].wait()
        out_ref[i] = complex_dot(dot_nn, kept, buf[i, 0], buf[i, 1], fields).astype(BF16)


def near_kernel(fields, pairs_ref, count_ref, before_ref, here_ref, after_ref, tiles_ref, out_ref, ext):
    units = out_ref.shape[0]
    slots, tile = tiles_ref.shape[1], tiles_ref.shape[2]
    per = tile // LANES
    edge = REACH * per
    if len(here_ref.shape) == 2:
        for k in range(edge):
            ext[k] = before_ref[:, k * LANES : (k + 1) * LANES]
            ext[edge + units + k] = after_ref[:, k * LANES : (k + 1) * LANES]
        for k in range(units):
            ext[edge + k] = here_ref[:, k * LANES : (k + 1) * LANES]
    else:
        ext[0:edge] = before_ref[...]
        ext[edge + units : 2 * edge + units] = after_ref[...]
        ext[edge : edge + units] = here_ref[...]
    out_ref[...] = jnp.zeros_like(out_ref)
    for s in range(slots):

        @pl.when(s < count_ref[0])
        def _(s=s):
            code = pairs_ref[s]
            target = lax.div(code, SPAN)
            source = target + lax.rem(code, SPAN)
            rows = jnp.concatenate([ext[source * per + k] for k in range(per)], axis=-1)
            value = complex_dot(dot_nt, rows, tiles_ref[0, s], tiles_ref[1, s], fields)
            for k in range(per):
                out_ref[target * per + k] += value[:, k * LANES : (k + 1) * LANES]


def far_kernel(
    fields, items, width, target_ref, offset_ref, leaf_ref, item_ref, partial_ref, exp_ref, trans_ref,
    out_ref, total, exp_buf, trans_buf, sem,
):
    count = leaf_ref.shape[1]
    windows, copies = [], []
    for i in range(items):
        trans_copy = pltpu.make_async_copy(trans_ref.at[offset_ref[i]], trans_buf.at[i], sem.at[i, 0])
        trans_copy.start()
        start, end, unit = leaf_window(leaf_ref, target_ref[i], count, width)
        first = pl.multiple_of(unit * LANES, LANES)
        exp_copy = pltpu.make_async_copy(
            exp_ref.at[:, pl.ds(first, width * LANES), :], exp_buf.at[i], sem.at[i, 1]
        )
        exp_copy.start()
        windows.append((start, end, unit))
        copies.append((trans_copy, exp_copy))
    total[...] = partial_ref[...]
    for i in range(items):
        start, end, unit = windows[i]
        copies[i][0].wait()
        local_field = complex_dot(dot_nn, item_ref[i], trans_buf[i, 0], trans_buf[i, 1], fields)
        copies[i][1].wait()
        image = complex_dot(dot_nt, local_field.astype(BF16), exp_buf[i, 0], exp_buf[i, 1], fields)
        image = jnp.where(window_mask(start, end, unit, 2 * fields, width), image, 0.0)
        for k in range(width):
            total[unit + k] += image[:, k * LANES : (k + 1) * LANES]
    out_ref[...] = total[...].astype(out_ref.dtype)


def final_kernel(fields, coef_ref, right_ref, image_ref, out_ref):
    units = image_ref.shape[0]
    a_real, a_imag, b_real, b_imag = [coef_ref[:, k : k + 1] for k in range(4)]
    for k in range(units):
        lanes = slice(k * LANES, (k + 1) * LANES)
        r_real, r_imag = right_ref[:fields, lanes], right_ref[fields:, lanes]
        z_real = image_ref[k, :fields].astype(F32)
        z_imag = image_ref[k, fields:].astype(F32)
        out_ref[:fields, lanes] = a_real * r_real - a_imag * r_imag + b_real * z_real - b_imag * z_imag
        out_ref[fields:, lanes] = a_real * r_imag + a_imag * r_real + b_real * z_imag + b_imag * z_real


def params():
    return pltpu.CompilerParams(vmem_limit_bytes=16 * 1024 * 1024)


def item_route(rows, group, columns, send):
    items = rows * send // group

    def flat(r, g):
        return (g // columns * rows + r) * columns + g % columns

    if items >= send:
        steps = items // send
        routes = []
        for t in range(steps):
            pairs = []
            for r in range(rows):
                for g in range(group):
                    d = g * steps + (t + r) % steps
                    pairs.append((flat(r, g), flat(d, r // steps)))
            routes.append(pairs)
        return items, steps, routes
    pairs = []
    for r in range(rows):
        for g in range(group):
            d, j = g // send, g % send
            pairs.append((flat(r, g), flat(d, r * send + j)))
    return items, 1, [pairs]


def local(
    right_side,
    near_tiles,
    tile_pairs,
    tile_count,
    panel_expansions,
    leaf_of_panel,
    far_pick,
    far_target,
    far_offset,
    translations,
):
    fields, panels = right_side.shape[1:]
    coefs = panel_expansions.shape[2]
    tile = near_tiles.shape[2]
    send = far_pick.shape[2]
    rows = lax.axis_size("row")
    group = lax.axis_size("grp") * lax.axis_size("col")
    row_here = lax.axis_index("row")
    own = lax.axis_index("grp") * lax.axis_size("col") + lax.axis_index("col")
    both = 2 * fields
    units = panels // LANES
    share = -(-units // group)
    edge = REACH * tile
    edge_units = edge // LANES
    width = tile // LANES + 1
    items, steps, routes = item_route(rows, group, lax.axis_size("col"), send)

    right = right_side.reshape(both, panels)
    picks = lax.dynamic_slice_in_dim(
        lax.dynamic_index_in_dim(far_pick, row_here, 1, keepdims=False).reshape(-1), own * items, items
    )
    targets = lax.dynamic_slice_in_dim(far_target[0], own * items, items)
    offsets = lax.dynamic_slice_in_dim(far_offset[0], own * items, items)
    up = [(i, (i + 1) % rows) for i in range(rows)]
    down = [(j, i) for i, j in up]

    def multipoles(low):
        return pl.pallas_call(
            functools.partial(multi_kernel, fields, items, width),
            out_shape=jax.ShapeDtypeStruct((items, both, coefs), BF16),
            in_specs=[SMEM, SMEM, VMEM, ANY],
            out_specs=VMEM,
            scratch_shapes=[
                pltpu.VMEM((items, 2, width * LANES, coefs), BF16),
                pltpu.SemaphoreType.DMA((items,)),
            ],
            compiler_params=params(),
            cost_estimate=pl.CostEstimate(
                flops=8 * items * fields * width * LANES * coefs,
                bytes_accessed=4 * items * width * LANES * coefs,
                transcendentals=0,
            ),
            name="multi",
        )(picks, leaf_of_panel, low, panel_expansions)

    def exchanged(made):
        if items < send:
            return lax.ppermute(made, EVERY, routes[0])
        taken = jnp.zeros_like(made)
        for t in range(steps):
            outgoing = lax.dynamic_slice_in_dim(made, lax.rem(t + row_here, steps) * send, send)
            arrived = lax.ppermute(outgoing, EVERY, routes[t])
            place = lax.rem(row_here - t + steps, steps) * send
            taken = lax.dynamic_update_slice_in_dim(taken, arrived, place, 0)
        return taken

    def near(before, low, after):
        low_units = (units + 2 * edge_units, both, LANES)
        return pl.pallas_call(
            functools.partial(near_kernel, fields),
            out_shape=jax.ShapeDtypeStruct((units, both, LANES), F32),
            in_specs=[SMEM, SMEM, VMEM, VMEM, VMEM, VMEM],
            out_specs=VMEM,
            scratch_shapes=[pltpu.VMEM(low_units, low.dtype)],
            compiler_params=params(),
            cost_estimate=pl.CostEstimate(
                flops=8 * fields * near_tiles.size // 2,
                bytes_accessed=2 * near_tiles.size,
                transcendentals=0,
            ),
            name="near",
        )(tile_pairs, tile_count, before, low, after, near_tiles)

    def far_added(taken, partial, dtype):
        return pl.pallas_call(
            functools.partial(far_kernel, fields, items, width),
            out_shape=jax.ShapeDtypeStruct((units, both, LANES), dtype),
            in_specs=[SMEM, SMEM, SMEM, VMEM, VMEM, ANY, ANY],
            out_specs=VMEM,
            scratch_shapes=[
                pltpu.VMEM((units, both, LANES), F32),
                pltpu.VMEM((items, 2, width * LANES, coefs), BF16),
                pltpu.VMEM((items, 2, coefs, coefs), BF16),
                pltpu.SemaphoreType.DMA((items, 2)),
            ],
            compiler_params=params(),
            name="far",
        )(targets, offsets, leaf_of_panel, taken, partial, panel_expansions, translations)

    def image_share(low, first, last, dtype):
        before = lax.ppermute(last, "row", up)
        after = lax.ppermute(first, "row", down)
        taken = exchanged(multipoles(low))
        partial = near(before, low, after)
        summands = far_added(taken, partial, dtype)
        summands = jnp.pad(summands, ((0, share * group - units), (0, 0), (0, 0)))
        parts = lax.all_to_all(summands, GROUP, 0, 0, tiled=True)
        return jnp.sum(parts.reshape(group, share, both, LANES).astype(F32), axis=0)

    def inner(left, right_one):
        l_real, l_imag = left[:, :fields], left[:, fields:]
        r_real, r_imag = right_one[:, :fields], right_one[:, fields:]
        real_part = jnp.sum(l_real * r_real + l_imag * r_imag, axis=(0, 2))
        imag_part = jnp.sum(l_real * r_imag - l_imag * r_real, axis=(0, 2))
        return real_part, imag_part

    z_share = image_share(right, right[:, :edge], right[:, panels - edge :], F32)
    z_low = z_share.astype(BF16)
    spread = jnp.broadcast_to(z_low[None], (group, share, both, LANES)).reshape(group * share, both, LANES)
    z_all = lax.all_to_all(spread, GROUP, 0, 0, tiled=True)[:units]
    q_share = image_share(z_all, z_all[:edge_units], z_all[units - edge_units :], BF16)

    right_units = jnp.pad(
        right.reshape(both, units, LANES), ((0, 0), (0, share * group - units), (0, 0))
    )
    r_share = lax.dynamic_slice_in_dim(right_units, own * share, share, 1).transpose(1, 0, 2)
    rr, _ = inner(r_share, r_share)
    rz_real, rz_imag = inner(r_share, z_share)
    zz, _ = inner(z_share, z_share)
    rq_real, rq_imag = inner(r_share, q_share)
    zq_real, zq_imag = inner(z_share, q_share)
    qq, _ = inner(q_share, q_share)
    sums = jnp.stack([rr, rz_real, rz_imag, zz, rq_real, rq_imag, zq_real, zq_imag, qq])
    devices = group * rows
    sums = jnp.broadcast_to(sums.reshape(1, -1), (devices, sums.size))
    sums = jnp.sum(lax.all_to_all(sums, EVERY, 0, 0, tiled=True), axis=0).reshape(9, fields)
    coef = krylov_coefficients(sums)
    coef = jnp.stack(coef, axis=1)
    out = pl.pallas_call(
        functools.partial(final_kernel, fields),
        out_shape=jax.ShapeDtypeStruct((both, panels), F32),
        in_specs=[VMEM, VMEM, VMEM],
        out_specs=VMEM,
        compiler_params=params(),
        name="combine",
    )(coef, right, z_all)
    return out.reshape(right_side.shape)


def krylov_coefficients(sums):
    rr, rz_real, rz_imag, zz, rq_real, rq_imag, zq_real, zq_imag, qq = [sums[k] for k in range(9)]

    def times(left, right):
        return left[0] * right[0] - left[1] * right[1], left[0] * right[1] + left[1] * right[0]

    def conj_times(left, right):
        return left[0] * right[0] + left[1] * right[1], left[0] * right[1] - left[1] * right[0]

    def scale(factor, value):
        return factor * value[0], factor * value[1]

    def plus(*values):
        return sum(v[0] for v in values), sum(v[1] for v in values)

    def size(value):
        return value[0] * value[0] + value[1] * value[1]

    rz, rq, zq = (rz_real, rz_imag), (rq_real, rq_imag), (zq_real, zq_imag)
    beta = jnp.sqrt(rr + EPSILON)
    inv = 1.0 / beta
    norm_one = rr * inv * inv
    product = scale(inv * inv, rz)
    h_first = (0.5 * norm_one + product[0], product[1])
    shift = (h_first[0] - 0.5, h_first[1])
    residue = zz * inv * inv - 2.0 * conj_times(shift, product)[0] + size(shift) * norm_one
    residue = jnp.maximum(residue, 0.0)
    h_sub = jnp.sqrt(residue + EPSILON)
    alpha = inv / h_sub
    gamma = scale(-alpha, shift)
    h_upper = scale(
        inv,
        plus(
            scale(0.5, plus(scale(alpha, rz), scale(rr, gamma))), scale(alpha, rq), times(gamma, rz)
        ),
    )
    second = plus(
        scale(alpha * alpha, zq),
        scale(alpha * zz, gamma),
        scale(alpha, conj_times(gamma, rq)),
        scale(size(gamma), rz),
    )
    h_middle = (0.5 * residue / (h_sub * h_sub) + second[0], second[1])
    keep = (h_middle[0] - 0.5, h_middle[1])
    on_z = plus(gamma, scale(-alpha, keep))
    on_r = plus(scale(-inv, h_upper), scale(-1.0, times(keep, gamma)))
    last = (
        alpha * alpha * qq
        + size(on_z) * zz
        + size(on_r) * rr
        + 2.0
        * (
            conj_times(on_r, times(on_z, rz))[0]
            + alpha * conj_times(on_r, rq)[0]
            + alpha * conj_times(on_z, zq)[0]
        )
    )
    h_last = jnp.sqrt(jnp.maximum(last, 0.0) + EPSILON)
    radius = jnp.sqrt(size(h_first) + h_sub * h_sub)
    cosine = scale(1.0 / radius, h_first)
    sine = h_sub / radius
    upper = plus(conj_times(cosine, h_upper), scale(sine, h_middle))
    lower = plus(times(cosine, h_middle), scale(-sine, h_upper))
    radius_two = jnp.sqrt(size(lower) + h_last * h_last)
    cosine_two = scale(1.0 / radius_two, lower)
    weight_two = scale(-sine * beta / radius_two, (cosine_two[0], -cosine_two[1]))
    goal = scale(beta, (cosine[0], -cosine[1]))
    weight_one = scale(1.0 / radius, plus(goal, scale(-1.0, times(upper, weight_two))))
    on_right = plus(scale(inv, weight_one), times(weight_two, gamma))
    on_image = scale(alpha, weight_two)
    return on_right[0], on_right[1], on_image[0], on_image[1]


def solution(mesh):
    return jax.shard_map(
        local,
        mesh=mesh,
        in_specs=(
            P(None, None, "row"),
            P(None, ("grp", "row", "col"), None, None),
            P(("grp", "row", "col")),
            P(("grp", "row", "col")),
            P(None, "row", None),
            P("row", None),
            P(),
            P("row", None),
            P("row", None),
            P(),
        ),
        out_specs=P(None, None, "row"),
        check_vma=False,
    )
```

```python
import functools

import jax
import jax.numpy as jnp
from jax import lax
from jax.experimental import pallas as pl
from jax.experimental.pallas import tpu as pltpu
from jax.sharding import PartitionSpec as P

REACH = 2
SPAN = 2 * REACH + 1
LANES = 128
EPSILON = 1e-06
GROUP = ("grp", "col")
EVERY = ("grp", "row", "col")

F32 = jnp.float32
BF16 = jnp.bfloat16
SMEM = pl.BlockSpec(memory_space=pltpu.SMEM)
VMEM = pl.BlockSpec(memory_space=pltpu.VMEM)
HBM = pl.BlockSpec(memory_space=pltpu.HBM)


def dot_nn(left, right):
    return lax.dot_general(left, right, (((1,), (0,)), ((), ())), preferred_element_type=F32)


def dot_nt(left, right):
    return lax.dot_general(left, right, (((1,), (1,)), ((), ())), preferred_element_type=F32)


def halves(rows):
    if rows.dtype != F32:
        return rows
    high = rows.astype(BF16)
    return jnp.concatenate([high, (rows - high.astype(F32)).astype(BF16)], axis=0)


def joined(sums, count):
    return sums if sums.shape[0] == count else sums[:count] + sums[count:]


def odd_lanes(shape):
    return lax.rem(lax.broadcasted_iota(jnp.int32, shape, 1), 2) == 1


def from_left(value):
    return pltpu.roll(value, 1, 1)


def from_right(value):
    return pltpu.roll(value, value.shape[1] - 1, 1)


def lower_bound(leaf_ref, value, count):
    def halve(_, bounds):
        low, high = bounds
        middle = lax.div(low + high, 2)
        below = leaf_ref[0, jnp.minimum(middle, count - 1)] < value
        go_up = jnp.logical_and(below, low < high)
        return (jnp.where(go_up, middle + 1, low), jnp.where(go_up, high, jnp.minimum(middle, high)))

    low, _ = lax.fori_loop(0, count.bit_length(), halve, (jnp.int32(0), jnp.int32(count)))
    return low


def leaf_window(leaf_ref, leaf, count, width):
    start = lower_bound(leaf_ref, leaf, count)
    end = lower_bound(leaf_ref, leaf + 1, count)
    unit = jnp.minimum(lax.div(start, LANES), count // LANES - width)
    return start, end, unit


def window_mask(start, end, unit, rows, width):
    lane = lax.broadcasted_iota(jnp.int32, (rows, width * LANES), 1) + unit * LANES
    return jnp.logical_and(lane >= start, lane < end)


def multi_rows(fields, width, item, range_ref, low_ref, window_ref):
    start, end, unit = range_ref[item, 0], range_ref[item, 1], range_ref[item, 2]
    if len(low_ref.shape) == 2:
        first = pl.multiple_of(unit * LANES, LANES)
        rows = low_ref[:, pl.ds(first, width * LANES)]
    else:
        rows = jnp.concatenate([low_ref[unit + k] for k in range(width)], axis=-1)
    mask = window_mask(start, end, unit, 2 * fields, width)
    rows = halves(jnp.where(mask, rows.astype(F32), 0.0).astype(rows.dtype))
    total = None
    for k in range(width):
        part = dot_nt(rows[:, k * LANES : (k + 1) * LANES], as_rows(window_ref.at[item, k]))
        total = part if total is None else total + part
    total = joined(total, 2 * fields)
    on_real, on_imag = total[:fields], total[fields:]
    odd = odd_lanes(on_real.shape)
    other = jnp.where(odd, from_left(on_imag), from_right(on_imag))
    return jnp.where(odd, -on_real, on_real) - other


def as_rows(ref):
    return ref.reshape(ref.shape[0] * 2, ref.shape[2])[...]


def first_multi_kernel(
    fields, items, width, pick_ref, target_ref, leaf_ref, low_ref, exp_ref,
    out_ref, range_ref, target_range_ref, window_ref, target_window_ref, spread_ref, sem,
):
    count = leaf_ref.shape[1]
    coefs = exp_ref.shape[0]
    copies = []
    for i in range(items):
        for which, leaf, ranges, window in (
            (0, pick_ref[i], range_ref, window_ref),
            (1, target_ref[i], target_range_ref, target_window_ref),
        ):
            start, end, unit = leaf_window(leaf_ref, leaf, count, width)
            ranges[i, 0], ranges[i, 1], ranges[i, 2] = start, end, unit
            for k in range(width):
                first = pl.multiple_of((unit + k) * LANES, LANES)
                copy = pltpu.make_async_copy(
                    exp_ref.at[:, :, pl.ds(first, LANES)],
                    window.at[i, k, pl.ds(0, coefs)],
                    sem.at[i, which, k],
                )
                copy.start()
                copies.append((which, copy))
                rest = window.shape[2] - coefs
                window[i, k, pl.ds(coefs, rest)] = jnp.zeros((rest, 2, LANES), BF16)
    shape = spread_ref.shape
    row = lax.broadcasted_iota(jnp.int32, shape, 0)
    column = lax.broadcasted_iota(jnp.int32, shape, 1)
    spread_ref[...] = jnp.where(column == 2 * row, 1.0, 0.0).astype(BF16)
    for which, copy in copies:
        if which == 0:
            copy.wait()
    for i in range(items):
        out_ref[i] = multi_rows(fields, width, i, range_ref, low_ref, window_ref).astype(BF16)
    for which, copy in copies:
        if which == 1:
            copy.wait()


def multi_kernel(fields, items, width, range_ref, low_ref, window_ref, out_ref):
    for i in range(items):
        out_ref[i] = multi_rows(fields, width, i, range_ref, low_ref, window_ref).astype(BF16)


def near_kernel(fields, pairs_ref, count_ref, before_ref, here_ref, after_ref, tiles_ref, out_ref, ext):
    units = out_ref.shape[0]
    slots, tile = tiles_ref.shape[1], tiles_ref.shape[2]
    per = tile // LANES
    edge = REACH * per
    if len(here_ref.shape) == 2:
        for k in range(edge):
            ext[k] = before_ref[:, k * LANES : (k + 1) * LANES]
            ext[edge + units + k] = after_ref[:, k * LANES : (k + 1) * LANES]
        for k in range(units):
            ext[edge + k] = here_ref[:, k * LANES : (k + 1) * LANES]
    else:
        ext[0:edge] = before_ref[...]
        ext[edge + units : 2 * edge + units] = after_ref[...]
        ext[edge : edge + units] = here_ref[...]
    out_ref[...] = jnp.zeros_like(out_ref)
    for s in range(slots):
        code = pairs_ref[s]
        target = lax.div(code, SPAN)
        source = target + lax.rem(code, SPAN)
        rows = halves(jnp.concatenate([ext[source * per + k] for k in range(per)], axis=-1))
        on_real = joined(dot_nt(rows, tiles_ref[0, s]), 2 * fields)
        on_imag = joined(dot_nt(rows, tiles_ref[1, s]), 2 * fields)
        value = jnp.concatenate(
            [on_real[:fields] - on_imag[fields:], on_real[fields:] + on_imag[:fields]], axis=0
        )
        value = jnp.where(s < count_ref[0], value, 0.0)
        for k in range(per):
            out_ref[target * per + k] += value[:, k * LANES : (k + 1) * LANES]


def far_kernel(
    fields, items, width, core_ref, range_ref, item_ref, partial_ref, trans_ref, spread_ref, window_ref,
    keep_ref, give_ref, total,
):
    units = partial_ref.shape[0]
    total[0:units] = partial_ref[...]
    if total.shape[0] > units:
        total[units:] = jnp.zeros((total.shape[0] - units, *total.shape[1:]), F32)
    for i in range(items):
        start, end, unit = range_ref[i, 0], range_ref[i, 1], range_ref[i, 2]
        plain = item_ref[i].astype(F32)
        odd = odd_lanes(plain.shape)
        turned = jnp.where(odd, from_left(plain), -from_right(plain))
        rows = jnp.concatenate([plain, turned], axis=0).astype(BF16)
        local_field = dot_nn(rows, trans_ref[i]).astype(BF16)
        apart = dot_nn(local_field, spread_ref[...])
        local_real, local_imag = apart[:fields], apart[fields:]
        rows = jnp.concatenate(
            [local_real - from_left(local_imag), local_imag + from_left(local_real)], axis=0
        ).astype(BF16)
        mask = window_mask(start, end, unit, 2 * fields, width)
        for k in range(width):
            image = dot_nn(rows, as_rows(window_ref.at[i, k]))
            total[unit + k] += jnp.where(mask[:, k * LANES : (k + 1) * LANES], image, 0.0)
    chips, share = keep_ref.shape[:2]
    core = core_ref[0]
    for c in range(chips):
        keep_ref[c] = total[pl.ds((2 * c + core) * share, share)].astype(keep_ref.dtype)
        give_ref[c] = total[pl.ds((2 * c + 1 - core) * share, share)].astype(give_ref.dtype)


def fold_kernel(chip_ref, keep_ref, got_ref, own_ref, *out_refs):
    for step, out_ref in enumerate((own_ref,) + out_refs):
        chip = lax.bitwise_xor(chip_ref[0], step)
        out_ref[...] = (keep_ref[chip].astype(F32) + got_ref[chip].astype(F32)).astype(out_ref.dtype)


def assemble_kernel(core_ref, chip_ref, mine_ref, theirs_ref, out_ref, first_ref, last_ref, whole):
    chips, share = mine_ref.shape[:2]
    units, edge = out_ref.shape[0], first_ref.shape[0]
    core = core_ref[0]
    for step in range(chips):
        chip = lax.bitwise_xor(chip_ref[0], step)
        whole[pl.ds((2 * chip + core) * share, share)] = mine_ref[step]
        whole[pl.ds((2 * chip + 1 - core) * share, share)] = theirs_ref[step]
    out_ref[...] = whole[0:units]
    first_ref[...] = whole[0:edge]
    last_ref[...] = whole[units - edge : units]


def final_kernel(fields, coef_ref, right_ref, image_ref, out_ref):
    units = image_ref.shape[0]
    a_real, a_imag, b_real, b_imag = [coef_ref[:, k : k + 1] for k in range(4)]
    for k in range(units):
        lanes = slice(k * LANES, (k + 1) * LANES)
        r_real, r_imag = right_ref[:fields, lanes], right_ref[fields:, lanes]
        z_real = image_ref[k, :fields].astype(F32)
        z_imag = image_ref[k, fields:].astype(F32)
        out_ref[:fields, lanes] = a_real * r_real - a_imag * r_imag + b_real * z_real - b_imag * z_imag
        out_ref[fields:, lanes] = a_real * r_imag + a_imag * r_real + b_real * z_imag + b_imag * z_real


def params(mebibytes=16):
    return pltpu.CompilerParams(vmem_limit_bytes=mebibytes * 1024 * 1024)


def item_route(rows, group, columns, send):
    items = rows * send // group

    def flat(r, g):
        return (g // columns * rows + r) * columns + g % columns

    if items >= send:
        steps = items // send
        routes = []
        for t in range(steps):
            pairs = []
            for r in range(rows):
                for g in range(group):
                    d = g * steps + (t + r) % steps
                    pairs.append((flat(r, g), flat(d, r // steps)))
            routes.append(pairs)
        return items, steps, routes
    pairs = []
    for r in range(rows):
        for g in range(group):
            d, j = g // send, g % send
            pairs.append((flat(r, g), flat(d, r * send + j)))
    return items, 1, [pairs]


def local(
    right_side,
    near_tiles,
    tile_pairs,
    tile_count,
    panel_expansions,
    leaf_of_panel,
    far_pick,
    far_target,
    far_offset,
    translations,
):
    fields, panels = right_side.shape[1:]
    coefs = panel_expansions.shape[2]
    tile = near_tiles.shape[2]
    send = far_pick.shape[2]
    rows = lax.axis_size("row")
    group = lax.axis_size("grp") * lax.axis_size("col")
    row_here = lax.axis_index("row")
    own = lax.axis_index("grp") * lax.axis_size("col") + lax.axis_index("col")
    both = 2 * fields
    units = panels // LANES
    share = -(-units // group)
    edge = REACH * tile
    edge_units = edge // LANES
    width = tile // LANES + 1
    items, steps, routes = item_route(rows, group, lax.axis_size("col"), send)

    right = right_side.reshape(both, panels)
    picks = lax.dynamic_slice_in_dim(
        lax.dynamic_index_in_dim(far_pick, row_here, 1, keepdims=False).reshape(-1), own * items, items
    )
    targets = lax.dynamic_slice_in_dim(far_target[0], own * items, items)
    offsets = lax.dynamic_slice_in_dim(far_offset[0], own * items, items)
    up = [(i, (i + 1) % rows) for i in range(rows)]
    down = [(j, i) for i, j in up]

    pad_coefs = -(-coefs // 8) * 8
    core, chip = lax.rem(own, 2).reshape(1), lax.div(own, 2).reshape(1)
    chips = group // 2
    steps_between = range(1, chips)
    assert group == 2 * chips and chips & (chips - 1) == 0
    window_shape = jax.ShapeDtypeStruct((items, width, pad_coefs, 2, LANES), BF16)
    item_shape = jax.ShapeDtypeStruct((items, fields, 2 * pad_coefs), BF16)
    range_shape = jax.ShapeDtypeStruct((items, 3), jnp.int32)
    part_shape = (share, both, LANES)

    def first_multipoles(low):
        return pl.pallas_call(
            functools.partial(first_multi_kernel, fields, items, width),
            out_shape=(
                item_shape,
                range_shape,
                range_shape,
                window_shape,
                window_shape,
                jax.ShapeDtypeStruct((coefs, 2 * pad_coefs), BF16),
            ),
            in_specs=[SMEM, SMEM, SMEM, VMEM, HBM],
            out_specs=(VMEM, SMEM, SMEM, VMEM, VMEM, VMEM),
            scratch_shapes=[pltpu.SemaphoreType.DMA((items, 2, width))],
            compiler_params=params(58),
            name="first_multi",
        )(picks, targets, leaf_of_panel, low, panel_expansions.transpose(2, 0, 1))

    def multipoles(low, ranges, windows):
        return pl.pallas_call(
            functools.partial(multi_kernel, fields, items, width),
            out_shape=item_shape,
            in_specs=[SMEM, VMEM, VMEM],
            out_specs=VMEM,
            compiler_params=params(),
            name="multi",
        )(ranges, low, windows)

    def exchanged(made):
        if items < send:
            return lax.ppermute(made, EVERY, routes[0])
        taken = jnp.zeros_like(made)
        for t in range(steps):
            outgoing = lax.dynamic_slice_in_dim(made, lax.rem(t + row_here, steps) * send, send)
            arrived = lax.ppermute(outgoing, EVERY, routes[t])
            place = lax.rem(row_here - t + steps, steps) * send
            taken = lax.dynamic_update_slice_in_dim(taken, arrived, place, 0)
        return taken

    def near(before, low, after):
        low_units = (units + 2 * edge_units, both, LANES)
        return pl.pallas_call(
            functools.partial(near_kernel, fields),
            out_shape=jax.ShapeDtypeStruct((units, both, LANES), F32),
            in_specs=[SMEM, SMEM, VMEM, VMEM, VMEM, VMEM],
            out_specs=VMEM,
            scratch_shapes=[pltpu.VMEM(low_units, low.dtype)],
            compiler_params=params(),
            cost_estimate=pl.CostEstimate(
                flops=8 * fields * near_tiles.size // 2,
                bytes_accessed=2 * near_tiles.size,
                transcendentals=0,
            ),
            name="near",
        )(tile_pairs, tile_count, before, low, after, near_tiles)

    def swapped(value, step):
        return lax.ppermute(value, GROUP, [(g, g ^ step) for g in range(group)])

    def reduced_share(taken, partial, dtype):
        half_shape = jax.ShapeDtypeStruct((chips, *part_shape), dtype)
        keep, give = pl.pallas_call(
            functools.partial(far_kernel, fields, items, width),
            out_shape=(half_shape, half_shape),
            in_specs=[SMEM, SMEM, VMEM, VMEM, VMEM, VMEM, VMEM],
            out_specs=(VMEM, VMEM),
            scratch_shapes=[pltpu.VMEM((share * group, both, LANES), F32)],
            compiler_params=params(),
            name="far",
        )(core, target_ranges, taken, partial, moved, spread, target_windows)
        got = swapped(give, 1)
        pieces = pl.pallas_call(
            fold_kernel,
            out_shape=(jax.ShapeDtypeStruct(part_shape, F32),)
            + (jax.ShapeDtypeStruct(part_shape, dtype),) * (chips - 1),
            in_specs=[SMEM, VMEM, VMEM],
            out_specs=(VMEM,) * chips,
            compiler_params=params(),
            name="fold",
        )(chip, keep, got)
        total = pieces[0]
        for step in steps_between:
            total = total + swapped(pieces[step], 2 * step).astype(F32)
        return total

    def gathered(low):
        mine = jnp.stack([low] + [swapped(low, 2 * step) for step in steps_between])
        theirs = swapped(mine, 1)
        edge_shape = jax.ShapeDtypeStruct((edge_units, both, LANES), BF16)
        return pl.pallas_call(
            assemble_kernel,
            out_shape=(jax.ShapeDtypeStruct((units, both, LANES), BF16), edge_shape, edge_shape),
            in_specs=[SMEM, SMEM, VMEM, VMEM],
            out_specs=(VMEM, VMEM, VMEM),
            scratch_shapes=[pltpu.VMEM((share * group, both, LANES), BF16)],
            compiler_params=params(),
            name="assemble",
        )(core, chip, mine, theirs)

    def inner(left, right_one):
        l_real, l_imag = left[:, :fields], left[:, fields:]
        r_real, r_imag = right_one[:, :fields], right_one[:, fields:]
        real_part = jnp.sum(l_real * r_real + l_imag * r_imag, axis=(0, 2))
        imag_part = jnp.sum(l_real * r_imag - l_imag * r_real, axis=(0, 2))
        return real_part, imag_part

    moved = translations.transpose(0, 2, 1, 3)
    moved = [lax.dynamic_index_in_dim(moved, offsets[i], 0, keepdims=False) for i in range(items)]
    moved = jnp.pad(jnp.stack(moved), ((0, 0), (0, pad_coefs - coefs), (0, 0), (0, 0)))
    moved = moved.reshape(items, 2 * pad_coefs, coefs)

    before = lax.ppermute(right[:, panels - edge :], "row", up)
    after = lax.ppermute(right[:, :edge], "row", down)
    made, ranges, target_ranges, windows, target_windows, spread = first_multipoles(right)
    taken = exchanged(made)
    z_share = reduced_share(taken, near(before, right, after), F32)
    z_all, first, last = gathered(z_share.astype(BF16))
    before = lax.ppermute(last, "row", up)
    after = lax.ppermute(first, "row", down)
    taken = exchanged(multipoles(z_all, ranges, windows))
    q_share = reduced_share(taken, near(before, z_all, after), BF16)

    right_units = jnp.pad(
        right.reshape(both, units, LANES), ((0, 0), (0, share * group - units), (0, 0))
    )
    r_share = lax.dynamic_slice_in_dim(right_units, own * share, share, 1).transpose(1, 0, 2)
    rr, _ = inner(r_share, r_share)
    rz_real, rz_imag = inner(r_share, z_share)
    zz, _ = inner(z_share, z_share)
    rq_real, rq_imag = inner(r_share, q_share)
    zq_real, zq_imag = inner(z_share, q_share)
    qq, _ = inner(q_share, q_share)
    sums = jnp.stack([rr, rz_real, rz_imag, zz, rq_real, rq_imag, zq_real, zq_imag, qq])
    devices = group * rows
    sums = jnp.broadcast_to(sums.reshape(1, -1), (devices, sums.size))
    sums = jnp.sum(lax.all_to_all(sums, EVERY, 0, 0, tiled=True), axis=0).reshape(9, fields)
    coef = krylov_coefficients(sums)
    coef = jnp.stack(coef, axis=1)
    out = pl.pallas_call(
        functools.partial(final_kernel, fields),
        out_shape=jax.ShapeDtypeStruct((both, panels), F32),
        in_specs=[VMEM, VMEM, VMEM],
        out_specs=VMEM,
        compiler_params=params(),
        name="combine",
    )(coef, right, z_all)
    return out.reshape(right_side.shape)


def krylov_coefficients(sums):
    rr, rz_real, rz_imag, zz, rq_real, rq_imag, zq_real, zq_imag, qq = [sums[k] for k in range(9)]

    def times(left, right):
        return left[0] * right[0] - left[1] * right[1], left[0] * right[1] + left[1] * right[0]

    def conj_times(left, right):
        return left[0] * right[0] + left[1] * right[1], left[0] * right[1] - left[1] * right[0]

    def scale(factor, value):
        return factor * value[0], factor * value[1]

    def plus(*values):
        return sum(v[0] for v in values), sum(v[1] for v in values)

    def size(value):
        return value[0] * value[0] + value[1] * value[1]

    rz, rq, zq = (rz_real, rz_imag), (rq_real, rq_imag), (zq_real, zq_imag)
    beta = jnp.sqrt(rr + EPSILON)
    inv = 1.0 / beta
    norm_one = rr * inv * inv
    product = scale(inv * inv, rz)
    h_first = (0.5 * norm_one + product[0], product[1])
    shift = (h_first[0] - 0.5, h_first[1])
    residue = zz * inv * inv - 2.0 * conj_times(shift, product)[0] + size(shift) * norm_one
    residue = jnp.maximum(residue, 0.0)
    h_sub = jnp.sqrt(residue + EPSILON)
    alpha = inv / h_sub
    gamma = scale(-alpha, shift)
    h_upper = scale(
        inv,
        plus(
            scale(0.5, plus(scale(alpha, rz), scale(rr, gamma))), scale(alpha, rq), times(gamma, rz)
        ),
    )
    second = plus(
        scale(alpha * alpha, zq),
        scale(alpha * zz, gamma),
        scale(alpha, conj_times(gamma, rq)),
        scale(size(gamma), rz),
    )
    h_middle = (0.5 * residue / (h_sub * h_sub) + second[0], second[1])
    keep = (h_middle[0] - 0.5, h_middle[1])
    on_z = plus(gamma, scale(-alpha, keep))
    on_r = plus(scale(-inv, h_upper), scale(-1.0, times(keep, gamma)))
    last = (
        alpha * alpha * qq
        + size(on_z) * zz
        + size(on_r) * rr
        + 2.0
        * (
            conj_times(on_r, times(on_z, rz))[0]
            + alpha * conj_times(on_r, rq)[0]
            + alpha * conj_times(on_z, zq)[0]
        )
    )
    h_last = jnp.sqrt(jnp.maximum(last, 0.0) + EPSILON)
    radius = jnp.sqrt(size(h_first) + h_sub * h_sub)
    cosine = scale(1.0 / radius, h_first)
    sine = h_sub / radius
    upper = plus(conj_times(cosine, h_upper), scale(sine, h_middle))
    lower = plus(times(cosine, h_middle), scale(-sine, h_upper))
    radius_two = jnp.sqrt(size(lower) + h_last * h_last)
    cosine_two = scale(1.0 / radius_two, lower)
    weight_two = scale(-sine * beta / radius_two, (cosine_two[0], -cosine_two[1]))
    goal = scale(beta, (cosine[0], -cosine[1]))
    weight_one = scale(1.0 / radius, plus(goal, scale(-1.0, times(upper, weight_two))))
    on_right = plus(scale(inv, weight_one), times(weight_two, gamma))
    on_image = scale(alpha, weight_two)
    return on_right[0], on_right[1], on_image[0], on_image[1]


def solution(mesh):
    return jax.shard_map(
        local,
        mesh=mesh,
        in_specs=(
            P(None, None, "row"),
            P(None, ("grp", "row", "col"), None, None),
            P(("grp", "row", "col")),
            P(("grp", "row", "col")),
            P(None, "row", None),
            P("row", None),
            P(),
            P("row", None),
            P("row", None),
            P(),
        ),
        out_specs=P(None, None, "row"),
        check_vma=False,
    )
```

```python
import functools

import jax
import jax.numpy as jnp
from jax import lax
from jax.experimental import pallas as pl
from jax.experimental.pallas import tpu as pltpu
from jax.sharding import PartitionSpec as P

REACH = 2
SPAN = 2 * REACH + 1
LANES = 128
EPSILON = 1e-06
GROUP = ("grp", "col")
CORE, CHIP, OWN, COUNT, CODES = range(5)
PER_ITEM = 5
EVERY = ("grp", "row", "col")

F32 = jnp.float32
BF16 = jnp.bfloat16
SMEM = pl.BlockSpec(memory_space=pltpu.SMEM)
VMEM = pl.BlockSpec(memory_space=pltpu.VMEM)
HBM = pl.BlockSpec(memory_space=pltpu.HBM)


def dot_nn(left, right):
    return lax.dot_general(left, right, (((1,), (0,)), ((), ())), preferred_element_type=F32)


def dot_nt(left, right):
    return lax.dot_general(left, right, (((1,), (1,)), ((), ())), preferred_element_type=F32)


def halves(rows):
    if rows.dtype != F32:
        return rows
    high = rows.astype(BF16)
    return jnp.concatenate([high, (rows - high.astype(F32)).astype(BF16)], axis=0)


def joined(sums, count):
    return sums if sums.shape[0] == count else sums[:count] + sums[count:]


def odd_lanes(shape):
    return lax.rem(lax.broadcasted_iota(jnp.int32, shape, 1), 2) == 1


def from_left(value):
    return pltpu.roll(value, 1, 1)


def from_right(value):
    return pltpu.roll(value, value.shape[1] - 1, 1)


def item_place(slots, item):
    return CODES + slots + PER_ITEM * item


def window_start(leaf_ref, leaf, width):
    units = leaf_ref.shape[1] // LANES
    before = jnp.int32(0)
    for k in range(units):
        before = before + (leaf_ref[0, k * LANES] < leaf).astype(jnp.int32)
    return jnp.clip(before - 1, 0, units - width)


def window_mask(leaves_ref, leaf, unit, rows, width):
    leaves = jnp.concatenate([leaves_ref[unit + k] for k in range(width)], axis=-1)
    return jnp.broadcast_to(leaves, (rows, width * LANES)) == leaf


def window_copies(exp_ref, unit, window_ref, sem, width):
    coefs = exp_ref.shape[0]
    return [
        pltpu.make_async_copy(exp_ref.at[:, unit + k], window_ref.at[k, pl.ds(0, coefs)], sem.at[k])
        for k in range(width)
    ]


def clear_rest(window_ref, coefs, width):
    rest = window_ref.shape[1] - coefs
    for k in range(width):
        window_ref[k, pl.ds(coefs, rest)] = jnp.zeros((rest, 2, LANES), BF16)


def multi_rows(fields, width, leaf, unit, leaves_ref, low_ref, window_ref):
    if len(low_ref.shape) == 2:
        first = pl.multiple_of(unit * LANES, LANES)
        rows = low_ref[:, pl.ds(first, width * LANES)]
    else:
        rows = jnp.concatenate([low_ref[unit + k] for k in range(width)], axis=-1)
    mask = window_mask(leaves_ref, leaf, unit, 2 * fields, width)
    rows = halves(jnp.where(mask, rows.astype(F32), 0.0).astype(rows.dtype))
    total = None
    for k in range(width):
        part = dot_nt(rows[:, k * LANES : (k + 1) * LANES], as_rows(window_ref.at[k]))
        total = part if total is None else total + part
    total = joined(total, 2 * fields)
    on_real, on_imag = total[:fields], total[fields:]
    odd = odd_lanes(on_real.shape)
    other = jnp.where(odd, from_left(on_imag), from_right(on_imag))
    return jnp.where(odd, -on_real, on_real) - other


def as_rows(ref):
    return ref.reshape(ref.shape[0] * 2, ref.shape[2])[...]


def begin_kernel(
    fields, items, width, send, edge, row_ref, own_ref, count_ref, pick_hbm, leaf_hbm, leaves_hbm, target_hbm,
    offset_hbm, pairs_hbm, right_hbm, exp_ref,
    plan_ref, out_ref, window_ref, leaves_ref, right_ref, first_ref, last_ref,
    pick_ref, leaf_ref, target_ref, offset_ref, pairs_ref, sem, window_sem,
):
    panels = right_ref.shape[1]
    loads = [
        pltpu.make_async_copy(source, place, sem.at[k])
        for k, (source, place) in enumerate(
            (
                (leaf_hbm, leaf_ref),
                (pick_hbm, pick_ref),
                (target_hbm, target_ref),
                (offset_hbm, offset_ref),
                (pairs_hbm, pairs_ref),
                (leaves_hbm, leaves_ref),
                (right_hbm, right_ref),
            )
        )
    ]
    for load in loads:
        load.start()
    for i in range(items):
        clear_rest(window_ref.at[i], exp_ref.shape[0], width)
    slots = pairs_ref.shape[0]
    own = own_ref[0]
    loads[0].wait()
    loads[1].wait()
    for i in range(items):
        outgoing = own * items + i
        leaf = pick_ref[lax.div(outgoing, send), lax.rem(outgoing, send), row_ref[0]]
        unit = window_start(leaf_ref, leaf, width)
        place = item_place(slots, i)
        plan_ref[place], plan_ref[place + 1] = leaf, unit
        for copy in window_copies(exp_ref, unit, window_ref.at[i], window_sem.at[i], width):
            copy.start()
    for load in loads[2:]:
        load.wait()
    first_ref[...] = right_ref[:, :edge]
    last_ref[...] = right_ref[:, panels - edge :]
    plan_ref[CORE], plan_ref[CHIP], plan_ref[OWN] = lax.rem(own, 2), lax.div(own, 2), own
    plan_ref[COUNT] = count_ref[0]
    for s in range(slots):
        plan_ref[CODES + s] = pairs_ref[s]
    for i in range(items):
        place = item_place(slots, i)
        leaf = target_ref[0, own * items + i]
        plan_ref[place + 2], plan_ref[place + 3] = leaf, window_start(leaf_ref, leaf, width)
        plan_ref[place + 4] = offset_ref[0, own * items + i]
    for i in range(items):
        place = item_place(slots, i)
        leaf, unit = plan_ref[place], plan_ref[place + 1]
        for copy in window_copies(exp_ref, unit, window_ref.at[i], window_sem.at[i], width):
            copy.wait()
        out_ref[i] = multi_rows(fields, width, leaf, unit, leaves_ref, right_ref, window_ref.at[i]).astype(BF16)


def multi_kernel(fields, items, width, slots, plan_ref, leaves_ref, low_ref, window_ref, out_ref):
    for i in range(items):
        place = item_place(slots, i)
        out_ref[i] = multi_rows(
            fields, width, plan_ref[place], plan_ref[place + 1], leaves_ref, low_ref, window_ref.at[i]
        ).astype(BF16)


def first_near_kernel(
    fields, items, width, plan_ref, exp_ref, trans_ref, before_ref, here_ref, after_ref, tiles_ref,
    out_ref, window_ref, moved_ref, spread_ref, ext, trans_buf, sem, trans_sem,
):
    coefs = trans_ref.shape[3]
    slots = tiles_ref.shape[1]

    def trans_copy(i):
        offset = plan_ref[item_place(slots, i) + 4]
        return pltpu.make_async_copy(trans_ref.at[offset], trans_buf.at[i], trans_sem.at[i])

    def exp_copies(i):
        unit = plan_ref[item_place(slots, i) + 3]
        return window_copies(exp_ref, unit, window_ref.at[i], sem.at[i], width)

    for i in range(items):
        trans_copy(i).start()
        for copy in exp_copies(i):
            copy.start()
        clear_rest(window_ref.at[i], coefs, width)
    shape = spread_ref.shape
    row = lax.broadcasted_iota(jnp.int32, shape, 0)
    column = lax.broadcasted_iota(jnp.int32, shape, 1)
    spread_ref[...] = jnp.where(column == 2 * row, 1.0, 0.0).astype(BF16)
    near_kernel(fields, plan_ref, before_ref, here_ref, after_ref, tiles_ref, out_ref, ext)
    rest = moved_ref.shape[1] - 2 * coefs
    for i in range(items):
        trans_copy(i).wait()
        moved_ref[i, pl.ds(0, 2 * coefs)] = trans_buf[i].reshape(2 * coefs, coefs)
        moved_ref[i, pl.ds(2 * coefs, rest)] = jnp.zeros((rest, coefs), BF16)
        for copy in exp_copies(i):
            copy.wait()


def near_kernel(fields, plan_ref, before_ref, here_ref, after_ref, tiles_ref, out_ref, ext):
    units = out_ref.shape[0]
    slots, tile = tiles_ref.shape[1], tiles_ref.shape[2]
    per = tile // LANES
    edge = REACH * per
    if len(here_ref.shape) == 2:
        for k in range(edge):
            ext[k] = before_ref[:, k * LANES : (k + 1) * LANES]
            ext[edge + units + k] = after_ref[:, k * LANES : (k + 1) * LANES]
        for k in range(units):
            ext[edge + k] = here_ref[:, k * LANES : (k + 1) * LANES]
    else:
        ext[0:edge] = before_ref[...]
        ext[edge + units : 2 * edge + units] = after_ref[...]
        ext[edge : edge + units] = here_ref[...]
    out_ref[...] = jnp.zeros_like(out_ref)
    for s in range(slots):
        code = plan_ref[CODES + s]
        target = lax.div(code, SPAN)
        source = target + lax.rem(code, SPAN)
        rows = halves(jnp.concatenate([ext[source * per + k] for k in range(per)], axis=-1))
        on_real = joined(dot_nt(rows, tiles_ref[0, s]), 2 * fields)
        on_imag = joined(dot_nt(rows, tiles_ref[1, s]), 2 * fields)
        value = jnp.concatenate(
            [on_real[:fields] - on_imag[fields:], on_real[fields:] + on_imag[:fields]], axis=0
        )
        value = jnp.where(s < plan_ref[COUNT], value, 0.0)
        for k in range(per):
            out_ref[target * per + k] += value[:, k * LANES : (k + 1) * LANES]


def far_kernel(
    fields, items, width, slots, plan_ref, leaves_ref, item_ref, partial_ref, trans_ref, spread_ref, window_ref,
    keep_ref, give_ref, total,
):
    units = partial_ref.shape[0]
    total[0:units] = partial_ref[...]
    if total.shape[0] > units:
        total[units:] = jnp.zeros((total.shape[0] - units, *total.shape[1:]), F32)
    for i in range(items):
        place = item_place(slots, i)
        leaf, unit = plan_ref[place + 2], plan_ref[place + 3]
        plain = item_ref[i].astype(F32)
        odd = odd_lanes(plain.shape)
        turned = jnp.where(odd, from_left(plain), -from_right(plain))
        rows = jnp.concatenate([plain, turned], axis=0).astype(BF16)
        local_field = dot_nn(rows, trans_ref[i]).astype(BF16)
        apart = dot_nn(local_field, spread_ref[...])
        local_real, local_imag = apart[:fields], apart[fields:]
        rows = jnp.concatenate(
            [local_real - from_left(local_imag), local_imag + from_left(local_real)], axis=0
        ).astype(BF16)
        mask = window_mask(leaves_ref, leaf, unit, 2 * fields, width)
        for k in range(width):
            image = dot_nn(rows, as_rows(window_ref.at[i, k]))
            total[unit + k] += jnp.where(mask[:, k * LANES : (k + 1) * LANES], image, 0.0)
    chips, share = keep_ref.shape[:2]
    core = plan_ref[CORE]
    for c in range(chips):
        keep_ref[c] = total[pl.ds((2 * c + core) * share, share)].astype(keep_ref.dtype)
        give_ref[c] = total[pl.ds((2 * c + 1 - core) * share, share)].astype(give_ref.dtype)


def fold_kernel(plan_ref, keep_ref, got_ref, own_ref, *out_refs):
    for step, out_ref in enumerate((own_ref,) + out_refs):
        chip = lax.bitwise_xor(plan_ref[CHIP], step)
        out_ref[...] = (keep_ref[chip].astype(F32) + got_ref[chip].astype(F32)).astype(out_ref.dtype)


def pair_kernel(keep_ref, got_ref, out_ref):
    out_ref[...] = (keep_ref[...].astype(F32) + got_ref[...].astype(F32)).astype(out_ref.dtype)


def tree_sum(values):
    while len(values) > 1:
        values = [values[k] + values[k + 1] for k in range(0, len(values), 2)]
    return values[0]


def close_kernel(*refs):
    refs[-1][...] = tree_sum([ref[...].astype(F32) for ref in refs[:-1]])


def assemble_kernel(plan_ref, mine_ref, theirs_ref, out_ref, low_ref, first_ref, last_ref, whole):
    chips, share = mine_ref.shape[:2]
    units, edge = out_ref.shape[0], first_ref.shape[0]
    core = plan_ref[CORE]
    for chip in range(chips):
        whole[pl.ds((2 * chip + core) * share, share)] = mine_ref[chip]
        whole[pl.ds((2 * chip + 1 - core) * share, share)] = theirs_ref[chip]
    out_ref[...] = whole[0:units]
    low_ref[...] = whole[0:units].astype(BF16)
    first_ref[...] = whole[0:edge].astype(BF16)
    last_ref[...] = whole[units - edge : units].astype(BF16)


def flat_lines(columns, fields):
    per = LANES // fields
    lines = []
    for first in range(0, len(columns), per):
        some = columns[first : first + per]
        if len(some) < per:
            some = some + [jnp.zeros(((per - len(some)) * fields, 1), F32)]
        square = jnp.broadcast_to(jnp.concatenate(some, axis=0), (LANES, LANES))
        lines.append(jnp.transpose(square)[:1])
    return jnp.concatenate(lines, axis=0)


def columns_of(lines, count, fields):
    per = LANES // fields
    columns = []
    for k in range(lines.shape[0]):
        square = jnp.transpose(jnp.broadcast_to(lines[k : k + 1], (LANES, LANES)))
        columns += [square[j * fields : (j + 1) * fields, :1] for j in range(per)]
    return columns[:count]


def gram_kernel(fields, plan_ref, right_ref, image_ref, *refs):
    out_ref = refs[-1]
    pieces = refs[:-1]
    units = image_ref.shape[0]
    share = pieces[0].shape[0]
    totals = None
    for k in range(share):
        unit = plan_ref[OWN] * share + k
        place = jnp.minimum(unit, units - 1)
        r = right_ref[:, pl.ds(pl.multiple_of(place * LANES, LANES), LANES)]
        z = image_ref[place]
        q = tree_sum([piece[k].astype(F32) for piece in pieces])
        r = jnp.where(unit < units, r, 0.0)
        z = jnp.where(unit < units, z, 0.0)
        (rr, ri), (zr, zi), (qr, qi) = [(v[:fields], v[fields:]) for v in (r, z, q)]
        products = [
            rr * rr + ri * ri,
            rr * zr + ri * zi,
            rr * zi - ri * zr,
            zr * zr + zi * zi,
            rr * qr + ri * qi,
            rr * qi - ri * qr,
            zr * qr + zi * qi,
            zr * qi - zi * qr,
            qr * qr + qi * qi,
        ]
        totals = products if totals is None else [t + p for t, p in zip(totals, products)]
    lines = flat_lines([jnp.sum(t, axis=1, keepdims=True) for t in totals], fields)
    out_ref[...] = jnp.broadcast_to(lines[None], out_ref.shape)


def final_kernel(fields, sums_ref, right_ref, image_ref, out_ref):
    units = image_ref.shape[0]
    sums = columns_of(jnp.sum(sums_ref[...], axis=0), 9, fields)
    a_real, a_imag, b_real, b_imag = [
        jnp.broadcast_to(value, (fields, LANES)) for value in krylov_coefficients(sums)
    ]
    for k in range(units):
        lanes = slice(k * LANES, (k + 1) * LANES)
        r_real, r_imag = right_ref[:fields, lanes], right_ref[fields:, lanes]
        z_real, z_imag = image_ref[k, :fields], image_ref[k, fields:]
        out_ref[:fields, lanes] = a_real * r_real - a_imag * r_imag + b_real * z_real - b_imag * z_imag
        out_ref[fields:, lanes] = a_real * r_imag + a_imag * r_real + b_real * z_imag + b_imag * z_real


def params(mebibytes=16):
    return pltpu.CompilerParams(vmem_limit_bytes=mebibytes * 1024 * 1024)


def item_route(rows, group, columns, send):
    items = rows * send // group

    def flat(r, g):
        return (g // columns * rows + r) * columns + g % columns

    if items >= send:
        steps = items // send
        routes = []
        for t in range(steps):
            pairs = []
            for r in range(rows):
                for g in range(group):
                    d = g * steps + (t + r) % steps
                    pairs.append((flat(r, g), flat(d, r // steps)))
            routes.append(pairs)
        return items, steps, routes
    pairs = []
    for r in range(rows):
        for g in range(group):
            d, j = g // send, g % send
            pairs.append((flat(r, g), flat(d, r * send + j)))
    return items, 1, [pairs]


def local(
    right_side,
    near_tiles,
    tile_pairs,
    tile_count,
    panel_expansions,
    leaf_of_panel,
    far_pick,
    far_target,
    far_offset,
    translations,
):
    fields, panels = right_side.shape[1:]
    coefs = panel_expansions.shape[2]
    tile = near_tiles.shape[2]
    send = far_pick.shape[2]
    rows = lax.axis_size("row")
    group = lax.axis_size("grp") * lax.axis_size("col")
    row_here = lax.axis_index("row")
    own = lax.axis_index("grp") * lax.axis_size("col") + lax.axis_index("col")
    both = 2 * fields
    units = panels // LANES
    share = -(-units // group)
    edge = REACH * tile
    edge_units = edge // LANES
    width = tile // LANES + 1
    items, steps, routes = item_route(rows, group, lax.axis_size("col"), send)

    up = [(i, (i + 1) % rows) for i in range(rows)]
    down = [(j, i) for i, j in up]

    slots = near_tiles.shape[1]
    pad_coefs = -(-coefs // 8) * 8
    chips = group // 2
    steps_between = range(chips - 1, 0, -1)
    assert group == 2 * chips and chips & (chips - 1) == 0 and LANES % fields == 0
    window_shape = jax.ShapeDtypeStruct((items, width, pad_coefs, 2, LANES), BF16)
    item_shape = jax.ShapeDtypeStruct((items, fields, 2 * pad_coefs), BF16)
    plan_shape = jax.ShapeDtypeStruct((item_place(slots, items),), jnp.int32)
    part_shape = (share, both, LANES)

    def in_hbm(value):
        return pltpu.with_memory_space_constraint(value, pltpu.HBM)

    leaves = leaf_of_panel.reshape(units, 1, LANES)
    expansions = panel_expansions.transpose(2, 0, 1).reshape(coefs, 2, units, LANES).transpose(0, 2, 1, 3)
    expansions = in_hbm(expansions)
    moves = in_hbm(translations.transpose(0, 2, 1, 3))
    picks = far_pick.transpose(0, 2, 1)
    edge_shape = jax.ShapeDtypeStruct((both, edge), F32)

    plan, made, windows, leaves, right, first, last = pl.pallas_call(
        functools.partial(begin_kernel, fields, items, width, send, edge),
        out_shape=(
            plan_shape,
            item_shape,
            window_shape,
            jax.ShapeDtypeStruct(leaves.shape, jnp.int32),
            jax.ShapeDtypeStruct((both, panels), F32),
            edge_shape,
            edge_shape,
        ),
        in_specs=[SMEM] * 3 + [HBM] * 8,
        out_specs=(SMEM,) + (VMEM,) * 6,
        scratch_shapes=[
            pltpu.SMEM(value.shape, jnp.int32)
            for value in (picks, leaf_of_panel, far_target, far_offset, tile_pairs)
        ]
        + [pltpu.SemaphoreType.DMA((7,)), pltpu.SemaphoreType.DMA((items, width))],
        compiler_params=params(),
        name="begin",
    )(
        row_here.reshape(1),
        own.reshape(1),
        tile_count,
        in_hbm(picks),
        in_hbm(leaf_of_panel),
        in_hbm(leaves),
        in_hbm(far_target),
        in_hbm(far_offset),
        in_hbm(tile_pairs),
        in_hbm(right_side.reshape(both, panels)),
        expansions,
    )

    def multipoles(low):
        return pl.pallas_call(
            functools.partial(multi_kernel, fields, items, width, slots),
            out_shape=item_shape,
            in_specs=[SMEM, VMEM, VMEM, VMEM],
            out_specs=VMEM,
            compiler_params=params(),
            name="multi",
        )(plan, leaves, low, windows)

    def exchanged(made):
        if items < send:
            return lax.ppermute(made, EVERY, routes[0])
        taken = jnp.zeros_like(made)
        for t in range(steps):
            outgoing = lax.dynamic_slice_in_dim(made, lax.rem(t + row_here, steps) * send, send)
            arrived = lax.ppermute(outgoing, EVERY, routes[t])
            place = lax.rem(row_here - t + steps, steps) * send
            taken = lax.dynamic_update_slice_in_dim(taken, arrived, place, 0)
        return taken

    image_shape = jax.ShapeDtypeStruct((units, both, LANES), F32)
    near_cost = pl.CostEstimate(
        flops=8 * fields * near_tiles.size // 2, bytes_accessed=2 * near_tiles.size, transcendentals=0
    )

    def first_near(before, low, after):
        return pl.pallas_call(
            functools.partial(first_near_kernel, fields, items, width),
            out_shape=(
                image_shape,
                window_shape,
                jax.ShapeDtypeStruct((items, 2 * pad_coefs, coefs), BF16),
                jax.ShapeDtypeStruct((coefs, 2 * pad_coefs), BF16),
            ),
            in_specs=[SMEM] + [HBM] * 2 + [VMEM] * 4,
            out_specs=(VMEM, VMEM, VMEM, VMEM),
            scratch_shapes=[
                pltpu.VMEM((units + 2 * edge_units, both, LANES), low.dtype),
                pltpu.VMEM((items, coefs, 2, coefs), BF16),
                pltpu.SemaphoreType.DMA((items, width)),
                pltpu.SemaphoreType.DMA((items,)),
            ],
            compiler_params=params(24),
            cost_estimate=near_cost,
            name="first_near",
        )(plan, expansions, moves, before, low, after, near_tiles)

    def near(before, low, after):
        return pl.pallas_call(
            functools.partial(near_kernel, fields),
            out_shape=image_shape,
            in_specs=[SMEM, VMEM, VMEM, VMEM, VMEM],
            out_specs=VMEM,
            scratch_shapes=[pltpu.VMEM((units + 2 * edge_units, both, LANES), low.dtype)],
            compiler_params=params(),
            cost_estimate=near_cost,
            name="near",
        )(plan, before, low, after, near_tiles)

    def swapped(value, step):
        return lax.ppermute(value, GROUP, [(g, g ^ step) for g in range(group)])

    def core_parts(taken, partial, dtype):
        half_shape = jax.ShapeDtypeStruct((chips, *part_shape), dtype)
        keep, give = pl.pallas_call(
            functools.partial(far_kernel, fields, items, width, slots),
            out_shape=(half_shape, half_shape),
            in_specs=[SMEM] + [VMEM] * 6,
            out_specs=(VMEM, VMEM),
            scratch_shapes=[pltpu.VMEM((share * group, both, LANES), F32)],
            compiler_params=params(),
            name="far",
        )(plan, leaves, taken, partial, moved, spread, target_windows)
        return keep, swapped(give, 1)

    def whole_sum(keep, got):
        pair = pl.pallas_call(
            pair_kernel,
            out_shape=jax.ShapeDtypeStruct(keep.shape, BF16),
            in_specs=[VMEM, VMEM],
            out_specs=VMEM,
            compiler_params=params(),
            name="pair",
        )(keep, got)
        arrived = {step: swapped(pair, 2 * step) for step in steps_between}
        mine = pl.pallas_call(
            close_kernel,
            out_shape=jax.ShapeDtypeStruct(keep.shape, F32),
            in_specs=[VMEM] * chips,
            out_specs=VMEM,
            compiler_params=params(),
            name="close",
        )(pair, *[arrived[step] for step in range(1, chips)])
        theirs = swapped(mine, 1)
        low_shape = jax.ShapeDtypeStruct((units, both, LANES), BF16)
        low_edge = jax.ShapeDtypeStruct((edge_units, both, LANES), BF16)
        return pl.pallas_call(
            assemble_kernel,
            out_shape=(image_shape, low_shape, low_edge, low_edge),
            in_specs=[SMEM, VMEM, VMEM],
            out_specs=(VMEM,) * 4,
            scratch_shapes=[pltpu.VMEM((share * group, both, LANES), F32)],
            compiler_params=params(),
            name="assemble",
        )(plan, mine, theirs)

    def share_pieces(keep, got):
        pieces = pl.pallas_call(
            fold_kernel,
            out_shape=(jax.ShapeDtypeStruct(part_shape, F32),)
            + (jax.ShapeDtypeStruct(part_shape, BF16),) * (chips - 1),
            in_specs=[SMEM, VMEM, VMEM],
            out_specs=(VMEM,) * chips,
            compiler_params=params(),
            name="fold",
        )(plan, keep, got)
        arrived = {step: swapped(pieces[step], 2 * step) for step in steps_between}
        return [pieces[0]] + [arrived[step] for step in range(1, chips)]

    before = lax.ppermute(last, "row", up)
    after = lax.ppermute(first, "row", down)
    taken = exchanged(made)
    partial, target_windows, moved, spread = first_near(before, right, after)
    z_all, z_low, first, last = whole_sum(*core_parts(taken, partial, F32))
    before = lax.ppermute(last, "row", up)
    after = lax.ppermute(first, "row", down)
    taken = exchanged(multipoles(z_low))
    pieces = share_pieces(*core_parts(taken, near(before, z_low, after), BF16))

    lines = -(-9 * fields // LANES)
    sums = pl.pallas_call(
        functools.partial(gram_kernel, fields),
        out_shape=jax.ShapeDtypeStruct((group * rows, lines, LANES), F32),
        in_specs=[SMEM] + [VMEM] * (2 + chips),
        out_specs=VMEM,
        compiler_params=params(),
        name="gram",
    )(plan, right, z_all, *pieces)
    sums = lax.all_to_all(sums, EVERY, 0, 0, tiled=True)
    out = pl.pallas_call(
        functools.partial(final_kernel, fields),
        out_shape=jax.ShapeDtypeStruct((both, panels), F32),
        in_specs=[VMEM, VMEM, VMEM],
        out_specs=VMEM,
        compiler_params=params(),
        name="combine",
    )(sums, right, z_all)
    return out.reshape(right_side.shape)


def krylov_coefficients(sums):
    rr, rz_real, rz_imag, zz, rq_real, rq_imag, zq_real, zq_imag, qq = sums

    def times(left, right):
        return left[0] * right[0] - left[1] * right[1], left[0] * right[1] + left[1] * right[0]

    def conj_times(left, right):
        return left[0] * right[0] + left[1] * right[1], left[0] * right[1] - left[1] * right[0]

    def scale(factor, value):
        return factor * value[0], factor * value[1]

    def plus(*values):
        return sum(v[0] for v in values), sum(v[1] for v in values)

    def size(value):
        return value[0] * value[0] + value[1] * value[1]

    rz, rq, zq = (rz_real, rz_imag), (rq_real, rq_imag), (zq_real, zq_imag)
    beta = jnp.sqrt(rr + EPSILON)
    inv = 1.0 / beta
    norm_one = rr * inv * inv
    product = scale(inv * inv, rz)
    h_first = (0.5 * norm_one + product[0], product[1])
    shift = (h_first[0] - 0.5, h_first[1])
    residue = zz * inv * inv - 2.0 * conj_times(shift, product)[0] + size(shift) * norm_one
    residue = jnp.maximum(residue, 0.0)
    h_sub = jnp.sqrt(residue + EPSILON)
    alpha = inv / h_sub
    gamma = scale(-alpha, shift)
    h_upper = scale(
        inv,
        plus(
            scale(0.5, plus(scale(alpha, rz), scale(rr, gamma))), scale(alpha, rq), times(gamma, rz)
        ),
    )
    second = plus(
        scale(alpha * alpha, zq),
        scale(alpha * zz, gamma),
        scale(alpha, conj_times(gamma, rq)),
        scale(size(gamma), rz),
    )
    h_middle = (0.5 * residue / (h_sub * h_sub) + second[0], second[1])
    keep = (h_middle[0] - 0.5, h_middle[1])
    on_z = plus(gamma, scale(-alpha, keep))
    on_r = plus(scale(-inv, h_upper), scale(-1.0, times(keep, gamma)))
    last = (
        alpha * alpha * qq
        + size(on_z) * zz
        + size(on_r) * rr
        + 2.0
        * (
            conj_times(on_r, times(on_z, rz))[0]
            + alpha * conj_times(on_r, rq)[0]
            + alpha * conj_times(on_z, zq)[0]
        )
    )
    h_last = jnp.sqrt(jnp.maximum(last, 0.0) + EPSILON)
    radius = jnp.sqrt(size(h_first) + h_sub * h_sub)
    cosine = scale(1.0 / radius, h_first)
    sine = h_sub / radius
    upper = plus(conj_times(cosine, h_upper), scale(sine, h_middle))
    lower = plus(times(cosine, h_middle), scale(-sine, h_upper))
    radius_two = jnp.sqrt(size(lower) + h_last * h_last)
    cosine_two = scale(1.0 / radius_two, lower)
    weight_two = scale(-sine * beta / radius_two, (cosine_two[0], -cosine_two[1]))
    goal = scale(beta, (cosine[0], -cosine[1]))
    weight_one = scale(1.0 / radius, plus(goal, scale(-1.0, times(upper, weight_two))))
    on_right = plus(scale(inv, weight_one), times(weight_two, gamma))
    on_image = scale(alpha, weight_two)
    return on_right[0], on_right[1], on_image[0], on_image[1]


def solution(mesh):
    return jax.shard_map(
        local,
        mesh=mesh,
        in_specs=(
            P(None, None, "row"),
            P(None, ("grp", "row", "col"), None, None),
            P(("grp", "row", "col")),
            P(("grp", "row", "col")),
            P(None, "row", None),
            P("row", None),
            P(),
            P("row", None),
            P("row", None),
            P(),
        ),
        out_specs=P(None, None, "row"),
        check_vma=False,
    )
```

```python
import functools

import jax
import jax.numpy as jnp
from jax import lax
from jax.experimental import pallas as pl
from jax.experimental.pallas import tpu as pltpu
from jax.sharding import PartitionSpec as P

REACH = 2
SPAN = 2 * REACH + 1
LANES = 128
EPSILON = 1e-06
GROUP = ("grp", "col")
COUNT, CODES = range(2)
PER_ITEM = 5
EVERY = ("grp", "row", "col")

F32 = jnp.float32
BF16 = jnp.bfloat16
SMEM = pl.BlockSpec(memory_space=pltpu.SMEM)
VMEM = pl.BlockSpec(memory_space=pltpu.VMEM)
HBM = pl.BlockSpec(memory_space=pltpu.HBM)
ANY = pl.BlockSpec(memory_space=pl.ANY)


def dot_nn(left, right):
    return lax.dot_general(left, right, (((1,), (0,)), ((), ())), preferred_element_type=F32)


def dot_nt(left, right):
    return lax.dot_general(left, right, (((1,), (1,)), ((), ())), preferred_element_type=F32)


def halves(rows):
    if rows.dtype != F32:
        return rows
    high = rows.astype(BF16)
    return jnp.concatenate([high, (rows - high.astype(F32)).astype(BF16)], axis=0)


def joined(sums, count):
    return sums if sums.shape[0] == count else sums[:count] + sums[count:]


def odd_lanes(shape):
    return lax.rem(lax.broadcasted_iota(jnp.int32, shape, 1), 2) == 1


def from_left(value):
    return pltpu.roll(value, 1, 1)


def from_right(value):
    return pltpu.roll(value, value.shape[1] - 1, 1)


def item_place(slots, item):
    return CODES + slots + PER_ITEM * item


def window_start(leaf_ref, leaf, width):
    units = leaf_ref.shape[1] // LANES
    before = jnp.int32(0)
    for k in range(units):
        before = before + (leaf_ref[0, k * LANES] < leaf).astype(jnp.int32)
    return jnp.clip(before - 1, 0, units - width)


def window_mask(leaves_ref, leaf, unit, rows, width):
    leaves = jnp.concatenate([leaves_ref[unit + k] for k in range(width)], axis=-1)
    return jnp.broadcast_to(leaves, (rows, width * LANES)) == leaf


def window_copies(exp_ref, unit, window_ref, sem, width):
    coefs = exp_ref.shape[0]
    return [
        pltpu.make_async_copy(exp_ref.at[:, unit + k], window_ref.at[k, pl.ds(0, coefs)], sem.at[k])
        for k in range(width)
    ]


def clear_rest(window_ref, coefs, width):
    rest = window_ref.shape[1] - coefs
    for k in range(width):
        window_ref[k, pl.ds(coefs, rest)] = jnp.zeros((rest, 2, LANES), BF16)


def multi_rows(fields, width, leaf, unit, leaves_ref, low_ref, window_ref):
    if len(low_ref.shape) == 2:
        first = pl.multiple_of(unit * LANES, LANES)
        rows = low_ref[:, pl.ds(first, width * LANES)]
    else:
        rows = jnp.concatenate([low_ref[unit + k] for k in range(width)], axis=-1)
    mask = window_mask(leaves_ref, leaf, unit, 2 * fields, width)
    rows = halves(jnp.where(mask, rows.astype(F32), 0.0).astype(rows.dtype))
    total = None
    for k in range(width):
        part = dot_nt(rows[:, k * LANES : (k + 1) * LANES], as_rows(window_ref.at[k]))
        total = part if total is None else total + part
    total = joined(total, 2 * fields)
    on_real, on_imag = total[:fields], total[fields:]
    odd = odd_lanes(on_real.shape)
    other = jnp.where(odd, from_left(on_imag), from_right(on_imag))
    return jnp.where(odd, -on_real, on_real) - other


def as_rows(ref):
    return ref.reshape(ref.shape[0] * 2, ref.shape[2])[...]


def write_edges(row, first, last, one_ref, two_ref):
    even = lax.rem(row, 2) == 0

    @pl.when(even)
    def _():
        one_ref[...], two_ref[...] = last, first

    @pl.when(jnp.logical_not(even))
    def _():
        one_ref[...], two_ref[...] = first, last


def begin_kernel(
    fields, items, width, send, rows, edge, row_ref, own_ref, count_ref, pick_hbm, leaf_hbm, leaves_hbm,
    target_hbm, offset_hbm, pairs_hbm, right_hbm, exp_ref,
    plan_ref, out_ref, window_ref, leaves_ref, right_ref, *edge_refs_and_scratch,
):
    edge_refs = edge_refs_and_scratch[:2]
    pick_ref, leaf_ref, target_ref, offset_ref, pairs_ref, sem, window_sem = edge_refs_and_scratch[2:]
    panels = right_ref.shape[1]
    loads = [
        pltpu.make_async_copy(source, place, sem.at[k])
        for k, (source, place) in enumerate(
            (
                (leaf_hbm, leaf_ref),
                (pick_hbm, pick_ref),
                (target_hbm, target_ref),
                (offset_hbm, offset_ref),
                (pairs_hbm, pairs_ref),
                (leaves_hbm, leaves_ref),
                (right_hbm, right_ref),
            )
        )
    ]
    for load in loads:
        load.start()
    for i in range(items):
        clear_rest(window_ref.at[i], exp_ref.shape[0], width)
    slots = pairs_ref.shape[0]
    own = own_ref[0]
    loads[0].wait()
    loads[1].wait()
    row = row_ref[0]

    def partner(i):
        number = own * items + i
        return lax.rem(lax.div(number, send) - row + rows, rows), lax.rem(number, send)

    for i in range(items):
        other, number = partner(i)
        leaf = pick_ref[other, number, row]
        unit = window_start(leaf_ref, leaf, width)
        place = item_place(slots, i)
        plan_ref[place], plan_ref[place + 1] = leaf, unit
        for copy in window_copies(exp_ref, unit, window_ref.at[i], window_sem.at[i], width):
            copy.start()
    for load in loads[2:]:
        load.wait()
    edges = right_ref[:, :edge].astype(BF16), right_ref[:, panels - edge :].astype(BF16)
    write_edges(row, *edges, *edge_refs)
    plan_ref[COUNT] = count_ref[0]
    for s in range(slots):
        plan_ref[CODES + s] = pairs_ref[s]
    for i in range(items):
        place = item_place(slots, i)
        other, number = partner(i)
        leaf = target_ref[0, other * send + number]
        plan_ref[place + 2], plan_ref[place + 3] = leaf, window_start(leaf_ref, leaf, width)
        plan_ref[place + 4] = offset_ref[0, other * send + number]
    for i in range(items):
        place = item_place(slots, i)
        leaf, unit = plan_ref[place], plan_ref[place + 1]
        for copy in window_copies(exp_ref, unit, window_ref.at[i], window_sem.at[i], width):
            copy.wait()
        out_ref[i] = multi_rows(fields, width, leaf, unit, leaves_ref, right_ref, window_ref.at[i]).astype(BF16)


def first_near_kernel(
    fields, items, width, row_ref, plan_any, exp_ref, trans_ref, one_ref, two_ref, here_ref, tiles_ref,
    out_ref, window_ref, moved_ref, spread_ref, ext, plan_ref, plan_sem, trans_buf, sem, trans_sem,
):
    plan_copy = pltpu.make_async_copy(plan_any, plan_ref, plan_sem)
    plan_copy.start()
    coefs = trans_ref.shape[3]
    slots = tiles_ref.shape[1]
    shape = spread_ref.shape
    row = lax.broadcasted_iota(jnp.int32, shape, 0)
    column = lax.broadcasted_iota(jnp.int32, shape, 1)
    spread_ref[...] = jnp.where(column == 2 * row, 1.0, 0.0).astype(BF16)
    near_sources(row_ref, one_ref, two_ref, here_ref, out_ref, ext)
    plan_copy.wait()

    def trans_copy(i):
        offset = plan_ref[item_place(slots, i) + 4]
        return pltpu.make_async_copy(trans_ref.at[offset], trans_buf.at[i], trans_sem.at[i])

    def exp_copies(i):
        unit = plan_ref[item_place(slots, i) + 3]
        return window_copies(exp_ref, unit, window_ref.at[i], sem.at[i], width)

    for i in range(items):
        trans_copy(i).start()
        for copy in exp_copies(i):
            copy.start()
        clear_rest(window_ref.at[i], coefs, width)
    near_slots(fields, plan_ref, tiles_ref, out_ref, ext)
    rest = moved_ref.shape[1] - 2 * coefs
    for i in range(items):
        trans_copy(i).wait()
        moved_ref[i, pl.ds(0, 2 * coefs)] = trans_buf[i].reshape(2 * coefs, coefs)
        moved_ref[i, pl.ds(2 * coefs, rest)] = jnp.zeros((rest, coefs), BF16)
        for copy in exp_copies(i):
            copy.wait()


def near_sources(row_ref, one_ref, two_ref, here_ref, out_ref, ext):
    units = out_ref.shape[0]
    edge = (ext.shape[0] - units) // 2
    even = lax.rem(row_ref[0], 2) == 0
    one_at = jnp.where(even, edge + units, 0)
    two_at = jnp.where(even, 0, edge + units)
    if len(here_ref.shape) == 2:
        for k in range(edge):
            lanes = slice(k * LANES, (k + 1) * LANES)
            ext[one_at + k] = one_ref[:, lanes].astype(ext.dtype)
            ext[two_at + k] = two_ref[:, lanes].astype(ext.dtype)
        for k in range(units):
            ext[edge + k] = here_ref[:, k * LANES : (k + 1) * LANES]
    else:
        ext[pl.ds(one_at, edge)] = one_ref[...]
        ext[pl.ds(two_at, edge)] = two_ref[...]
        ext[edge : edge + units] = here_ref[...]
    out_ref[...] = jnp.zeros_like(out_ref)


def near_kernel(fields, row_ref, plan_any, one_ref, two_ref, here_ref, tiles_ref, out_ref, ext, plan_ref, plan_sem):
    plan_copy = pltpu.make_async_copy(plan_any, plan_ref, plan_sem)
    plan_copy.start()
    near_sources(row_ref, one_ref, two_ref, here_ref, out_ref, ext)
    plan_copy.wait()
    near_slots(fields, plan_ref, tiles_ref, out_ref, ext)


def near_slots(fields, plan_ref, tiles_ref, out_ref, ext):
    slots, tile = tiles_ref.shape[1], tiles_ref.shape[2]
    per = tile // LANES
    for s in range(slots):
        code = plan_ref[CODES + s]
        target = lax.div(code, SPAN)
        source = target + lax.rem(code, SPAN)
        rows = halves(jnp.concatenate([ext[source * per + k] for k in range(per)], axis=-1))
        on_real = joined(dot_nt(rows, tiles_ref[0, s]), 2 * fields)
        on_imag = joined(dot_nt(rows, tiles_ref[1, s]), 2 * fields)
        value = jnp.concatenate(
            [on_real[:fields] - on_imag[fields:], on_real[fields:] + on_imag[:fields]], axis=0
        )
        value = jnp.where(s < plan_ref[COUNT], value, 0.0)
        for k in range(per):
            out_ref[target * per + k] += value[:, k * LANES : (k + 1) * LANES]


def far_kernel(
    fields, items, width, slots, core_ref, plan_any, leaves_ref, item_ref, partial_ref, trans_ref, spread_ref,
    window_ref, keep_ref, give_ref, total, plan_ref, plan_sem,
):
    plan_copy = pltpu.make_async_copy(plan_any, plan_ref, plan_sem)
    plan_copy.start()
    units = partial_ref.shape[0]
    total[0:units] = partial_ref[...]
    if total.shape[0] > units:
        total[units:] = jnp.zeros((total.shape[0] - units, *total.shape[1:]), F32)
    for i in range(items):
        plain = item_ref[i].astype(F32)
        odd = odd_lanes(plain.shape)
        turned = jnp.where(odd, from_left(plain), -from_right(plain))
        rows = jnp.concatenate([plain, turned], axis=0).astype(BF16)
        local_field = dot_nn(rows, trans_ref[i]).astype(BF16)
        apart = dot_nn(local_field, spread_ref[...])
        local_real, local_imag = apart[:fields], apart[fields:]
        rows = jnp.concatenate(
            [local_real - from_left(local_imag), local_imag + from_left(local_real)], axis=0
        ).astype(BF16)
        if i == 0:
            plan_copy.wait()
        place = item_place(slots, i)
        leaf, unit = plan_ref[place + 2], plan_ref[place + 3]
        mask = window_mask(leaves_ref, leaf, unit, 2 * fields, width)
        for k in range(width):
            image = dot_nn(rows, as_rows(window_ref.at[i, k]))
            total[unit + k] += jnp.where(mask[:, k * LANES : (k + 1) * LANES], image, 0.0)
    chips, share = keep_ref.shape[:2]
    core = core_ref[0]
    for c in range(chips):
        keep_ref[c] = total[pl.ds((2 * c + core) * share, share)].astype(keep_ref.dtype)
        give_ref[c] = total[pl.ds((2 * c + 1 - core) * share, share)].astype(give_ref.dtype)


def halve_kernel(level, chip_ref, mine_ref, got_ref, keep_ref, give_ref):
    bit = lax.rem(lax.div(chip_ref[0], 1 << level), 2)
    for k in range(keep_ref.shape[0]):
        for out_ref, place in ((keep_ref, 2 * k + bit), (give_ref, 2 * k + 1 - bit)):
            out_ref[k] = (mine_ref[place].astype(F32) + got_ref[place].astype(F32)).astype(out_ref.dtype)


def pair_kernel(keep_ref, got_ref, out_ref):
    out_ref[...] = (keep_ref[...].astype(F32) + got_ref[...].astype(F32)).astype(out_ref.dtype)


def tree_sum(values):
    while len(values) > 1:
        values = [values[k] + values[k + 1] for k in range(0, len(values), 2)]
    return values[0]


def close_kernel(*refs):
    refs[-1][...] = tree_sum([ref[...].astype(F32) for ref in refs[:-1]])


def assemble_kernel(
    fields, items, width, slots, core_ref, row_ref, plan_any, leaves_ref, mine_ref, theirs_ref, window_ref,
    out_ref, low_ref, one_ref, two_ref, made_ref, whole, plan_ref, plan_sem,
):
    plan_copy = pltpu.make_async_copy(plan_any, plan_ref, plan_sem)
    plan_copy.start()
    chips, share = mine_ref.shape[:2]
    units, edge = out_ref.shape[0], one_ref.shape[0]
    core = core_ref[0]
    for chip in range(chips):
        whole[pl.ds((2 * chip + core) * share, share)] = mine_ref[chip]
        whole[pl.ds((2 * chip + 1 - core) * share, share)] = theirs_ref[chip]
    out_ref[...] = whole[0:units]
    low_ref[...] = whole[0:units].astype(BF16)
    write_edges(
        row_ref[0], whole[0:edge].astype(BF16), whole[units - edge : units].astype(BF16), one_ref, two_ref
    )
    plan_copy.wait()
    for i in range(items):
        place = item_place(slots, i)
        made_ref[i] = multi_rows(
            fields, width, plan_ref[place], plan_ref[place + 1], leaves_ref, low_ref, window_ref.at[i]
        ).astype(BF16)


def flat_lines(columns, fields):
    per = LANES // fields
    lines = []
    for first in range(0, len(columns), per):
        some = columns[first : first + per]
        if len(some) < per:
            some = some + [jnp.zeros(((per - len(some)) * fields, 1), F32)]
        square = jnp.broadcast_to(jnp.concatenate(some, axis=0), (LANES, LANES))
        lines.append(jnp.transpose(square)[:1])
    return jnp.concatenate(lines, axis=0)


def columns_of(lines, count, fields):
    per = LANES // fields
    columns = []
    for k in range(lines.shape[0]):
        square = jnp.transpose(jnp.broadcast_to(lines[k : k + 1], (LANES, LANES)))
        columns += [square[j * fields : (j + 1) * fields, :1] for j in range(per)]
    return columns[:count]


def gram_kernel(fields, own_ref, right_ref, image_ref, mine_ref, got_ref, out_ref):
    units = image_ref.shape[0]
    share = mine_ref.shape[1]
    totals = None
    for k in range(share):
        unit = own_ref[0] * share + k
        place = jnp.minimum(unit, units - 1)
        r = right_ref[:, pl.ds(pl.multiple_of(place * LANES, LANES), LANES)]
        z = image_ref[place]
        q = mine_ref[0, k].astype(F32) + got_ref[0, k].astype(F32)
        r = jnp.where(unit < units, r, 0.0)
        z = jnp.where(unit < units, z, 0.0)
        (rr, ri), (zr, zi), (qr, qi) = [(v[:fields], v[fields:]) for v in (r, z, q)]
        products = [
            rr * rr + ri * ri,
            rr * zr + ri * zi,
            rr * zi - ri * zr,
            zr * zr + zi * zi,
            rr * qr + ri * qi,
            rr * qi - ri * qr,
            zr * qr + zi * qi,
            zr * qi - zi * qr,
            qr * qr + qi * qi,
        ]
        totals = products if totals is None else [t + p for t, p in zip(totals, products)]
    lines = flat_lines([jnp.sum(t, axis=1, keepdims=True) for t in totals], fields)
    out_ref[...] = jnp.broadcast_to(lines[None], out_ref.shape)


def final_kernel(fields, sums_ref, right_ref, image_ref, out_ref):
    units = image_ref.shape[0]
    sums = columns_of(jnp.sum(sums_ref[...], axis=0), 9, fields)
    a_real, a_imag, b_real, b_imag = [
        jnp.broadcast_to(value, (fields, LANES)) for value in krylov_coefficients(sums)
    ]
    for k in range(units):
        lanes = slice(k * LANES, (k + 1) * LANES)
        r_real, r_imag = right_ref[:fields, lanes], right_ref[fields:, lanes]
        z_real, z_imag = image_ref[k, :fields], image_ref[k, fields:]
        out_ref[:fields, lanes] = a_real * r_real - a_imag * r_imag + b_real * z_real - b_imag * z_imag
        out_ref[fields:, lanes] = a_real * r_imag + a_imag * r_real + b_real * z_imag + b_imag * z_real


def params(mebibytes=16):
    return pltpu.CompilerParams(vmem_limit_bytes=mebibytes * 1024 * 1024)


def item_route(rows, group, columns, send):
    items = rows * send // group

    def flat(r, g):
        return (g // columns * rows + r) * columns + g % columns

    assert items * group == rows * send and (items % send == 0 or send % items == 0)
    routes = []
    for first in range(0, items, send):
        numbers = [(g * items + first) // send for g in range(group)]
        routes.append([(flat(r, g), flat((numbers[g] - r) % rows, g)) for r in range(rows) for g in range(group)])
    return items, routes


def local(
    right_side,
    near_tiles,
    tile_pairs,
    tile_count,
    panel_expansions,
    leaf_of_panel,
    far_pick,
    far_target,
    far_offset,
    translations,
):
    fields, panels = right_side.shape[1:]
    coefs = panel_expansions.shape[2]
    tile = near_tiles.shape[2]
    send = far_pick.shape[2]
    rows = lax.axis_size("row")
    group = lax.axis_size("grp") * lax.axis_size("col")
    row_here = lax.axis_index("row")
    own = lax.axis_index("grp") * lax.axis_size("col") + lax.axis_index("col")
    both = 2 * fields
    units = panels // LANES
    share = -(-units // group)
    edge = REACH * tile
    edge_units = edge // LANES
    width = tile // LANES + 1
    items, routes = item_route(rows, group, lax.axis_size("col"), send)

    assert rows % 2 == 0
    neighbours = [[r + 1 - 2 * (r % 2) for r in range(rows)], [(r - 1 + 2 * (r % 2)) % rows for r in range(rows)]]
    own_place, row_place = own.reshape(1), row_here.reshape(1)
    core_place, chip_place = lax.rem(own, 2).reshape(1), lax.div(own, 2).reshape(1)
    slots = near_tiles.shape[1]
    pad_coefs = -(-coefs // 8) * 8
    chips = group // 2
    steps_between = range(chips - 1, 0, -1)
    assert group == 2 * chips and chips & (chips - 1) == 0 and LANES % fields == 0
    window_shape = jax.ShapeDtypeStruct((items, width, pad_coefs, 2, LANES), BF16)
    item_shape = jax.ShapeDtypeStruct((items, fields, 2 * pad_coefs), BF16)
    plan_shape = jax.ShapeDtypeStruct((item_place(slots, items),), jnp.int32)
    part_shape = (share, both, LANES)

    def in_hbm(value):
        return pltpu.with_memory_space_constraint(value, pltpu.HBM)

    leaves = leaf_of_panel.reshape(units, 1, LANES)
    expansions = panel_expansions.transpose(2, 0, 1).reshape(coefs, 2, units, LANES).transpose(0, 2, 1, 3)
    expansions = in_hbm(expansions)
    moves = in_hbm(translations.transpose(0, 2, 1, 3))
    picks = far_pick.transpose(0, 2, 1)
    edge_shape = jax.ShapeDtypeStruct((both, edge), BF16)
    plan_scratch = [pltpu.SMEM(plan_shape.shape, jnp.int32), pltpu.SemaphoreType.DMA]

    plan, made, windows, leaves, right, one, two = pl.pallas_call(
        functools.partial(begin_kernel, fields, items, width, send, rows, edge),
        out_shape=(
            plan_shape,
            item_shape,
            window_shape,
            jax.ShapeDtypeStruct(leaves.shape, jnp.int32),
            jax.ShapeDtypeStruct((both, panels), F32),
            edge_shape,
            edge_shape,
        ),
        in_specs=[SMEM] * 3 + [HBM] * 8,
        out_specs=(SMEM,) + (VMEM,) * 6,
        scratch_shapes=[
            pltpu.SMEM(value.shape, jnp.int32)
            for value in (picks, leaf_of_panel, far_target, far_offset, tile_pairs)
        ]
        + [pltpu.SemaphoreType.DMA((7,)), pltpu.SemaphoreType.DMA((items, width))],
        compiler_params=params(),
        name="begin",
    )(
        row_place,
        own_place,
        tile_count,
        in_hbm(picks),
        in_hbm(leaf_of_panel),
        in_hbm(leaves),
        in_hbm(far_target),
        in_hbm(far_offset),
        in_hbm(tile_pairs),
        in_hbm(right_side.reshape(both, panels)),
        expansions,
    )

    def exchanged(made):
        parts = [
            lax.ppermute(made[k * send : k * send + min(send, items)], EVERY, route) for k, route in enumerate(routes)
        ]
        return parts[0] if len(parts) == 1 else jnp.concatenate(parts)

    def to_neighbours(one, two):
        return [
            lax.ppermute(value, "row", list(enumerate(targets))) for value, targets in zip((one, two), neighbours)
        ]

    image_shape = jax.ShapeDtypeStruct((units, both, LANES), F32)
    near_cost = pl.CostEstimate(
        flops=8 * fields * near_tiles.size // 2, bytes_accessed=2 * near_tiles.size, transcendentals=0
    )

    def first_near(one, two, low):
        return pl.pallas_call(
            functools.partial(first_near_kernel, fields, items, width),
            out_shape=(
                image_shape,
                window_shape,
                jax.ShapeDtypeStruct((items, 2 * pad_coefs, coefs), BF16),
                jax.ShapeDtypeStruct((coefs, 2 * pad_coefs), BF16),
            ),
            in_specs=[SMEM, ANY] + [HBM] * 2 + [VMEM] * 4,
            out_specs=(VMEM, VMEM, VMEM, VMEM),
            scratch_shapes=[pltpu.VMEM((units + 2 * edge_units, both, LANES), low.dtype)]
            + plan_scratch
            + [
                pltpu.VMEM((items, coefs, 2, coefs), BF16),
                pltpu.SemaphoreType.DMA((items, width)),
                pltpu.SemaphoreType.DMA((items,)),
            ],
            compiler_params=params(24),
            cost_estimate=near_cost,
            name="first_near",
        )(row_place, plan, expansions, moves, one, two, low, near_tiles)

    def near(one, two, low):
        return pl.pallas_call(
            functools.partial(near_kernel, fields),
            out_shape=image_shape,
            in_specs=[SMEM, ANY, VMEM, VMEM, VMEM, VMEM],
            out_specs=VMEM,
            scratch_shapes=[pltpu.VMEM((units + 2 * edge_units, both, LANES), low.dtype)] + plan_scratch,
            compiler_params=params(),
            cost_estimate=near_cost,
            name="near",
        )(row_place, plan, one, two, low, near_tiles)

    def swapped(value, step):
        return lax.ppermute(value, GROUP, [(g, g ^ step) for g in range(group)])

    def core_parts(taken, partial, dtype):
        half_shape = jax.ShapeDtypeStruct((chips, *part_shape), dtype)
        keep, give = pl.pallas_call(
            functools.partial(far_kernel, fields, items, width, slots),
            out_shape=(half_shape, half_shape),
            in_specs=[SMEM, ANY] + [VMEM] * 6,
            out_specs=(VMEM, VMEM),
            scratch_shapes=[pltpu.VMEM((share * group, both, LANES), F32)] + plan_scratch,
            compiler_params=params(),
            name="far",
        )(core_place, plan, leaves, taken, partial, moved, spread, target_windows)
        return keep, swapped(give, 1)

    def whole_sum(keep, got):
        pair = pl.pallas_call(
            pair_kernel,
            out_shape=jax.ShapeDtypeStruct(keep.shape, BF16),
            in_specs=[VMEM, VMEM],
            out_specs=VMEM,
            compiler_params=params(),
            name="pair",
        )(keep, got)
        arrived = {step: swapped(pair, 2 * step) for step in steps_between}
        mine = pl.pallas_call(
            close_kernel,
            out_shape=jax.ShapeDtypeStruct(keep.shape, F32),
            in_specs=[VMEM] * chips,
            out_specs=VMEM,
            compiler_params=params(),
            name="close",
        )(pair, *[arrived[step] for step in range(1, chips)])
        theirs = swapped(mine, 1)
        low_shape = jax.ShapeDtypeStruct((units, both, LANES), BF16)
        low_edge = jax.ShapeDtypeStruct((edge_units, both, LANES), BF16)
        return pl.pallas_call(
            functools.partial(assemble_kernel, fields, items, width, slots),
            out_shape=(image_shape, low_shape, low_edge, low_edge, item_shape),
            in_specs=[SMEM, SMEM, ANY] + [VMEM] * 4,
            out_specs=(VMEM,) * 5,
            scratch_shapes=[pltpu.VMEM((share * group, both, LANES), F32)] + plan_scratch,
            compiler_params=params(),
            name="assemble",
        )(core_place, row_place, plan, leaves, mine, theirs, windows)

    def own_share(keep, got):
        pieces = chips
        for level in range(chips.bit_length() - 1):
            pieces //= 2
            keep, give = pl.pallas_call(
                functools.partial(halve_kernel, level),
                out_shape=(
                    jax.ShapeDtypeStruct((pieces, *part_shape), F32),
                    jax.ShapeDtypeStruct((pieces, *part_shape), BF16),
                ),
                in_specs=[SMEM, VMEM, VMEM],
                out_specs=(VMEM, VMEM),
                compiler_params=params(),
                name="halve",
            )(chip_place, keep, got)
            got = swapped(give, 2 << level)
        return keep, got

    taken = exchanged(made)
    partial, target_windows, moved, spread = first_near(*to_neighbours(one, two), right)
    z_all, z_low, one, two, made = whole_sum(*core_parts(taken, partial, F32))
    taken = exchanged(made)
    partial = near(*to_neighbours(one, two), z_low)
    keep, got = own_share(*core_parts(taken, partial, BF16))

    lines = -(-9 * fields // LANES)
    sums = pl.pallas_call(
        functools.partial(gram_kernel, fields),
        out_shape=jax.ShapeDtypeStruct((group * rows, lines, LANES), F32),
        in_specs=[SMEM] + [VMEM] * 4,
        out_specs=VMEM,
        compiler_params=params(),
        name="gram",
    )(own_place, right, z_all, keep, got)
    sums = lax.all_to_all(sums, EVERY, 0, 0, tiled=True)
    out = pl.pallas_call(
        functools.partial(final_kernel, fields),
        out_shape=jax.ShapeDtypeStruct((both, panels), F32),
        in_specs=[VMEM, VMEM, VMEM],
        out_specs=VMEM,
        compiler_params=params(),
        name="combine",
    )(sums, right, z_all)
    return out.reshape(right_side.shape)


def krylov_coefficients(sums):
    rr, rz_real, rz_imag, zz, rq_real, rq_imag, zq_real, zq_imag, qq = sums

    def times(left, right):
        return left[0] * right[0] - left[1] * right[1], left[0] * right[1] + left[1] * right[0]

    def conj_times(left, right):
        return left[0] * right[0] + left[1] * right[1], left[0] * right[1] - left[1] * right[0]

    def scale(factor, value):
        return factor * value[0], factor * value[1]

    def plus(*values):
        return sum(v[0] for v in values), sum(v[1] for v in values)

    def size(value):
        return value[0] * value[0] + value[1] * value[1]

    rz, rq, zq = (rz_real, rz_imag), (rq_real, rq_imag), (zq_real, zq_imag)
    beta = jnp.sqrt(rr + EPSILON)
    inv = 1.0 / beta
    norm_one = rr * inv * inv
    product = scale(inv * inv, rz)
    h_first = (0.5 * norm_one + product[0], product[1])
    shift = (h_first[0] - 0.5, h_first[1])
    residue = zz * inv * inv - 2.0 * conj_times(shift, product)[0] + size(shift) * norm_one
    residue = jnp.maximum(residue, 0.0)
    h_sub = jnp.sqrt(residue + EPSILON)
    alpha = inv / h_sub
    gamma = scale(-alpha, shift)
    h_upper = scale(
        inv,
        plus(
            scale(0.5, plus(scale(alpha, rz), scale(rr, gamma))), scale(alpha, rq), times(gamma, rz)
        ),
    )
    second = plus(
        scale(alpha * alpha, zq),
        scale(alpha * zz, gamma),
        scale(alpha, conj_times(gamma, rq)),
        scale(size(gamma), rz),
    )
    h_middle = (0.5 * residue / (h_sub * h_sub) + second[0], second[1])
    keep = (h_middle[0] - 0.5, h_middle[1])
    on_z = plus(gamma, scale(-alpha, keep))
    on_r = plus(scale(-inv, h_upper), scale(-1.0, times(keep, gamma)))
    last = (
        alpha * alpha * qq
        + size(on_z) * zz
        + size(on_r) * rr
        + 2.0
        * (
            conj_times(on_r, times(on_z, rz))[0]
            + alpha * conj_times(on_r, rq)[0]
            + alpha * conj_times(on_z, zq)[0]
        )
    )
    h_last = jnp.sqrt(jnp.maximum(last, 0.0) + EPSILON)
    radius = jnp.sqrt(size(h_first) + h_sub * h_sub)
    cosine = scale(1.0 / radius, h_first)
    sine = h_sub / radius
    upper = plus(conj_times(cosine, h_upper), scale(sine, h_middle))
    lower = plus(times(cosine, h_middle), scale(-sine, h_upper))
    radius_two = jnp.sqrt(size(lower) + h_last * h_last)
    cosine_two = scale(1.0 / radius_two, lower)
    weight_two = scale(-sine * beta / radius_two, (cosine_two[0], -cosine_two[1]))
    goal = scale(beta, (cosine[0], -cosine[1]))
    weight_one = scale(1.0 / radius, plus(goal, scale(-1.0, times(upper, weight_two))))
    on_right = plus(scale(inv, weight_one), times(weight_two, gamma))
    on_image = scale(alpha, weight_two)
    return on_right[0], on_right[1], on_image[0], on_image[1]


def solution(mesh):
    return jax.shard_map(
        local,
        mesh=mesh,
        in_specs=(
            P(None, None, "row"),
            P(None, ("grp", "row", "col"), None, None),
            P(("grp", "row", "col")),
            P(("grp", "row", "col")),
            P(None, "row", None),
            P("row", None),
            P(),
            P("row", None),
            P("row", None),
            P(),
        ),
        out_specs=P(None, None, "row"),
        check_vma=False,
    )
```

```python
import functools

import jax
import jax.numpy as jnp
from jax import lax
from jax.experimental import pallas as pl
from jax.experimental.pallas import tpu as pltpu
from jax.sharding import PartitionSpec as P

REACH = 2
SPAN = 2 * REACH + 1
LANES = 128
EPSILON = 1e-06
GROUP = ("grp", "col")
CODES = 0
PER_ITEM = 5
ITEM_REST = 2 * LANES
EVERY = ("grp", "row", "col")

F32 = jnp.float32
BF16 = jnp.bfloat16
SMEM = pl.BlockSpec(memory_space=pltpu.SMEM)
VMEM = pl.BlockSpec(memory_space=pltpu.VMEM)
HBM = pl.BlockSpec(memory_space=pltpu.HBM)
ANY = pl.BlockSpec(memory_space=pl.ANY)


def dot_nn(left, right):
    return lax.dot_general(left, right, (((1,), (0,)), ((), ())), preferred_element_type=F32)


def dot_nt(left, right):
    return lax.dot_general(left, right, (((1,), (1,)), ((), ())), preferred_element_type=F32)


def halves(rows):
    if rows.dtype != F32:
        return rows
    high = rows.astype(BF16)
    return jnp.concatenate([high, (rows - high.astype(F32)).astype(BF16)], axis=0)


def joined(sums, count):
    return sums if sums.shape[0] == count else sums[:count] + sums[count:]


def odd_lanes(shape):
    return lax.rem(lax.broadcasted_iota(jnp.int32, shape, 1), 2) == 1


def twice(value, width):
    rows = value.shape[0]
    parts = []
    for k in range(width // LANES):
        first = (k // 2) * LANES
        part = value[:, first : first + LANES]
        if part.shape[1] < LANES:
            part = jnp.concatenate([part, jnp.zeros((rows, LANES - part.shape[1]), part.dtype)], axis=-1)
        lane = lax.broadcasted_iota(jnp.int32, (rows, LANES), 1)
        parts.append(jnp.take_along_axis(part, lax.div(lane, 2) + (k % 2) * (LANES // 2), axis=1))
    return jnp.concatenate(parts, axis=-1)


def from_left(value):
    return pltpu.roll(value, 1, 1)


def from_right(value):
    return pltpu.roll(value, value.shape[1] - 1, 1)


def item_place(slots, item):
    return CODES + slots + PER_ITEM * item


def window_start(leaf_ref, leaf, width):
    units = leaf_ref.shape[1] // LANES
    before = jnp.int32(0)
    for k in range(units):
        before = before + (leaf_ref[0, k * LANES] < leaf).astype(jnp.int32)
    return jnp.clip(before - 1, 0, units - width)


def window_mask(leaves_ref, leaf, unit, rows, width):
    leaves = jnp.concatenate([leaves_ref[unit + k] for k in range(width)], axis=-1)
    return jnp.broadcast_to(leaves, (rows, width * LANES)) == leaf


def window_copies(exp_ref, unit, window_ref, sem, width):
    coefs = exp_ref.shape[0]
    return [
        pltpu.make_async_copy(exp_ref.at[:, unit + k], window_ref.at[k, pl.ds(0, coefs)], sem.at[k])
        for k in range(width)
    ]


def clear_rest(window_ref, coefs, width):
    rest = window_ref.shape[1] - coefs
    for k in range(width):
        window_ref[k, pl.ds(coefs, rest)] = jnp.zeros((rest, 2, LANES), BF16)


def multi_rows(fields, width, leaf, unit, leaves_ref, low_ref, window_ref):
    if len(low_ref.shape) == 2:
        first = pl.multiple_of(unit * LANES, LANES)
        rows = low_ref[:, pl.ds(first, width * LANES)]
    else:
        rows = jnp.concatenate([low_ref[unit + k] for k in range(width)], axis=-1)
    mask = window_mask(leaves_ref, leaf, unit, 2 * fields, width)
    rows = halves(jnp.where(mask, rows.astype(F32), 0.0).astype(rows.dtype))
    expansions = jnp.concatenate([as_rows(window_ref.at[k]) for k in range(width)], axis=-1)
    total = joined(dot_nt(rows, expansions), 2 * fields)
    on_real, on_imag = total[:fields], total[fields:]
    odd = odd_lanes(on_real.shape)
    other = jnp.where(odd, from_left(on_imag), from_right(on_imag))
    return jnp.where(odd, -on_real, on_real) - other


def as_rows(ref):
    return ref.reshape(ref.shape[0] * 2, ref.shape[2])[...]


def edge_kernel(row_ref, image_ref, one_ref, two_ref):
    even = lax.rem(row_ref[0], 2) == 0
    if len(image_ref.shape) == 2:
        edge = one_ref.shape[1]
        first, last = image_ref[:, :edge], image_ref[:, image_ref.shape[1] - edge :]
    else:
        edge = one_ref.shape[0]
        first, last = image_ref[:edge], image_ref[image_ref.shape[0] - edge :]
    first, last = first.astype(one_ref.dtype), last.astype(one_ref.dtype)

    @pl.when(even)
    def _():
        one_ref[...], two_ref[...] = last, first

    @pl.when(jnp.logical_not(even))
    def _():
        one_ref[...], two_ref[...] = first, last


def begin_kernel(
    fields, items, width, send, rows, row_ref, own_ref, pick_hbm, leaf_hbm, leaves_hbm,
    target_hbm, offset_hbm, pairs_hbm, right_hbm, exp_ref,
    plan_ref, out_ref, window_ref, leaves_ref, right_ref,
    pick_ref, leaf_ref, target_ref, offset_ref, pairs_ref, sem, window_sem,
):
    loads = [
        pltpu.make_async_copy(source, place, sem.at[k])
        for k, (source, place) in enumerate(
            (
                (leaf_hbm, leaf_ref),
                (pick_hbm, pick_ref),
                (target_hbm, target_ref),
                (offset_hbm, offset_ref),
                (pairs_hbm, pairs_ref),
                (leaves_hbm, leaves_ref),
                (right_hbm, right_ref),
            )
        )
    ]
    for load in loads:
        load.start()
    for i in range(items):
        clear_rest(window_ref.at[i], exp_ref.shape[0], width)
    slots = pairs_ref.shape[0]
    own = own_ref[0]
    loads[0].wait()
    loads[1].wait()
    row = row_ref[0]

    def partner(i):
        number = own * items + i
        return lax.rem(lax.div(number, send) - row + rows, rows), lax.rem(number, send)

    for i in range(items):
        other, number = partner(i)
        leaf = pick_ref[other, number, row]
        unit = window_start(leaf_ref, leaf, width)
        place = item_place(slots, i)
        plan_ref[place], plan_ref[place + 1] = leaf, unit
        for copy in window_copies(exp_ref, unit, window_ref.at[i], window_sem.at[i], width):
            copy.start()
    for load in loads[2:]:
        load.wait()
    for s in range(slots):
        plan_ref[CODES + s] = pairs_ref[s]
    for i in range(items):
        place = item_place(slots, i)
        other, number = partner(i)
        leaf = target_ref[0, other * send + number]
        plan_ref[place + 2], plan_ref[place + 3] = leaf, window_start(leaf_ref, leaf, width)
        plan_ref[place + 4] = offset_ref[0, other * send + number]
    for i in range(items):
        place = item_place(slots, i)
        leaf, unit = plan_ref[place], plan_ref[place + 1]
        for copy in window_copies(exp_ref, unit, window_ref.at[i], window_sem.at[i], width):
            copy.wait()
        made = multi_rows(fields, width, leaf, unit, leaves_ref, right_ref, window_ref.at[i])
        out_ref[i, :, : made.shape[1]] = made.astype(BF16)


def fetch_kernel(items, width, slots, plan_any, exp_ref, trans_ref, window_ref, moved_ref, plan_ref, plan_sem, trans_buf, sem, trans_sem):
    plan_copy = pltpu.make_async_copy(plan_any, plan_ref, plan_sem)
    plan_copy.start()
    coefs = trans_ref.shape[3]
    for i in range(items):
        clear_rest(window_ref.at[i], coefs, width)
    plan_copy.wait()

    def trans_copy(i):
        offset = plan_ref[item_place(slots, i) + 4]
        return pltpu.make_async_copy(trans_ref.at[offset], trans_buf.at[i], trans_sem.at[i])

    def exp_copies(i):
        unit = plan_ref[item_place(slots, i) + 3]
        return window_copies(exp_ref, unit, window_ref.at[i], sem.at[i], width)

    for i in range(items):
        trans_copy(i).start()
        for copy in exp_copies(i):
            copy.start()
    rest = moved_ref.shape[1] - 2 * coefs
    for i in range(items):
        trans_copy(i).wait()
        moved_ref[i, pl.ds(0, 2 * coefs)] = trans_buf[i].reshape(2 * coefs, coefs)
        moved_ref[i, pl.ds(2 * coefs, rest)] = jnp.zeros((rest, coefs), BF16)
        for copy in exp_copies(i):
            copy.wait()


def near_sources(row_ref, one_ref, two_ref, here_ref, units, ext):
    edge = (ext.shape[0] - units) // 2
    even = lax.rem(row_ref[0], 2) == 0
    one_at = jnp.where(even, edge + units, 0)
    two_at = jnp.where(even, 0, edge + units)
    if len(here_ref.shape) == 2:
        for k in range(edge):
            lanes = slice(k * LANES, (k + 1) * LANES)
            ext[one_at + k] = one_ref[:, lanes].astype(ext.dtype)
            ext[two_at + k] = two_ref[:, lanes].astype(ext.dtype)
        for k in range(units):
            ext[edge + k] = here_ref[:, k * LANES : (k + 1) * LANES]
    else:
        ext[pl.ds(one_at, edge)] = one_ref[...]
        ext[pl.ds(two_at, edge)] = two_ref[...]
        ext[edge : edge + units] = here_ref[...]


def near_kernel(
    fields, units, core_ref, row_ref, count_ref, plan_any, image_ref, one_ref, two_ref, here_ref, tiles_ref,
    keep_ref, give_ref, ext, total, plan_ref, plan_sem,
):
    plan_copy = pltpu.make_async_copy(plan_any, plan_ref, plan_sem)
    plan_copy.start()
    near_sources(row_ref, one_ref, two_ref, here_ref, units, ext)
    total[...] = jnp.zeros_like(total)
    slots, tile = tiles_ref.shape[1], tiles_ref.shape[2]
    per = tile // LANES
    plan_copy.wait()
    items, width = image_ref.shape[:2]
    for i in range(items):
        unit = plan_ref[item_place(slots, i) + 3]
        for k in range(width):
            total[unit + k] += image_ref[i, k]
    for s in range(slots):
        code = plan_ref[CODES + s]
        target = lax.div(code, SPAN)
        source = target + lax.rem(code, SPAN)
        rows = halves(jnp.concatenate([ext[source * per + k] for k in range(per)], axis=-1))
        on_real = joined(dot_nt(rows, tiles_ref[0, s]), 2 * fields)
        on_imag = joined(dot_nt(rows, tiles_ref[1, s]), 2 * fields)
        value = jnp.concatenate(
            [on_real[:fields] - on_imag[fields:], on_real[fields:] + on_imag[:fields]], axis=0
        )
        value = jnp.where(s < count_ref[0], value, 0.0)
        for k in range(per):
            total[target * per + k] += value[:, k * LANES : (k + 1) * LANES]
    chips, share = keep_ref.shape[:2]
    core = core_ref[0]
    for c in range(chips):
        keep_ref[c] = total[pl.ds((2 * c + core) * share, share)].astype(keep_ref.dtype)
        give_ref[c] = total[pl.ds((2 * c + 1 - core) * share, share)].astype(give_ref.dtype)


def far_kernel(
    fields, items, width, slots, plan_any, leaves_ref, item_ref, trans_ref, window_ref, image_ref, plan_ref, plan_sem
):
    plan_copy = pltpu.make_async_copy(plan_any, plan_ref, plan_sem)
    plan_copy.start()
    images = []
    for i in range(items):
        plain = item_ref[i, :, : trans_ref.shape[1]].astype(F32)
        odd = odd_lanes(plain.shape)
        turned = jnp.where(odd, from_left(plain), -from_right(plain))
        rows = jnp.concatenate([plain, turned], axis=0).astype(BF16)
        local_field = dot_nn(rows, trans_ref[i]).astype(BF16).astype(F32)
        local_field = twice(local_field, plain.shape[1])
        local_real, local_imag = local_field[:fields], local_field[fields:]
        rows = jnp.concatenate(
            [jnp.where(odd, -local_imag, local_real), jnp.where(odd, local_real, local_imag)], axis=0
        ).astype(BF16)
        expansions = jnp.concatenate([as_rows(window_ref.at[i, k]) for k in range(width)], axis=-1)
        images.append(dot_nn(rows, expansions))
    plan_copy.wait()
    for i in range(items):
        place = item_place(slots, i)
        mask = window_mask(leaves_ref, plan_ref[place + 2], plan_ref[place + 3], 2 * fields, width)
        image = jnp.where(mask, images[i], 0.0)
        for k in range(width):
            image_ref[i, k] = image[:, k * LANES : (k + 1) * LANES]


def fold_kernel(chip_ref, keep_ref, got_ref, own_ref, *out_refs):
    for step, out_ref in enumerate((own_ref,) + out_refs):
        chip = lax.bitwise_xor(chip_ref[0], step)
        out_ref[...] = (keep_ref[chip].astype(F32) + got_ref[chip].astype(F32)).astype(out_ref.dtype)


def pair_kernel(keep_ref, got_ref, out_ref):
    out_ref[...] = (keep_ref[...].astype(F32) + got_ref[...].astype(F32)).astype(out_ref.dtype)


def tree_sum(values):
    while len(values) > 1:
        values = [values[k] + values[k + 1] for k in range(0, len(values), 2)]
    return values[0]


def close_kernel(*refs):
    refs[-1][...] = tree_sum([ref[...].astype(F32) for ref in refs[:-1]])


def assemble_kernel(
    fields, items, width, slots, core_ref, plan_any, leaves_ref, mine_ref, theirs_ref, window_ref,
    out_ref, low_ref, made_ref, whole, plan_ref, plan_sem,
):
    plan_copy = pltpu.make_async_copy(plan_any, plan_ref, plan_sem)
    plan_copy.start()
    chips, share = mine_ref.shape[:2]
    units = out_ref.shape[0]
    core = core_ref[0]
    for chip in range(chips):
        whole[pl.ds((2 * chip + core) * share, share)] = mine_ref[chip]
        whole[pl.ds((2 * chip + 1 - core) * share, share)] = theirs_ref[chip]
    out_ref[...] = whole[0:units]
    low_ref[...] = whole[0:units].astype(BF16)
    plan_copy.wait()
    for i in range(items):
        place = item_place(slots, i)
        made = multi_rows(
            fields, width, plan_ref[place], plan_ref[place + 1], leaves_ref, low_ref, window_ref.at[i]
        )
        made_ref[i, :, : made.shape[1]] = made.astype(BF16)


def flat_lines(columns, fields):
    per = LANES // fields
    lines = []
    for first in range(0, len(columns), per):
        some = columns[first : first + per]
        if len(some) < per:
            some = some + [jnp.zeros(((per - len(some)) * fields, 1), F32)]
        square = jnp.broadcast_to(jnp.concatenate(some, axis=0), (LANES, LANES))
        lines.append(jnp.transpose(square)[:1])
    return jnp.concatenate(lines, axis=0)


def columns_of(lines, count, fields):
    per = LANES // fields
    columns = []
    for k in range(lines.shape[0]):
        square = jnp.transpose(jnp.broadcast_to(lines[k : k + 1], (LANES, LANES)))
        columns += [square[j * fields : (j + 1) * fields, :1] for j in range(per)]
    return columns[:count]


def gram_kernel(fields, own_ref, right_ref, image_ref, *pieces_and_out):
    *pieces, out_ref = pieces_and_out
    units = image_ref.shape[0]
    share = pieces[0].shape[0]
    totals = None
    for k in range(share):
        unit = own_ref[0] * share + k
        place = jnp.minimum(unit, units - 1)
        r = right_ref[:, pl.ds(pl.multiple_of(place * LANES, LANES), LANES)]
        z = image_ref[place]
        q = tree_sum([piece[k].astype(F32) for piece in pieces])
        r = jnp.where(unit < units, r, 0.0)
        z = jnp.where(unit < units, z, 0.0)
        (rr, ri), (zr, zi), (qr, qi) = [(v[:fields], v[fields:]) for v in (r, z, q)]
        products = [
            rr * rr + ri * ri,
            rr * zr + ri * zi,
            rr * zi - ri * zr,
            zr * zr + zi * zi,
            rr * qr + ri * qi,
            rr * qi - ri * qr,
            zr * qr + zi * qi,
            zr * qi - zi * qr,
            qr * qr + qi * qi,
        ]
        totals = products if totals is None else [t + p for t, p in zip(totals, products)]
    lines = flat_lines([jnp.sum(t, axis=1, keepdims=True) for t in totals], fields)
    out_ref[...] = jnp.broadcast_to(lines[None], out_ref.shape)


def final_kernel(fields, sums_ref, right_ref, image_ref, out_ref):
    units = image_ref.shape[0]
    sums = columns_of(jnp.sum(sums_ref[...], axis=0), 9, fields)
    a_real, a_imag, b_real, b_imag = [
        jnp.broadcast_to(value, (fields, LANES)) for value in krylov_coefficients(sums)
    ]
    for k in range(units):
        lanes = slice(k * LANES, (k + 1) * LANES)
        r_real, r_imag = right_ref[:fields, lanes], right_ref[fields:, lanes]
        z_real, z_imag = image_ref[k, :fields], image_ref[k, fields:]
        out_ref[:fields, lanes] = a_real * r_real - a_imag * r_imag + b_real * z_real - b_imag * z_imag
        out_ref[fields:, lanes] = a_real * r_imag + a_imag * r_real + b_real * z_imag + b_imag * z_real


def params(mebibytes=16):
    return pltpu.CompilerParams(vmem_limit_bytes=mebibytes * 1024 * 1024)


def item_route(rows, group, columns, send):
    items = rows * send // group

    def flat(r, g):
        return (g // columns * rows + r) * columns + g % columns

    assert items * group == rows * send and (items % send == 0 or send % items == 0)
    routes = []
    for first in range(0, items, send):
        numbers = [(g * items + first) // send for g in range(group)]
        routes.append([(flat(r, g), flat((numbers[g] - r) % rows, g)) for r in range(rows) for g in range(group)])
    return items, routes


def local(
    right_side,
    near_tiles,
    tile_pairs,
    tile_count,
    panel_expansions,
    leaf_of_panel,
    far_pick,
    far_target,
    far_offset,
    translations,
):
    fields, panels = right_side.shape[1:]
    coefs = panel_expansions.shape[2]
    tile = near_tiles.shape[2]
    send = far_pick.shape[2]
    rows = lax.axis_size("row")
    group = lax.axis_size("grp") * lax.axis_size("col")
    row_here = lax.axis_index("row")
    own = lax.axis_index("grp") * lax.axis_size("col") + lax.axis_index("col")
    both = 2 * fields
    units = panels // LANES
    share = -(-units // group)
    edge = REACH * tile
    edge_units = edge // LANES
    width = tile // LANES + 1
    items, routes = item_route(rows, group, lax.axis_size("col"), send)

    assert rows % 2 == 0
    neighbours = [[r + 1 - 2 * (r % 2) for r in range(rows)], [(r - 1 + 2 * (r % 2)) % rows for r in range(rows)]]
    own_place, row_place = own.reshape(1), row_here.reshape(1)
    core_place, chip_place = lax.rem(own, 2).reshape(1), lax.div(own, 2).reshape(1)
    slots = near_tiles.shape[1]
    pad_coefs = -(-coefs // 8) * 8
    chips = group // 2
    steps_between = range(chips - 1, 0, -1)
    assert group == 2 * chips and chips & (chips - 1) == 0 and LANES % fields == 0
    window_shape = jax.ShapeDtypeStruct((items, width, pad_coefs, 2, LANES), BF16)
    item_shape = jax.ShapeDtypeStruct((items, fields, 2 * pad_coefs + ITEM_REST), BF16)
    plan_shape = jax.ShapeDtypeStruct((item_place(slots, items),), jnp.int32)
    part_shape = (share, both, LANES)

    def in_hbm(value):
        return pltpu.with_memory_space_constraint(value, pltpu.HBM)

    leaves = leaf_of_panel.reshape(units, 1, LANES)
    expansions = panel_expansions.transpose(2, 0, 1).reshape(coefs, 2, units, LANES).transpose(0, 2, 1, 3)
    expansions = in_hbm(expansions)
    moves = in_hbm(translations.transpose(0, 2, 1, 3))
    picks = far_pick.transpose(0, 2, 1)
    plan_scratch = [pltpu.SMEM(plan_shape.shape, jnp.int32), pltpu.SemaphoreType.DMA]

    plan, made, windows, leaves, right = pl.pallas_call(
        functools.partial(begin_kernel, fields, items, width, send, rows),
        out_shape=(
            plan_shape,
            item_shape,
            pltpu.VMEM(window_shape.shape, BF16),
            jax.ShapeDtypeStruct(leaves.shape, jnp.int32),
            jax.ShapeDtypeStruct((both, panels), F32),
        ),
        in_specs=[SMEM] * 2 + [HBM] * 8,
        out_specs=(SMEM,) + (VMEM,) * 4,
        scratch_shapes=[
            pltpu.SMEM(value.shape, jnp.int32)
            for value in (picks, leaf_of_panel, far_target, far_offset, tile_pairs)
        ]
        + [pltpu.SemaphoreType.DMA((7,)), pltpu.SemaphoreType.DMA((items, width))],
        compiler_params=params(),
        name="begin",
    )(
        row_place,
        own_place,
        in_hbm(picks),
        in_hbm(leaf_of_panel),
        in_hbm(leaves),
        in_hbm(far_target),
        in_hbm(far_offset),
        in_hbm(tile_pairs),
        in_hbm(right_side.reshape(both, panels)),
        expansions,
    )

    def exchanged(made):
        parts = [
            lax.ppermute(made[k * send : k * send + min(send, items)], EVERY, route) for k, route in enumerate(routes)
        ]
        return parts[0] if len(parts) == 1 else jnp.concatenate(parts)

    def from_neighbours(image):
        edge_shape = (both, edge) if image.ndim == 2 else (edge_units, both, LANES)
        one, two = pl.pallas_call(
            edge_kernel,
            out_shape=(jax.ShapeDtypeStruct(edge_shape, BF16),) * 2,
            in_specs=[SMEM, VMEM],
            out_specs=(VMEM, VMEM),
            compiler_params=params(),
            name="edges",
        )(row_place, image)
        return [
            lax.ppermute(value, "row", list(enumerate(targets))) for value, targets in zip((one, two), neighbours)
        ]

    image_shape = jax.ShapeDtypeStruct((units, both, LANES), F32)
    target_windows, moved = pl.pallas_call(
        functools.partial(fetch_kernel, items, width, slots),
        out_shape=(
            pltpu.VMEM(window_shape.shape, BF16),
            pltpu.VMEM((items, 2 * pad_coefs, coefs), BF16),
        ),
        in_specs=[ANY, HBM, HBM],
        out_specs=(VMEM, VMEM),
        scratch_shapes=plan_scratch
        + [
            pltpu.VMEM((items, coefs, 2, coefs), BF16),
            pltpu.SemaphoreType.DMA((items, width)),
            pltpu.SemaphoreType.DMA((items,)),
        ],
        compiler_params=params(24),
        cost_estimate=pl.CostEstimate(flops=0, bytes_accessed=6 * window_shape.size, transcendentals=0),
        name="fetch",
    )(plan, expansions, moves)

    def far(taken):
        return pl.pallas_call(
            functools.partial(far_kernel, fields, items, width, slots),
            out_shape=jax.ShapeDtypeStruct((items, width, both, LANES), F32),
            in_specs=[ANY] + [VMEM] * 4,
            out_specs=VMEM,
            scratch_shapes=plan_scratch,
            compiler_params=params(),
            name="far",
        )(plan, leaves, taken, moved, target_windows)

    def core_parts(image, one, two, low, dtype):
        half_shape = jax.ShapeDtypeStruct((chips, *part_shape), dtype)
        keep, give = pl.pallas_call(
            functools.partial(near_kernel, fields, units),
            out_shape=(half_shape, half_shape),
            in_specs=[SMEM, SMEM, SMEM, ANY] + [VMEM] * 5,
            out_specs=(VMEM, VMEM),
            scratch_shapes=[
                pltpu.VMEM((units + 2 * edge_units, both, LANES), low.dtype),
                pltpu.VMEM((share * group, both, LANES), F32),
            ]
            + plan_scratch,
            compiler_params=params(),
            cost_estimate=pl.CostEstimate(
                flops=8 * fields * near_tiles.size // 2, bytes_accessed=2 * near_tiles.size, transcendentals=0
            ),
            name="near",
        )(core_place, row_place, tile_count, plan, image, one, two, low, near_tiles)
        return keep, swapped(give, 1)

    def swapped(value, step):
        return lax.ppermute(value, GROUP, [(g, g ^ step) for g in range(group)])

    def whole_sum(keep, got):
        pair = pl.pallas_call(
            pair_kernel,
            out_shape=jax.ShapeDtypeStruct(keep.shape, BF16),
            in_specs=[VMEM, VMEM],
            out_specs=VMEM,
            compiler_params=params(),
            name="pair",
        )(keep, got)
        arrived = {step: swapped(pair, 2 * step) for step in steps_between}
        mine = pl.pallas_call(
            close_kernel,
            out_shape=jax.ShapeDtypeStruct(keep.shape, F32),
            in_specs=[VMEM] * chips,
            out_specs=VMEM,
            compiler_params=params(),
            name="close",
        )(pair, *[arrived[step] for step in range(1, chips)])
        theirs = swapped(mine, 1)
        low_shape = jax.ShapeDtypeStruct((units, both, LANES), BF16)
        return pl.pallas_call(
            functools.partial(assemble_kernel, fields, items, width, slots),
            out_shape=(image_shape, low_shape, item_shape),
            in_specs=[SMEM, ANY] + [VMEM] * 4,
            out_specs=(VMEM,) * 3,
            scratch_shapes=[pltpu.VMEM((share * group, both, LANES), F32)] + plan_scratch,
            compiler_params=params(),
            name="assemble",
        )(core_place, plan, leaves, mine, theirs, windows)

    def share_pieces(keep, got):
        pieces = pl.pallas_call(
            fold_kernel,
            out_shape=(jax.ShapeDtypeStruct(part_shape, F32),)
            + (jax.ShapeDtypeStruct(part_shape, BF16),) * (chips - 1),
            in_specs=[SMEM, VMEM, VMEM],
            out_specs=(VMEM,) * chips,
            compiler_params=params(),
            name="fold",
        )(chip_place, keep, got)
        arrived = {step: swapped(pieces[step], 2 * step) for step in steps_between}
        return [pieces[0]] + [arrived[step] for step in range(1, chips)]

    image = far(exchanged(made))
    z_all, z_low, made = whole_sum(*core_parts(image, *from_neighbours(right), right, F32))
    image = far(exchanged(made))
    pieces = share_pieces(*core_parts(image, *from_neighbours(z_low), z_low, BF16))

    lines = -(-9 * fields // LANES)
    sums = pl.pallas_call(
        functools.partial(gram_kernel, fields),
        out_shape=jax.ShapeDtypeStruct((group * rows, lines, LANES), F32),
        in_specs=[SMEM] + [VMEM] * (2 + chips),
        out_specs=VMEM,
        compiler_params=params(),
        name="gram",
    )(own_place, right, z_all, *pieces)
    sums = lax.all_to_all(sums, EVERY, 0, 0, tiled=True)
    out = pl.pallas_call(
        functools.partial(final_kernel, fields),
        out_shape=jax.ShapeDtypeStruct((both, panels), F32),
        in_specs=[VMEM, VMEM, VMEM],
        out_specs=VMEM,
        compiler_params=params(),
        name="combine",
    )(sums, right, z_all)
    return out.reshape(right_side.shape)


def krylov_coefficients(sums):
    rr, rz_real, rz_imag, zz, rq_real, rq_imag, zq_real, zq_imag, qq = sums

    def times(left, right):
        return left[0] * right[0] - left[1] * right[1], left[0] * right[1] + left[1] * right[0]

    def conj_times(left, right):
        return left[0] * right[0] + left[1] * right[1], left[0] * right[1] - left[1] * right[0]

    def scale(factor, value):
        return factor * value[0], factor * value[1]

    def plus(*values):
        return sum(v[0] for v in values), sum(v[1] for v in values)

    def size(value):
        return value[0] * value[0] + value[1] * value[1]

    rz, rq, zq = (rz_real, rz_imag), (rq_real, rq_imag), (zq_real, zq_imag)
    beta = jnp.sqrt(rr + EPSILON)
    inv = 1.0 / beta
    norm_one = rr * inv * inv
    product = scale(inv * inv, rz)
    h_first = (0.5 * norm_one + product[0], product[1])
    shift = (h_first[0] - 0.5, h_first[1])
    residue = zz * inv * inv - 2.0 * conj_times(shift, product)[0] + size(shift) * norm_one
    residue = jnp.maximum(residue, 0.0)
    h_sub = jnp.sqrt(residue + EPSILON)
    alpha = inv / h_sub
    gamma = scale(-alpha, shift)
    h_upper = scale(
        inv,
        plus(
            scale(0.5, plus(scale(alpha, rz), scale(rr, gamma))), scale(alpha, rq), times(gamma, rz)
        ),
    )
    second = plus(
        scale(alpha * alpha, zq),
        scale(alpha * zz, gamma),
        scale(alpha, conj_times(gamma, rq)),
        scale(size(gamma), rz),
    )
    h_middle = (0.5 * residue / (h_sub * h_sub) + second[0], second[1])
    keep = (h_middle[0] - 0.5, h_middle[1])
    on_z = plus(gamma, scale(-alpha, keep))
    on_r = plus(scale(-inv, h_upper), scale(-1.0, times(keep, gamma)))
    last = (
        alpha * alpha * qq
        + size(on_z) * zz
        + size(on_r) * rr
        + 2.0
        * (
            conj_times(on_r, times(on_z, rz))[0]
            + alpha * conj_times(on_r, rq)[0]
            + alpha * conj_times(on_z, zq)[0]
        )
    )
    h_last = jnp.sqrt(jnp.maximum(last, 0.0) + EPSILON)
    radius = jnp.sqrt(size(h_first) + h_sub * h_sub)
    cosine = scale(1.0 / radius, h_first)
    sine = h_sub / radius
    upper = plus(conj_times(cosine, h_upper), scale(sine, h_middle))
    lower = plus(times(cosine, h_middle), scale(-sine, h_upper))
    radius_two = jnp.sqrt(size(lower) + h_last * h_last)
    cosine_two = scale(1.0 / radius_two, lower)
    weight_two = scale(-sine * beta / radius_two, (cosine_two[0], -cosine_two[1]))
    goal = scale(beta, (cosine[0], -cosine[1]))
    weight_one = scale(1.0 / radius, plus(goal, scale(-1.0, times(upper, weight_two))))
    on_right = plus(scale(inv, weight_one), times(weight_two, gamma))
    on_image = scale(alpha, weight_two)
    return on_right[0], on_right[1], on_image[0], on_image[1]


def solution(mesh):
    return jax.shard_map(
        local,
        mesh=mesh,
        in_specs=(
            P(None, None, "row"),
            P(None, ("grp", "row", "col"), None, None),
            P(("grp", "row", "col")),
            P(("grp", "row", "col")),
            P(None, "row", None),
            P("row", None),
            P(),
            P("row", None),
            P("row", None),
            P(),
        ),
        out_specs=P(None, None, "row"),
        check_vma=False,
    )
```

```python
import functools

import jax
import jax.numpy as jnp
from jax import lax
from jax.experimental import pallas as pl
from jax.experimental.pallas import tpu as pltpu
from jax.sharding import PartitionSpec as P

REACH = 2
SPAN = 2 * REACH + 1
LANES = 128
EPSILON = 1e-06
GROUP = ("grp", "col")
CODES = 0
PER_ITEM = 5
PIECES = 4
EVERY = ("grp", "row", "col")

F32 = jnp.float32
BF16 = jnp.bfloat16
SMEM = pl.BlockSpec(memory_space=pltpu.SMEM)
VMEM = pl.BlockSpec(memory_space=pltpu.VMEM)
HBM = pl.BlockSpec(memory_space=pltpu.HBM)


def dot_nn(left, right):
    return lax.dot_general(left, right, (((1,), (0,)), ((), ())), preferred_element_type=F32)


def dot_nt(left, right):
    return lax.dot_general(left, right, (((1,), (1,)), ((), ())), preferred_element_type=F32)


def halves(rows):
    if rows.dtype != F32:
        return rows
    high = rows.astype(BF16)
    return jnp.concatenate([high, (rows - high.astype(F32)).astype(BF16)], axis=0)


def joined(sums, count):
    return sums if sums.shape[0] == count else sums[:count] + sums[count:]


def odd_lanes(shape):
    return lax.rem(lax.broadcasted_iota(jnp.int32, shape, 1), 2) == 1


def twice(value, width):
    rows = value.shape[0]
    parts = []
    for k in range(width // LANES):
        first = (k // 2) * LANES
        part = value[:, first : first + LANES]
        if part.shape[1] < LANES:
            part = jnp.concatenate([part, jnp.zeros((rows, LANES - part.shape[1]), part.dtype)], axis=-1)
        lane = lax.broadcasted_iota(jnp.int32, (rows, LANES), 1)
        parts.append(jnp.take_along_axis(part, lax.div(lane, 2) + (k % 2) * (LANES // 2), axis=1))
    return jnp.concatenate(parts, axis=-1)


def from_left(value):
    return pltpu.roll(value, 1, 1)


def from_right(value):
    return pltpu.roll(value, value.shape[1] - 1, 1)


def item_place(slots, item):
    return CODES + slots + PER_ITEM * item


def window_start(leaf_ref, leaf, width):
    units = leaf_ref.shape[1] // LANES
    before = jnp.int32(0)
    for k in range(units):
        before = before + (leaf_ref[0, k * LANES] < leaf).astype(jnp.int32)
    return jnp.clip(before - 1, 0, units - width)


def window_mask(leaves_ref, leaf, unit, rows, width):
    leaves = jnp.concatenate([leaves_ref[unit + k] for k in range(width)], axis=-1)
    return jnp.broadcast_to(leaves, (rows, width * LANES)) == leaf


def window_copies(exp_ref, unit, window_ref, sem, width):
    coefs = exp_ref.shape[0]
    step = -(-coefs // PIECES)
    copies = []
    for k in range(width):
        for p in range(PIECES):
            part = pl.ds(p * step, min(step, coefs - p * step))
            copies.append(
                pltpu.make_async_copy(exp_ref.at[part, unit + k], window_ref.at[k, part], sem.at[k, p])
            )
    return copies


def clear_rest(window_ref, coefs, width):
    rest = window_ref.shape[1] - coefs
    for k in range(width):
        window_ref[k, pl.ds(coefs, rest)] = jnp.zeros((rest, 2, LANES), BF16)


def multi_rows(fields, width, leaf, unit, leaves_ref, low_ref, window_ref):
    if len(low_ref.shape) == 2:
        first = pl.multiple_of(unit * LANES, LANES)
        rows = low_ref[:, pl.ds(first, width * LANES)]
    else:
        rows = jnp.concatenate([low_ref[unit + k] for k in range(width)], axis=-1)
    mask = window_mask(leaves_ref, leaf, unit, 2 * fields, width)
    rows = halves(jnp.where(mask, rows.astype(F32), 0.0).astype(rows.dtype))
    expansions = jnp.concatenate([as_rows(window_ref.at[k]) for k in range(width)], axis=-1)
    total = joined(dot_nt(rows, expansions), 2 * fields)
    on_real, on_imag = total[:fields], total[fields:]
    odd = odd_lanes(on_real.shape)
    other = jnp.where(odd, from_left(on_imag), from_right(on_imag))
    return jnp.where(odd, -on_real, on_real) - other


def as_rows(ref):
    return ref.reshape(ref.shape[0] * 2, ref.shape[2])[...]


def edge_kernel(row_ref, image_ref, one_ref, two_ref):
    even = lax.rem(row_ref[0], 2) == 0
    if len(image_ref.shape) == 2:
        edge = one_ref.shape[1]
        first, last = image_ref[:, :edge], image_ref[:, image_ref.shape[1] - edge :]
    else:
        edge = one_ref.shape[0]
        first, last = image_ref[:edge], image_ref[image_ref.shape[0] - edge :]
    first, last = first.astype(one_ref.dtype), last.astype(one_ref.dtype)

    @pl.when(even)
    def _():
        one_ref[...], two_ref[...] = last, first

    @pl.when(jnp.logical_not(even))
    def _():
        one_ref[...], two_ref[...] = first, last


def begin_kernel(
    fields, items, width, send, rows, row_ref, own_ref, pick_hbm, leaf_hbm, leaves_hbm,
    target_hbm, offset_hbm, pairs_hbm, right_hbm, exp_ref,
    plan_ref, out_ref, window_ref, leaves_ref, right_ref,
    pick_ref, leaf_ref, target_ref, offset_ref, pairs_ref, sem, window_sem,
):
    loads = [
        pltpu.make_async_copy(source, place, sem.at[k])
        for k, (source, place) in enumerate(
            (
                (leaf_hbm, leaf_ref),
                (pick_hbm, pick_ref),
                (target_hbm, target_ref),
                (offset_hbm, offset_ref),
                (pairs_hbm, pairs_ref),
                (leaves_hbm, leaves_ref),
                (right_hbm, right_ref),
            )
        )
    ]
    for load in loads:
        load.start()
    for i in range(items):
        clear_rest(window_ref.at[i], exp_ref.shape[0], width)
    slots = pairs_ref.shape[0]
    own = own_ref[0]
    loads[0].wait()
    loads[1].wait()
    row = row_ref[0]

    def partner(i, coming):
        number = own * items + i
        pair, number = lax.div(number, send), lax.rem(number, send)
        if not is_power(rows):
            return lax.rem(pair - row + rows, rows), number
        if coming and items == 1 and send == 2:
            number = jnp.where(pair == 0, 1 - number, number)
        return lax.bitwise_xor(pair, row), number

    for i in range(items):
        other, number = partner(i, False)
        leaf = pick_ref[other, number, row]
        unit = window_start(leaf_ref, leaf, width)
        place = item_place(slots, i)
        plan_ref[place], plan_ref[place + 1] = leaf, unit
        for copy in window_copies(exp_ref, unit, window_ref.at[i], window_sem.at[i], width):
            copy.start()
    for load in loads[2:]:
        load.wait()
    for s in range(slots):
        plan_ref[CODES + s] = pairs_ref[s]
    for i in range(items):
        place = item_place(slots, i)
        other, number = partner(i, True)
        leaf = target_ref[0, other * send + number]
        plan_ref[place + 2], plan_ref[place + 3] = leaf, window_start(leaf_ref, leaf, width)
        plan_ref[place + 4] = offset_ref[0, other * send + number]
    for i in range(items):
        place = item_place(slots, i)
        leaf, unit = plan_ref[place], plan_ref[place + 1]
        for copy in window_copies(exp_ref, unit, window_ref.at[i], window_sem.at[i], width):
            copy.wait()
        out_ref[i] = multi_rows(fields, width, leaf, unit, leaves_ref, right_ref, window_ref.at[i]).astype(BF16)


def fetch_kernel(items, width, slots, plan_ref, exp_ref, trans_ref, window_ref, moved_ref, trans_buf, sem, trans_sem):
    coefs = trans_ref.shape[3]
    for i in range(items):
        clear_rest(window_ref.at[i], coefs, width)

    def trans_copy(i):
        offset = plan_ref[item_place(slots, i) + 4]
        return pltpu.make_async_copy(trans_ref.at[offset], trans_buf.at[i], trans_sem.at[i])

    def exp_copies(i):
        unit = plan_ref[item_place(slots, i) + 3]
        return window_copies(exp_ref, unit, window_ref.at[i], sem.at[i], width)

    for i in range(items):
        trans_copy(i).start()
        for copy in exp_copies(i):
            copy.start()
    rest = moved_ref.shape[1] - 2 * coefs
    for i in range(items):
        trans_copy(i).wait()
        moved_ref[i, pl.ds(0, 2 * coefs)] = trans_buf[i].reshape(2 * coefs, coefs)
        moved_ref[i, pl.ds(2 * coefs, rest)] = jnp.zeros((rest, coefs), BF16)
        for copy in exp_copies(i):
            copy.wait()


def near_sources(row_ref, one_ref, two_ref, here_ref, units, ext):
    edge = (ext.shape[0] - units) // 2
    even = lax.rem(row_ref[0], 2) == 0
    one_at = jnp.where(even, edge + units, 0)
    two_at = jnp.where(even, 0, edge + units)
    if len(here_ref.shape) == 2:
        for k in range(edge):
            lanes = slice(k * LANES, (k + 1) * LANES)
            ext[one_at + k] = one_ref[:, lanes].astype(ext.dtype)
            ext[two_at + k] = two_ref[:, lanes].astype(ext.dtype)
        for k in range(units):
            ext[edge + k] = here_ref[:, k * LANES : (k + 1) * LANES]
    else:
        ext[pl.ds(one_at, edge)] = one_ref[...]
        ext[pl.ds(two_at, edge)] = two_ref[...]
        ext[edge : edge + units] = here_ref[...]


def near_kernel(
    fields, row_ref, count_ref, plan_ref, one_ref, two_ref, here_ref, tiles_ref, out_ref, ext
):
    near_sources(row_ref, one_ref, two_ref, here_ref, out_ref.shape[0], ext)
    out_ref[...] = jnp.zeros_like(out_ref)
    slots, tile = tiles_ref.shape[1], tiles_ref.shape[2]
    per = tile // LANES
    for s in range(slots):
        code = plan_ref[CODES + s]
        target = lax.div(code, SPAN)
        source = target + lax.rem(code, SPAN)
        rows = halves(jnp.concatenate([ext[source * per + k] for k in range(per)], axis=-1))
        on_real = joined(dot_nt(rows, tiles_ref[0, s]), 2 * fields)
        on_imag = joined(dot_nt(rows, tiles_ref[1, s]), 2 * fields)
        value = jnp.concatenate(
            [on_real[:fields] - on_imag[fields:], on_real[fields:] + on_imag[:fields]], axis=0
        )
        value = jnp.where(s < count_ref[0], value, 0.0)
        for k in range(per):
            out_ref[target * per + k] += value[:, k * LANES : (k + 1) * LANES]


def far_kernel(
    fields, items, width, slots, core_ref, plan_ref, leaves_ref, partial_ref, item_ref, trans_ref, window_ref,
    keep_ref, give_ref, total,
):
    units = partial_ref.shape[0]
    total[0:units] = partial_ref[...]
    if total.shape[0] > units:
        total[units:] = jnp.zeros((total.shape[0] - units, *total.shape[1:]), F32)
    for i in range(items):
        plain = item_ref[i].astype(F32)
        odd = odd_lanes(plain.shape)
        turned = jnp.where(odd, from_left(plain), -from_right(plain))
        rows = jnp.concatenate([plain, turned], axis=0).astype(BF16)
        local_field = dot_nn(rows, trans_ref[i]).astype(BF16).astype(F32)
        local_field = twice(local_field, plain.shape[1])
        local_real, local_imag = local_field[:fields], local_field[fields:]
        rows = jnp.concatenate(
            [jnp.where(odd, -local_imag, local_real), jnp.where(odd, local_real, local_imag)], axis=0
        ).astype(BF16)
        expansions = jnp.concatenate([as_rows(window_ref.at[i, k]) for k in range(width)], axis=-1)
        place = item_place(slots, i)
        leaf, unit = plan_ref[place + 2], plan_ref[place + 3]
        mask = window_mask(leaves_ref, leaf, unit, 2 * fields, width)
        image = jnp.where(mask, dot_nn(rows, expansions), 0.0)
        for k in range(width):
            total[unit + k] += image[:, k * LANES : (k + 1) * LANES]
    chips, share = keep_ref.shape[:2]
    core = core_ref[0]
    for c in range(chips):
        keep_ref[c] = total[pl.ds((2 * c + core) * share, share)].astype(keep_ref.dtype)
        give_ref[c] = total[pl.ds((2 * c + 1 - core) * share, share)].astype(give_ref.dtype)


def fold_kernel(chip_ref, keep_ref, got_ref, own_ref, *out_refs):
    for step, out_ref in enumerate((own_ref,) + out_refs):
        chip = lax.bitwise_xor(chip_ref[0], step)
        out_ref[...] = (keep_ref[chip].astype(F32) + got_ref[chip].astype(F32)).astype(out_ref.dtype)


def pair_kernel(keep_ref, got_ref, out_ref):
    out_ref[...] = (keep_ref[...].astype(F32) + got_ref[...].astype(F32)).astype(out_ref.dtype)


def tree_sum(values):
    while len(values) > 1:
        values = [values[k] + values[k + 1] for k in range(0, len(values), 2)]
    return values[0]


def close_kernel(*refs):
    refs[-1][...] = tree_sum([ref[...].astype(F32) for ref in refs[:-1]])


def assemble_kernel(
    fields, items, width, slots, core_ref, plan_ref, leaves_ref, mine_ref, theirs_ref, window_ref,
    out_ref, low_ref, made_ref, whole,
):
    chips, share = mine_ref.shape[:2]
    units = out_ref.shape[0]
    core = core_ref[0]
    for chip in range(chips):
        whole[pl.ds((2 * chip + core) * share, share)] = mine_ref[chip]
        whole[pl.ds((2 * chip + 1 - core) * share, share)] = theirs_ref[chip]
    out_ref[...] = whole[0:units]
    low_ref[...] = whole[0:units].astype(BF16)
    for i in range(items):
        place = item_place(slots, i)
        made_ref[i] = multi_rows(
            fields, width, plan_ref[place], plan_ref[place + 1], leaves_ref, low_ref, window_ref.at[i]
        ).astype(BF16)


def flat_lines(columns, fields):
    per = LANES // fields
    lines = []
    for first in range(0, len(columns), per):
        some = columns[first : first + per]
        if len(some) < per:
            some = some + [jnp.zeros(((per - len(some)) * fields, 1), F32)]
        square = jnp.broadcast_to(jnp.concatenate(some, axis=0), (LANES, LANES))
        lines.append(jnp.transpose(square)[:1])
    return jnp.concatenate(lines, axis=0)


def columns_of(lines, count, fields):
    per = LANES // fields
    columns = []
    for k in range(lines.shape[0]):
        square = jnp.transpose(jnp.broadcast_to(lines[k : k + 1], (LANES, LANES)))
        columns += [square[j * fields : (j + 1) * fields, :1] for j in range(per)]
    return columns[:count]


def gram_kernel(fields, own_ref, right_ref, image_ref, *pieces_and_out):
    *pieces, out_ref = pieces_and_out
    units = image_ref.shape[0]
    share = pieces[0].shape[0]
    totals = None
    for k in range(share):
        unit = own_ref[0] * share + k
        place = jnp.minimum(unit, units - 1)
        r = right_ref[:, pl.ds(pl.multiple_of(place * LANES, LANES), LANES)]
        z = image_ref[place]
        q = tree_sum([piece[k].astype(F32) for piece in pieces])
        r = jnp.where(unit < units, r, 0.0)
        z = jnp.where(unit < units, z, 0.0)
        (rr, ri), (zr, zi), (qr, qi) = [(v[:fields], v[fields:]) for v in (r, z, q)]
        products = [
            rr * rr + ri * ri,
            rr * zr + ri * zi,
            rr * zi - ri * zr,
            zr * zr + zi * zi,
            rr * qr + ri * qi,
            rr * qi - ri * qr,
            zr * qr + zi * qi,
            zr * qi - zi * qr,
            qr * qr + qi * qi,
        ]
        totals = products if totals is None else [t + p for t, p in zip(totals, products)]
    lines = flat_lines([jnp.sum(t, axis=1, keepdims=True) for t in totals], fields)
    out_ref[...] = jnp.broadcast_to(lines[None], out_ref.shape)


def final_kernel(fields, sums_ref, right_ref, image_ref, out_ref):
    units = image_ref.shape[0]
    sums = columns_of(jnp.sum(sums_ref[...], axis=0), 9, fields)
    a_real, a_imag, b_real, b_imag = [
        jnp.broadcast_to(value, (fields, LANES)) for value in krylov_coefficients(sums)
    ]
    for k in range(units):
        lanes = slice(k * LANES, (k + 1) * LANES)
        r_real, r_imag = right_ref[:fields, lanes], right_ref[fields:, lanes]
        z_real, z_imag = image_ref[k, :fields], image_ref[k, fields:]
        out_ref[:fields, lanes] = a_real * r_real - a_imag * r_imag + b_real * z_real - b_imag * z_imag
        out_ref[fields:, lanes] = a_real * r_imag + a_imag * r_real + b_real * z_imag + b_imag * z_real


def params(mebibytes=16):
    return pltpu.CompilerParams(vmem_limit_bytes=mebibytes * 1024 * 1024)


def is_power(count):
    return count & (count - 1) == 0


def item_route(rows, group, columns, send):
    items = rows * send // group

    def flat(r, g):
        return (g // columns * rows + r) * columns + g % columns

    def target(r, g, pair):
        if not is_power(rows):
            return flat((pair - r) % rows, g)
        return flat(r ^ pair, g ^ 1 if pair == 0 and items == 1 and send == 2 else g)

    assert items * group == rows * send and (items % send == 0 or send % items == 0)
    routes = []
    for first in range(0, items, send):
        pairs = [(g * items + first) // send for g in range(group)]
        routes.append([(flat(r, g), target(r, g, pairs[g])) for r in range(rows) for g in range(group)])
    return items, routes


def local(
    right_side,
    near_tiles,
    tile_pairs,
    tile_count,
    panel_expansions,
    leaf_of_panel,
    far_pick,
    far_target,
    far_offset,
    translations,
):
    fields, panels = right_side.shape[1:]
    coefs = panel_expansions.shape[2]
    tile = near_tiles.shape[2]
    send = far_pick.shape[2]
    rows = lax.axis_size("row")
    group = lax.axis_size("grp") * lax.axis_size("col")
    row_here = lax.axis_index("row")
    own = lax.axis_index("grp") * lax.axis_size("col") + lax.axis_index("col")
    both = 2 * fields
    units = panels // LANES
    share = -(-units // group)
    edge = REACH * tile
    edge_units = edge // LANES
    width = tile // LANES + 1
    items, routes = item_route(rows, group, lax.axis_size("col"), send)

    assert rows % 2 == 0
    neighbours = [[r + 1 - 2 * (r % 2) for r in range(rows)], [(r - 1 + 2 * (r % 2)) % rows for r in range(rows)]]
    own_place, row_place = own.reshape(1), row_here.reshape(1)
    core_place, chip_place = lax.rem(own, 2).reshape(1), lax.div(own, 2).reshape(1)
    slots = near_tiles.shape[1]
    pad_coefs = -(-coefs // 8) * 8
    chips = group // 2
    steps_between = range(chips - 1, 0, -1)
    assert group == 2 * chips and chips & (chips - 1) == 0 and LANES % fields == 0
    window_shape = jax.ShapeDtypeStruct((items, width, pad_coefs, 2, LANES), BF16)
    item_shape = jax.ShapeDtypeStruct((items, fields, 2 * pad_coefs), BF16)
    part_shape = (share, both, LANES)

    def in_hbm(value):
        return pltpu.with_memory_space_constraint(value, pltpu.HBM)

    leaves = leaf_of_panel.reshape(units, 1, LANES)
    expansions = panel_expansions.transpose(2, 0, 1).reshape(coefs, 2, units, LANES).transpose(0, 2, 1, 3)
    expansions = in_hbm(expansions)
    moves = in_hbm(translations.transpose(0, 2, 1, 3))
    picks = far_pick.transpose(0, 2, 1)

    plan, made, windows, leaves, right = pl.pallas_call(
        functools.partial(begin_kernel, fields, items, width, send, rows),
        out_shape=(
            pltpu.SMEM((item_place(slots, items),), jnp.int32),
            item_shape,
            pltpu.VMEM(window_shape.shape, BF16),
            jax.ShapeDtypeStruct(leaves.shape, jnp.int32),
            jax.ShapeDtypeStruct((both, panels), F32),
        ),
        in_specs=[SMEM] * 2 + [HBM] * 8,
        out_specs=(SMEM,) + (VMEM,) * 4,
        scratch_shapes=[
            pltpu.SMEM(value.shape, jnp.int32)
            for value in (picks, leaf_of_panel, far_target, far_offset, tile_pairs)
        ]
        + [pltpu.SemaphoreType.DMA((7,)), pltpu.SemaphoreType.DMA((items, width, PIECES))],
        compiler_params=params(),
        name="begin",
    )(
        row_place,
        own_place,
        in_hbm(picks),
        in_hbm(leaf_of_panel),
        in_hbm(leaves),
        in_hbm(far_target),
        in_hbm(far_offset),
        in_hbm(tile_pairs),
        in_hbm(right_side.reshape(both, panels)),
        expansions,
    )

    def exchanged(made):
        parts = [
            lax.ppermute(made[k * send : k * send + min(send, items)], EVERY, route) for k, route in enumerate(routes)
        ]
        return parts[0] if len(parts) == 1 else jnp.concatenate(parts)

    def from_neighbours(image):
        edge_shape = (both, edge) if image.ndim == 2 else (edge_units, both, LANES)
        one, two = pl.pallas_call(
            edge_kernel,
            out_shape=(jax.ShapeDtypeStruct(edge_shape, BF16),) * 2,
            in_specs=[SMEM, VMEM],
            out_specs=(VMEM, VMEM),
            compiler_params=params(),
            name="edges",
        )(row_place, image)
        return [
            lax.ppermute(value, "row", list(enumerate(targets))) for value, targets in zip((one, two), neighbours)
        ]

    image_shape = jax.ShapeDtypeStruct((units, both, LANES), F32)
    target_windows, moved = pl.pallas_call(
        functools.partial(fetch_kernel, items, width, slots),
        out_shape=(
            pltpu.VMEM(window_shape.shape, BF16),
            pltpu.VMEM((items, 2 * pad_coefs, coefs), BF16),
        ),
        in_specs=[SMEM, HBM, HBM],
        out_specs=(VMEM, VMEM),
        scratch_shapes=[
            pltpu.VMEM((items, coefs, 2, coefs), BF16),
            pltpu.SemaphoreType.DMA((items, width, PIECES)),
            pltpu.SemaphoreType.DMA((items,)),
        ],
        compiler_params=params(24),
        cost_estimate=pl.CostEstimate(flops=0, bytes_accessed=6 * window_shape.size, transcendentals=0),
        name="fetch",
    )(plan, expansions, moves)

    def swapped(value, step):
        return lax.ppermute(value, GROUP, [(g, g ^ step) for g in range(group)])

    def near(one, two, low):
        return pl.pallas_call(
            functools.partial(near_kernel, fields),
            out_shape=image_shape,
            in_specs=[SMEM] * 3 + [VMEM] * 4,
            out_specs=VMEM,
            scratch_shapes=[pltpu.VMEM((units + 2 * edge_units, both, LANES), low.dtype)],
            compiler_params=params(),
            cost_estimate=pl.CostEstimate(
                flops=8 * fields * near_tiles.size // 2, bytes_accessed=2 * near_tiles.size, transcendentals=0
            ),
            name="near",
        )(row_place, tile_count, plan, one, two, low, near_tiles)

    def core_parts(partial, taken, dtype):
        half_shape = jax.ShapeDtypeStruct((chips, *part_shape), dtype)
        keep, give = pl.pallas_call(
            functools.partial(far_kernel, fields, items, width, slots),
            out_shape=(half_shape, half_shape),
            in_specs=[SMEM, SMEM] + [VMEM] * 5,
            out_specs=(VMEM, VMEM),
            scratch_shapes=[pltpu.VMEM((share * group, both, LANES), F32)],
            compiler_params=params(),
            name="far",
        )(core_place, plan, leaves, partial, taken, moved, target_windows)
        return keep, swapped(give, 1)

    def whole_sum(keep, got):
        pair = pl.pallas_call(
            pair_kernel,
            out_shape=jax.ShapeDtypeStruct(keep.shape, BF16),
            in_specs=[VMEM, VMEM],
            out_specs=VMEM,
            compiler_params=params(),
            name="pair",
        )(keep, got)
        arrived = {step: swapped(pair, 2 * step) for step in steps_between}
        mine = pl.pallas_call(
            close_kernel,
            out_shape=jax.ShapeDtypeStruct(keep.shape, F32),
            in_specs=[VMEM] * chips,
            out_specs=VMEM,
            compiler_params=params(),
            name="close",
        )(pair, *[arrived[step] for step in range(1, chips)])
        theirs = swapped(mine, 1)
        low_shape = jax.ShapeDtypeStruct((units, both, LANES), BF16)
        return pl.pallas_call(
            functools.partial(assemble_kernel, fields, items, width, slots),
            out_shape=(image_shape, low_shape, item_shape),
            in_specs=[SMEM, SMEM] + [VMEM] * 4,
            out_specs=(VMEM,) * 3,
            scratch_shapes=[pltpu.VMEM((share * group, both, LANES), F32)],
            compiler_params=params(),
            name="assemble",
        )(core_place, plan, leaves, mine, theirs, windows)

    def share_pieces(keep, got):
        pieces = pl.pallas_call(
            fold_kernel,
            out_shape=(jax.ShapeDtypeStruct(part_shape, F32),)
            + (jax.ShapeDtypeStruct(part_shape, BF16),) * (chips - 1),
            in_specs=[SMEM, VMEM, VMEM],
            out_specs=(VMEM,) * chips,
            compiler_params=params(),
            name="fold",
        )(chip_place, keep, got)
        arrived = {step: swapped(pieces[step], 2 * step) for step in steps_between}
        return [pieces[0]] + [arrived[step] for step in steps_between]

    partial = near(*from_neighbours(right), right)
    z_all, z_low, made = whole_sum(*core_parts(partial, exchanged(made), F32))
    partial = near(*from_neighbours(z_low), z_low)
    pieces = share_pieces(*core_parts(partial, exchanged(made), BF16))

    lines = -(-9 * fields // LANES)
    sums = pl.pallas_call(
        functools.partial(gram_kernel, fields),
        out_shape=jax.ShapeDtypeStruct((group * rows, lines, LANES), F32),
        in_specs=[SMEM] + [VMEM] * (2 + chips),
        out_specs=VMEM,
        compiler_params=params(),
        name="gram",
    )(own_place, right, z_all, *pieces)
    sums = lax.all_to_all(sums, EVERY, 0, 0, tiled=True)
    out = pl.pallas_call(
        functools.partial(final_kernel, fields),
        out_shape=jax.ShapeDtypeStruct((both, panels), F32),
        in_specs=[VMEM, VMEM, VMEM],
        out_specs=VMEM,
        compiler_params=params(),
        name="combine",
    )(sums, right, z_all)
    return out.reshape(right_side.shape)


def krylov_coefficients(sums):
    rr, rz_real, rz_imag, zz, rq_real, rq_imag, zq_real, zq_imag, qq = sums

    def times(left, right):
        return left[0] * right[0] - left[1] * right[1], left[0] * right[1] + left[1] * right[0]

    def conj_times(left, right):
        return left[0] * right[0] + left[1] * right[1], left[0] * right[1] - left[1] * right[0]

    def scale(factor, value):
        return factor * value[0], factor * value[1]

    def plus(*values):
        return sum(v[0] for v in values), sum(v[1] for v in values)

    def size(value):
        return value[0] * value[0] + value[1] * value[1]

    rz, rq, zq = (rz_real, rz_imag), (rq_real, rq_imag), (zq_real, zq_imag)
    beta = jnp.sqrt(rr + EPSILON)
    inv = 1.0 / beta
    norm_one = rr * inv * inv
    product = scale(inv * inv, rz)
    h_first = (0.5 * norm_one + product[0], product[1])
    shift = (h_first[0] - 0.5, h_first[1])
    residue = zz * inv * inv - 2.0 * conj_times(shift, product)[0] + size(shift) * norm_one
    residue = jnp.maximum(residue, 0.0)
    h_sub = jnp.sqrt(residue + EPSILON)
    alpha = inv / h_sub
    gamma = scale(-alpha, shift)
    h_upper = scale(
        inv,
        plus(
            scale(0.5, plus(scale(alpha, rz), scale(rr, gamma))), scale(alpha, rq), times(gamma, rz)
        ),
    )
    second = plus(
        scale(alpha * alpha, zq),
        scale(alpha * zz, gamma),
        scale(alpha, conj_times(gamma, rq)),
        scale(size(gamma), rz),
    )
    h_middle = (0.5 * residue / (h_sub * h_sub) + second[0], second[1])
    keep = (h_middle[0] - 0.5, h_middle[1])
    on_z = plus(gamma, scale(-alpha, keep))
    on_r = plus(scale(-inv, h_upper), scale(-1.0, times(keep, gamma)))
    last = (
        alpha * alpha * qq
        + size(on_z) * zz
        + size(on_r) * rr
        + 2.0
        * (
            conj_times(on_r, times(on_z, rz))[0]
            + alpha * conj_times(on_r, rq)[0]
            + alpha * conj_times(on_z, zq)[0]
        )
    )
    h_last = jnp.sqrt(jnp.maximum(last, 0.0) + EPSILON)
    radius = jnp.sqrt(size(h_first) + h_sub * h_sub)
    cosine = scale(1.0 / radius, h_first)
    sine = h_sub / radius
    upper = plus(conj_times(cosine, h_upper), scale(sine, h_middle))
    lower = plus(times(cosine, h_middle), scale(-sine, h_upper))
    radius_two = jnp.sqrt(size(lower) + h_last * h_last)
    cosine_two = scale(1.0 / radius_two, lower)
    weight_two = scale(-sine * beta / radius_two, (cosine_two[0], -cosine_two[1]))
    goal = scale(beta, (cosine[0], -cosine[1]))
    weight_one = scale(1.0 / radius, plus(goal, scale(-1.0, times(upper, weight_two))))
    on_right = plus(scale(inv, weight_one), times(weight_two, gamma))
    on_image = scale(alpha, weight_two)
    return on_right[0], on_right[1], on_image[0], on_image[1]


def solution(mesh):
    return jax.shard_map(
        local,
        mesh=mesh,
        in_specs=(
            P(None, None, "row"),
            P(None, ("grp", "row", "col"), None, None),
            P(("grp", "row", "col")),
            P(("grp", "row", "col")),
            P(None, "row", None),
            P("row", None),
            P(),
            P("row", None),
            P("row", None),
            P(),
        ),
        out_specs=P(None, None, "row"),
        check_vma=False,
    )
```

```python
import functools

import jax
import jax.numpy as jnp
from jax import lax
from jax.experimental import pallas as pl
from jax.experimental.pallas import tpu as pltpu
from jax.sharding import PartitionSpec as P

REACH = 2
SPAN = 2 * REACH + 1
LANES = 128
EPSILON = 1e-06
GROUP = ("grp", "col")
CODES = 0
PER_ITEM = 4
PIECES = 4
EVERY = ("grp", "row", "col")

F32 = jnp.float32
BF16 = jnp.bfloat16
SMEM = pl.BlockSpec(memory_space=pltpu.SMEM)
VMEM = pl.BlockSpec(memory_space=pltpu.VMEM)
HBM = pl.BlockSpec(memory_space=pltpu.HBM)


def dot_nn(left, right):
    return lax.dot_general(left, right, (((1,), (0,)), ((), ())), preferred_element_type=F32)


def dot_nt(left, right):
    return lax.dot_general(left, right, (((1,), (1,)), ((), ())), preferred_element_type=F32)


def halves(rows):
    if rows.dtype != F32:
        return rows
    high = rows.astype(BF16)
    return jnp.concatenate([high, (rows - high.astype(F32)).astype(BF16)], axis=0)


def joined(sums, count):
    return sums if sums.shape[0] == count else sums[:count] + sums[count:]


def odd_lanes(shape):
    return lax.rem(lax.broadcasted_iota(jnp.int32, shape, 1), 2) == 1


def twice(value, width):
    rows = value.shape[0]
    parts = []
    for k in range(width // LANES):
        first = (k // 2) * LANES
        part = value[:, first : first + LANES]
        if part.shape[1] < LANES:
            part = jnp.concatenate([part, jnp.zeros((rows, LANES - part.shape[1]), part.dtype)], axis=-1)
        lane = lax.broadcasted_iota(jnp.int32, (rows, LANES), 1)
        parts.append(jnp.take_along_axis(part, lax.div(lane, 2) + (k % 2) * (LANES // 2), axis=1))
    return jnp.concatenate(parts, axis=-1)


def from_left(value):
    return pltpu.roll(value, 1, 1)


def from_right(value):
    return pltpu.roll(value, value.shape[1] - 1, 1)


def item_place(slots, item):
    return CODES + slots + PER_ITEM * item


def window_start(leaf_ref, leaf, width):
    units = leaf_ref.shape[1] // LANES
    before = jnp.int32(0)
    for k in range(units):
        before = before + (leaf_ref[0, k * LANES] < leaf).astype(jnp.int32)
    return jnp.clip(before - 1, 0, units - width)


def window_mask(leaves_ref, leaf, unit, rows, width):
    leaves = jnp.concatenate([leaves_ref[unit + k] for k in range(width)], axis=-1)
    return jnp.broadcast_to(leaves, (rows, width * LANES)) == leaf


def window_copies(exp_ref, unit, window_ref, sem, width):
    coefs = exp_ref.shape[0]
    step = -(-coefs // PIECES)
    copies = []
    for k in range(width):
        for p in range(PIECES):
            part = pl.ds(p * step, min(step, coefs - p * step))
            copies.append(
                pltpu.make_async_copy(exp_ref.at[part, unit + k], window_ref.at[k, part], sem.at[k, p])
            )
    return copies


def clear_rest(window_ref, coefs, width):
    rest = window_ref.shape[1] - coefs
    for k in range(width):
        window_ref[k, pl.ds(coefs, rest)] = jnp.zeros((rest, 2, LANES), BF16)


def multi_rows(fields, width, leaf, unit, leaves_ref, low_ref, window_ref):
    if len(low_ref.shape) == 2:
        first = pl.multiple_of(unit * LANES, LANES)
        rows = low_ref[:, pl.ds(first, width * LANES)]
    else:
        rows = jnp.concatenate([low_ref[unit + k] for k in range(width)], axis=-1)
    mask = window_mask(leaves_ref, leaf, unit, 2 * fields, width)
    rows = halves(jnp.where(mask, rows.astype(F32), 0.0).astype(rows.dtype))
    expansions = jnp.concatenate([as_rows(window_ref.at[k]) for k in range(width)], axis=-1)
    total = joined(dot_nt(rows, expansions), 2 * fields)
    on_real, on_imag = total[:fields], total[fields:]
    odd = odd_lanes(on_real.shape)
    other = jnp.where(odd, from_left(on_imag), from_right(on_imag))
    return jnp.where(odd, -on_real, on_real) - other


def as_rows(ref):
    return ref.reshape(ref.shape[0] * 2, ref.shape[2])[...]


def edge_kernel(row_ref, image_ref, one_ref, two_ref):
    even = lax.rem(row_ref[0], 2) == 0
    if len(image_ref.shape) == 2:
        edge = one_ref.shape[1]
        first, last = image_ref[:, :edge], image_ref[:, image_ref.shape[1] - edge :]
    else:
        edge = one_ref.shape[0]
        first, last = image_ref[:edge], image_ref[image_ref.shape[0] - edge :]
    first, last = first.astype(one_ref.dtype), last.astype(one_ref.dtype)

    @pl.when(even)
    def _():
        one_ref[...], two_ref[...] = last, first

    @pl.when(jnp.logical_not(even))
    def _():
        one_ref[...], two_ref[...] = first, last


def begin_kernel(
    fields, items, width, send, rows, row_ref, own_ref, pick_hbm, leaf_hbm, leaves_hbm,
    target_hbm, offset_hbm, pairs_hbm, right_hbm, exp_ref, trans_ref,
    plan_ref, out_ref, window_ref, target_window_ref, trans_out, leaves_ref, right_ref,
    pick_ref, leaf_ref, target_ref, offset_ref, pairs_ref, sem, window_sem, target_sem, trans_sem,
):
    loads = [
        pltpu.make_async_copy(source, place, sem.at[k])
        for k, (source, place) in enumerate(
            (
                (leaf_hbm, leaf_ref),
                (pick_hbm, pick_ref),
                (target_hbm, target_ref),
                (offset_hbm, offset_ref),
                (pairs_hbm, pairs_ref),
                (leaves_hbm, leaves_ref),
                (right_hbm, right_ref),
            )
        )
    ]
    for load in loads:
        load.start()
    for i in range(items):
        clear_rest(window_ref.at[i], exp_ref.shape[0], width)
    slots = pairs_ref.shape[0]
    own = own_ref[0]
    loads[0].wait()
    loads[1].wait()
    row = row_ref[0]

    def partner(i, coming):
        number = own * items + i
        pair, number = lax.div(number, send), lax.rem(number, send)
        other = source_row(row, pair, rows) if coming else target_row(row, pair, rows)
        if coming and own_items_change_cores(rows, items, send):
            number = jnp.where(other == row, 1 - number, number)
        return other, number

    for i in range(items):
        other, number = partner(i, False)
        leaf = pick_ref[other, number, row]
        unit = window_start(leaf_ref, leaf, width)
        place = item_place(slots, i)
        plan_ref[place], plan_ref[place + 1] = leaf, unit
        for copy in window_copies(exp_ref, unit, window_ref.at[i], window_sem.at[i], width):
            copy.start()
    for load in loads[2:]:
        load.wait()
    later = []
    for s in range(slots):
        plan_ref[CODES + s] = pairs_ref[s]
    for i in range(items):
        place = item_place(slots, i)
        other, number = partner(i, True)
        leaf = target_ref[0, other * send + number]
        plan_ref[place + 2], plan_ref[place + 3] = leaf, window_start(leaf_ref, leaf, width)
        offset = offset_ref[0, other * send + number]
        later += window_copies(exp_ref, plan_ref[place + 3], target_window_ref.at[i], target_sem.at[i], width)
        later.append(pltpu.make_async_copy(trans_ref.at[offset], trans_out.at[i], trans_sem.at[i]))
    for copy in later:
        copy.start()
    for i in range(items):
        clear_rest(target_window_ref.at[i], exp_ref.shape[0], width)
    for i in range(items):
        place = item_place(slots, i)
        leaf, unit = plan_ref[place], plan_ref[place + 1]
        for copy in window_copies(exp_ref, unit, window_ref.at[i], window_sem.at[i], width):
            copy.wait()
        out_ref[i] = multi_rows(fields, width, leaf, unit, leaves_ref, right_ref, window_ref.at[i]).astype(BF16)
    for copy in later:
        copy.wait()


def rows_kernel(trans_ref, moved_ref):
    items, coefs = trans_ref.shape[:2]
    rest = moved_ref.shape[1] - 2 * coefs
    for i in range(items):
        moved_ref[i, pl.ds(0, 2 * coefs)] = trans_ref[i].reshape(2 * coefs, coefs)
        moved_ref[i, pl.ds(2 * coefs, rest)] = jnp.zeros((rest, coefs), BF16)


def near_sources(row_ref, one_ref, two_ref, here_ref, units, ext):
    edge = (ext.shape[0] - units) // 2
    even = lax.rem(row_ref[0], 2) == 0
    one_at = jnp.where(even, edge + units, 0)
    two_at = jnp.where(even, 0, edge + units)
    if len(here_ref.shape) == 2:
        for k in range(edge):
            lanes = slice(k * LANES, (k + 1) * LANES)
            ext[one_at + k] = one_ref[:, lanes].astype(ext.dtype)
            ext[two_at + k] = two_ref[:, lanes].astype(ext.dtype)
        for k in range(units):
            ext[edge + k] = here_ref[:, k * LANES : (k + 1) * LANES]
    else:
        ext[pl.ds(one_at, edge)] = one_ref[...]
        ext[pl.ds(two_at, edge)] = two_ref[...]
        ext[edge : edge + units] = here_ref[...]


def near_kernel(
    fields, row_ref, count_ref, plan_ref, one_ref, two_ref, here_ref, tiles_ref, out_ref, ext
):
    near_sources(row_ref, one_ref, two_ref, here_ref, out_ref.shape[0], ext)
    out_ref[...] = jnp.zeros_like(out_ref)
    slots, tile = tiles_ref.shape[1], tiles_ref.shape[2]
    per = tile // LANES
    for s in range(slots):
        code = plan_ref[CODES + s]
        target = lax.div(code, SPAN)
        source = target + lax.rem(code, SPAN)
        rows = halves(jnp.concatenate([ext[source * per + k] for k in range(per)], axis=-1))
        on_real = joined(dot_nt(rows, tiles_ref[0, s]), 2 * fields)
        on_imag = joined(dot_nt(rows, tiles_ref[1, s]), 2 * fields)
        value = jnp.concatenate(
            [on_real[:fields] - on_imag[fields:], on_real[fields:] + on_imag[:fields]], axis=0
        )
        value = jnp.where(s < count_ref[0], value, 0.0)
        for k in range(per):
            out_ref[target * per + k] += value[:, k * LANES : (k + 1) * LANES]


def far_kernel(
    fields, items, width, slots, core_ref, plan_ref, leaves_ref, partial_ref, item_ref, trans_ref, window_ref,
    keep_ref, give_ref, total,
):
    units = partial_ref.shape[0]
    total[0:units] = partial_ref[...]
    if total.shape[0] > units:
        total[units:] = jnp.zeros((total.shape[0] - units, *total.shape[1:]), F32)
    for i in range(items):
        plain = item_ref[i].astype(F32)
        odd = odd_lanes(plain.shape)
        turned = jnp.where(odd, from_left(plain), -from_right(plain))
        rows = jnp.concatenate([plain, turned], axis=0).astype(BF16)
        local_field = dot_nn(rows, trans_ref[i]).astype(BF16).astype(F32)
        local_field = twice(local_field, plain.shape[1])
        local_real, local_imag = local_field[:fields], local_field[fields:]
        rows = jnp.concatenate(
            [jnp.where(odd, -local_imag, local_real), jnp.where(odd, local_real, local_imag)], axis=0
        ).astype(BF16)
        expansions = jnp.concatenate([as_rows(window_ref.at[i, k]) for k in range(width)], axis=-1)
        place = item_place(slots, i)
        leaf, unit = plan_ref[place + 2], plan_ref[place + 3]
        mask = window_mask(leaves_ref, leaf, unit, 2 * fields, width)
        image = jnp.where(mask, dot_nn(rows, expansions), 0.0)
        for k in range(width):
            total[unit + k] += image[:, k * LANES : (k + 1) * LANES]
    chips, share = keep_ref.shape[:2]
    core = core_ref[0]
    for c in range(chips):
        keep_ref[c] = total[pl.ds((2 * c + core) * share, share)].astype(keep_ref.dtype)
        give_ref[c] = total[pl.ds((2 * c + 1 - core) * share, share)].astype(give_ref.dtype)


def pair_kernel(keep_ref, got_ref, out_ref):
    out_ref[...] = (keep_ref[...].astype(F32) + got_ref[...].astype(F32)).astype(out_ref.dtype)


def tree_sum(values):
    while len(values) > 1:
        values = [values[k] + values[k + 1] for k in range(0, len(values), 2)]
    return values[0]


def close_kernel(*refs):
    refs[-1][...] = tree_sum([ref[...].astype(F32) for ref in refs[:-1]])


def assemble_kernel(
    fields, items, width, slots, core_ref, plan_ref, leaves_ref, mine_ref, theirs_ref, window_ref,
    out_ref, low_ref, made_ref, whole,
):
    chips, share = mine_ref.shape[:2]
    units = out_ref.shape[0]
    core = core_ref[0]
    for chip in range(chips):
        whole[pl.ds((2 * chip + core) * share, share)] = mine_ref[chip]
        whole[pl.ds((2 * chip + 1 - core) * share, share)] = theirs_ref[chip]
    out_ref[...] = whole[0:units]
    low_ref[...] = whole[0:units].astype(BF16)
    for i in range(items):
        place = item_place(slots, i)
        made_ref[i] = multi_rows(
            fields, width, plan_ref[place], plan_ref[place + 1], leaves_ref, low_ref, window_ref.at[i]
        ).astype(BF16)


def flat_lines(columns, fields):
    per = LANES // fields
    lines = []
    for first in range(0, len(columns), per):
        some = columns[first : first + per]
        if len(some) < per:
            some = some + [jnp.zeros(((per - len(some)) * fields, 1), F32)]
        square = jnp.broadcast_to(jnp.concatenate(some, axis=0), (LANES, LANES))
        lines.append(jnp.transpose(square)[:1])
    return jnp.concatenate(lines, axis=0)


def columns_of(lines, count, fields):
    per = LANES // fields
    columns = []
    for k in range(lines.shape[0]):
        square = jnp.transpose(jnp.broadcast_to(lines[k : k + 1], (LANES, LANES)))
        columns += [square[j * fields : (j + 1) * fields, :1] for j in range(per)]
    return columns[:count]


def gram_kernel(fields, core_ref, right_ref, image_ref, *refs):
    *parts, out_ref = refs
    units = image_ref.shape[0]
    chips, share = parts[0].shape[:2]
    totals = None
    for k in range(chips * share):
        chip, within = divmod(k, share)
        unit = (2 * chip + core_ref[0]) * share + within
        place = jnp.minimum(unit, units - 1)
        r = right_ref[:, pl.ds(pl.multiple_of(place * LANES, LANES), LANES)]
        z = image_ref[place]
        q = tree_sum([part[chip, within].astype(F32) for part in parts])
        if 2 * chips * share > units:
            r = jnp.where(unit < units, r, 0.0)
            z = jnp.where(unit < units, z, 0.0)
        (rr, ri), (zr, zi), (qr, qi) = [(v[:fields], v[fields:]) for v in (r, z, q)]
        products = [
            rr * rr + ri * ri,
            rr * zr + ri * zi,
            rr * zi - ri * zr,
            zr * zr + zi * zi,
            rr * qr + ri * qi,
            rr * qi - ri * qr,
            zr * qr + zi * qi,
            zr * qi - zi * qr,
            qr * qr + qi * qi,
        ]
        totals = products if totals is None else [t + p for t, p in zip(totals, products)]
    lines = flat_lines([jnp.sum(t, axis=1, keepdims=True) for t in totals], fields)
    out_ref[...] = lines


def final_kernel(fields, right_ref, image_ref, *refs):
    *sums_refs, out_ref = refs
    units = image_ref.shape[0]
    sums = columns_of(tree_sum([ref[...] for ref in sums_refs]), 9, fields)
    a_real, a_imag, b_real, b_imag = [
        jnp.broadcast_to(value, (fields, LANES)) for value in krylov_coefficients(sums)
    ]
    for k in range(units):
        lanes = slice(k * LANES, (k + 1) * LANES)
        r_real, r_imag = right_ref[:fields, lanes], right_ref[fields:, lanes]
        z_real, z_imag = image_ref[k, :fields], image_ref[k, fields:]
        out_ref[:fields, lanes] = a_real * r_real - a_imag * r_imag + b_real * z_real - b_imag * z_imag
        out_ref[fields:, lanes] = a_real * r_imag + a_imag * r_real + b_real * z_imag + b_imag * z_real


def params(mebibytes=16):
    return pltpu.CompilerParams(vmem_limit_bytes=mebibytes * 1024 * 1024)


def is_power(count):
    return count & (count - 1) == 0


def reversed_bits(value, count):
    bits = count.bit_length() - 1
    return sum(((value >> k) & 1) << (bits - 1 - k) for k in range(bits))


def target_row(row, pair, rows):
    if not is_power(rows):
        return (pair - row + rows) % rows
    return pair ^ reversed_bits(row, rows)


def source_row(row, pair, rows):
    if not is_power(rows):
        return (pair - row + rows) % rows
    return reversed_bits(pair ^ row, rows)


def own_items_change_cores(rows, items, send):
    return items == 1 and send == 2


def item_route(rows, group, columns, send):
    items = rows * send // group

    def flat(r, g):
        return (g // columns * rows + r) * columns + g % columns

    def target(r, g, pair):
        d = target_row(r, pair, rows)
        return flat(d, g ^ 1 if d == r and own_items_change_cores(rows, items, send) else g)

    assert items * group == rows * send and (items % send == 0 or send % items == 0)
    routes = []
    for first in range(0, items, send):
        pairs = [(g * items + first) // send for g in range(group)]
        routes.append([(flat(r, g), target(r, g, pairs[g])) for r in range(rows) for g in range(group)])
    return items, routes


def local(
    right_side,
    near_tiles,
    tile_pairs,
    tile_count,
    panel_expansions,
    leaf_of_panel,
    far_pick,
    far_target,
    far_offset,
    translations,
):
    fields, panels = right_side.shape[1:]
    coefs = panel_expansions.shape[2]
    tile = near_tiles.shape[2]
    send = far_pick.shape[2]
    rows = lax.axis_size("row")
    group = lax.axis_size("grp") * lax.axis_size("col")
    row_here = lax.axis_index("row")
    own = lax.axis_index("grp") * lax.axis_size("col") + lax.axis_index("col")
    both = 2 * fields
    units = panels // LANES
    share = -(-units // group)
    edge = REACH * tile
    edge_units = edge // LANES
    width = tile // LANES + 1
    items, routes = item_route(rows, group, lax.axis_size("col"), send)

    assert rows % 2 == 0
    neighbours = [[r + 1 - 2 * (r % 2) for r in range(rows)], [(r - 1 + 2 * (r % 2)) % rows for r in range(rows)]]
    own_place, row_place = own.reshape(1), row_here.reshape(1)
    core_place = lax.rem(own, 2).reshape(1)
    slots = near_tiles.shape[1]
    pad_coefs = -(-coefs // 8) * 8
    chips = group // 2
    assert group == 2 * chips and chips & (chips - 1) == 0 and LANES % fields == 0
    window_shape = jax.ShapeDtypeStruct((items, width, pad_coefs, 2, LANES), BF16)
    item_shape = jax.ShapeDtypeStruct((items, fields, 2 * pad_coefs), BF16)
    part_shape = (share, both, LANES)

    def in_hbm(value):
        return pltpu.with_memory_space_constraint(value, pltpu.HBM)

    leaves = leaf_of_panel.reshape(units, 1, LANES)
    expansions = panel_expansions.transpose(2, 0, 1).reshape(coefs, 2, units, LANES).transpose(0, 2, 1, 3)
    expansions = in_hbm(expansions)
    moves = in_hbm(translations.transpose(0, 2, 1, 3))
    picks = far_pick.transpose(0, 2, 1)

    plan, made, windows, target_windows, moves, leaves, right = pl.pallas_call(
        functools.partial(begin_kernel, fields, items, width, send, rows),
        out_shape=(
            pltpu.SMEM((item_place(slots, items),), jnp.int32),
            item_shape,
            pltpu.VMEM(window_shape.shape, BF16),
            pltpu.VMEM(window_shape.shape, BF16),
            pltpu.VMEM((items, coefs, 2, coefs), BF16),
            jax.ShapeDtypeStruct(leaves.shape, jnp.int32),
            jax.ShapeDtypeStruct((both, panels), F32),
        ),
        in_specs=[SMEM] * 2 + [HBM] * 9,
        out_specs=(SMEM,) + (VMEM,) * 6,
        scratch_shapes=[
            pltpu.SMEM(value.shape, jnp.int32)
            for value in (picks, leaf_of_panel, far_target, far_offset, tile_pairs)
        ]
        + [
            pltpu.SemaphoreType.DMA((7,)),
            pltpu.SemaphoreType.DMA((items, width, PIECES)),
            pltpu.SemaphoreType.DMA((items, width, PIECES)),
            pltpu.SemaphoreType.DMA((items,)),
        ],
        compiler_params=params(24),
        name="begin",
    )(
        row_place,
        own_place,
        in_hbm(picks),
        in_hbm(leaf_of_panel),
        in_hbm(leaves),
        in_hbm(far_target),
        in_hbm(far_offset),
        in_hbm(tile_pairs),
        in_hbm(right_side.reshape(both, panels)),
        expansions,
        moves,
    )

    def exchanged(made):
        parts = [
            lax.ppermute(made[k * send : k * send + min(send, items)], EVERY, route) for k, route in enumerate(routes)
        ]
        return parts[0] if len(parts) == 1 else jnp.concatenate(parts)

    def from_neighbours(image):
        edge_shape = (both, edge) if image.ndim == 2 else (edge_units, both, LANES)
        one, two = pl.pallas_call(
            edge_kernel,
            out_shape=(jax.ShapeDtypeStruct(edge_shape, BF16),) * 2,
            in_specs=[SMEM, VMEM],
            out_specs=(VMEM, VMEM),
            compiler_params=params(),
            name="edges",
        )(row_place, image)
        return [
            lax.ppermute(value, "row", list(enumerate(targets))) for value, targets in zip((one, two), neighbours)
        ]

    image_shape = jax.ShapeDtypeStruct((units, both, LANES), F32)
    moved = pl.pallas_call(
        rows_kernel,
        out_shape=pltpu.VMEM((items, 2 * pad_coefs, coefs), BF16),
        in_specs=[VMEM],
        out_specs=VMEM,
        compiler_params=params(),
        cost_estimate=pl.CostEstimate(flops=0, bytes_accessed=6 * window_shape.size, transcendentals=0),
        name="translation_rows",
    )(moves)

    def swapped(value, step):
        return lax.ppermute(value, GROUP, [(g, g ^ step) for g in range(group)])

    def near(one, two, low):
        return pl.pallas_call(
            functools.partial(near_kernel, fields),
            out_shape=image_shape,
            in_specs=[SMEM] * 3 + [VMEM] * 4,
            out_specs=VMEM,
            scratch_shapes=[pltpu.VMEM((units + 2 * edge_units, both, LANES), low.dtype)],
            compiler_params=params(),
            cost_estimate=pl.CostEstimate(
                flops=8 * fields * near_tiles.size // 2, bytes_accessed=2 * near_tiles.size, transcendentals=0
            ),
            name="near",
        )(row_place, tile_count, plan, one, two, low, near_tiles)

    def core_parts(partial, taken, dtype):
        half_shape = jax.ShapeDtypeStruct((chips, *part_shape), dtype)
        keep, give = pl.pallas_call(
            functools.partial(far_kernel, fields, items, width, slots),
            out_shape=(half_shape, half_shape),
            in_specs=[SMEM, SMEM] + [VMEM] * 5,
            out_specs=(VMEM, VMEM),
            scratch_shapes=[pltpu.VMEM((share * group, both, LANES), F32)],
            compiler_params=params(),
            name="far",
        )(core_place, plan, leaves, partial, taken, moved, target_windows)
        return keep, swapped(give, 1)

    def pair_sums(keep, got):
        pair = pl.pallas_call(
            pair_kernel,
            out_shape=jax.ShapeDtypeStruct(keep.shape, BF16),
            in_specs=[VMEM, VMEM],
            out_specs=VMEM,
            compiler_params=params(),
            name="pair",
        )(keep, got)
        arrived = {step: swapped(pair, 2 * step) for step in range(chips - 1, 0, -1)}
        return [pair] + [arrived[step] for step in range(1, chips)]

    def whole_sum(parts):
        mine = pl.pallas_call(
            close_kernel,
            out_shape=jax.ShapeDtypeStruct((chips, *part_shape), F32),
            in_specs=[VMEM] * chips,
            out_specs=VMEM,
            compiler_params=params(),
            name="close",
        )(*parts)
        theirs = swapped(mine, 1)
        low_shape = jax.ShapeDtypeStruct((units, both, LANES), BF16)
        return pl.pallas_call(
            functools.partial(assemble_kernel, fields, items, width, slots),
            out_shape=(image_shape, low_shape, item_shape),
            in_specs=[SMEM, SMEM] + [VMEM] * 4,
            out_specs=(VMEM,) * 3,
            scratch_shapes=[pltpu.VMEM((share * group, both, LANES), F32)],
            compiler_params=params(),
            name="assemble",
        )(core_place, plan, leaves, mine, theirs, windows)

    def row_sums(lines):
        lines = pl.pallas_call(
            close_kernel,
            out_shape=jax.ShapeDtypeStruct(lines.shape, F32),
            in_specs=[VMEM] * 2,
            out_specs=VMEM,
            compiler_params=params(),
            name="cores",
        )(lines, swapped(lines, 1))
        if rows != 4:
            return [lax.psum(lines, "row")]
        others = [lax.ppermute(lines, "row", [(r, r ^ step) for r in range(rows)]) for step in (3, 2, 1)]
        return [lines] + others[::-1]

    partial = near(*from_neighbours(right), right)
    z_all, z_low, made = whole_sum(pair_sums(*core_parts(partial, exchanged(made), F32)))
    partial = near(*from_neighbours(z_low), z_low)
    parts = pair_sums(*core_parts(partial, exchanged(made), BF16))

    lines = pl.pallas_call(
        functools.partial(gram_kernel, fields),
        out_shape=jax.ShapeDtypeStruct((-(-9 * fields // LANES), LANES), F32),
        in_specs=[SMEM] + [VMEM] * (2 + chips),
        out_specs=VMEM,
        compiler_params=params(),
        name="gram",
    )(core_place, right, z_all, *parts)
    sums = row_sums(lines)
    out = pl.pallas_call(
        functools.partial(final_kernel, fields),
        out_shape=jax.ShapeDtypeStruct((both, panels), F32),
        in_specs=[VMEM] * (2 + len(sums)),
        out_specs=VMEM,
        compiler_params=params(),
        name="combine",
    )(right, z_all, *sums)
    return out.reshape(right_side.shape)


def krylov_coefficients(sums):
    rr, rz_real, rz_imag, zz, rq_real, rq_imag, zq_real, zq_imag, qq = sums

    def times(left, right):
        return left[0] * right[0] - left[1] * right[1], left[0] * right[1] + left[1] * right[0]

    def conj_times(left, right):
        return left[0] * right[0] + left[1] * right[1], left[0] * right[1] - left[1] * right[0]

    def scale(factor, value):
        return factor * value[0], factor * value[1]

    def plus(*values):
        return sum(v[0] for v in values), sum(v[1] for v in values)

    def size(value):
        return value[0] * value[0] + value[1] * value[1]

    rz, rq, zq = (rz_real, rz_imag), (rq_real, rq_imag), (zq_real, zq_imag)
    beta = jnp.sqrt(rr + EPSILON)
    inv = 1.0 / beta
    norm_one = rr * inv * inv
    product = scale(inv * inv, rz)
    h_first = (0.5 * norm_one + product[0], product[1])
    shift = (h_first[0] - 0.5, h_first[1])
    residue = zz * inv * inv - 2.0 * conj_times(shift, product)[0] + size(shift) * norm_one
    residue = jnp.maximum(residue, 0.0)
    h_sub = jnp.sqrt(residue + EPSILON)
    alpha = inv / h_sub
    gamma = scale(-alpha, shift)
    h_upper = scale(
        inv,
        plus(
            scale(0.5, plus(scale(alpha, rz), scale(rr, gamma))), scale(alpha, rq), times(gamma, rz)
        ),
    )
    second = plus(
        scale(alpha * alpha, zq),
        scale(alpha * zz, gamma),
        scale(alpha, conj_times(gamma, rq)),
        scale(size(gamma), rz),
    )
    h_middle = (0.5 * residue / (h_sub * h_sub) + second[0], second[1])
    keep = (h_middle[0] - 0.5, h_middle[1])
    on_z = plus(gamma, scale(-alpha, keep))
    on_r = plus(scale(-inv, h_upper), scale(-1.0, times(keep, gamma)))
    last = (
        alpha * alpha * qq
        + size(on_z) * zz
        + size(on_r) * rr
        + 2.0
        * (
            conj_times(on_r, times(on_z, rz))[0]
            + alpha * conj_times(on_r, rq)[0]
            + alpha * conj_times(on_z, zq)[0]
        )
    )
    h_last = jnp.sqrt(jnp.maximum(last, 0.0) + EPSILON)
    radius = jnp.sqrt(size(h_first) + h_sub * h_sub)
    cosine = scale(1.0 / radius, h_first)
    sine = h_sub / radius
    upper = plus(conj_times(cosine, h_upper), scale(sine, h_middle))
    lower = plus(times(cosine, h_middle), scale(-sine, h_upper))
    radius_two = jnp.sqrt(size(lower) + h_last * h_last)
    cosine_two = scale(1.0 / radius_two, lower)
    weight_two = scale(-sine * beta / radius_two, (cosine_two[0], -cosine_two[1]))
    goal = scale(beta, (cosine[0], -cosine[1]))
    weight_one = scale(1.0 / radius, plus(goal, scale(-1.0, times(upper, weight_two))))
    on_right = plus(scale(inv, weight_one), times(weight_two, gamma))
    on_image = scale(alpha, weight_two)
    return on_right[0], on_right[1], on_image[0], on_image[1]


def solution(mesh):
    return jax.shard_map(
        local,
        mesh=mesh,
        in_specs=(
            P(None, None, "row"),
            P(None, ("grp", "row", "col"), None, None),
            P(("grp", "row", "col")),
            P(("grp", "row", "col")),
            P(None, "row", None),
            P("row", None),
            P(),
            P("row", None),
            P("row", None),
            P(),
        ),
        out_specs=P(None, None, "row"),
        check_vma=False,
    )
```

```python
import functools

import jax
import jax.numpy as jnp
from jax import lax
from jax.experimental import pallas as pl
from jax.experimental.pallas import tpu as pltpu
from jax.sharding import PartitionSpec as P

REACH = 2
SPAN = 2 * REACH + 1
LANES = 128
EPSILON = 1e-06
GROUP = ("grp", "col")
CODES = 0
PER_ITEM = 5
PIECES = 4
EVERY = ("grp", "row", "col")

F32 = jnp.float32
BF16 = jnp.bfloat16
SMEM = pl.BlockSpec(memory_space=pltpu.SMEM)
VMEM = pl.BlockSpec(memory_space=pltpu.VMEM)
HBM = pl.BlockSpec(memory_space=pltpu.HBM)


def dot_nn(left, right):
    return lax.dot_general(left, right, (((1,), (0,)), ((), ())), preferred_element_type=F32)


def dot_nt(left, right):
    return lax.dot_general(left, right, (((1,), (1,)), ((), ())), preferred_element_type=F32)


def halves(rows):
    if rows.dtype != F32:
        return rows
    high = rows.astype(BF16)
    return jnp.concatenate([high, (rows - high.astype(F32)).astype(BF16)], axis=0)


def joined(sums, count):
    return sums if sums.shape[0] == count else sums[:count] + sums[count:]


def odd_lanes(shape):
    return lax.rem(lax.broadcasted_iota(jnp.int32, shape, 1), 2) == 1


def twice(value, width):
    rows = value.shape[0]
    parts = []
    for k in range(width // LANES):
        first = (k // 2) * LANES
        part = value[:, first : first + LANES]
        if part.shape[1] < LANES:
            part = jnp.concatenate([part, jnp.zeros((rows, LANES - part.shape[1]), part.dtype)], axis=-1)
        lane = lax.broadcasted_iota(jnp.int32, (rows, LANES), 1)
        parts.append(jnp.take_along_axis(part, lax.div(lane, 2) + (k % 2) * (LANES // 2), axis=1))
    return jnp.concatenate(parts, axis=-1)


def from_left(value):
    return pltpu.roll(value, 1, 1)


def from_right(value):
    return pltpu.roll(value, value.shape[1] - 1, 1)


def item_place(slots, item):
    return CODES + slots + PER_ITEM * item


def window_start(leaf_ref, leaf, width):
    units = leaf_ref.shape[1] // LANES
    before = jnp.int32(0)
    for k in range(units):
        before = before + (leaf_ref[0, k * LANES] < leaf).astype(jnp.int32)
    return jnp.clip(before - 1, 0, units - width)


def window_mask(leaves_ref, leaf, unit, rows, width):
    leaves = jnp.concatenate([leaves_ref[unit + k] for k in range(width)], axis=-1)
    return jnp.broadcast_to(leaves, (rows, width * LANES)) == leaf


def window_copies(exp_ref, unit, window_ref, sem, width):
    coefs = exp_ref.shape[0]
    step = -(-coefs // PIECES)
    copies = []
    for k in range(width):
        for p in range(PIECES):
            part = pl.ds(p * step, min(step, coefs - p * step))
            copies.append(
                pltpu.make_async_copy(exp_ref.at[part, unit + k], window_ref.at[k, part], sem.at[k, p])
            )
    return copies


def clear_rest(window_ref, coefs, width):
    rest = window_ref.shape[1] - coefs
    for k in range(width):
        window_ref[k, pl.ds(coefs, rest)] = jnp.zeros((rest, 2, LANES), BF16)


def multi_rows(fields, width, leaf, unit, leaves_ref, low_ref, window_ref):
    if len(low_ref.shape) == 2:
        first = pl.multiple_of(unit * LANES, LANES)
        rows = low_ref[:, pl.ds(first, width * LANES)]
    else:
        rows = jnp.concatenate([low_ref[unit + k] for k in range(width)], axis=-1)
    mask = window_mask(leaves_ref, leaf, unit, 2 * fields, width)
    rows = halves(jnp.where(mask, rows.astype(F32), 0.0).astype(rows.dtype))
    expansions = jnp.concatenate([as_rows(window_ref.at[k]) for k in range(width)], axis=-1)
    total = joined(dot_nt(rows, expansions), 2 * fields)
    on_real, on_imag = total[:fields], total[fields:]
    odd = odd_lanes(on_real.shape)
    other = jnp.where(odd, from_left(on_imag), from_right(on_imag))
    return jnp.where(odd, -on_real, on_real) - other


def as_rows(ref):
    return ref.reshape(ref.shape[0] * 2, ref.shape[2])[...]


def edge_kernel(row_ref, image_ref, one_ref, two_ref):
    even = lax.rem(row_ref[0], 2) == 0
    if len(image_ref.shape) == 2:
        edge = one_ref.shape[1]
        first, last = image_ref[:, :edge], image_ref[:, image_ref.shape[1] - edge :]
    else:
        edge = one_ref.shape[0]
        first, last = image_ref[:edge], image_ref[image_ref.shape[0] - edge :]
    first, last = first.astype(one_ref.dtype), last.astype(one_ref.dtype)

    @pl.when(even)
    def _():
        one_ref[...], two_ref[...] = last, first

    @pl.when(jnp.logical_not(even))
    def _():
        one_ref[...], two_ref[...] = first, last


def begin_kernel(
    fields, items, width, send, rows, row_ref, own_ref, pick_hbm, leaf_hbm, leaves_hbm,
    target_hbm, offset_hbm, pairs_hbm, right_hbm, exp_ref,
    plan_ref, out_ref, window_ref, leaves_ref, right_ref,
    pick_ref, leaf_ref, target_ref, offset_ref, pairs_ref, sem, window_sem,
):
    loads = [
        pltpu.make_async_copy(source, place, sem.at[k])
        for k, (source, place) in enumerate(
            (
                (leaf_hbm, leaf_ref),
                (pick_hbm, pick_ref),
                (target_hbm, target_ref),
                (offset_hbm, offset_ref),
                (pairs_hbm, pairs_ref),
                (leaves_hbm, leaves_ref),
                (right_hbm, right_ref),
            )
        )
    ]
    for load in loads:
        load.start()
    for i in range(items):
        clear_rest(window_ref.at[i], exp_ref.shape[0], width)
    slots = pairs_ref.shape[0]
    own = own_ref[0]
    loads[0].wait()
    loads[1].wait()
    row = row_ref[0]

    def partner(i, coming):
        number = own * items + i
        pair, number = lax.div(number, send), lax.rem(number, send)
        other = source_row(row, pair, rows) if coming else target_row(row, pair, rows)
        if coming and own_items_change_cores(rows, items, send):
            number = jnp.where(other == row, 1 - number, number)
        return other, number

    for i in range(items):
        other, number = partner(i, False)
        leaf = pick_ref[other, number, row]
        unit = window_start(leaf_ref, leaf, width)
        place = item_place(slots, i)
        plan_ref[place], plan_ref[place + 1] = leaf, unit
        for copy in window_copies(exp_ref, unit, window_ref.at[i], window_sem.at[i], width):
            copy.start()
    for load in loads[2:]:
        load.wait()
    for s in range(slots):
        plan_ref[CODES + s] = pairs_ref[s]
    for i in range(items):
        place = item_place(slots, i)
        other, number = partner(i, True)
        leaf = target_ref[0, other * send + number]
        plan_ref[place + 2], plan_ref[place + 3] = leaf, window_start(leaf_ref, leaf, width)
        plan_ref[place + 4] = offset_ref[0, other * send + number]
    for i in range(items):
        place = item_place(slots, i)
        leaf, unit = plan_ref[place], plan_ref[place + 1]
        for copy in window_copies(exp_ref, unit, window_ref.at[i], window_sem.at[i], width):
            copy.wait()
        out_ref[i] = multi_rows(fields, width, leaf, unit, leaves_ref, right_ref, window_ref.at[i]).astype(BF16)


def fetch_kernel(items, width, slots, plan_ref, exp_ref, trans_ref, window_ref, moved_ref, trans_buf, sem, trans_sem):
    coefs = trans_ref.shape[3]
    for i in range(items):
        clear_rest(window_ref.at[i], coefs, width)

    def trans_copy(i):
        offset = plan_ref[item_place(slots, i) + 4]
        return pltpu.make_async_copy(trans_ref.at[offset], trans_buf.at[i], trans_sem.at[i])

    def exp_copies(i):
        unit = plan_ref[item_place(slots, i) + 3]
        return window_copies(exp_ref, unit, window_ref.at[i], sem.at[i], width)

    for i in range(items):
        trans_copy(i).start()
        for copy in exp_copies(i):
            copy.start()
    rest = moved_ref.shape[1] - 2 * coefs
    for i in range(items):
        trans_copy(i).wait()
        moved_ref[i, pl.ds(0, 2 * coefs)] = trans_buf[i].reshape(2 * coefs, coefs)
        moved_ref[i, pl.ds(2 * coefs, rest)] = jnp.zeros((rest, coefs), BF16)
        for copy in exp_copies(i):
            copy.wait()


def near_sources(row_ref, one_ref, two_ref, here_ref, units, ext):
    edge = (ext.shape[0] - units) // 2
    even = lax.rem(row_ref[0], 2) == 0
    one_at = jnp.where(even, edge + units, 0)
    two_at = jnp.where(even, 0, edge + units)
    if len(here_ref.shape) == 2:
        for k in range(edge):
            lanes = slice(k * LANES, (k + 1) * LANES)
            ext[one_at + k] = one_ref[:, lanes].astype(ext.dtype)
            ext[two_at + k] = two_ref[:, lanes].astype(ext.dtype)
        for k in range(units):
            ext[edge + k] = here_ref[:, k * LANES : (k + 1) * LANES]
    else:
        ext[pl.ds(one_at, edge)] = one_ref[...]
        ext[pl.ds(two_at, edge)] = two_ref[...]
        ext[edge : edge + units] = here_ref[...]


def near_kernel(
    fields, row_ref, count_ref, plan_ref, one_ref, two_ref, here_ref, tiles_ref, out_ref, ext
):
    near_sources(row_ref, one_ref, two_ref, here_ref, out_ref.shape[0], ext)
    out_ref[...] = jnp.zeros_like(out_ref)
    slots, tile = tiles_ref.shape[1], tiles_ref.shape[2]
    per = tile // LANES
    for s in range(slots):
        code = plan_ref[CODES + s]
        target = lax.div(code, SPAN)
        source = target + lax.rem(code, SPAN)
        rows = halves(jnp.concatenate([ext[source * per + k] for k in range(per)], axis=-1))
        on_real = joined(dot_nt(rows, tiles_ref[0, s]), 2 * fields)
        on_imag = joined(dot_nt(rows, tiles_ref[1, s]), 2 * fields)
        value = jnp.concatenate(
            [on_real[:fields] - on_imag[fields:], on_real[fields:] + on_imag[:fields]], axis=0
        )
        value = jnp.where(s < count_ref[0], value, 0.0)
        for k in range(per):
            out_ref[target * per + k] += value[:, k * LANES : (k + 1) * LANES]


def far_kernel(
    fields, items, width, slots, core_ref, plan_ref, leaves_ref, partial_ref, item_ref, trans_ref, window_ref,
    keep_ref, give_ref, total,
):
    units = partial_ref.shape[0]
    total[0:units] = partial_ref[...]
    if total.shape[0] > units:
        total[units:] = jnp.zeros((total.shape[0] - units, *total.shape[1:]), F32)
    for i in range(items):
        plain = item_ref[i].astype(F32)
        odd = odd_lanes(plain.shape)
        turned = jnp.where(odd, from_left(plain), -from_right(plain))
        rows = jnp.concatenate([plain, turned], axis=0).astype(BF16)
        local_field = dot_nn(rows, trans_ref[i]).astype(BF16).astype(F32)
        local_field = twice(local_field, plain.shape[1])
        local_real, local_imag = local_field[:fields], local_field[fields:]
        rows = jnp.concatenate(
            [jnp.where(odd, -local_imag, local_real), jnp.where(odd, local_real, local_imag)], axis=0
        ).astype(BF16)
        expansions = jnp.concatenate([as_rows(window_ref.at[i, k]) for k in range(width)], axis=-1)
        place = item_place(slots, i)
        leaf, unit = plan_ref[place + 2], plan_ref[place + 3]
        mask = window_mask(leaves_ref, leaf, unit, 2 * fields, width)
        image = jnp.where(mask, dot_nn(rows, expansions), 0.0)
        for k in range(width):
            total[unit + k] += image[:, k * LANES : (k + 1) * LANES]
    chips, share = keep_ref.shape[:2]
    core = core_ref[0]
    for c in range(chips):
        keep_ref[c] = total[pl.ds((2 * c + core) * share, share)].astype(keep_ref.dtype)
        give_ref[c] = total[pl.ds((2 * c + 1 - core) * share, share)].astype(give_ref.dtype)


def pair_kernel(keep_ref, got_ref, out_ref):
    out_ref[...] = (keep_ref[...].astype(F32) + got_ref[...].astype(F32)).astype(out_ref.dtype)


def tree_sum(values):
    while len(values) > 1:
        values = [values[k] + values[k + 1] for k in range(0, len(values), 2)]
    return values[0]


def close_kernel(*refs):
    refs[-1][...] = tree_sum([ref[...].astype(F32) for ref in refs[:-1]])


def assemble_kernel(
    fields, items, width, slots, core_ref, plan_ref, leaves_ref, mine_ref, theirs_ref, window_ref,
    out_ref, low_ref, made_ref, whole,
):
    chips, share = mine_ref.shape[:2]
    units = out_ref.shape[0]
    core = core_ref[0]
    for chip in range(chips):
        whole[pl.ds((2 * chip + core) * share, share)] = mine_ref[chip]
        whole[pl.ds((2 * chip + 1 - core) * share, share)] = theirs_ref[chip]
    out_ref[...] = whole[0:units]
    low_ref[...] = whole[0:units].astype(BF16)
    for i in range(items):
        place = item_place(slots, i)
        made_ref[i] = multi_rows(
            fields, width, plan_ref[place], plan_ref[place + 1], leaves_ref, low_ref, window_ref.at[i]
        ).astype(BF16)


def flat_lines(totals, fields):
    per = LANES // fields
    lane = lax.broadcasted_iota(jnp.int32, (fields, LANES), 1)
    field = lax.broadcasted_iota(jnp.int32, (fields, LANES), 0)
    lines = []
    for first in range(0, len(totals), per):
        line = jnp.zeros((fields, LANES), F32)
        for k, total in enumerate(totals[first : first + per]):
            line = jnp.where(lane == field + k * fields, jnp.sum(total, axis=1, keepdims=True), line)
        lines.append(jnp.sum(line, axis=0, keepdims=True))
    return jnp.concatenate(lines, axis=0)


def down(line, fields):
    shape = (fields, fields)
    own = lax.broadcasted_iota(jnp.int32, shape, 1) == lax.broadcasted_iota(jnp.int32, shape, 0)
    column = jnp.sum(jnp.where(own, jnp.broadcast_to(line, shape), 0.0), axis=1, keepdims=True)
    return jnp.broadcast_to(column, (fields, LANES))


def gram_kernel(fields, core_ref, right_ref, image_ref, *refs):
    *parts, out_ref = refs
    units = image_ref.shape[0]
    chips, share = parts[0].shape[:2]
    totals = None
    for k in range(chips * share):
        chip, within = divmod(k, share)
        unit = (2 * chip + core_ref[0]) * share + within
        place = jnp.minimum(unit, units - 1)
        r = right_ref[:, pl.ds(pl.multiple_of(place * LANES, LANES), LANES)]
        z = image_ref[place]
        q = tree_sum([part[chip, within].astype(F32) for part in parts])
        if 2 * chips * share > units:
            r = jnp.where(unit < units, r, 0.0)
            z = jnp.where(unit < units, z, 0.0)
        (rr, ri), (zr, zi), (qr, qi) = [(v[:fields], v[fields:]) for v in (r, z, q)]
        products = [
            rr * rr + ri * ri,
            rr * zr + ri * zi,
            rr * zi - ri * zr,
            zr * zr + zi * zi,
            rr * qr + ri * qi,
            rr * qi - ri * qr,
            zr * qr + zi * qi,
            zr * qi - zi * qr,
            qr * qr + qi * qi,
        ]
        totals = products if totals is None else [t + p for t, p in zip(totals, products)]
    out_ref[...] = flat_lines(totals, fields)


def final_kernel(fields, right_ref, image_ref, *refs):
    *sums_refs, out_ref = refs
    units = image_ref.shape[0]
    lines = tree_sum([ref[...] for ref in sums_refs])
    per = LANES // fields
    sums = [lines[k // per : k // per + 1, (k % per) * fields : (k % per + 1) * fields] for k in range(9)]
    a_real, a_imag, b_real, b_imag = [down(value, fields) for value in krylov_coefficients(sums)]
    for k in range(units):
        lanes = slice(k * LANES, (k + 1) * LANES)
        r_real, r_imag = right_ref[:fields, lanes], right_ref[fields:, lanes]
        z_real, z_imag = image_ref[k, :fields], image_ref[k, fields:]
        out_ref[:fields, lanes] = a_real * r_real - a_imag * r_imag + b_real * z_real - b_imag * z_imag
        out_ref[fields:, lanes] = a_real * r_imag + a_imag * r_real + b_real * z_imag + b_imag * z_real


def params(mebibytes=16):
    return pltpu.CompilerParams(vmem_limit_bytes=mebibytes * 1024 * 1024)


def is_power(count):
    return count & (count - 1) == 0


def reversed_bits(value, count):
    bits = count.bit_length() - 1
    return sum(((value >> k) & 1) << (bits - 1 - k) for k in range(bits))


def target_row(row, pair, rows):
    if not is_power(rows):
        return (pair - row + rows) % rows
    return pair ^ reversed_bits(row, rows)


def source_row(row, pair, rows):
    if not is_power(rows):
        return (pair - row + rows) % rows
    return reversed_bits(pair ^ row, rows)


def own_items_change_cores(rows, items, send):
    return items == 1 and send == 2


def item_route(rows, group, columns, send):
    items = rows * send // group

    def flat(r, g):
        return (g // columns * rows + r) * columns + g % columns

    def target(r, g, pair):
        d = target_row(r, pair, rows)
        return flat(d, g ^ 1 if d == r and own_items_change_cores(rows, items, send) else g)

    assert items * group == rows * send and (items % send == 0 or send % items == 0)
    routes = []
    for first in range(0, items, send):
        pairs = [(g * items + first) // send for g in range(group)]
        routes.append([(flat(r, g), target(r, g, pairs[g])) for r in range(rows) for g in range(group)])
    return items, routes


def local(
    right_side,
    near_tiles,
    tile_pairs,
    tile_count,
    panel_expansions,
    leaf_of_panel,
    far_pick,
    far_target,
    far_offset,
    translations,
):
    fields, panels = right_side.shape[1:]
    coefs = panel_expansions.shape[2]
    tile = near_tiles.shape[2]
    send = far_pick.shape[2]
    rows = lax.axis_size("row")
    group = lax.axis_size("grp") * lax.axis_size("col")
    row_here = lax.axis_index("row")
    own = lax.axis_index("grp") * lax.axis_size("col") + lax.axis_index("col")
    both = 2 * fields
    units = panels // LANES
    share = -(-units // group)
    edge = REACH * tile
    edge_units = edge // LANES
    width = tile // LANES + 1
    items, routes = item_route(rows, group, lax.axis_size("col"), send)

    assert rows % 2 == 0
    neighbours = [[r + 1 - 2 * (r % 2) for r in range(rows)], [(r - 1 + 2 * (r % 2)) % rows for r in range(rows)]]
    own_place, row_place = own.reshape(1), row_here.reshape(1)
    core_place = lax.rem(own, 2).reshape(1)
    slots = near_tiles.shape[1]
    pad_coefs = -(-coefs // 8) * 8
    chips = group // 2
    assert group == 2 * chips and chips & (chips - 1) == 0 and LANES % fields == 0
    window_shape = jax.ShapeDtypeStruct((items, width, pad_coefs, 2, LANES), BF16)
    item_shape = jax.ShapeDtypeStruct((items, fields, 2 * pad_coefs), BF16)
    part_shape = (share, both, LANES)

    def in_hbm(value):
        return pltpu.with_memory_space_constraint(value, pltpu.HBM)

    leaves = leaf_of_panel.reshape(units, 1, LANES)
    expansions = panel_expansions.transpose(2, 0, 1).reshape(coefs, 2, units, LANES).transpose(0, 2, 1, 3)
    expansions = in_hbm(expansions)
    moves = in_hbm(translations.transpose(0, 2, 1, 3))
    picks = far_pick.transpose(0, 2, 1)

    plan, made, windows, leaves, right = pl.pallas_call(
        functools.partial(begin_kernel, fields, items, width, send, rows),
        out_shape=(
            pltpu.SMEM((item_place(slots, items),), jnp.int32),
            item_shape,
            pltpu.VMEM(window_shape.shape, BF16),
            jax.ShapeDtypeStruct(leaves.shape, jnp.int32),
            jax.ShapeDtypeStruct((both, panels), F32),
        ),
        in_specs=[SMEM] * 2 + [HBM] * 8,
        out_specs=(SMEM,) + (VMEM,) * 4,
        scratch_shapes=[
            pltpu.SMEM(value.shape, jnp.int32)
            for value in (picks, leaf_of_panel, far_target, far_offset, tile_pairs)
        ]
        + [
            pltpu.SemaphoreType.DMA((7,)),
            pltpu.SemaphoreType.DMA((items, width, PIECES)),
        ],
        compiler_params=params(),
        name="begin",
    )(
        row_place,
        own_place,
        in_hbm(picks),
        in_hbm(leaf_of_panel),
        in_hbm(leaves),
        in_hbm(far_target),
        in_hbm(far_offset),
        in_hbm(tile_pairs),
        in_hbm(right_side.reshape(both, panels)),
        expansions,
    )

    def exchanged(made):
        parts = [
            lax.ppermute(made[k * send : k * send + min(send, items)], EVERY, route) for k, route in enumerate(routes)
        ]
        return parts[0] if len(parts) == 1 else jnp.concatenate(parts)

    def from_neighbours(image):
        edge_shape = (both, edge) if image.ndim == 2 else (edge_units, both, LANES)
        one, two = pl.pallas_call(
            edge_kernel,
            out_shape=(jax.ShapeDtypeStruct(edge_shape, BF16),) * 2,
            in_specs=[SMEM, VMEM],
            out_specs=(VMEM, VMEM),
            compiler_params=params(),
            name="edges",
        )(row_place, image)
        return [
            lax.ppermute(value, "row", list(enumerate(targets))) for value, targets in zip((one, two), neighbours)
        ]

    image_shape = jax.ShapeDtypeStruct((units, both, LANES), F32)
    target_windows, moved = pl.pallas_call(
        functools.partial(fetch_kernel, items, width, slots),
        out_shape=(
            pltpu.VMEM(window_shape.shape, BF16),
            pltpu.VMEM((items, 2 * pad_coefs, coefs), BF16),
        ),
        in_specs=[SMEM, HBM, HBM],
        out_specs=(VMEM, VMEM),
        scratch_shapes=[
            pltpu.VMEM((items, coefs, 2, coefs), BF16),
            pltpu.SemaphoreType.DMA((items, width, PIECES)),
            pltpu.SemaphoreType.DMA((items,)),
        ],
        compiler_params=params(24),
        cost_estimate=pl.CostEstimate(flops=0, bytes_accessed=6 * window_shape.size, transcendentals=0),
        name="fetch",
    )(plan, expansions, moves)

    def swapped(value, step):
        return lax.ppermute(value, GROUP, [(g, g ^ step) for g in range(group)])

    def near(one, two, low):
        return pl.pallas_call(
            functools.partial(near_kernel, fields),
            out_shape=image_shape,
            in_specs=[SMEM] * 3 + [VMEM] * 4,
            out_specs=VMEM,
            scratch_shapes=[pltpu.VMEM((units + 2 * edge_units, both, LANES), low.dtype)],
            compiler_params=params(),
            cost_estimate=pl.CostEstimate(
                flops=8 * fields * near_tiles.size // 2, bytes_accessed=2 * near_tiles.size, transcendentals=0
            ),
            name="near",
        )(row_place, tile_count, plan, one, two, low, near_tiles)

    def core_parts(partial, taken, dtype):
        half_shape = jax.ShapeDtypeStruct((chips, *part_shape), dtype)
        keep, give = pl.pallas_call(
            functools.partial(far_kernel, fields, items, width, slots),
            out_shape=(half_shape, half_shape),
            in_specs=[SMEM, SMEM] + [VMEM] * 5,
            out_specs=(VMEM, VMEM),
            scratch_shapes=[pltpu.VMEM((share * group, both, LANES), F32)],
            compiler_params=params(),
            name="far",
        )(core_place, plan, leaves, partial, taken, moved, target_windows)
        return keep, swapped(give, 1)

    def pair_sums(keep, got):
        pair = pl.pallas_call(
            pair_kernel,
            out_shape=jax.ShapeDtypeStruct(keep.shape, BF16),
            in_specs=[VMEM, VMEM],
            out_specs=VMEM,
            compiler_params=params(),
            name="pair",
        )(keep, got)
        arrived = {step: swapped(pair, 2 * step) for step in range(chips - 1, 0, -1)}
        return [pair] + [arrived[step] for step in range(1, chips)]

    def whole_sum(parts):
        mine = pl.pallas_call(
            close_kernel,
            out_shape=jax.ShapeDtypeStruct((chips, *part_shape), F32),
            in_specs=[VMEM] * chips,
            out_specs=VMEM,
            compiler_params=params(),
            name="close",
        )(*parts)
        theirs = swapped(mine, 1)
        low_shape = jax.ShapeDtypeStruct((units, both, LANES), BF16)
        return pl.pallas_call(
            functools.partial(assemble_kernel, fields, items, width, slots),
            out_shape=(image_shape, low_shape, item_shape),
            in_specs=[SMEM, SMEM] + [VMEM] * 4,
            out_specs=(VMEM,) * 3,
            scratch_shapes=[pltpu.VMEM((share * group, both, LANES), F32)],
            compiler_params=params(),
            name="assemble",
        )(core_place, plan, leaves, mine, theirs, windows)

    def row_sums(lines):
        def added(*values):
            return pl.pallas_call(
                close_kernel,
                out_shape=jax.ShapeDtypeStruct(lines.shape, F32),
                in_specs=[VMEM] * 2,
                out_specs=VMEM,
                compiler_params=params(),
                name="add",
            )(*values)

        lines = added(lines, swapped(lines, 1))
        if not is_power(rows):
            return (lax.psum(lines, "row"),)
        step = 1
        while step < rows:
            other = lax.ppermute(lines, "row", [(r, r ^ step) for r in range(rows)])
            if 2 * step == rows:
                return lines, other
            lines = added(lines, other)
            step *= 2
        return (lines,)

    partial = near(*from_neighbours(right), right)
    z_all, z_low, made = whole_sum(pair_sums(*core_parts(partial, exchanged(made), F32)))
    partial = near(*from_neighbours(z_low), z_low)
    parts = pair_sums(*core_parts(partial, exchanged(made), BF16))

    lines = pl.pallas_call(
        functools.partial(gram_kernel, fields),
        out_shape=jax.ShapeDtypeStruct((-(-9 * fields // LANES), LANES), F32),
        in_specs=[SMEM] + [VMEM] * (2 + chips),
        out_specs=VMEM,
        compiler_params=params(),
        name="gram",
    )(core_place, right, z_all, *parts)
    sums = row_sums(lines)
    out = pl.pallas_call(
        functools.partial(final_kernel, fields),
        out_shape=jax.ShapeDtypeStruct((both, panels), F32),
        in_specs=[VMEM] * (2 + len(sums)),
        out_specs=VMEM,
        compiler_params=params(),
        name="combine",
    )(right, z_all, *sums)
    return out.reshape(right_side.shape)


def krylov_coefficients(sums):
    rr, rz_real, rz_imag, zz, rq_real, rq_imag, zq_real, zq_imag, qq = sums

    def times(left, right):
        return left[0] * right[0] - left[1] * right[1], left[0] * right[1] + left[1] * right[0]

    def conj_times(left, right):
        return left[0] * right[0] + left[1] * right[1], left[0] * right[1] - left[1] * right[0]

    def scale(factor, value):
        return factor * value[0], factor * value[1]

    def plus(*values):
        return sum(v[0] for v in values), sum(v[1] for v in values)

    def size(value):
        return value[0] * value[0] + value[1] * value[1]

    rz, rq, zq = (rz_real, rz_imag), (rq_real, rq_imag), (zq_real, zq_imag)
    beta = jnp.sqrt(rr + EPSILON)
    inv = 1.0 / beta
    norm_one = rr * inv * inv
    product = scale(inv * inv, rz)
    h_first = (0.5 * norm_one + product[0], product[1])
    shift = (h_first[0] - 0.5, h_first[1])
    residue = zz * inv * inv - 2.0 * conj_times(shift, product)[0] + size(shift) * norm_one
    residue = jnp.maximum(residue, 0.0)
    h_sub = jnp.sqrt(residue + EPSILON)
    alpha = inv / h_sub
    gamma = scale(-alpha, shift)
    h_upper = scale(
        inv,
        plus(
            scale(0.5, plus(scale(alpha, rz), scale(rr, gamma))), scale(alpha, rq), times(gamma, rz)
        ),
    )
    second = plus(
        scale(alpha * alpha, zq),
        scale(alpha * zz, gamma),
        scale(alpha, conj_times(gamma, rq)),
        scale(size(gamma), rz),
    )
    h_middle = (0.5 * residue / (h_sub * h_sub) + second[0], second[1])
    keep = (h_middle[0] - 0.5, h_middle[1])
    on_z = plus(gamma, scale(-alpha, keep))
    on_r = plus(scale(-inv, h_upper), scale(-1.0, times(keep, gamma)))
    last = (
        alpha * alpha * qq
        + size(on_z) * zz
        + size(on_r) * rr
        + 2.0
        * (
            conj_times(on_r, times(on_z, rz))[0]
            + alpha * conj_times(on_r, rq)[0]
            + alpha * conj_times(on_z, zq)[0]
        )
    )
    h_last = jnp.sqrt(jnp.maximum(last, 0.0) + EPSILON)
    radius = jnp.sqrt(size(h_first) + h_sub * h_sub)
    cosine = scale(1.0 / radius, h_first)
    sine = h_sub / radius
    upper = plus(conj_times(cosine, h_upper), scale(sine, h_middle))
    lower = plus(times(cosine, h_middle), scale(-sine, h_upper))
    radius_two = jnp.sqrt(size(lower) + h_last * h_last)
    cosine_two = scale(1.0 / radius_two, lower)
    weight_two = scale(-sine * beta / radius_two, (cosine_two[0], -cosine_two[1]))
    goal = scale(beta, (cosine[0], -cosine[1]))
    weight_one = scale(1.0 / radius, plus(goal, scale(-1.0, times(upper, weight_two))))
    on_right = plus(scale(inv, weight_one), times(weight_two, gamma))
    on_image = scale(alpha, weight_two)
    return on_right[0], on_right[1], on_image[0], on_image[1]


def solution(mesh):
    return jax.shard_map(
        local,
        mesh=mesh,
        in_specs=(
            P(None, None, "row"),
            P(None, ("grp", "row", "col"), None, None),
            P(("grp", "row", "col")),
            P(("grp", "row", "col")),
            P(None, "row", None),
            P("row", None),
            P(),
            P("row", None),
            P("row", None),
            P(),
        ),
        out_specs=P(None, None, "row"),
        check_vma=False,
    )
```

```python
import functools

import jax
import jax.numpy as jnp
from jax import lax
from jax.experimental import pallas as pl
from jax.experimental.pallas import tpu as pltpu
from jax.sharding import PartitionSpec as P

REACH = 2
SPAN = 2 * REACH + 1
LANES = 128
EPSILON = 1e-06
GROUP = ("grp", "col")
CODES = 0
PER_ITEM = 5
PIECES = 4
EVERY = ("grp", "row", "col")

F32 = jnp.float32
BF16 = jnp.bfloat16
SMEM = pl.BlockSpec(memory_space=pltpu.SMEM)
VMEM = pl.BlockSpec(memory_space=pltpu.VMEM)
HBM = pl.BlockSpec(memory_space=pltpu.HBM)


def dot_nn(left, right):
    return lax.dot_general(left, right, (((1,), (0,)), ((), ())), preferred_element_type=F32)


def dot_nt(left, right):
    return lax.dot_general(left, right, (((1,), (1,)), ((), ())), preferred_element_type=F32)


def halves(rows):
    if rows.dtype != F32:
        return rows
    high = rows.astype(BF16)
    return jnp.concatenate([high, (rows - high.astype(F32)).astype(BF16)], axis=0)


def joined(sums, count):
    return sums if sums.shape[0] == count else sums[:count] + sums[count:]


def odd_lanes(shape):
    return lax.rem(lax.broadcasted_iota(jnp.int32, shape, 1), 2) == 1


def twice(value, width):
    rows = value.shape[0]
    parts = []
    for k in range(width // LANES):
        first = (k // 2) * LANES
        part = value[:, first : first + LANES]
        if part.shape[1] < LANES:
            part = jnp.concatenate([part, jnp.zeros((rows, LANES - part.shape[1]), part.dtype)], axis=-1)
        lane = lax.broadcasted_iota(jnp.int32, (rows, LANES), 1)
        parts.append(jnp.take_along_axis(part, lax.div(lane, 2) + (k % 2) * (LANES // 2), axis=1))
    return jnp.concatenate(parts, axis=-1)


def from_left(value):
    return pltpu.roll(value, 1, 1)


def from_right(value):
    return pltpu.roll(value, value.shape[1] - 1, 1)


def item_place(slots, item):
    return CODES + slots + PER_ITEM * item


def window_start(leaf_ref, leaf, width):
    units = leaf_ref.shape[1] // LANES
    before = jnp.int32(0)
    for k in range(units):
        before = before + (leaf_ref[0, k * LANES] < leaf).astype(jnp.int32)
    return jnp.clip(before - 1, 0, units - width)


def window_mask(leaves_ref, leaf, unit, rows, width):
    leaves = jnp.concatenate([leaves_ref[unit + k] for k in range(width)], axis=-1)
    return jnp.broadcast_to(leaves, (rows, width * LANES)) == leaf


def window_copies(exp_ref, unit, window_ref, sem, width):
    coefs = exp_ref.shape[0]
    step = -(-coefs // PIECES)
    copies = []
    for k in range(width):
        for p in range(PIECES):
            part = pl.ds(p * step, min(step, coefs - p * step))
            copies.append(
                pltpu.make_async_copy(exp_ref.at[part, unit + k], window_ref.at[k, part], sem.at[k, p])
            )
    return copies


def clear_rest(window_ref, coefs, width):
    rest = window_ref.shape[1] - coefs
    for k in range(width):
        window_ref[k, pl.ds(coefs, rest)] = jnp.zeros((rest, 2, LANES), BF16)


def multi_rows(fields, width, leaf, unit, leaves_ref, low_ref, window_ref):
    if len(low_ref.shape) == 2:
        first = pl.multiple_of(unit * LANES, LANES)
        rows = low_ref[:, pl.ds(first, width * LANES)]
    else:
        rows = jnp.concatenate([low_ref[unit + k] for k in range(width)], axis=-1)
    mask = window_mask(leaves_ref, leaf, unit, 2 * fields, width)
    rows = halves(jnp.where(mask, rows.astype(F32), 0.0).astype(rows.dtype))
    expansions = jnp.concatenate([as_rows(window_ref.at[k]) for k in range(width)], axis=-1)
    total = joined(dot_nt(rows, expansions), 2 * fields)
    on_real, on_imag = total[:fields], total[fields:]
    odd = odd_lanes(on_real.shape)
    other = jnp.where(odd, from_left(on_imag), from_right(on_imag))
    return jnp.where(odd, -on_real, on_real) - other


def as_rows(ref):
    return ref.reshape(ref.shape[0] * 2, ref.shape[2])[...]


def edge_kernel(row_ref, image_ref, one_ref, two_ref):
    even = lax.rem(row_ref[0], 2) == 0
    if len(image_ref.shape) == 2:
        edge = one_ref.shape[1]
        first, last = image_ref[:, :edge], image_ref[:, image_ref.shape[1] - edge :]
    else:
        edge = one_ref.shape[0]
        first, last = image_ref[:edge], image_ref[image_ref.shape[0] - edge :]
    first, last = first.astype(one_ref.dtype), last.astype(one_ref.dtype)

    @pl.when(even)
    def _():
        one_ref[...], two_ref[...] = last, first

    @pl.when(jnp.logical_not(even))
    def _():
        one_ref[...], two_ref[...] = first, last


def begin_kernel(
    fields, items, width, send, rows, row_ref, own_ref, pick_hbm, leaf_hbm, leaves_hbm,
    target_hbm, offset_hbm, pairs_hbm, right_hbm, exp_ref,
    plan_ref, out_ref, window_ref, leaves_ref, right_ref,
    pick_ref, leaf_ref, target_ref, offset_ref, pairs_ref, sem, window_sem,
):
    loads = [
        pltpu.make_async_copy(source, place, sem.at[k])
        for k, (source, place) in enumerate(
            (
                (leaf_hbm, leaf_ref),
                (pick_hbm, pick_ref),
                (target_hbm, target_ref),
                (offset_hbm, offset_ref),
                (pairs_hbm, pairs_ref),
                (leaves_hbm, leaves_ref),
                (right_hbm, right_ref),
            )
        )
    ]
    for load in loads:
        load.start()
    for i in range(items):
        clear_rest(window_ref.at[i], exp_ref.shape[0], width)
    slots = pairs_ref.shape[0]
    own = own_ref[0]
    loads[0].wait()
    loads[1].wait()
    row = row_ref[0]

    def partner(i, coming):
        number = own * items + i
        pair, number = lax.div(number, send), lax.rem(number, send)
        other = source_row(row, pair, rows) if coming else target_row(row, pair, rows)
        if coming and own_items_change_cores(rows, items, send):
            number = jnp.where(other == row, 1 - number, number)
        return other, number

    for i in range(items):
        other, number = partner(i, False)
        leaf = pick_ref[other, number, row]
        unit = window_start(leaf_ref, leaf, width)
        place = item_place(slots, i)
        plan_ref[place], plan_ref[place + 1] = leaf, unit
        for copy in window_copies(exp_ref, unit, window_ref.at[i], window_sem.at[i], width):
            copy.start()
    for load in loads[2:]:
        load.wait()
    for s in range(slots):
        plan_ref[CODES + s] = pairs_ref[s]
    for i in range(items):
        place = item_place(slots, i)
        other, number = partner(i, True)
        leaf = target_ref[0, other * send + number]
        plan_ref[place + 2], plan_ref[place + 3] = leaf, window_start(leaf_ref, leaf, width)
        plan_ref[place + 4] = offset_ref[0, other * send + number]
    for i in range(items):
        place = item_place(slots, i)
        leaf, unit = plan_ref[place], plan_ref[place + 1]
        for copy in window_copies(exp_ref, unit, window_ref.at[i], window_sem.at[i], width):
            copy.wait()
        out_ref[i] = multi_rows(fields, width, leaf, unit, leaves_ref, right_ref, window_ref.at[i]).astype(BF16)


def fetch_kernel(items, width, slots, plan_ref, exp_ref, trans_ref, window_ref, moved_ref, trans_buf, sem, trans_sem):
    coefs = trans_ref.shape[3]
    for i in range(items):
        clear_rest(window_ref.at[i], coefs, width)

    def trans_copy(i):
        offset = plan_ref[item_place(slots, i) + 4]
        return pltpu.make_async_copy(trans_ref.at[offset], trans_buf.at[i], trans_sem.at[i])

    def exp_copies(i):
        unit = plan_ref[item_place(slots, i) + 3]
        return window_copies(exp_ref, unit, window_ref.at[i], sem.at[i], width)

    for i in range(items):
        trans_copy(i).start()
        for copy in exp_copies(i):
            copy.start()
    rest = moved_ref.shape[1] - 2 * coefs
    for i in range(items):
        trans_copy(i).wait()
        moved_ref[i, pl.ds(0, 2 * coefs)] = trans_buf[i].reshape(2 * coefs, coefs)
        moved_ref[i, pl.ds(2 * coefs, rest)] = jnp.zeros((rest, coefs), BF16)
        for copy in exp_copies(i):
            copy.wait()


def near_sources(row_ref, one_ref, two_ref, here_ref, units, ext):
    edge = (ext.shape[0] - units) // 2
    even = lax.rem(row_ref[0], 2) == 0
    one_at = jnp.where(even, edge + units, 0)
    two_at = jnp.where(even, 0, edge + units)
    if len(here_ref.shape) == 2:
        for k in range(edge):
            lanes = slice(k * LANES, (k + 1) * LANES)
            ext[one_at + k] = one_ref[:, lanes].astype(ext.dtype)
            ext[two_at + k] = two_ref[:, lanes].astype(ext.dtype)
        for k in range(units):
            ext[edge + k] = here_ref[:, k * LANES : (k + 1) * LANES]
    else:
        ext[pl.ds(one_at, edge)] = one_ref[...]
        ext[pl.ds(two_at, edge)] = two_ref[...]
        ext[edge : edge + units] = here_ref[...]


def near_kernel(
    fields, row_ref, count_ref, plan_ref, one_ref, two_ref, here_ref, tiles_ref, out_ref, ext
):
    near_sources(row_ref, one_ref, two_ref, here_ref, out_ref.shape[0], ext)
    out_ref[...] = jnp.zeros_like(out_ref)
    slots, tile = tiles_ref.shape[1], tiles_ref.shape[2]
    per = tile // LANES
    for s in range(slots):
        code = plan_ref[CODES + s]
        target = lax.div(code, SPAN)
        source = target + lax.rem(code, SPAN)
        rows = halves(jnp.concatenate([ext[source * per + k] for k in range(per)], axis=-1))
        on_real = joined(dot_nt(rows, tiles_ref[0, s]), 2 * fields)
        on_imag = joined(dot_nt(rows, tiles_ref[1, s]), 2 * fields)
        value = jnp.concatenate(
            [on_real[:fields] - on_imag[fields:], on_real[fields:] + on_imag[:fields]], axis=0
        )
        value = jnp.where(s < count_ref[0], value, 0.0)
        for k in range(per):
            out_ref[target * per + k] += value[:, k * LANES : (k + 1) * LANES]


def far_kernel(
    fields, items, width, slots, core_ref, plan_ref, leaves_ref, partial_ref, item_ref, trans_ref, window_ref,
    keep_ref, give_ref, total,
):
    units = partial_ref.shape[0]
    total[0:units] = partial_ref[...]
    if total.shape[0] > units:
        total[units:] = jnp.zeros((total.shape[0] - units, *total.shape[1:]), F32)
    for i in range(items):
        plain = item_ref[i].astype(F32)
        odd = odd_lanes(plain.shape)
        turned = jnp.where(odd, from_left(plain), -from_right(plain))
        rows = jnp.concatenate([plain, turned], axis=0).astype(BF16)
        local_field = dot_nn(rows, trans_ref[i]).astype(BF16).astype(F32)
        local_field = twice(local_field, plain.shape[1])
        local_real, local_imag = local_field[:fields], local_field[fields:]
        rows = jnp.concatenate(
            [jnp.where(odd, -local_imag, local_real), jnp.where(odd, local_real, local_imag)], axis=0
        ).astype(BF16)
        expansions = jnp.concatenate([as_rows(window_ref.at[i, k]) for k in range(width)], axis=-1)
        place = item_place(slots, i)
        leaf, unit = plan_ref[place + 2], plan_ref[place + 3]
        mask = window_mask(leaves_ref, leaf, unit, 2 * fields, width)
        image = jnp.where(mask, dot_nn(rows, expansions), 0.0)
        for k in range(width):
            total[unit + k] += image[:, k * LANES : (k + 1) * LANES]
    chips, share = keep_ref.shape[:2]
    core = core_ref[0]
    for c in range(chips):
        keep_ref[c] = total[pl.ds((2 * c + core) * share, share)].astype(keep_ref.dtype)
        give_ref[c] = total[pl.ds((2 * c + 1 - core) * share, share)].astype(give_ref.dtype)


def pair_kernel(keep_ref, got_ref, out_ref):
    out_ref[...] = (keep_ref[...].astype(F32) + got_ref[...].astype(F32)).astype(out_ref.dtype)


def tree_sum(values):
    while len(values) > 1:
        values = [values[k] + values[k + 1] for k in range(0, len(values), 2)]
    return values[0]


def close_kernel(*refs):
    refs[-1][...] = tree_sum([ref[...].astype(F32) for ref in refs[:-1]])


def assemble_kernel(
    fields, items, width, slots, core_ref, plan_ref, leaves_ref, mine_ref, theirs_ref, window_ref,
    out_ref, low_ref, made_ref, whole,
):
    chips, share = mine_ref.shape[:2]
    units = out_ref.shape[0]
    core = core_ref[0]
    for chip in range(chips):
        whole[pl.ds((2 * chip + core) * share, share)] = mine_ref[chip]
        whole[pl.ds((2 * chip + 1 - core) * share, share)] = theirs_ref[chip]
    out_ref[...] = whole[0:units]
    low_ref[...] = whole[0:units].astype(BF16)
    for i in range(items):
        place = item_place(slots, i)
        made_ref[i] = multi_rows(
            fields, width, plan_ref[place], plan_ref[place + 1], leaves_ref, low_ref, window_ref.at[i]
        ).astype(BF16)


def flat_lines(totals, fields):
    per = LANES // fields
    lane = lax.broadcasted_iota(jnp.int32, (fields, LANES), 1)
    field = lax.broadcasted_iota(jnp.int32, (fields, LANES), 0)
    lines = []
    for first in range(0, len(totals), per):
        line = jnp.zeros((fields, LANES), F32)
        for k, total in enumerate(totals[first : first + per]):
            line = jnp.where(lane == field + k * fields, jnp.sum(total, axis=1, keepdims=True), line)
        lines.append(jnp.sum(line, axis=0, keepdims=True))
    return jnp.concatenate(lines, axis=0)


def columns_of(lines, count, fields):
    per = LANES // fields
    columns = []
    for k in range(lines.shape[0]):
        square = jnp.transpose(jnp.broadcast_to(lines[k : k + 1], (LANES, LANES)))
        columns += [square[j * fields : (j + 1) * fields, :1] for j in range(per)]
    return columns[:count]


def gram_kernel(fields, core_ref, right_ref, image_ref, *refs):
    *parts, out_ref = refs
    units = image_ref.shape[0]
    chips, share = parts[0].shape[:2]
    totals = None
    for k in range(chips * share):
        chip, within = divmod(k, share)
        unit = (2 * chip + core_ref[0]) * share + within
        place = jnp.minimum(unit, units - 1)
        r = right_ref[:, pl.ds(pl.multiple_of(place * LANES, LANES), LANES)]
        z = image_ref[place]
        q = tree_sum([part[chip, within].astype(F32) for part in parts])
        if 2 * chips * share > units:
            r = jnp.where(unit < units, r, 0.0)
            z = jnp.where(unit < units, z, 0.0)
        (rr, ri), (zr, zi), (qr, qi) = [(v[:fields], v[fields:]) for v in (r, z, q)]
        products = [
            rr * rr + ri * ri,
            rr * zr + ri * zi,
            rr * zi - ri * zr,
            zr * zr + zi * zi,
            rr * qr + ri * qi,
            rr * qi - ri * qr,
            zr * qr + zi * qi,
            zr * qi - zi * qr,
            qr * qr + qi * qi,
        ]
        totals = products if totals is None else [t + p for t, p in zip(totals, products)]
    out_ref[...] = jnp.broadcast_to(flat_lines(totals, fields)[None], out_ref.shape)


def final_kernel(fields, sums_ref, right_ref, image_ref, out_ref):
    units = image_ref.shape[0]
    sums = columns_of(jnp.sum(sums_ref[...], axis=0), 9, fields)
    a_real, a_imag, b_real, b_imag = [
        jnp.broadcast_to(value, (fields, LANES)) for value in krylov_coefficients(sums)
    ]
    for k in range(units):
        lanes = slice(k * LANES, (k + 1) * LANES)
        r_real, r_imag = right_ref[:fields, lanes], right_ref[fields:, lanes]
        z_real, z_imag = image_ref[k, :fields], image_ref[k, fields:]
        out_ref[:fields, lanes] = a_real * r_real - a_imag * r_imag + b_real * z_real - b_imag * z_imag
        out_ref[fields:, lanes] = a_real * r_imag + a_imag * r_real + b_real * z_imag + b_imag * z_real


def params(mebibytes=16):
    return pltpu.CompilerParams(vmem_limit_bytes=mebibytes * 1024 * 1024)


def is_power(count):
    return count & (count - 1) == 0


def reversed_bits(value, count):
    bits = count.bit_length() - 1
    return sum(((value >> k) & 1) << (bits - 1 - k) for k in range(bits))


def target_row(row, pair, rows):
    if not is_power(rows):
        return (pair - row + rows) % rows
    return pair ^ reversed_bits(row, rows)


def source_row(row, pair, rows):
    if not is_power(rows):
        return (pair - row + rows) % rows
    return reversed_bits(pair ^ row, rows)


def own_items_change_cores(rows, items, send):
    return items == 1 and send == 2


def item_route(rows, group, columns, send):
    items = rows * send // group

    def flat(r, g):
        return (g // columns * rows + r) * columns + g % columns

    def target(r, g, pair):
        d = target_row(r, pair, rows)
        return flat(d, g ^ 1 if d == r and own_items_change_cores(rows, items, send) else g)

    assert items * group == rows * send and (items % send == 0 or send % items == 0)
    routes = []
    for first in range(0, items, send):
        pairs = [(g * items + first) // send for g in range(group)]
        routes.append([(flat(r, g), target(r, g, pairs[g])) for r in range(rows) for g in range(group)])
    return items, routes


def local(
    right_side,
    near_tiles,
    tile_pairs,
    tile_count,
    panel_expansions,
    leaf_of_panel,
    far_pick,
    far_target,
    far_offset,
    translations,
):
    fields, panels = right_side.shape[1:]
    coefs = panel_expansions.shape[2]
    tile = near_tiles.shape[2]
    send = far_pick.shape[2]
    rows = lax.axis_size("row")
    group = lax.axis_size("grp") * lax.axis_size("col")
    row_here = lax.axis_index("row")
    own = lax.axis_index("grp") * lax.axis_size("col") + lax.axis_index("col")
    both = 2 * fields
    units = panels // LANES
    share = -(-units // group)
    edge = REACH * tile
    edge_units = edge // LANES
    width = tile // LANES + 1
    items, routes = item_route(rows, group, lax.axis_size("col"), send)

    assert rows % 2 == 0
    neighbours = [[r + 1 - 2 * (r % 2) for r in range(rows)], [(r - 1 + 2 * (r % 2)) % rows for r in range(rows)]]
    own_place, row_place = own.reshape(1), row_here.reshape(1)
    core_place = lax.rem(own, 2).reshape(1)
    slots = near_tiles.shape[1]
    pad_coefs = -(-coefs // 8) * 8
    chips = group // 2
    assert group == 2 * chips and chips & (chips - 1) == 0 and LANES % fields == 0
    window_shape = jax.ShapeDtypeStruct((items, width, pad_coefs, 2, LANES), BF16)
    item_shape = jax.ShapeDtypeStruct((items, fields, 2 * pad_coefs), BF16)
    part_shape = (share, both, LANES)

    def in_hbm(value):
        return pltpu.with_memory_space_constraint(value, pltpu.HBM)

    leaves = leaf_of_panel.reshape(units, 1, LANES)
    expansions = panel_expansions.transpose(2, 0, 1).reshape(coefs, 2, units, LANES).transpose(0, 2, 1, 3)
    expansions = in_hbm(expansions)
    moves = in_hbm(translations.transpose(0, 2, 1, 3))
    picks = far_pick.transpose(0, 2, 1)

    plan, made, windows, leaves, right = pl.pallas_call(
        functools.partial(begin_kernel, fields, items, width, send, rows),
        out_shape=(
            pltpu.SMEM((item_place(slots, items),), jnp.int32),
            item_shape,
            pltpu.VMEM(window_shape.shape, BF16),
            jax.ShapeDtypeStruct(leaves.shape, jnp.int32),
            jax.ShapeDtypeStruct((both, panels), F32),
        ),
        in_specs=[SMEM] * 2 + [HBM] * 8,
        out_specs=(SMEM,) + (VMEM,) * 4,
        scratch_shapes=[
            pltpu.SMEM(value.shape, jnp.int32)
            for value in (picks, leaf_of_panel, far_target, far_offset, tile_pairs)
        ]
        + [
            pltpu.SemaphoreType.DMA((7,)),
            pltpu.SemaphoreType.DMA((items, width, PIECES)),
        ],
        compiler_params=params(),
        name="begin",
    )(
        row_place,
        own_place,
        in_hbm(picks),
        in_hbm(leaf_of_panel),
        in_hbm(leaves),
        in_hbm(far_target),
        in_hbm(far_offset),
        in_hbm(tile_pairs),
        in_hbm(right_side.reshape(both, panels)),
        expansions,
    )

    def exchanged(made):
        parts = [
            lax.ppermute(made[k * send : k * send + min(send, items)], EVERY, route) for k, route in enumerate(routes)
        ]
        return parts[0] if len(parts) == 1 else jnp.concatenate(parts)

    def from_neighbours(image):
        edge_shape = (both, edge) if image.ndim == 2 else (edge_units, both, LANES)
        one, two = pl.pallas_call(
            edge_kernel,
            out_shape=(jax.ShapeDtypeStruct(edge_shape, BF16),) * 2,
            in_specs=[SMEM, VMEM],
            out_specs=(VMEM, VMEM),
            compiler_params=params(),
            name="edges",
        )(row_place, image)
        return [
            lax.ppermute(value, "row", list(enumerate(targets))) for value, targets in zip((one, two), neighbours)
        ]

    image_shape = jax.ShapeDtypeStruct((units, both, LANES), F32)
    target_windows, moved = pl.pallas_call(
        functools.partial(fetch_kernel, items, width, slots),
        out_shape=(
            pltpu.VMEM(window_shape.shape, BF16),
            pltpu.VMEM((items, 2 * pad_coefs, coefs), BF16),
        ),
        in_specs=[SMEM, HBM, HBM],
        out_specs=(VMEM, VMEM),
        scratch_shapes=[
            pltpu.VMEM((items, coefs, 2, coefs), BF16),
            pltpu.SemaphoreType.DMA((items, width, PIECES)),
            pltpu.SemaphoreType.DMA((items,)),
        ],
        compiler_params=params(24),
        cost_estimate=pl.CostEstimate(flops=0, bytes_accessed=6 * window_shape.size, transcendentals=0),
        name="fetch",
    )(plan, expansions, moves)

    def swapped(value, step):
        return lax.ppermute(value, GROUP, [(g, g ^ step) for g in range(group)])

    def near(one, two, low):
        return pl.pallas_call(
            functools.partial(near_kernel, fields),
            out_shape=image_shape,
            in_specs=[SMEM] * 3 + [VMEM] * 4,
            out_specs=VMEM,
            scratch_shapes=[pltpu.VMEM((units + 2 * edge_units, both, LANES), low.dtype)],
            compiler_params=params(),
            cost_estimate=pl.CostEstimate(
                flops=8 * fields * near_tiles.size // 2, bytes_accessed=2 * near_tiles.size, transcendentals=0
            ),
            name="near",
        )(row_place, tile_count, plan, one, two, low, near_tiles)

    def core_parts(partial, taken, dtype):
        half_shape = jax.ShapeDtypeStruct((chips, *part_shape), dtype)
        keep, give = pl.pallas_call(
            functools.partial(far_kernel, fields, items, width, slots),
            out_shape=(half_shape, half_shape),
            in_specs=[SMEM, SMEM] + [VMEM] * 5,
            out_specs=(VMEM, VMEM),
            scratch_shapes=[pltpu.VMEM((share * group, both, LANES), F32)],
            compiler_params=params(),
            name="far",
        )(core_place, plan, leaves, partial, taken, moved, target_windows)
        return keep, swapped(give, 1)

    def pair_sums(keep, got):
        pair = pl.pallas_call(
            pair_kernel,
            out_shape=jax.ShapeDtypeStruct(keep.shape, BF16),
            in_specs=[VMEM, VMEM],
            out_specs=VMEM,
            compiler_params=params(),
            name="pair",
        )(keep, got)
        arrived = {step: swapped(pair, 2 * step) for step in range(chips - 1, 0, -1)}
        return [pair] + [arrived[step] for step in range(1, chips)]

    def whole_sum(parts):
        mine = pl.pallas_call(
            close_kernel,
            out_shape=jax.ShapeDtypeStruct((chips, *part_shape), F32),
            in_specs=[VMEM] * chips,
            out_specs=VMEM,
            compiler_params=params(),
            name="close",
        )(*parts)
        theirs = swapped(mine, 1)
        low_shape = jax.ShapeDtypeStruct((units, both, LANES), BF16)
        return pl.pallas_call(
            functools.partial(assemble_kernel, fields, items, width, slots),
            out_shape=(image_shape, low_shape, item_shape),
            in_specs=[SMEM, SMEM] + [VMEM] * 4,
            out_specs=(VMEM,) * 3,
            scratch_shapes=[pltpu.VMEM((share * group, both, LANES), F32)],
            compiler_params=params(),
            name="assemble",
        )(core_place, plan, leaves, mine, theirs, windows)

    partial = near(*from_neighbours(right), right)
    z_all, z_low, made = whole_sum(pair_sums(*core_parts(partial, exchanged(made), F32)))
    partial = near(*from_neighbours(z_low), z_low)
    parts = pair_sums(*core_parts(partial, exchanged(made), BF16))

    lines = pl.pallas_call(
        functools.partial(gram_kernel, fields),
        out_shape=jax.ShapeDtypeStruct((2 * rows, -(-9 * fields // LANES), LANES), F32),
        in_specs=[SMEM] + [VMEM] * (2 + chips),
        out_specs=VMEM,
        compiler_params=params(),
        name="gram",
    )(core_place, right, z_all, *parts)
    columns = lax.axis_size("col")
    same_chip = [
        [((g + k) // columns * rows + r) * columns + (g + k) % columns for r in range(rows) for k in range(2)]
        for g in range(0, group, 2)
    ]
    sums = lax.all_to_all(lines, EVERY, 0, 0, axis_index_groups=same_chip, tiled=True)
    out = pl.pallas_call(
        functools.partial(final_kernel, fields),
        out_shape=jax.ShapeDtypeStruct((both, panels), F32),
        in_specs=[VMEM] * 3,
        out_specs=VMEM,
        compiler_params=params(),
        name="combine",
    )(sums, right, z_all)
    return out.reshape(right_side.shape)


def krylov_coefficients(sums):
    rr, rz_real, rz_imag, zz, rq_real, rq_imag, zq_real, zq_imag, qq = sums

    def times(left, right):
        return left[0] * right[0] - left[1] * right[1], left[0] * right[1] + left[1] * right[0]

    def conj_times(left, right):
        return left[0] * right[0] + left[1] * right[1], left[0] * right[1] - left[1] * right[0]

    def scale(factor, value):
        return factor * value[0], factor * value[1]

    def plus(*values):
        return sum(v[0] for v in values), sum(v[1] for v in values)

    def size(value):
        return value[0] * value[0] + value[1] * value[1]

    rz, rq, zq = (rz_real, rz_imag), (rq_real, rq_imag), (zq_real, zq_imag)
    beta = jnp.sqrt(rr + EPSILON)
    inv = 1.0 / beta
    norm_one = rr * inv * inv
    product = scale(inv * inv, rz)
    h_first = (0.5 * norm_one + product[0], product[1])
    shift = (h_first[0] - 0.5, h_first[1])
    residue = zz * inv * inv - 2.0 * conj_times(shift, product)[0] + size(shift) * norm_one
    residue = jnp.maximum(residue, 0.0)
    h_sub = jnp.sqrt(residue + EPSILON)
    alpha = inv / h_sub
    gamma = scale(-alpha, shift)
    h_upper = scale(
        inv,
        plus(
            scale(0.5, plus(scale(alpha, rz), scale(rr, gamma))), scale(alpha, rq), times(gamma, rz)
        ),
    )
    second = plus(
        scale(alpha * alpha, zq),
        scale(alpha * zz, gamma),
        scale(alpha, conj_times(gamma, rq)),
        scale(size(gamma), rz),
    )
    h_middle = (0.5 * residue / (h_sub * h_sub) + second[0], second[1])
    keep = (h_middle[0] - 0.5, h_middle[1])
    on_z = plus(gamma, scale(-alpha, keep))
    on_r = plus(scale(-inv, h_upper), scale(-1.0, times(keep, gamma)))
    last = (
        alpha * alpha * qq
        + size(on_z) * zz
        + size(on_r) * rr
        + 2.0
        * (
            conj_times(on_r, times(on_z, rz))[0]
            + alpha * conj_times(on_r, rq)[0]
            + alpha * conj_times(on_z, zq)[0]
        )
    )
    h_last = jnp.sqrt(jnp.maximum(last, 0.0) + EPSILON)
    radius = jnp.sqrt(size(h_first) + h_sub * h_sub)
    cosine = scale(1.0 / radius, h_first)
    sine = h_sub / radius
    upper = plus(conj_times(cosine, h_upper), scale(sine, h_middle))
    lower = plus(times(cosine, h_middle), scale(-sine, h_upper))
    radius_two = jnp.sqrt(size(lower) + h_last * h_last)
    cosine_two = scale(1.0 / radius_two, lower)
    weight_two = scale(-sine * beta / radius_two, (cosine_two[0], -cosine_two[1]))
    goal = scale(beta, (cosine[0], -cosine[1]))
    weight_one = scale(1.0 / radius, plus(goal, scale(-1.0, times(upper, weight_two))))
    on_right = plus(scale(inv, weight_one), times(weight_two, gamma))
    on_image = scale(alpha, weight_two)
    return on_right[0], on_right[1], on_image[0], on_image[1]


def solution(mesh):
    return jax.shard_map(
        local,
        mesh=mesh,
        in_specs=(
            P(None, None, "row"),
            P(None, ("grp", "row", "col"), None, None),
            P(("grp", "row", "col")),
            P(("grp", "row", "col")),
            P(None, "row", None),
            P("row", None),
            P(),
            P("row", None),
            P("row", None),
            P(),
        ),
        out_specs=P(None, None, "row"),
        check_vma=False,
    )
```

```python
import functools

import jax
import jax.numpy as jnp
from jax import lax
from jax.experimental import pallas as pl
from jax.experimental.pallas import tpu as pltpu
from jax.sharding import PartitionSpec as P

REACH = 2
SPAN = 2 * REACH + 1
LANES = 128
EPSILON = 1e-06
GROUP = ("grp", "col")
CODES = 0
PER_ITEM = 5
ITEM_REST = 2 * LANES
PIECES = 4
EVERY = ("grp", "row", "col")

F32 = jnp.float32
BF16 = jnp.bfloat16
SMEM = pl.BlockSpec(memory_space=pltpu.SMEM)
VMEM = pl.BlockSpec(memory_space=pltpu.VMEM)
HBM = pl.BlockSpec(memory_space=pltpu.HBM)
ANY = pl.BlockSpec(memory_space=pl.ANY)


def dot_nn(left, right):
    return lax.dot_general(left, right, (((1,), (0,)), ((), ())), preferred_element_type=F32)


def dot_nt(left, right):
    return lax.dot_general(left, right, (((1,), (1,)), ((), ())), preferred_element_type=F32)


def halves(rows):
    if rows.dtype != F32:
        return rows
    high = rows.astype(BF16)
    return jnp.concatenate([high, (rows - high.astype(F32)).astype(BF16)], axis=0)


def joined(sums, count):
    return sums if sums.shape[0] == count else sums[:count] + sums[count:]


def odd_lanes(shape):
    return lax.rem(lax.broadcasted_iota(jnp.int32, shape, 1), 2) == 1


def twice(value, width):
    rows = value.shape[0]
    parts = []
    for k in range(width // LANES):
        first = (k // 2) * LANES
        part = value[:, first : first + LANES]
        if part.shape[1] < LANES:
            part = jnp.concatenate([part, jnp.zeros((rows, LANES - part.shape[1]), part.dtype)], axis=-1)
        lane = lax.broadcasted_iota(jnp.int32, (rows, LANES), 1)
        parts.append(jnp.take_along_axis(part, lax.div(lane, 2) + (k % 2) * (LANES // 2), axis=1))
    return jnp.concatenate(parts, axis=-1)


def from_left(value):
    return pltpu.roll(value, 1, 1)


def from_right(value):
    return pltpu.roll(value, value.shape[1] - 1, 1)


def item_place(slots, item):
    return CODES + slots + PER_ITEM * item


def window_start(leaf_ref, leaf, width):
    units = leaf_ref.shape[1] // LANES
    before = jnp.int32(0)
    for k in range(units):
        before = before + (leaf_ref[0, k * LANES] < leaf).astype(jnp.int32)
    return jnp.clip(before - 1, 0, units - width)


def window_mask(leaves_ref, leaf, unit, rows, width):
    leaves = jnp.concatenate([leaves_ref[unit + k] for k in range(width)], axis=-1)
    return jnp.broadcast_to(leaves, (rows, width * LANES)) == leaf


def window_copies(exp_ref, unit, window_ref, sem, width):
    coefs = exp_ref.shape[0]
    step = -(-coefs // PIECES)
    copies = []
    for k in range(width):
        for p in range(PIECES):
            part = pl.ds(p * step, min(step, coefs - p * step))
            copies.append(
                pltpu.make_async_copy(exp_ref.at[part, unit + k], window_ref.at[k, part], sem.at[k, p])
            )
    return copies


def clear_rest(window_ref, coefs, width):
    rest = window_ref.shape[1] - coefs
    for k in range(width):
        window_ref[k, pl.ds(coefs, rest)] = jnp.zeros((rest, 2, LANES), BF16)


def multi_rows(fields, width, leaf, unit, leaves_ref, low_ref, window_ref):
    if len(low_ref.shape) == 2:
        first = pl.multiple_of(unit * LANES, LANES)
        rows = low_ref[:, pl.ds(first, width * LANES)]
    else:
        rows = jnp.concatenate([low_ref[unit + k] for k in range(width)], axis=-1)
    mask = window_mask(leaves_ref, leaf, unit, 2 * fields, width)
    rows = halves(jnp.where(mask, rows.astype(F32), 0.0).astype(rows.dtype))
    expansions = jnp.concatenate([as_rows(window_ref.at[k]) for k in range(width)], axis=-1)
    total = joined(dot_nt(rows, expansions), 2 * fields)
    on_real, on_imag = total[:fields], total[fields:]
    odd = odd_lanes(on_real.shape)
    other = jnp.where(odd, from_left(on_imag), from_right(on_imag))
    return jnp.where(odd, -on_real, on_real) - other


def as_rows(ref):
    return ref.reshape(ref.shape[0] * 2, ref.shape[2])[...]


def edge_kernel(row_ref, image_ref, one_ref, two_ref):
    even = lax.rem(row_ref[0], 2) == 0
    if len(image_ref.shape) == 2:
        edge = one_ref.shape[1]
        first, last = image_ref[:, :edge], image_ref[:, image_ref.shape[1] - edge :]
    else:
        edge = one_ref.shape[0]
        first, last = image_ref[:edge], image_ref[image_ref.shape[0] - edge :]
    first, last = first.astype(one_ref.dtype), last.astype(one_ref.dtype)

    @pl.when(even)
    def _():
        one_ref[...], two_ref[...] = first, last

    @pl.when(jnp.logical_not(even))
    def _():
        one_ref[...], two_ref[...] = last, first


def join_kernel(one_ref, two_ref, after_ref, out_ref):
    del after_ref
    edge = one_ref.shape[0]
    out_ref[:edge], out_ref[edge:] = one_ref[...], two_ref[...]


def begin_kernel(
    fields, items, width, send, rows, row_ref, own_ref, pick_hbm, leaf_hbm, leaves_hbm,
    target_hbm, offset_hbm, pairs_hbm, right_hbm, exp_ref,
    plan_ref, out_ref, window_ref, leaves_ref, right_ref,
    pick_ref, leaf_ref, target_ref, offset_ref, pairs_ref, sem, window_sem,
):
    loads = [
        pltpu.make_async_copy(source, place, sem.at[k])
        for k, (source, place) in enumerate(
            (
                (leaf_hbm, leaf_ref),
                (pick_hbm, pick_ref),
                (target_hbm, target_ref),
                (offset_hbm, offset_ref),
                (pairs_hbm, pairs_ref),
                (leaves_hbm, leaves_ref),
                (right_hbm, right_ref),
            )
        )
    ]
    for load in loads:
        load.start()
    for i in range(items):
        clear_rest(window_ref.at[i], exp_ref.shape[0], width)
    slots = pairs_ref.shape[0]
    own = own_ref[0]
    loads[0].wait()
    loads[1].wait()
    row = row_ref[0]

    def partner(i, coming):
        number = own * items + i
        pair, number = lax.div(number, send), lax.rem(number, send)
        other = source_row(row, pair, rows) if coming else target_row(row, pair, rows)
        if coming and own_items_change_cores(rows, items, send):
            number = jnp.where(other == row, 1 - number, number)
        return other, number

    for i in range(items):
        other, number = partner(i, False)
        leaf = pick_ref[other, number, row]
        unit = window_start(leaf_ref, leaf, width)
        place = item_place(slots, i)
        plan_ref[place], plan_ref[place + 1] = leaf, unit
        for copy in window_copies(exp_ref, unit, window_ref.at[i], window_sem.at[i], width):
            copy.start()
    for load in loads[2:]:
        load.wait()
    for s in range(slots):
        plan_ref[CODES + s] = pairs_ref[s]
    for i in range(items):
        place = item_place(slots, i)
        other, number = partner(i, True)
        leaf = target_ref[0, other * send + number]
        plan_ref[place + 2], plan_ref[place + 3] = leaf, window_start(leaf_ref, leaf, width)
        plan_ref[place + 4] = offset_ref[0, other * send + number]
    for i in range(items):
        place = item_place(slots, i)
        leaf, unit = plan_ref[place], plan_ref[place + 1]
        for copy in window_copies(exp_ref, unit, window_ref.at[i], window_sem.at[i], width):
            copy.wait()
        out_ref[i] = multi_rows(fields, width, leaf, unit, leaves_ref, right_ref, window_ref.at[i]).astype(BF16)


def fetch_kernel(items, width, slots, plan_ref, exp_ref, trans_ref, window_ref, moved_ref, trans_buf, sem, trans_sem):
    coefs = trans_ref.shape[3]
    for i in range(items):
        clear_rest(window_ref.at[i], coefs, width)

    def trans_copy(i):
        offset = plan_ref[item_place(slots, i) + 4]
        return pltpu.make_async_copy(trans_ref.at[offset], trans_buf.at[i], trans_sem.at[i])

    def exp_copies(i):
        unit = plan_ref[item_place(slots, i) + 3]
        return window_copies(exp_ref, unit, window_ref.at[i], sem.at[i], width)

    for i in range(items):
        trans_copy(i).start()
        for copy in exp_copies(i):
            copy.start()
    rest = moved_ref.shape[1] - 2 * coefs
    for i in range(items):
        trans_copy(i).wait()
        moved_ref[i, pl.ds(0, 2 * coefs)] = trans_buf[i].reshape(2 * coefs, coefs)
        moved_ref[i, pl.ds(2 * coefs, rest)] = jnp.zeros((rest, coefs), BF16)
        for copy in exp_copies(i):
            copy.wait()


def near_sources(core_ref, row_ref, one_ref, two_ref, here_ref, units, ext):
    edge = (ext.shape[0] - units) // 2
    even = lax.rem(row_ref[0], 2) == 0
    one_at = jnp.where(even, 0, edge + units)
    two_at = jnp.where(even, edge + units, 0)
    if len(here_ref.shape) == 2:
        for k in range(edge):
            lanes = slice(k * LANES, (k + 1) * LANES)
            ext[one_at + k] = one_ref[:, lanes].astype(ext.dtype)
            ext[two_at + k] = two_ref[:, lanes].astype(ext.dtype)
        for k in range(units):
            ext[edge + k] = here_ref[:, k * LANES : (k + 1) * LANES]
        return
    half = edge // 2
    for ref, core in ((one_ref, core_ref[0]), (two_ref, 1 - core_ref[0])):
        for k in range(half):
            ext[one_at + 2 * k + core] = ref[k]
            ext[two_at + 2 * k + core] = ref[half + k]
    ext[edge : edge + units] = here_ref[...]


def part(total, core, keep_ref, give_ref):
    for k in range(keep_ref.shape[0]):
        keep_ref[k] = total[2 * k + core].astype(keep_ref.dtype)
        give_ref[k] = total[2 * k + 1 - core].astype(give_ref.dtype)


def near_kernel(
    fields, core_ref, row_ref, count_ref, plan_ref, one_ref, two_ref, here_ref, tiles_ref, out_ref, ext
):
    near_sources(core_ref, row_ref, one_ref, two_ref, here_ref, out_ref.shape[0], ext)
    out_ref[...] = jnp.zeros_like(out_ref)
    near_slots(fields, count_ref, plan_ref, tiles_ref, out_ref, ext)


def last_near_kernel(
    fields, core_ref, row_ref, count_ref, plan_ref, one_ref, two_ref, here_ref, tiles_ref, image_ref,
    keep_ref, give_ref, ext, total,
):
    near_sources(core_ref, row_ref, one_ref, two_ref, here_ref, total.shape[0], ext)
    total[...] = jnp.zeros_like(total)
    items, width = image_ref.shape[:2]
    for i in range(items):
        unit = plan_ref[item_place(tiles_ref.shape[1], i) + 3]
        for k in range(width):
            total[unit + k] += image_ref[i, k]
    near_slots(fields, count_ref, plan_ref, tiles_ref, total, ext)
    part(total, core_ref[0], keep_ref, give_ref)


def near_slots(fields, count_ref, plan_ref, tiles_ref, out_ref, ext):
    slots, tile = tiles_ref.shape[1], tiles_ref.shape[2]
    per = tile // LANES
    for s in range(slots):
        code = plan_ref[CODES + s]
        target = lax.div(code, SPAN)
        source = target + lax.rem(code, SPAN)
        rows = halves(jnp.concatenate([ext[source * per + k] for k in range(per)], axis=-1))
        on_real = joined(dot_nt(rows, tiles_ref[0, s]), 2 * fields)
        on_imag = joined(dot_nt(rows, tiles_ref[1, s]), 2 * fields)
        value = jnp.concatenate(
            [on_real[:fields] - on_imag[fields:], on_real[fields:] + on_imag[:fields]], axis=0
        )
        value = jnp.where(s < count_ref[0], value, 0.0)
        for k in range(per):
            out_ref[target * per + k] += value[:, k * LANES : (k + 1) * LANES]


def far_kernel(
    fields, items, width, slots, core_ref, plan_ref, leaves_ref, partial_ref, item_ref, trans_ref, window_ref,
    keep_ref, give_ref, total,
):
    total[...] = partial_ref[...]

    def add(i, unit, image):
        for k in range(width):
            total[unit + k] += image[:, k * LANES : (k + 1) * LANES]

    far_images(fields, items, width, slots, plan_ref, leaves_ref, item_ref, trans_ref, window_ref, add)
    part(total, core_ref[0], keep_ref, give_ref)


def first_far_kernel(
    fields, items, width, slots, plan_ref, leaves_ref, item_ref, trans_ref, window_ref, image_ref
):
    def store(i, unit, image):
        for k in range(width):
            image_ref[i, k] = image[:, k * LANES : (k + 1) * LANES]

    far_images(fields, items, width, slots, plan_ref, leaves_ref, item_ref, trans_ref, window_ref, store)


def far_images(fields, items, width, slots, plan_ref, leaves_ref, item_ref, trans_ref, window_ref, give):
    for i in range(items):
        plain = item_ref[i, :, : trans_ref.shape[1]].astype(F32)
        odd = odd_lanes(plain.shape)
        turned = jnp.where(odd, from_left(plain), -from_right(plain))
        rows = jnp.concatenate([plain, turned], axis=0).astype(BF16)
        local_field = dot_nn(rows, trans_ref[i]).astype(BF16).astype(F32)
        local_field = twice(local_field, plain.shape[1])
        local_real, local_imag = local_field[:fields], local_field[fields:]
        rows = jnp.concatenate(
            [jnp.where(odd, -local_imag, local_real), jnp.where(odd, local_real, local_imag)], axis=0
        ).astype(BF16)
        expansions = jnp.concatenate([as_rows(window_ref.at[i, k]) for k in range(width)], axis=-1)
        place = item_place(slots, i)
        leaf, unit = plan_ref[place + 2], plan_ref[place + 3]
        mask = window_mask(leaves_ref, leaf, unit, 2 * fields, width)
        image = jnp.where(mask, dot_nn(rows, expansions), 0.0)
        give(i, unit, image)


def pair_kernel(keep_ref, got_ref, out_ref):
    out_ref[...] = (keep_ref[...].astype(F32) + got_ref[...].astype(F32)).astype(out_ref.dtype)


def tree_sum(values):
    while len(values) > 1:
        values = [values[k] + values[k + 1] for k in range(0, len(values), 2)]
    return values[0]


def by_step(parts):
    return [parts[0], *reversed(parts[1:])]


def close_kernel(*refs):
    refs[-1][...] = tree_sum([ref[...].astype(F32) for ref in by_step(refs[:-1])])


def assemble_kernel(
    fields, items, width, slots, core_ref, plan_ref, leaves_ref, mine_ref, theirs_ref, window_ref,
    out_ref, low_ref, made_ref,
):
    core = core_ref[0]
    for k in range(mine_ref.shape[0]):
        for ref, unit in ((mine_ref, 2 * k + core), (theirs_ref, 2 * k + 1 - core)):
            out_ref[unit] = ref[k]
            low_ref[unit] = ref[k].astype(BF16)
    for i in range(items):
        place = item_place(slots, i)
        made = multi_rows(
            fields, width, plan_ref[place], plan_ref[place + 1], leaves_ref, low_ref, window_ref.at[i]
        )
        made_ref[i, :, : made.shape[1]] = made.astype(BF16)


def flat_lines(totals, fields):
    per = LANES // fields
    lane = lax.broadcasted_iota(jnp.int32, (fields, LANES), 1)
    field = lax.broadcasted_iota(jnp.int32, (fields, LANES), 0)
    lines = []
    for first in range(0, len(totals), per):
        line = jnp.zeros((fields, LANES), F32)
        for k, total in enumerate(totals[first : first + per]):
            line = jnp.where(lane == field + k * fields, jnp.sum(total, axis=1, keepdims=True), line)
        lines.append(jnp.sum(line, axis=0, keepdims=True))
    return jnp.concatenate(lines, axis=0)


def columns_of(lines, count, fields):
    per = LANES // fields
    columns = []
    for k in range(lines.shape[0]):
        square = jnp.transpose(jnp.broadcast_to(lines[k : k + 1], (LANES, LANES)))
        columns += [square[j * fields : (j + 1) * fields, :1] for j in range(per)]
    return columns[:count]


def gram_kernel(fields, core_ref, right_ref, image_ref, *refs):
    *parts, out_ref = refs
    totals = None
    for k in range(parts[0].shape[0]):
        unit = 2 * k + core_ref[0]
        r = right_ref[:, pl.ds(pl.multiple_of(unit * LANES, LANES), LANES)]
        z = image_ref[unit]
        q = tree_sum([part[k].astype(F32) for part in by_step(parts)])
        (rr, ri), (zr, zi), (qr, qi) = [(v[:fields], v[fields:]) for v in (r, z, q)]
        products = [
            rr * rr + ri * ri,
            rr * zr + ri * zi,
            rr * zi - ri * zr,
            zr * zr + zi * zi,
            rr * qr + ri * qi,
            rr * qi - ri * qr,
            zr * qr + zi * qi,
            zr * qi - zi * qr,
            qr * qr + qi * qi,
        ]
        totals = products if totals is None else [t + p for t, p in zip(totals, products)]
    out_ref[...] = jnp.broadcast_to(flat_lines(totals, fields)[None], out_ref.shape)


def final_kernel(fields, sums_ref, right_ref, image_ref, out_ref):
    units = image_ref.shape[0]
    sums = columns_of(jnp.sum(sums_ref[...], axis=0), 9, fields)
    a_real, a_imag, b_real, b_imag = [
        jnp.broadcast_to(value, (fields, LANES)) for value in krylov_coefficients(sums)
    ]
    for k in range(units):
        lanes = slice(k * LANES, (k + 1) * LANES)
        r_real, r_imag = right_ref[:fields, lanes], right_ref[fields:, lanes]
        z_real, z_imag = image_ref[k, :fields], image_ref[k, fields:]
        out_ref[:fields, lanes] = a_real * r_real - a_imag * r_imag + b_real * z_real - b_imag * z_imag
        out_ref[fields:, lanes] = a_real * r_imag + a_imag * r_real + b_real * z_imag + b_imag * z_real


def params(mebibytes=16):
    return pltpu.CompilerParams(vmem_limit_bytes=mebibytes * 1024 * 1024)


def is_power(count):
    return count & (count - 1) == 0


def reversed_bits(value, count):
    bits = count.bit_length() - 1
    return sum(((value >> k) & 1) << (bits - 1 - k) for k in range(bits))


def target_row(row, pair, rows):
    if not is_power(rows):
        return (pair - row + rows) % rows
    return pair ^ reversed_bits(row, rows)


def source_row(row, pair, rows):
    if not is_power(rows):
        return (pair - row + rows) % rows
    return reversed_bits(pair ^ row, rows)


def own_items_change_cores(rows, items, send):
    return items == 1 and send == 2


def item_route(rows, group, columns, send):
    items = rows * send // group

    def flat(r, g):
        return (g // columns * rows + r) * columns + g % columns

    def target(r, g, pair):
        d = target_row(r, pair, rows)
        return flat(d, g ^ 1 if d == r and own_items_change_cores(rows, items, send) else g)

    assert items * group == rows * send and (items % send == 0 or send % items == 0)
    routes = []
    for first in range(0, items, send):
        pairs = [(g * items + first) // send for g in range(group)]
        routes.append([(flat(r, g), target(r, g, pairs[g])) for r in range(rows) for g in range(group)])
    return items, routes


def local(
    right_side,
    near_tiles,
    tile_pairs,
    tile_count,
    panel_expansions,
    leaf_of_panel,
    far_pick,
    far_target,
    far_offset,
    translations,
):
    fields, panels = right_side.shape[1:]
    coefs = panel_expansions.shape[2]
    tile = near_tiles.shape[2]
    send = far_pick.shape[2]
    rows = lax.axis_size("row")
    group = lax.axis_size("grp") * lax.axis_size("col")
    row_here = lax.axis_index("row")
    own = lax.axis_index("grp") * lax.axis_size("col") + lax.axis_index("col")
    both = 2 * fields
    units = panels // LANES
    edge = REACH * tile
    edge_units = edge // LANES
    width = tile // LANES + 1
    items, routes = item_route(rows, group, lax.axis_size("col"), send)

    assert rows % 2 == 0
    neighbours = [[(r - 1 + 2 * (r % 2)) % rows for r in range(rows)], [r + 1 - 2 * (r % 2) for r in range(rows)]]
    own_place, row_place = own.reshape(1), row_here.reshape(1)
    core_place = lax.rem(own, 2).reshape(1)
    slots = near_tiles.shape[1]
    pad_coefs = -(-coefs // 8) * 8
    chips = group // 2
    assert group == 2 * chips and chips & (chips - 1) == 0 and LANES % fields == 0
    window_shape = jax.ShapeDtypeStruct((items, width, pad_coefs, 2, LANES), BF16)
    item_shape = jax.ShapeDtypeStruct((items, fields, 2 * pad_coefs), BF16)
    half_units = (units // 2, both, LANES)
    assert units % 2 == 0 and edge_units % 2 == 0

    def in_hbm(value):
        return pltpu.with_memory_space_constraint(value, pltpu.HBM)

    leaves = leaf_of_panel.reshape(units, 1, LANES)
    expansions = panel_expansions.transpose(2, 0, 1).reshape(coefs, 2, units, LANES).transpose(0, 2, 1, 3)
    expansions = in_hbm(expansions)
    moves = in_hbm(translations.transpose(0, 2, 1, 3))
    picks = far_pick.transpose(0, 2, 1)

    plan, made, windows, leaves, right = pl.pallas_call(
        functools.partial(begin_kernel, fields, items, width, send, rows),
        out_shape=(
            pltpu.SMEM((item_place(slots, items),), jnp.int32),
            item_shape,
            pltpu.VMEM(window_shape.shape, BF16),
            jax.ShapeDtypeStruct(leaves.shape, jnp.int32),
            jax.ShapeDtypeStruct((both, panels), F32),
        ),
        in_specs=[SMEM] * 2 + [HBM] * 8,
        out_specs=(SMEM,) + (VMEM,) * 4,
        scratch_shapes=[
            pltpu.SMEM(value.shape, jnp.int32)
            for value in (picks, leaf_of_panel, far_target, far_offset, tile_pairs)
        ]
        + [
            pltpu.SemaphoreType.DMA((7,)),
            pltpu.SemaphoreType.DMA((items, width, PIECES)),
        ],
        compiler_params=params(),
        name="begin",
    )(
        row_place,
        own_place,
        in_hbm(picks),
        in_hbm(leaf_of_panel),
        in_hbm(leaves),
        in_hbm(far_target),
        in_hbm(far_offset),
        in_hbm(tile_pairs),
        in_hbm(right_side.reshape(both, panels)),
        expansions,
    )

    def exchanged(made):
        parts = [
            lax.ppermute(made[k * send : k * send + min(send, items)], EVERY, route) for k, route in enumerate(routes)
        ]
        return parts[0] if len(parts) == 1 else jnp.concatenate(parts)

    def from_neighbours(image):
        edge_shape = (both, edge) if image.ndim == 2 else (edge_units // 2, both, LANES)
        one, two = pl.pallas_call(
            edge_kernel,
            out_shape=(jax.ShapeDtypeStruct(edge_shape, BF16),) * 2,
            in_specs=[SMEM, VMEM],
            out_specs=(VMEM, VMEM),
            compiler_params=params(),
            name="edges",
        )(row_place, image)
        return [
            lax.ppermute(value, "row", list(enumerate(targets))) for value, targets in zip((one, two), neighbours)
        ]

    image_shape = jax.ShapeDtypeStruct((units, both, LANES), F32)
    target_windows, moved = pl.pallas_call(
        functools.partial(fetch_kernel, items, width, slots),
        out_shape=(
            pltpu.VMEM(window_shape.shape, BF16),
            pltpu.VMEM((items, 2 * pad_coefs, coefs), BF16),
        ),
        in_specs=[SMEM, HBM, HBM],
        out_specs=(VMEM, VMEM),
        scratch_shapes=[
            pltpu.VMEM((items, coefs, 2, coefs), BF16),
            pltpu.SemaphoreType.DMA((items, width, PIECES)),
            pltpu.SemaphoreType.DMA((items,)),
        ],
        compiler_params=params(24),
        cost_estimate=pl.CostEstimate(flops=0, bytes_accessed=6 * window_shape.size, transcendentals=0),
        name="fetch",
    )(plan, expansions, moves)

    def swapped(value, step):
        return lax.ppermute(value, GROUP, [(g, g ^ step) for g in range(group)])

    def near(one, two, low):
        return pl.pallas_call(
            functools.partial(near_kernel, fields),
            out_shape=image_shape,
            in_specs=[SMEM] * 4 + [VMEM] * 4,
            out_specs=VMEM,
            scratch_shapes=[pltpu.VMEM((units + 2 * edge_units, both, LANES), low.dtype)],
            compiler_params=params(),
            cost_estimate=pl.CostEstimate(
                flops=8 * fields * near_tiles.size // 2, bytes_accessed=2 * near_tiles.size, transcendentals=0
            ),
            name="near",
        )(core_place, row_place, tile_count, plan, one, two, low, near_tiles)

    def core_parts(partial, taken):
        half_shape = jax.ShapeDtypeStruct(half_units, F32)
        keep, give = pl.pallas_call(
            functools.partial(far_kernel, fields, items, width, slots),
            out_shape=(half_shape, half_shape),
            in_specs=[SMEM, SMEM] + [VMEM] * 5,
            out_specs=(VMEM, VMEM),
            scratch_shapes=[pltpu.VMEM(image_shape.shape, F32)],
            compiler_params=params(),
            name="far",
        )(core_place, plan, leaves, partial, taken, moved, target_windows)
        return keep, swapped(give, 1)

    def first_far(taken):
        return pl.pallas_call(
            functools.partial(first_far_kernel, fields, items, width, slots),
            out_shape=jax.ShapeDtypeStruct((items, width, both, LANES), F32),
            in_specs=[SMEM] + [VMEM] * 4,
            out_specs=VMEM,
            compiler_params=params(),
            name="first_far",
        )(plan, leaves, taken, moved, target_windows)

    def last_core_parts(one, two, low, image):
        half_shape = jax.ShapeDtypeStruct(half_units, BF16)
        keep, give = pl.pallas_call(
            functools.partial(last_near_kernel, fields),
            out_shape=(half_shape, half_shape),
            in_specs=[SMEM] * 4 + [VMEM] * 5,
            out_specs=(VMEM, VMEM),
            scratch_shapes=[
                pltpu.VMEM((units + 2 * edge_units, both, LANES), low.dtype),
                pltpu.VMEM(image_shape.shape, F32),
            ],
            compiler_params=params(),
            name="last_near",
        )(core_place, row_place, tile_count, plan, one, two, low, near_tiles, image)
        return keep, swapped(give, 1)

    def pair_sums(keep, got):
        pair = pl.pallas_call(
            pair_kernel,
            out_shape=jax.ShapeDtypeStruct(keep.shape, BF16),
            in_specs=[VMEM, VMEM],
            out_specs=VMEM,
            compiler_params=params(),
            name="pair",
        )(keep, got)
        arrived = {step: swapped(pair, 2 * step) for step in range(chips - 1, 0, -1)}
        return [pair] + list(arrived.values())

    def half_sum(parts):
        return pl.pallas_call(
            close_kernel,
            out_shape=jax.ShapeDtypeStruct(half_units, F32),
            in_specs=[VMEM] * chips,
            out_specs=VMEM,
            compiler_params=params(),
            name="close",
        )(*parts)

    def whole(mine, theirs):
        return pl.pallas_call(
            functools.partial(assemble_kernel, fields, items, width, slots),
            out_shape=(
                image_shape,
                jax.ShapeDtypeStruct(image_shape.shape, BF16),
                jax.ShapeDtypeStruct((items, fields, 2 * pad_coefs + ITEM_REST), BF16),
            ),
            in_specs=[SMEM, SMEM] + [VMEM] * 4,
            out_specs=(VMEM,) * 3,
            compiler_params=params(),
            name="assemble",
        )(core_place, plan, leaves, mine, theirs, windows)

    def joined_edges(one, two, made):
        return pl.pallas_call(
            join_kernel,
            out_shape=jax.ShapeDtypeStruct((edge_units, both, LANES), BF16),
            in_specs=[VMEM, VMEM, ANY],
            out_specs=VMEM,
            compiler_params=params(),
            name="join",
        )(one, two, made)

    partial = near(*from_neighbours(right), right)
    mine = half_sum(pair_sums(*core_parts(partial, exchanged(made))))
    theirs = swapped(mine, 1)
    one, two = from_neighbours(mine)
    z_all, z_low, made = whole(mine, theirs)
    edges = joined_edges(one, two, made)
    image = first_far(exchanged(made))
    parts = pair_sums(*last_core_parts(edges, swapped(edges, 1), z_low, image))

    lines = pl.pallas_call(
        functools.partial(gram_kernel, fields),
        out_shape=jax.ShapeDtypeStruct((2 * rows, -(-9 * fields // LANES), LANES), F32),
        in_specs=[SMEM] + [VMEM] * (2 + chips),
        out_specs=VMEM,
        compiler_params=params(),
        name="gram",
    )(core_place, right, z_all, *parts)
    columns = lax.axis_size("col")
    same_chip = [
        [((g + k) // columns * rows + r) * columns + (g + k) % columns for r in range(rows) for k in range(2)]
        for g in range(0, group, 2)
    ]
    sums = lax.all_to_all(lines, EVERY, 0, 0, axis_index_groups=same_chip, tiled=True)
    out = pl.pallas_call(
        functools.partial(final_kernel, fields),
        out_shape=jax.ShapeDtypeStruct((both, panels), F32),
        in_specs=[VMEM] * 3,
        out_specs=VMEM,
        compiler_params=params(),
        name="combine",
    )(sums, right, z_all)
    return out.reshape(right_side.shape)


def krylov_coefficients(sums):
    rr, rz_real, rz_imag, zz, rq_real, rq_imag, zq_real, zq_imag, qq = sums

    def times(left, right):
        return left[0] * right[0] - left[1] * right[1], left[0] * right[1] + left[1] * right[0]

    def conj_times(left, right):
        return left[0] * right[0] + left[1] * right[1], left[0] * right[1] - left[1] * right[0]

    def scale(factor, value):
        return factor * value[0], factor * value[1]

    def plus(*values):
        return sum(v[0] for v in values), sum(v[1] for v in values)

    def size(value):
        return value[0] * value[0] + value[1] * value[1]

    rz, rq, zq = (rz_real, rz_imag), (rq_real, rq_imag), (zq_real, zq_imag)
    beta = jnp.sqrt(rr + EPSILON)
    inv = 1.0 / beta
    norm_one = rr * inv * inv
    product = scale(inv * inv, rz)
    h_first = (0.5 * norm_one + product[0], product[1])
    shift = (h_first[0] - 0.5, h_first[1])
    residue = zz * inv * inv - 2.0 * conj_times(shift, product)[0] + size(shift) * norm_one
    residue = jnp.maximum(residue, 0.0)
    h_sub = jnp.sqrt(residue + EPSILON)
    alpha = inv / h_sub
    gamma = scale(-alpha, shift)
    h_upper = scale(
        inv,
        plus(
            scale(0.5, plus(scale(alpha, rz), scale(rr, gamma))), scale(alpha, rq), times(gamma, rz)
        ),
    )
    second = plus(
        scale(alpha * alpha, zq),
        scale(alpha * zz, gamma),
        scale(alpha, conj_times(gamma, rq)),
        scale(size(gamma), rz),
    )
    h_middle = (0.5 * residue / (h_sub * h_sub) + second[0], second[1])
    keep = (h_middle[0] - 0.5, h_middle[1])
    on_z = plus(gamma, scale(-alpha, keep))
    on_r = plus(scale(-inv, h_upper), scale(-1.0, times(keep, gamma)))
    last = (
        alpha * alpha * qq
        + size(on_z) * zz
        + size(on_r) * rr
        + 2.0
        * (
            conj_times(on_r, times(on_z, rz))[0]
            + alpha * conj_times(on_r, rq)[0]
            + alpha * conj_times(on_z, zq)[0]
        )
    )
    h_last = jnp.sqrt(jnp.maximum(last, 0.0) + EPSILON)
    radius = jnp.sqrt(size(h_first) + h_sub * h_sub)
    cosine = scale(1.0 / radius, h_first)
    sine = h_sub / radius
    upper = plus(conj_times(cosine, h_upper), scale(sine, h_middle))
    lower = plus(times(cosine, h_middle), scale(-sine, h_upper))
    radius_two = jnp.sqrt(size(lower) + h_last * h_last)
    cosine_two = scale(1.0 / radius_two, lower)
    weight_two = scale(-sine * beta / radius_two, (cosine_two[0], -cosine_two[1]))
    goal = scale(beta, (cosine[0], -cosine[1]))
    weight_one = scale(1.0 / radius, plus(goal, scale(-1.0, times(upper, weight_two))))
    on_right = plus(scale(inv, weight_one), times(weight_two, gamma))
    on_image = scale(alpha, weight_two)
    return on_right[0], on_right[1], on_image[0], on_image[1]


def solution(mesh):
    return jax.shard_map(
        local,
        mesh=mesh,
        in_specs=(
            P(None, None, "row"),
            P(None, ("grp", "row", "col"), None, None),
            P(("grp", "row", "col")),
            P(("grp", "row", "col")),
            P(None, "row", None),
            P("row", None),
            P(),
            P("row", None),
            P("row", None),
            P(),
        ),
        out_specs=P(None, None, "row"),
        check_vma=False,
    )
```

```python
import functools

import jax
import jax.numpy as jnp
from jax import lax
from jax.experimental import pallas as pl
from jax.experimental.pallas import tpu as pltpu
from jax.sharding import PartitionSpec as P

REACH = 2
SPAN = 2 * REACH + 1
LANES = 128
EPSILON = 1e-06
GROUP = ("grp", "col")
CODES = 0
PER_ITEM = 5
ITEM_REST = LANES
PIECES = 4
EVERY = ("grp", "row", "col")

F32 = jnp.float32
BF16 = jnp.bfloat16
SMEM = pl.BlockSpec(memory_space=pltpu.SMEM)
VMEM = pl.BlockSpec(memory_space=pltpu.VMEM)
HBM = pl.BlockSpec(memory_space=pltpu.HBM)
ANY = pl.BlockSpec(memory_space=pl.ANY)


def dot_nn(left, right):
    return lax.dot_general(left, right, (((1,), (0,)), ((), ())), preferred_element_type=F32)


def dot_nt(left, right):
    return lax.dot_general(left, right, (((1,), (1,)), ((), ())), preferred_element_type=F32)


def halves(rows):
    if rows.dtype != F32:
        return rows
    high = rows.astype(BF16)
    return jnp.concatenate([high, (rows - high.astype(F32)).astype(BF16)], axis=0)


def joined(sums, count):
    return sums if sums.shape[0] == count else sums[:count] + sums[count:]


def odd_lanes(shape):
    return lax.rem(lax.broadcasted_iota(jnp.int32, shape, 1), 2) == 1


def twice(value, width):
    rows = value.shape[0]
    parts = []
    for k in range(width // LANES):
        first = (k // 2) * LANES
        part = value[:, first : first + LANES]
        if part.shape[1] < LANES:
            part = jnp.concatenate([part, jnp.zeros((rows, LANES - part.shape[1]), part.dtype)], axis=-1)
        lane = lax.broadcasted_iota(jnp.int32, (rows, LANES), 1)
        parts.append(jnp.take_along_axis(part, lax.div(lane, 2) + (k % 2) * (LANES // 2), axis=1))
    return jnp.concatenate(parts, axis=-1)


def from_left(value):
    return pltpu.roll(value, 1, 1)


def from_right(value):
    return pltpu.roll(value, value.shape[1] - 1, 1)


def item_place(slots, item):
    return CODES + slots + PER_ITEM * item


def window_start(leaf_ref, leaf, width):
    units = leaf_ref.shape[1] // LANES
    before = jnp.int32(0)
    for k in range(units):
        before = before + (leaf_ref[0, k * LANES] < leaf).astype(jnp.int32)
    return jnp.clip(before - 1, 0, units - width)


def window_mask(leaves_ref, leaf, unit, rows, width):
    leaves = jnp.concatenate([leaves_ref[unit + k] for k in range(width)], axis=-1)
    return jnp.broadcast_to(leaves, (rows, width * LANES)) == leaf


def window_copies(exp_ref, unit, window_ref, sem, width):
    coefs = exp_ref.shape[0]
    step = -(-coefs // PIECES)
    copies = []
    for k in range(width):
        for p in range(PIECES):
            part = pl.ds(p * step, min(step, coefs - p * step))
            copies.append(
                pltpu.make_async_copy(exp_ref.at[part, unit + k], window_ref.at[k, part], sem.at[k, p])
            )
    return copies


def clear_rest(window_ref, coefs, width):
    rest = window_ref.shape[1] - coefs
    for k in range(width):
        window_ref[k, pl.ds(coefs, rest)] = jnp.zeros((rest, 2, LANES), BF16)


def multi_rows(fields, width, leaf, unit, leaves_ref, low_ref, window_ref):
    if len(low_ref.shape) == 2:
        first = pl.multiple_of(unit * LANES, LANES)
        rows = low_ref[:, pl.ds(first, width * LANES)]
    else:
        rows = jnp.concatenate([low_ref[unit + k] for k in range(width)], axis=-1)
    mask = window_mask(leaves_ref, leaf, unit, 2 * fields, width)
    rows = halves(jnp.where(mask, rows.astype(F32), 0.0).astype(rows.dtype))
    expansions = jnp.concatenate([as_rows(window_ref.at[k]) for k in range(width)], axis=-1)
    total = joined(dot_nt(rows, expansions), 2 * fields)
    on_real, on_imag = total[:fields], total[fields:]
    odd = odd_lanes(on_real.shape)
    other = jnp.where(odd, from_left(on_imag), from_right(on_imag))
    return jnp.where(odd, -on_real, on_real) - other


def as_rows(ref):
    return ref.reshape(ref.shape[0] * 2, ref.shape[2])[...]


def edge_kernel(row_ref, image_ref, one_ref, two_ref):
    even = lax.rem(row_ref[0], 2) == 0
    if len(image_ref.shape) == 2:
        edge = one_ref.shape[1]
        first, last = image_ref[:, :edge], image_ref[:, image_ref.shape[1] - edge :]
    else:
        edge = one_ref.shape[0]
        first, last = image_ref[:edge], image_ref[image_ref.shape[0] - edge :]
    first, last = first.astype(one_ref.dtype), last.astype(one_ref.dtype)

    @pl.when(even)
    def _():
        one_ref[...], two_ref[...] = first, last

    @pl.when(jnp.logical_not(even))
    def _():
        one_ref[...], two_ref[...] = last, first


def join_kernel(one_ref, two_ref, after_ref, out_ref):
    del after_ref
    edge = one_ref.shape[0]
    out_ref[:edge], out_ref[edge:] = one_ref[...], two_ref[...]


def begin_kernel(
    fields, items, width, send, rows, row_ref, own_ref, pick_hbm, leaf_hbm, leaves_hbm,
    target_hbm, offset_hbm, pairs_hbm, right_hbm, exp_ref,
    plan_ref, out_ref, window_ref, leaves_ref, right_ref,
    pick_ref, leaf_ref, target_ref, offset_ref, pairs_ref, sem, window_sem,
):
    loads = [
        pltpu.make_async_copy(source, place, sem.at[k])
        for k, (source, place) in enumerate(
            (
                (leaf_hbm, leaf_ref),
                (pick_hbm, pick_ref),
                (target_hbm, target_ref),
                (offset_hbm, offset_ref),
                (pairs_hbm, pairs_ref),
                (leaves_hbm, leaves_ref),
                (right_hbm, right_ref),
            )
        )
    ]
    for load in loads:
        load.start()
    for i in range(items):
        clear_rest(window_ref.at[i], exp_ref.shape[0], width)
    slots = pairs_ref.shape[0]
    own = own_ref[0]
    loads[0].wait()
    loads[1].wait()
    row = row_ref[0]

    def partner(i, coming):
        number = own * items + i
        pair, number = lax.div(number, send), lax.rem(number, send)
        other = source_row(row, pair, rows) if coming else target_row(row, pair, rows)
        if coming and own_items_change_cores(rows, items, send):
            number = jnp.where(other == row, 1 - number, number)
        return other, number

    for i in range(items):
        other, number = partner(i, False)
        leaf = pick_ref[other, number, row]
        unit = window_start(leaf_ref, leaf, width)
        place = item_place(slots, i)
        plan_ref[place], plan_ref[place + 1] = leaf, unit
        for copy in window_copies(exp_ref, unit, window_ref.at[i], window_sem.at[i], width):
            copy.start()
    for load in loads[2:]:
        load.wait()
    for s in range(slots):
        plan_ref[CODES + s] = pairs_ref[s]
    for i in range(items):
        place = item_place(slots, i)
        other, number = partner(i, True)
        leaf = target_ref[0, other * send + number]
        plan_ref[place + 2], plan_ref[place + 3] = leaf, window_start(leaf_ref, leaf, width)
        plan_ref[place + 4] = offset_ref[0, other * send + number]
    for i in range(items):
        place = item_place(slots, i)
        leaf, unit = plan_ref[place], plan_ref[place + 1]
        for copy in window_copies(exp_ref, unit, window_ref.at[i], window_sem.at[i], width):
            copy.wait()
        out_ref[i] = multi_rows(fields, width, leaf, unit, leaves_ref, right_ref, window_ref.at[i]).astype(BF16)


def fetch_kernel(items, width, slots, plan_ref, exp_ref, trans_ref, window_ref, moved_ref, trans_buf, sem, trans_sem):
    coefs = trans_ref.shape[3]
    for i in range(items):
        clear_rest(window_ref.at[i], coefs, width)

    def trans_copy(i):
        offset = plan_ref[item_place(slots, i) + 4]
        return pltpu.make_async_copy(trans_ref.at[offset], trans_buf.at[i], trans_sem.at[i])

    def exp_copies(i):
        unit = plan_ref[item_place(slots, i) + 3]
        return window_copies(exp_ref, unit, window_ref.at[i], sem.at[i], width)

    for i in range(items):
        trans_copy(i).start()
        for copy in exp_copies(i):
            copy.start()
    rest = moved_ref.shape[1] - 2 * coefs
    for i in range(items):
        trans_copy(i).wait()
        moved_ref[i, pl.ds(0, 2 * coefs)] = trans_buf[i].reshape(2 * coefs, coefs)
        moved_ref[i, pl.ds(2 * coefs, rest)] = jnp.zeros((rest, coefs), BF16)
        for copy in exp_copies(i):
            copy.wait()


def near_sources(core_ref, row_ref, one_ref, two_ref, here_ref, units, ext):
    edge = (ext.shape[0] - units) // 2
    even = lax.rem(row_ref[0], 2) == 0
    one_at = jnp.where(even, 0, edge + units)
    two_at = jnp.where(even, edge + units, 0)
    if len(here_ref.shape) == 2:
        for k in range(edge):
            lanes = slice(k * LANES, (k + 1) * LANES)
            ext[one_at + k] = one_ref[:, lanes].astype(ext.dtype)
            ext[two_at + k] = two_ref[:, lanes].astype(ext.dtype)
        for k in range(units):
            ext[edge + k] = here_ref[:, k * LANES : (k + 1) * LANES]
        return
    half = edge // 2
    for ref, core in ((one_ref, core_ref[0]), (two_ref, 1 - core_ref[0])):
        for k in range(half):
            ext[one_at + 2 * k + core] = ref[k]
            ext[two_at + 2 * k + core] = ref[half + k]
    ext[edge : edge + units] = here_ref[...]


def part(total, core, keep_ref, give_ref):
    for k in range(keep_ref.shape[0]):
        keep_ref[k] = total[2 * k + core].astype(keep_ref.dtype)
        give_ref[k] = total[2 * k + 1 - core].astype(give_ref.dtype)


def near_kernel(
    fields, core_ref, row_ref, count_ref, plan_ref, one_ref, two_ref, here_ref, tiles_ref, out_ref, ext
):
    near_sources(core_ref, row_ref, one_ref, two_ref, here_ref, out_ref.shape[0], ext)
    out_ref[...] = jnp.zeros_like(out_ref)
    near_slots(fields, count_ref, plan_ref, tiles_ref, out_ref, ext)


def last_near_kernel(
    fields, core_ref, row_ref, count_ref, plan_ref, one_ref, two_ref, here_ref, tiles_ref, image_ref,
    keep_ref, give_ref, ext, total,
):
    near_sources(core_ref, row_ref, one_ref, two_ref, here_ref, total.shape[0], ext)
    total[...] = jnp.zeros_like(total)
    items, width = image_ref.shape[:2]
    for i in range(items):
        unit = plan_ref[item_place(tiles_ref.shape[1], i) + 3]
        for k in range(width):
            total[unit + k] += image_ref[i, k]
    near_slots(fields, count_ref, plan_ref, tiles_ref, total, ext)
    part(total, core_ref[0], keep_ref, give_ref)


def near_slots(fields, count_ref, plan_ref, tiles_ref, out_ref, ext):
    slots, tile = tiles_ref.shape[1], tiles_ref.shape[2]
    per = tile // LANES
    for s in range(slots):
        code = plan_ref[CODES + s]
        target = lax.div(code, SPAN)
        source = target + lax.rem(code, SPAN)
        rows = halves(jnp.concatenate([ext[source * per + k] for k in range(per)], axis=-1))
        on_real = joined(dot_nt(rows, tiles_ref[0, s]), 2 * fields)
        on_imag = joined(dot_nt(rows, tiles_ref[1, s]), 2 * fields)
        value = jnp.concatenate(
            [on_real[:fields] - on_imag[fields:], on_real[fields:] + on_imag[:fields]], axis=0
        )
        value = jnp.where(s < count_ref[0], value, 0.0)
        for k in range(per):
            out_ref[target * per + k] += value[:, k * LANES : (k + 1) * LANES]


def far_kernel(
    fields, items, width, slots, core_ref, plan_ref, leaves_ref, partial_ref, item_ref, trans_ref, window_ref,
    keep_ref, give_ref, total,
):
    total[...] = partial_ref[...]

    def add(i, unit, image):
        for k in range(width):
            total[unit + k] += image[:, k * LANES : (k + 1) * LANES]

    far_images(fields, items, width, slots, plan_ref, leaves_ref, item_ref, trans_ref, window_ref, add)
    part(total, core_ref[0], keep_ref, give_ref)


def first_far_kernel(
    fields, items, width, slots, plan_ref, leaves_ref, item_ref, trans_ref, window_ref, image_ref
):
    def store(i, unit, image):
        for k in range(width):
            image_ref[i, k] = image[:, k * LANES : (k + 1) * LANES]

    far_images(fields, items, width, slots, plan_ref, leaves_ref, item_ref, trans_ref, window_ref, store)


def far_images(fields, items, width, slots, plan_ref, leaves_ref, item_ref, trans_ref, window_ref, give):
    for i in range(items):
        plain = item_ref[i, :, : trans_ref.shape[1]].astype(F32)
        odd = odd_lanes(plain.shape)
        turned = jnp.where(odd, from_left(plain), -from_right(plain))
        rows = jnp.concatenate([plain, turned], axis=0).astype(BF16)
        local_field = dot_nn(rows, trans_ref[i]).astype(BF16).astype(F32)
        local_field = twice(local_field, plain.shape[1])
        local_real, local_imag = local_field[:fields], local_field[fields:]
        rows = jnp.concatenate(
            [jnp.where(odd, -local_imag, local_real), jnp.where(odd, local_real, local_imag)], axis=0
        ).astype(BF16)
        expansions = jnp.concatenate([as_rows(window_ref.at[i, k]) for k in range(width)], axis=-1)
        place = item_place(slots, i)
        leaf, unit = plan_ref[place + 2], plan_ref[place + 3]
        mask = window_mask(leaves_ref, leaf, unit, 2 * fields, width)
        image = jnp.where(mask, dot_nn(rows, expansions), 0.0)
        give(i, unit, image)


def pair_kernel(keep_ref, got_ref, out_ref):
    out_ref[...] = (keep_ref[...].astype(F32) + got_ref[...].astype(F32)).astype(out_ref.dtype)


def tree_sum(values):
    while len(values) > 1:
        values = [values[k] + values[k + 1] for k in range(0, len(values), 2)]
    return values[0]


def swap_order(chips):
    steps = list(range(chips - 1, 0, -1))
    return [chips // 2] + [step for step in steps if step != chips // 2]


def by_step(parts):
    arrived = dict(zip(swap_order(len(parts)), parts[1:]))
    return [parts[0]] + [arrived[step] for step in range(1, len(parts))]


def close_kernel(*refs):
    refs[-1][...] = tree_sum([ref[...].astype(F32) for ref in by_step(refs[:-1])])


def assemble_kernel(
    fields, items, width, slots, core_ref, plan_ref, leaves_ref, mine_ref, theirs_ref, window_ref,
    out_ref, low_ref, made_ref,
):
    core = core_ref[0]
    for k in range(mine_ref.shape[0]):
        for ref, unit in ((mine_ref, 2 * k + core), (theirs_ref, 2 * k + 1 - core)):
            out_ref[unit] = ref[k]
            low_ref[unit] = ref[k].astype(BF16)
    for i in range(items):
        place = item_place(slots, i)
        made = multi_rows(
            fields, width, plan_ref[place], plan_ref[place + 1], leaves_ref, low_ref, window_ref.at[i]
        )
        made_ref[i, :, : made.shape[1]] = made.astype(BF16)


def flat_lines(totals, fields):
    per = LANES // fields
    lane = lax.broadcasted_iota(jnp.int32, (fields, LANES), 1)
    field = lax.broadcasted_iota(jnp.int32, (fields, LANES), 0)
    lines = []
    for first in range(0, len(totals), per):
        line = jnp.zeros((fields, LANES), F32)
        for k, total in enumerate(totals[first : first + per]):
            line = jnp.where(lane == field + k * fields, jnp.sum(total, axis=1, keepdims=True), line)
        lines.append(jnp.sum(line, axis=0, keepdims=True))
    return jnp.concatenate(lines, axis=0)


def columns_of(lines, count, fields):
    per = LANES // fields
    columns = []
    for k in range(lines.shape[0]):
        square = jnp.transpose(jnp.broadcast_to(lines[k : k + 1], (LANES, LANES)))
        columns += [square[j * fields : (j + 1) * fields] for j in range(per)]
    return columns[:count]


def gram_kernel(fields, core_ref, right_ref, image_ref, *refs):
    *parts, out_ref = refs
    totals = None
    for k in range(parts[0].shape[0]):
        unit = 2 * k + core_ref[0]
        r = right_ref[:, pl.ds(pl.multiple_of(unit * LANES, LANES), LANES)]
        z = image_ref[unit]
        q = tree_sum([part[k].astype(F32) for part in by_step(parts)])
        (rr, ri), (zr, zi), (qr, qi) = [(v[:fields], v[fields:]) for v in (r, z, q)]
        products = [
            rr * rr + ri * ri,
            rr * zr + ri * zi,
            rr * zi - ri * zr,
            zr * zr + zi * zi,
            rr * qr + ri * qi,
            rr * qi - ri * qr,
            zr * qr + zi * qi,
            zr * qi - zi * qr,
            qr * qr + qi * qi,
        ]
        totals = products if totals is None else [t + p for t, p in zip(totals, products)]
    out_ref[...] = jnp.broadcast_to(flat_lines(totals, fields)[None], out_ref.shape)


def final_kernel(fields, sums_ref, right_ref, image_ref, out_ref):
    units = image_ref.shape[0]
    sums = columns_of(jnp.sum(sums_ref[...], axis=0), 9, fields)
    a_real, a_imag, b_real, b_imag = krylov_coefficients(sums)
    for k in range(units):
        lanes = slice(k * LANES, (k + 1) * LANES)
        r_real, r_imag = right_ref[:fields, lanes], right_ref[fields:, lanes]
        z_real, z_imag = image_ref[k, :fields], image_ref[k, fields:]
        out_ref[:fields, lanes] = a_real * r_real - a_imag * r_imag + b_real * z_real - b_imag * z_imag
        out_ref[fields:, lanes] = a_real * r_imag + a_imag * r_real + b_real * z_imag + b_imag * z_real


def params(mebibytes=16):
    return pltpu.CompilerParams(vmem_limit_bytes=mebibytes * 1024 * 1024)


def is_power(count):
    return count & (count - 1) == 0


def reversed_bits(value, count):
    bits = count.bit_length() - 1
    return sum(((value >> k) & 1) << (bits - 1 - k) for k in range(bits))


def target_row(row, pair, rows):
    if not is_power(rows):
        return (pair - row + rows) % rows
    return pair ^ reversed_bits(row, rows)


def source_row(row, pair, rows):
    if not is_power(rows):
        return (pair - row + rows) % rows
    return reversed_bits(pair ^ row, rows)


def own_items_change_cores(rows, items, send):
    return items == 1 and send == 2


def item_route(rows, group, columns, send):
    items = rows * send // group

    def flat(r, g):
        return (g // columns * rows + r) * columns + g % columns

    def target(r, g, pair):
        d = target_row(r, pair, rows)
        return flat(d, g ^ 1 if d == r and own_items_change_cores(rows, items, send) else g)

    assert items * group == rows * send and (items % send == 0 or send % items == 0)
    routes = []
    for first in range(0, items, send):
        pairs = [(g * items + first) // send for g in range(group)]
        routes.append([(flat(r, g), target(r, g, pairs[g])) for r in range(rows) for g in range(group)])
    return items, routes


def local(
    right_side,
    near_tiles,
    tile_pairs,
    tile_count,
    panel_expansions,
    leaf_of_panel,
    far_pick,
    far_target,
    far_offset,
    translations,
):
    fields, panels = right_side.shape[1:]
    coefs = panel_expansions.shape[2]
    tile = near_tiles.shape[2]
    send = far_pick.shape[2]
    rows = lax.axis_size("row")
    group = lax.axis_size("grp") * lax.axis_size("col")
    row_here = lax.axis_index("row")
    own = lax.axis_index("grp") * lax.axis_size("col") + lax.axis_index("col")
    both = 2 * fields
    units = panels // LANES
    edge = REACH * tile
    edge_units = edge // LANES
    width = tile // LANES + 1
    items, routes = item_route(rows, group, lax.axis_size("col"), send)

    assert rows % 2 == 0
    neighbours = [[(r - 1 + 2 * (r % 2)) % rows for r in range(rows)], [r + 1 - 2 * (r % 2) for r in range(rows)]]
    own_place, row_place = own.reshape(1), row_here.reshape(1)
    core_place = lax.rem(own, 2).reshape(1)
    slots = near_tiles.shape[1]
    pad_coefs = -(-coefs // 8) * 8
    chips = group // 2
    assert group == 2 * chips and chips & (chips - 1) == 0 and LANES % fields == 0
    window_shape = jax.ShapeDtypeStruct((items, width, pad_coefs, 2, LANES), BF16)
    item_shape = jax.ShapeDtypeStruct((items, fields, 2 * pad_coefs), BF16)
    half_units = (units // 2, both, LANES)
    assert units % 2 == 0 and edge_units % 2 == 0

    def in_hbm(value):
        return pltpu.with_memory_space_constraint(value, pltpu.HBM)

    leaves = leaf_of_panel.reshape(units, 1, LANES)
    expansions = panel_expansions.transpose(2, 0, 1).reshape(coefs, 2, units, LANES).transpose(0, 2, 1, 3)
    expansions = in_hbm(expansions)
    moves = in_hbm(translations.transpose(0, 2, 1, 3))
    picks = far_pick.transpose(0, 2, 1)

    plan, made, windows, leaves, right = pl.pallas_call(
        functools.partial(begin_kernel, fields, items, width, send, rows),
        out_shape=(
            pltpu.SMEM((item_place(slots, items),), jnp.int32),
            item_shape,
            pltpu.VMEM(window_shape.shape, BF16),
            jax.ShapeDtypeStruct(leaves.shape, jnp.int32),
            jax.ShapeDtypeStruct((both, panels), F32),
        ),
        in_specs=[SMEM] * 2 + [HBM] * 8,
        out_specs=(SMEM,) + (VMEM,) * 4,
        scratch_shapes=[
            pltpu.SMEM(value.shape, jnp.int32)
            for value in (picks, leaf_of_panel, far_target, far_offset, tile_pairs)
        ]
        + [
            pltpu.SemaphoreType.DMA((7,)),
            pltpu.SemaphoreType.DMA((items, width, PIECES)),
        ],
        compiler_params=params(),
        name="begin",
    )(
        row_place,
        own_place,
        in_hbm(picks),
        in_hbm(leaf_of_panel),
        in_hbm(leaves),
        in_hbm(far_target),
        in_hbm(far_offset),
        in_hbm(tile_pairs),
        in_hbm(right_side.reshape(both, panels)),
        expansions,
    )

    def exchanged(made):
        parts = [
            lax.ppermute(made[k * send : k * send + min(send, items)], EVERY, route) for k, route in enumerate(routes)
        ]
        return parts[0] if len(parts) == 1 else jnp.concatenate(parts)

    def from_neighbours(image):
        edge_shape = (both, edge) if image.ndim == 2 else (edge_units // 2, both, LANES)
        one, two = pl.pallas_call(
            edge_kernel,
            out_shape=(jax.ShapeDtypeStruct(edge_shape, BF16),) * 2,
            in_specs=[SMEM, VMEM],
            out_specs=(VMEM, VMEM),
            compiler_params=params(),
            name="edges",
        )(row_place, image)
        return [
            lax.ppermute(value, "row", list(enumerate(targets))) for value, targets in zip((one, two), neighbours)
        ]

    image_shape = jax.ShapeDtypeStruct((units, both, LANES), F32)
    target_windows, moved = pl.pallas_call(
        functools.partial(fetch_kernel, items, width, slots),
        out_shape=(
            pltpu.VMEM(window_shape.shape, BF16),
            pltpu.VMEM((items, 2 * pad_coefs, coefs), BF16),
        ),
        in_specs=[SMEM, HBM, HBM],
        out_specs=(VMEM, VMEM),
        scratch_shapes=[
            pltpu.VMEM((items, coefs, 2, coefs), BF16),
            pltpu.SemaphoreType.DMA((items, width, PIECES)),
            pltpu.SemaphoreType.DMA((items,)),
        ],
        compiler_params=params(24),
        cost_estimate=pl.CostEstimate(flops=0, bytes_accessed=6 * window_shape.size, transcendentals=0),
        name="fetch",
    )(plan, expansions, moves)

    def swapped(value, step):
        return lax.ppermute(value, GROUP, [(g, g ^ step) for g in range(group)])

    def near(one, two, low):
        return pl.pallas_call(
            functools.partial(near_kernel, fields),
            out_shape=image_shape,
            in_specs=[SMEM] * 4 + [VMEM] * 4,
            out_specs=VMEM,
            scratch_shapes=[pltpu.VMEM((units + 2 * edge_units, both, LANES), low.dtype)],
            compiler_params=params(),
            cost_estimate=pl.CostEstimate(
                flops=8 * fields * near_tiles.size // 2, bytes_accessed=2 * near_tiles.size, transcendentals=0
            ),
            name="near",
        )(core_place, row_place, tile_count, plan, one, two, low, near_tiles)

    def core_parts(partial, taken):
        half_shape = jax.ShapeDtypeStruct(half_units, F32)
        keep, give = pl.pallas_call(
            functools.partial(far_kernel, fields, items, width, slots),
            out_shape=(half_shape, half_shape),
            in_specs=[SMEM, SMEM] + [VMEM] * 5,
            out_specs=(VMEM, VMEM),
            scratch_shapes=[pltpu.VMEM(image_shape.shape, F32)],
            compiler_params=params(),
            name="far",
        )(core_place, plan, leaves, partial, taken, moved, target_windows)
        return keep, swapped(give, 1)

    def first_far(taken):
        return pl.pallas_call(
            functools.partial(first_far_kernel, fields, items, width, slots),
            out_shape=jax.ShapeDtypeStruct((items, width, both, LANES), F32),
            in_specs=[SMEM] + [VMEM] * 4,
            out_specs=VMEM,
            compiler_params=params(),
            name="first_far",
        )(plan, leaves, taken, moved, target_windows)

    def last_core_parts(one, two, low, image):
        half_shape = jax.ShapeDtypeStruct(half_units, BF16)
        keep, give = pl.pallas_call(
            functools.partial(last_near_kernel, fields),
            out_shape=(half_shape, half_shape),
            in_specs=[SMEM] * 4 + [VMEM] * 5,
            out_specs=(VMEM, VMEM),
            scratch_shapes=[
                pltpu.VMEM((units + 2 * edge_units, both, LANES), low.dtype),
                pltpu.VMEM(image_shape.shape, F32),
            ],
            compiler_params=params(),
            name="last_near",
        )(core_place, row_place, tile_count, plan, one, two, low, near_tiles, image)
        return keep, swapped(give, 1)

    def pair_sums(keep, got):
        pair = pl.pallas_call(
            pair_kernel,
            out_shape=jax.ShapeDtypeStruct(keep.shape, BF16),
            in_specs=[VMEM, VMEM],
            out_specs=VMEM,
            compiler_params=params(),
            name="pair",
        )(keep, got)
        arrived = {step: swapped(pair, 2 * step) for step in swap_order(chips)}
        return [pair] + list(arrived.values())

    def half_sum(parts):
        return pl.pallas_call(
            close_kernel,
            out_shape=jax.ShapeDtypeStruct(half_units, F32),
            in_specs=[VMEM] * chips,
            out_specs=VMEM,
            compiler_params=params(),
            name="close",
        )(*parts)

    def whole(mine, theirs):
        return pl.pallas_call(
            functools.partial(assemble_kernel, fields, items, width, slots),
            out_shape=(
                image_shape,
                jax.ShapeDtypeStruct(image_shape.shape, BF16),
                jax.ShapeDtypeStruct((items, fields, 2 * pad_coefs + ITEM_REST), BF16),
            ),
            in_specs=[SMEM, SMEM] + [VMEM] * 4,
            out_specs=(VMEM,) * 3,
            compiler_params=params(),
            name="assemble",
        )(core_place, plan, leaves, mine, theirs, windows)

    def joined_edges(one, two, made):
        return pl.pallas_call(
            join_kernel,
            out_shape=jax.ShapeDtypeStruct((edge_units, both, LANES), BF16),
            in_specs=[VMEM, VMEM, ANY],
            out_specs=VMEM,
            compiler_params=params(),
            name="join",
        )(one, two, made)

    partial = near(*from_neighbours(right), right)
    mine = half_sum(pair_sums(*core_parts(partial, exchanged(made))))
    theirs = swapped(mine, 1)
    one, two = from_neighbours(mine)
    z_all, z_low, made = whole(mine, theirs)
    edges = joined_edges(one, two, made)
    image = first_far(exchanged(made))
    parts = pair_sums(*last_core_parts(edges, swapped(edges, 1), z_low, image))

    lines = pl.pallas_call(
        functools.partial(gram_kernel, fields),
        out_shape=jax.ShapeDtypeStruct((2 * rows, -(-9 * fields // LANES), LANES), F32),
        in_specs=[SMEM] + [VMEM] * (2 + chips),
        out_specs=VMEM,
        compiler_params=params(),
        name="gram",
    )(core_place, right, z_all, *parts)
    columns = lax.axis_size("col")
    same_chip = [
        [((g + k) // columns * rows + r) * columns + (g + k) % columns for r in range(rows) for k in range(2)]
        for g in range(0, group, 2)
    ]
    sums = lax.all_to_all(lines, EVERY, 0, 0, axis_index_groups=same_chip, tiled=True)
    out = pl.pallas_call(
        functools.partial(final_kernel, fields),
        out_shape=jax.ShapeDtypeStruct((both, panels), F32),
        in_specs=[VMEM] * 3,
        out_specs=VMEM,
        compiler_params=params(),
        name="combine",
    )(sums, right, z_all)
    return out.reshape(right_side.shape)


def krylov_coefficients(sums):
    rr, rz_real, rz_imag, zz, rq_real, rq_imag, zq_real, zq_imag, qq = sums

    def times(left, right):
        return left[0] * right[0] - left[1] * right[1], left[0] * right[1] + left[1] * right[0]

    def conj_times(left, right):
        return left[0] * right[0] + left[1] * right[1], left[0] * right[1] - left[1] * right[0]

    def scale(factor, value):
        return factor * value[0], factor * value[1]

    def plus(*values):
        return sum(v[0] for v in values), sum(v[1] for v in values)

    def size(value):
        return value[0] * value[0] + value[1] * value[1]

    rz, rq, zq = (rz_real, rz_imag), (rq_real, rq_imag), (zq_real, zq_imag)
    beta = jnp.sqrt(rr + EPSILON)
    inv = 1.0 / beta
    norm_one = rr * inv * inv
    product = scale(inv * inv, rz)
    h_first = (0.5 * norm_one + product[0], product[1])
    shift = (h_first[0] - 0.5, h_first[1])
    residue = zz * inv * inv - 2.0 * conj_times(shift, product)[0] + size(shift) * norm_one
    residue = jnp.maximum(residue, 0.0)
    h_sub = jnp.sqrt(residue + EPSILON)
    alpha = inv / h_sub
    gamma = scale(-alpha, shift)
    h_upper = scale(
        inv,
        plus(
            scale(0.5, plus(scale(alpha, rz), scale(rr, gamma))), scale(alpha, rq), times(gamma, rz)
        ),
    )
    second = plus(
        scale(alpha * alpha, zq),
        scale(alpha * zz, gamma),
        scale(alpha, conj_times(gamma, rq)),
        scale(size(gamma), rz),
    )
    h_middle = (0.5 * residue / (h_sub * h_sub) + second[0], second[1])
    keep = (h_middle[0] - 0.5, h_middle[1])
    on_z = plus(gamma, scale(-alpha, keep))
    on_r = plus(scale(-inv, h_upper), scale(-1.0, times(keep, gamma)))
    last = (
        alpha * alpha * qq
        + size(on_z) * zz
        + size(on_r) * rr
        + 2.0
        * (
            conj_times(on_r, times(on_z, rz))[0]
            + alpha * conj_times(on_r, rq)[0]
            + alpha * conj_times(on_z, zq)[0]
        )
    )
    h_last = jnp.sqrt(jnp.maximum(last, 0.0) + EPSILON)
    radius = jnp.sqrt(size(h_first) + h_sub * h_sub)
    cosine = scale(1.0 / radius, h_first)
    sine = h_sub / radius
    upper = plus(conj_times(cosine, h_upper), scale(sine, h_middle))
    lower = plus(times(cosine, h_middle), scale(-sine, h_upper))
    radius_two = jnp.sqrt(size(lower) + h_last * h_last)
    cosine_two = scale(1.0 / radius_two, lower)
    weight_two = scale(-sine * beta / radius_two, (cosine_two[0], -cosine_two[1]))
    goal = scale(beta, (cosine[0], -cosine[1]))
    weight_one = scale(1.0 / radius, plus(goal, scale(-1.0, times(upper, weight_two))))
    on_right = plus(scale(inv, weight_one), times(weight_two, gamma))
    on_image = scale(alpha, weight_two)
    return on_right[0], on_right[1], on_image[0], on_image[1]


def solution(mesh):
    return jax.shard_map(
        local,
        mesh=mesh,
        in_specs=(
            P(None, None, "row"),
            P(None, ("grp", "row", "col"), None, None),
            P(("grp", "row", "col")),
            P(("grp", "row", "col")),
            P(None, "row", None),
            P("row", None),
            P(),
            P("row", None),
            P("row", None),
            P(),
        ),
        out_specs=P(None, None, "row"),
        check_vma=False,
    )
```

```python
import functools

import jax
import jax.numpy as jnp
from jax import lax
from jax.experimental import pallas as pl
from jax.experimental.pallas import tpu as pltpu
from jax.sharding import PartitionSpec as P

REACH = 2
SPAN = 2 * REACH + 1
LANES = 128
EPSILON = 1e-06
GROUP = ("grp", "col")
CODES = 0
PER_ITEM = 5
ITEM_REST = LANES
PIECES = 4
EVERY = ("grp", "row", "col")

F32 = jnp.float32
BF16 = jnp.bfloat16
SMEM = pl.BlockSpec(memory_space=pltpu.SMEM)
VMEM = pl.BlockSpec(memory_space=pltpu.VMEM)
HBM = pl.BlockSpec(memory_space=pltpu.HBM)
ANY = pl.BlockSpec(memory_space=pl.ANY)


def dot_nn(left, right):
    return lax.dot_general(left, right, (((1,), (0,)), ((), ())), preferred_element_type=F32)


def dot_nt(left, right):
    return lax.dot_general(left, right, (((1,), (1,)), ((), ())), preferred_element_type=F32)


def halves(rows):
    if rows.dtype != F32:
        return rows
    high = rows.astype(BF16)
    return jnp.concatenate([high, (rows - high.astype(F32)).astype(BF16)], axis=0)


def joined(sums, count):
    return sums if sums.shape[0] == count else sums[:count] + sums[count:]


def odd_lanes(shape):
    return lax.rem(lax.broadcasted_iota(jnp.int32, shape, 1), 2) == 1


def twice(value, width):
    rows = value.shape[0]
    parts = []
    for k in range(width // LANES):
        first = (k // 2) * LANES
        part = value[:, first : first + LANES]
        if part.shape[1] < LANES:
            part = jnp.concatenate([part, jnp.zeros((rows, LANES - part.shape[1]), part.dtype)], axis=-1)
        lane = lax.broadcasted_iota(jnp.int32, (rows, LANES), 1)
        parts.append(jnp.take_along_axis(part, lax.div(lane, 2) + (k % 2) * (LANES // 2), axis=1))
    return jnp.concatenate(parts, axis=-1)


def from_left(value):
    return pltpu.roll(value, 1, 1)


def from_right(value):
    return pltpu.roll(value, value.shape[1] - 1, 1)


def item_place(slots, item):
    return CODES + slots + PER_ITEM * item


def window_start(leaf_ref, leaf, width):
    units = leaf_ref.shape[1] // LANES
    before = jnp.int32(0)
    for k in range(units):
        before = before + (leaf_ref[0, k * LANES] < leaf).astype(jnp.int32)
    return jnp.clip(before - 1, 0, units - width)


def window_mask(leaves_ref, leaf, unit, rows, width):
    leaves = jnp.concatenate([leaves_ref[unit + k] for k in range(width)], axis=-1)
    return jnp.broadcast_to(leaves, (rows, width * LANES)) == leaf


def window_copies(exp_ref, unit, window_ref, sem, width):
    coefs = exp_ref.shape[0]
    step = -(-coefs // PIECES)
    copies = []
    for k in range(width):
        for p in range(PIECES):
            part = pl.ds(p * step, min(step, coefs - p * step))
            copies.append(
                pltpu.make_async_copy(exp_ref.at[part, unit + k], window_ref.at[k, part], sem.at[k, p])
            )
    return copies


def clear_rest(window_ref, coefs, width):
    rest = window_ref.shape[1] - coefs
    for k in range(width):
        window_ref[k, pl.ds(coefs, rest)] = jnp.zeros((rest, 2, LANES), BF16)


def multi_rows(fields, width, leaf, unit, leaves_ref, low_ref, window_ref):
    if len(low_ref.shape) == 2:
        first = pl.multiple_of(unit * LANES, LANES)
        rows = low_ref[:, pl.ds(first, width * LANES)]
    else:
        rows = jnp.concatenate([low_ref[unit + k] for k in range(width)], axis=-1)
    mask = window_mask(leaves_ref, leaf, unit, 2 * fields, width)
    rows = halves(jnp.where(mask, rows.astype(F32), 0.0).astype(rows.dtype))
    expansions = jnp.concatenate([as_rows(window_ref.at[k]) for k in range(width)], axis=-1)
    total = joined(dot_nt(rows, expansions), 2 * fields)
    on_real, on_imag = total[:fields], total[fields:]
    odd = odd_lanes(on_real.shape)
    other = jnp.where(odd, from_left(on_imag), from_right(on_imag))
    return jnp.where(odd, -on_real, on_real) - other


def as_rows(ref):
    return ref.reshape(ref.shape[0] * 2, ref.shape[2])[...]


def edge_kernel(row_ref, image_ref, one_ref, two_ref):
    edge_of(row_ref, image_ref, one_ref, True)
    edge_of(row_ref, image_ref, two_ref, False)


def one_edge_kernel(early, row_ref, image_ref, out_ref):
    edge_of(row_ref, image_ref, out_ref, early)


def edge_of(row_ref, image_ref, out_ref, early):
    first_edge = (lax.rem(row_ref[0], 2) == 0) if early else (lax.rem(row_ref[0], 2) == 1)
    if len(image_ref.shape) == 2:
        edge = out_ref.shape[1]
        first, last = image_ref[:, :edge], image_ref[:, image_ref.shape[1] - edge :]
    else:
        edge = out_ref.shape[0]
        first, last = image_ref[:edge], image_ref[image_ref.shape[0] - edge :]

    @pl.when(first_edge)
    def _():
        out_ref[...] = first.astype(out_ref.dtype)

    @pl.when(jnp.logical_not(first_edge))
    def _():
        out_ref[...] = last.astype(out_ref.dtype)


def begin_kernel(
    fields, items, width, send, rows, row_ref, own_ref, pick_hbm, leaf_hbm, leaves_hbm,
    target_hbm, offset_hbm, pairs_hbm, right_hbm, exp_ref,
    plan_ref, out_ref, window_ref, leaves_ref, right_ref,
    pick_ref, leaf_ref, target_ref, offset_ref, pairs_ref, sem, window_sem,
):
    loads = [
        pltpu.make_async_copy(source, place, sem.at[k])
        for k, (source, place) in enumerate(
            (
                (leaf_hbm, leaf_ref),
                (pick_hbm, pick_ref),
                (target_hbm, target_ref),
                (offset_hbm, offset_ref),
                (pairs_hbm, pairs_ref),
                (leaves_hbm, leaves_ref),
                (right_hbm, right_ref),
            )
        )
    ]
    for load in loads:
        load.start()
    for i in range(items):
        clear_rest(window_ref.at[i], exp_ref.shape[0], width)
    slots = pairs_ref.shape[0]
    own = own_ref[0]
    loads[0].wait()
    loads[1].wait()
    row = row_ref[0]

    def partner(i, coming):
        number = own * items + i
        pair, number = lax.div(number, send), lax.rem(number, send)
        other = source_row(row, pair, rows) if coming else target_row(row, pair, rows)
        if coming and own_items_change_cores(rows, items, send):
            number = jnp.where(other == row, 1 - number, number)
        return other, number

    for i in range(items):
        other, number = partner(i, False)
        leaf = pick_ref[other, number, row]
        unit = window_start(leaf_ref, leaf, width)
        place = item_place(slots, i)
        plan_ref[place], plan_ref[place + 1] = leaf, unit
        for copy in window_copies(exp_ref, unit, window_ref.at[i], window_sem.at[i], width):
            copy.start()
    for load in loads[2:]:
        load.wait()
    for s in range(slots):
        plan_ref[CODES + s] = pairs_ref[s]
    for i in range(items):
        place = item_place(slots, i)
        other, number = partner(i, True)
        leaf = target_ref[0, other * send + number]
        plan_ref[place + 2], plan_ref[place + 3] = leaf, window_start(leaf_ref, leaf, width)
        plan_ref[place + 4] = offset_ref[0, other * send + number]
    for i in range(items):
        place = item_place(slots, i)
        leaf, unit = plan_ref[place], plan_ref[place + 1]
        for copy in window_copies(exp_ref, unit, window_ref.at[i], window_sem.at[i], width):
            copy.wait()
        out_ref[i] = multi_rows(fields, width, leaf, unit, leaves_ref, right_ref, window_ref.at[i]).astype(BF16)


def fetch_kernel(items, width, slots, plan_ref, exp_ref, trans_ref, window_ref, moved_ref, trans_buf, sem, trans_sem):
    coefs = trans_ref.shape[3]
    for i in range(items):
        clear_rest(window_ref.at[i], coefs, width)

    def trans_copy(i):
        offset = plan_ref[item_place(slots, i) + 4]
        return pltpu.make_async_copy(trans_ref.at[offset], trans_buf.at[i], trans_sem.at[i])

    def exp_copies(i):
        unit = plan_ref[item_place(slots, i) + 3]
        return window_copies(exp_ref, unit, window_ref.at[i], sem.at[i], width)

    for i in range(items):
        trans_copy(i).start()
        for copy in exp_copies(i):
            copy.start()
    rest = moved_ref.shape[1] - 2 * coefs
    for i in range(items):
        trans_copy(i).wait()
        moved_ref[i, pl.ds(0, 2 * coefs)] = trans_buf[i].reshape(2 * coefs, coefs)
        moved_ref[i, pl.ds(2 * coefs, rest)] = jnp.zeros((rest, coefs), BF16)
        for copy in exp_copies(i):
            copy.wait()


def edge_places(row_ref, edge, units):
    even = lax.rem(row_ref[0], 2) == 0
    return jnp.where(even, 0, edge + units), jnp.where(even, edge + units, 0)


def part(total, core, keep_ref, give_ref):
    for k in range(keep_ref.shape[0]):
        keep_ref[k] = total[2 * k + core].astype(keep_ref.dtype)
        give_ref[k] = total[2 * k + 1 - core].astype(give_ref.dtype)


def near_kernel(fields, row_ref, count_ref, plan_ref, one_ref, two_ref, here_ref, tiles_ref, out_ref, ext):
    units = out_ref.shape[0]
    edge = (ext.shape[0] - units) // 2
    one_at, two_at = edge_places(row_ref, edge, units)
    for k in range(edge):
        lanes = slice(k * LANES, (k + 1) * LANES)
        ext[one_at + k] = one_ref[:, lanes].astype(ext.dtype)
        ext[two_at + k] = two_ref[:, lanes].astype(ext.dtype)
    for k in range(units):
        ext[edge + k] = here_ref[:, k * LANES : (k + 1) * LANES]
    out_ref[...] = jnp.zeros_like(out_ref)
    near_slots(fields, count_ref, plan_ref, tiles_ref, out_ref, ext)


def last_near_kernel(
    fields, core_ref, row_ref, count_ref, plan_ref, one_ref, other_one_ref, two_ref, here_ref, tiles_ref, image_ref,
    keep_ref, give_ref, ext, total,
):
    units = total.shape[0]
    edge = (ext.shape[0] - units) // 2
    core = core_ref[0]
    one_at, two_at = edge_places(row_ref, edge, units)
    for k in range(edge // 2):
        ext[one_at + 2 * k + core] = one_ref[k]
        ext[one_at + 2 * k + 1 - core] = other_one_ref[k]
    ext[pl.ds(two_at, edge)] = two_ref[...]
    ext[edge : edge + units] = here_ref[...]
    total[...] = jnp.zeros_like(total)
    items, width = image_ref.shape[:2]
    for i in range(items):
        unit = plan_ref[item_place(tiles_ref.shape[1], i) + 3]
        for k in range(width):
            total[unit + k] += image_ref[i, k]
    near_slots(fields, count_ref, plan_ref, tiles_ref, total, ext)
    part(total, core_ref[0], keep_ref, give_ref)


def near_slots(fields, count_ref, plan_ref, tiles_ref, out_ref, ext):
    slots, tile = tiles_ref.shape[1], tiles_ref.shape[2]
    per = tile // LANES
    for s in range(slots):
        code = plan_ref[CODES + s]
        target = lax.div(code, SPAN)
        source = target + lax.rem(code, SPAN)
        rows = halves(jnp.concatenate([ext[source * per + k] for k in range(per)], axis=-1))
        on_real = joined(dot_nt(rows, tiles_ref[0, s]), 2 * fields)
        on_imag = joined(dot_nt(rows, tiles_ref[1, s]), 2 * fields)
        value = jnp.concatenate(
            [on_real[:fields] - on_imag[fields:], on_real[fields:] + on_imag[:fields]], axis=0
        )
        value = jnp.where(s < count_ref[0], value, 0.0)
        for k in range(per):
            out_ref[target * per + k] += value[:, k * LANES : (k + 1) * LANES]


def far_kernel(
    fields, items, width, slots, core_ref, plan_ref, leaves_ref, partial_ref, item_ref, trans_ref, window_ref,
    keep_ref, give_ref, total,
):
    total[...] = partial_ref[...]

    def add(i, unit, image):
        for k in range(width):
            total[unit + k] += image[:, k * LANES : (k + 1) * LANES]

    far_images(fields, items, width, slots, plan_ref, leaves_ref, item_ref, trans_ref, window_ref, add)
    part(total, core_ref[0], keep_ref, give_ref)


def first_far_kernel(
    fields, items, width, slots, plan_ref, leaves_ref, item_ref, trans_ref, window_ref, image_ref
):
    def store(i, unit, image):
        for k in range(width):
            image_ref[i, k] = image[:, k * LANES : (k + 1) * LANES]

    far_images(fields, items, width, slots, plan_ref, leaves_ref, item_ref, trans_ref, window_ref, store)


def far_images(fields, items, width, slots, plan_ref, leaves_ref, item_ref, trans_ref, window_ref, give):
    for i in range(items):
        plain = item_ref[i, :, : trans_ref.shape[1]].astype(F32)
        odd = odd_lanes(plain.shape)
        turned = jnp.where(odd, from_left(plain), -from_right(plain))
        rows = jnp.concatenate([plain, turned], axis=0).astype(BF16)
        local_field = dot_nn(rows, trans_ref[i]).astype(BF16).astype(F32)
        local_field = twice(local_field, plain.shape[1])
        local_real, local_imag = local_field[:fields], local_field[fields:]
        rows = jnp.concatenate(
            [jnp.where(odd, -local_imag, local_real), jnp.where(odd, local_real, local_imag)], axis=0
        ).astype(BF16)
        expansions = jnp.concatenate([as_rows(window_ref.at[i, k]) for k in range(width)], axis=-1)
        place = item_place(slots, i)
        leaf, unit = plan_ref[place + 2], plan_ref[place + 3]
        mask = window_mask(leaves_ref, leaf, unit, 2 * fields, width)
        image = jnp.where(mask, dot_nn(rows, expansions), 0.0)
        give(i, unit, image)


def pair_kernel(keep_ref, got_ref, out_ref):
    out_ref[...] = (keep_ref[...].astype(F32) + got_ref[...].astype(F32)).astype(out_ref.dtype)


def tree_sum(values):
    while len(values) > 1:
        values = [values[k] + values[k + 1] for k in range(0, len(values), 2)]
    return values[0]


def swap_order(chips):
    return list(range(chips - 1, 0, -1))


def by_step(parts):
    arrived = dict(zip(swap_order(len(parts)), parts[1:]))
    return [parts[0]] + [arrived[step] for step in range(1, len(parts))]


def close_kernel(*refs):
    refs[-1][...] = tree_sum([ref[...].astype(F32) for ref in by_step(refs[:-1])])


def assemble_kernel(
    fields, items, width, slots, core_ref, plan_ref, leaves_ref, mine_ref, theirs_ref, window_ref,
    out_ref, low_ref, made_ref,
):
    core = core_ref[0]
    for k in range(mine_ref.shape[0]):
        for ref, unit in ((mine_ref, 2 * k + core), (theirs_ref, 2 * k + 1 - core)):
            out_ref[unit] = ref[k]
            low_ref[unit] = ref[k].astype(BF16)
    for i in range(items):
        place = item_place(slots, i)
        made = multi_rows(
            fields, width, plan_ref[place], plan_ref[place + 1], leaves_ref, low_ref, window_ref.at[i]
        )
        made_ref[i, :, : made.shape[1]] = made.astype(BF16)


def flat_lines(totals, fields):
    per = LANES // fields
    lane = lax.broadcasted_iota(jnp.int32, (fields, LANES), 1)
    field = lax.broadcasted_iota(jnp.int32, (fields, LANES), 0)
    lines = []
    for first in range(0, len(totals), per):
        line = jnp.zeros((fields, LANES), F32)
        for k, total in enumerate(totals[first : first + per]):
            line = jnp.where(lane == field + k * fields, jnp.sum(total, axis=1, keepdims=True), line)
        lines.append(jnp.sum(line, axis=0, keepdims=True))
    return jnp.concatenate(lines, axis=0)


def columns_of(lines, count, fields):
    per = LANES // fields
    columns = []
    for k in range(lines.shape[0]):
        square = jnp.transpose(jnp.broadcast_to(lines[k : k + 1], (LANES, LANES)))
        columns += [square[j * fields : (j + 1) * fields] for j in range(per)]
    return columns[:count]


def gram_kernel(fields, core_ref, right_ref, image_ref, *refs):
    *parts, out_ref = refs
    totals = None
    for k in range(parts[0].shape[0]):
        unit = 2 * k + core_ref[0]
        r = right_ref[:, pl.ds(pl.multiple_of(unit * LANES, LANES), LANES)]
        z = image_ref[unit]
        q = tree_sum([part[k].astype(F32) for part in by_step(parts)])
        (rr, ri), (zr, zi), (qr, qi) = [(v[:fields], v[fields:]) for v in (r, z, q)]
        products = [
            rr * rr + ri * ri,
            rr * zr + ri * zi,
            rr * zi - ri * zr,
            zr * zr + zi * zi,
            rr * qr + ri * qi,
            rr * qi - ri * qr,
            zr * qr + zi * qi,
            zr * qi - zi * qr,
            qr * qr + qi * qi,
        ]
        totals = products if totals is None else [t + p for t, p in zip(totals, products)]
    out_ref[...] = jnp.broadcast_to(flat_lines(totals, fields)[None], out_ref.shape)


def final_kernel(fields, sums_ref, right_ref, image_ref, out_ref):
    units = image_ref.shape[0]
    sums = columns_of(jnp.sum(sums_ref[...], axis=0), 9, fields)
    a_real, a_imag, b_real, b_imag = krylov_coefficients(sums)
    for k in range(units):
        lanes = slice(k * LANES, (k + 1) * LANES)
        r_real, r_imag = right_ref[:fields, lanes], right_ref[fields:, lanes]
        z_real, z_imag = image_ref[k, :fields], image_ref[k, fields:]
        out_ref[:fields, lanes] = a_real * r_real - a_imag * r_imag + b_real * z_real - b_imag * z_imag
        out_ref[fields:, lanes] = a_real * r_imag + a_imag * r_real + b_real * z_imag + b_imag * z_real


def params(mebibytes=16):
    return pltpu.CompilerParams(vmem_limit_bytes=mebibytes * 1024 * 1024)


def is_power(count):
    return count & (count - 1) == 0


def reversed_bits(value, count):
    bits = count.bit_length() - 1
    return sum(((value >> k) & 1) << (bits - 1 - k) for k in range(bits))


def target_row(row, pair, rows):
    if not is_power(rows):
        return (pair - row + rows) % rows
    return pair ^ reversed_bits(row, rows)


def source_row(row, pair, rows):
    if not is_power(rows):
        return (pair - row + rows) % rows
    return reversed_bits(pair ^ row, rows)


def own_items_change_cores(rows, items, send):
    return items == 1 and send == 2


def item_route(rows, group, columns, send):
    items = rows * send // group

    def flat(r, g):
        return (g // columns * rows + r) * columns + g % columns

    def target(r, g, pair):
        d = target_row(r, pair, rows)
        return flat(d, g ^ 1 if d == r and own_items_change_cores(rows, items, send) else g)

    assert items * group == rows * send and (items % send == 0 or send % items == 0)
    routes = []
    for first in range(0, items, send):
        pairs = [(g * items + first) // send for g in range(group)]
        routes.append([(flat(r, g), target(r, g, pairs[g])) for r in range(rows) for g in range(group)])
    return items, routes


def local(
    right_side,
    near_tiles,
    tile_pairs,
    tile_count,
    panel_expansions,
    leaf_of_panel,
    far_pick,
    far_target,
    far_offset,
    translations,
):
    fields, panels = right_side.shape[1:]
    coefs = panel_expansions.shape[2]
    tile = near_tiles.shape[2]
    send = far_pick.shape[2]
    rows = lax.axis_size("row")
    group = lax.axis_size("grp") * lax.axis_size("col")
    row_here = lax.axis_index("row")
    own = lax.axis_index("grp") * lax.axis_size("col") + lax.axis_index("col")
    both = 2 * fields
    units = panels // LANES
    edge = REACH * tile
    edge_units = edge // LANES
    width = tile // LANES + 1
    items, routes = item_route(rows, group, lax.axis_size("col"), send)

    assert rows % 2 == 0
    neighbours = [[(r - 1 + 2 * (r % 2)) % rows for r in range(rows)], [r + 1 - 2 * (r % 2) for r in range(rows)]]
    own_place, row_place = own.reshape(1), row_here.reshape(1)
    core_place = lax.rem(own, 2).reshape(1)
    slots = near_tiles.shape[1]
    pad_coefs = -(-coefs // 8) * 8
    chips = group // 2
    assert group == 2 * chips and chips & (chips - 1) == 0 and LANES % fields == 0
    window_shape = jax.ShapeDtypeStruct((items, width, pad_coefs, 2, LANES), BF16)
    item_shape = jax.ShapeDtypeStruct((items, fields, 2 * pad_coefs), BF16)
    half_units = (units // 2, both, LANES)
    assert units % 2 == 0 and edge_units % 2 == 0

    def in_hbm(value):
        return pltpu.with_memory_space_constraint(value, pltpu.HBM)

    leaves = leaf_of_panel.reshape(units, 1, LANES)
    expansions = panel_expansions.transpose(2, 0, 1).reshape(coefs, 2, units, LANES).transpose(0, 2, 1, 3)
    expansions = in_hbm(expansions)
    moves = in_hbm(translations.transpose(0, 2, 1, 3))
    picks = far_pick.transpose(0, 2, 1)

    plan, made, windows, leaves, right = pl.pallas_call(
        functools.partial(begin_kernel, fields, items, width, send, rows),
        out_shape=(
            pltpu.SMEM((item_place(slots, items),), jnp.int32),
            item_shape,
            pltpu.VMEM(window_shape.shape, BF16),
            jax.ShapeDtypeStruct(leaves.shape, jnp.int32),
            jax.ShapeDtypeStruct((both, panels), F32),
        ),
        in_specs=[SMEM] * 2 + [HBM] * 8,
        out_specs=(SMEM,) + (VMEM,) * 4,
        scratch_shapes=[
            pltpu.SMEM(value.shape, jnp.int32)
            for value in (picks, leaf_of_panel, far_target, far_offset, tile_pairs)
        ]
        + [
            pltpu.SemaphoreType.DMA((7,)),
            pltpu.SemaphoreType.DMA((items, width, PIECES)),
        ],
        compiler_params=params(),
        name="begin",
    )(
        row_place,
        own_place,
        in_hbm(picks),
        in_hbm(leaf_of_panel),
        in_hbm(leaves),
        in_hbm(far_target),
        in_hbm(far_offset),
        in_hbm(tile_pairs),
        in_hbm(right_side.reshape(both, panels)),
        expansions,
    )

    def exchanged(made):
        parts = [
            lax.ppermute(made[k * send : k * send + min(send, items)], EVERY, route) for k, route in enumerate(routes)
        ]
        return parts[0] if len(parts) == 1 else jnp.concatenate(parts)

    def along_row(value, which):
        return lax.ppermute(value, "row", list(enumerate(neighbours[which])))

    def from_neighbours(image):
        one, two = pl.pallas_call(
            edge_kernel,
            out_shape=(jax.ShapeDtypeStruct((both, edge), BF16),) * 2,
            in_specs=[SMEM, VMEM],
            out_specs=(VMEM, VMEM),
            compiler_params=params(),
            name="edges",
        )(row_place, image)
        return along_row(one, 0), along_row(two, 1)

    def one_edge(image, edge_units, early):
        return pl.pallas_call(
            functools.partial(one_edge_kernel, early),
            out_shape=jax.ShapeDtypeStruct((edge_units, both, LANES), BF16),
            in_specs=[SMEM, VMEM],
            out_specs=VMEM,
            compiler_params=params(),
            name="edge",
        )(row_place, image)

    image_shape = jax.ShapeDtypeStruct((units, both, LANES), F32)
    target_windows, moved = pl.pallas_call(
        functools.partial(fetch_kernel, items, width, slots),
        out_shape=(
            pltpu.VMEM(window_shape.shape, BF16),
            pltpu.VMEM((items, 2 * pad_coefs, coefs), BF16),
        ),
        in_specs=[SMEM, HBM, HBM],
        out_specs=(VMEM, VMEM),
        scratch_shapes=[
            pltpu.VMEM((items, coefs, 2, coefs), BF16),
            pltpu.SemaphoreType.DMA((items, width, PIECES)),
            pltpu.SemaphoreType.DMA((items,)),
        ],
        compiler_params=params(24),
        cost_estimate=pl.CostEstimate(flops=0, bytes_accessed=6 * window_shape.size, transcendentals=0),
        name="fetch",
    )(plan, expansions, moves)

    def swapped(value, step):
        return lax.ppermute(value, GROUP, [(g, g ^ step) for g in range(group)])

    def near(one, two, low):
        return pl.pallas_call(
            functools.partial(near_kernel, fields),
            out_shape=image_shape,
            in_specs=[SMEM] * 3 + [VMEM] * 4,
            out_specs=VMEM,
            scratch_shapes=[pltpu.VMEM((units + 2 * edge_units, both, LANES), low.dtype)],
            compiler_params=params(),
            cost_estimate=pl.CostEstimate(
                flops=8 * fields * near_tiles.size // 2, bytes_accessed=2 * near_tiles.size, transcendentals=0
            ),
            name="near",
        )(row_place, tile_count, plan, one, two, low, near_tiles)

    def core_parts(partial, taken):
        half_shape = jax.ShapeDtypeStruct(half_units, F32)
        keep, give = pl.pallas_call(
            functools.partial(far_kernel, fields, items, width, slots),
            out_shape=(half_shape, half_shape),
            in_specs=[SMEM, SMEM] + [VMEM] * 5,
            out_specs=(VMEM, VMEM),
            scratch_shapes=[pltpu.VMEM(image_shape.shape, F32)],
            compiler_params=params(),
            name="far",
        )(core_place, plan, leaves, partial, taken, moved, target_windows)
        return keep, swapped(give, 1)

    def first_far(taken):
        return pl.pallas_call(
            functools.partial(first_far_kernel, fields, items, width, slots),
            out_shape=jax.ShapeDtypeStruct((items, width, both, LANES), F32),
            in_specs=[SMEM] + [VMEM] * 4,
            out_specs=VMEM,
            compiler_params=params(),
            name="first_far",
        )(plan, leaves, taken, moved, target_windows)

    def last_core_parts(one, other_one, two, low, image):
        half_shape = jax.ShapeDtypeStruct(half_units, BF16)
        keep, give = pl.pallas_call(
            functools.partial(last_near_kernel, fields),
            out_shape=(half_shape, half_shape),
            in_specs=[SMEM] * 4 + [VMEM] * 6,
            out_specs=(VMEM, VMEM),
            scratch_shapes=[
                pltpu.VMEM((units + 2 * edge_units, both, LANES), low.dtype),
                pltpu.VMEM(image_shape.shape, F32),
            ],
            compiler_params=params(),
            name="last_near",
        )(core_place, row_place, tile_count, plan, one, other_one, two, low, near_tiles, image)
        return keep, swapped(give, 1)

    def pair_sums(keep, got):
        pair = pl.pallas_call(
            pair_kernel,
            out_shape=jax.ShapeDtypeStruct(keep.shape, BF16),
            in_specs=[VMEM, VMEM],
            out_specs=VMEM,
            compiler_params=params(),
            name="pair",
        )(keep, got)
        arrived = {step: swapped(pair, 2 * step) for step in swap_order(chips)}
        return [pair] + list(arrived.values())

    def half_sum(parts):
        return pl.pallas_call(
            close_kernel,
            out_shape=jax.ShapeDtypeStruct(half_units, F32),
            in_specs=[VMEM] * chips,
            out_specs=VMEM,
            compiler_params=params(),
            name="close",
        )(*parts)

    def whole(mine, theirs):
        return pl.pallas_call(
            functools.partial(assemble_kernel, fields, items, width, slots),
            out_shape=(
                image_shape,
                jax.ShapeDtypeStruct(image_shape.shape, BF16),
                jax.ShapeDtypeStruct((items, fields, 2 * pad_coefs + ITEM_REST), BF16),
            ),
            in_specs=[SMEM, SMEM] + [VMEM] * 4,
            out_specs=(VMEM,) * 3,
            compiler_params=params(),
            name="assemble",
        )(core_place, plan, leaves, mine, theirs, windows)

    partial = near(*from_neighbours(right), right)
    mine = half_sum(pair_sums(*core_parts(partial, exchanged(made))))
    theirs = swapped(mine, 1)
    one = along_row(one_edge(mine, edge_units // 2, True), 0)
    z_all, z_low, made = whole(mine, theirs)
    image = first_far(exchanged(made))
    two = along_row(one_edge(z_low, edge_units, False), 1)
    parts = pair_sums(*last_core_parts(one, swapped(one, 1), two, z_low, image))

    lines = pl.pallas_call(
        functools.partial(gram_kernel, fields),
        out_shape=jax.ShapeDtypeStruct((2 * rows, -(-9 * fields // LANES), LANES), F32),
        in_specs=[SMEM] + [VMEM] * (2 + chips),
        out_specs=VMEM,
        compiler_params=params(),
        name="gram",
    )(core_place, right, z_all, *parts)
    columns = lax.axis_size("col")
    same_chip = [
        [((g + k) // columns * rows + r) * columns + (g + k) % columns for r in range(rows) for k in range(2)]
        for g in range(0, group, 2)
    ]
    sums = lax.all_to_all(lines, EVERY, 0, 0, axis_index_groups=same_chip, tiled=True)
    out = pl.pallas_call(
        functools.partial(final_kernel, fields),
        out_shape=jax.ShapeDtypeStruct((both, panels), F32),
        in_specs=[VMEM] * 3,
        out_specs=VMEM,
        compiler_params=params(),
        name="combine",
    )(sums, right, z_all)
    return out.reshape(right_side.shape)


def krylov_coefficients(sums):
    rr, rz_real, rz_imag, zz, rq_real, rq_imag, zq_real, zq_imag, qq = sums

    def times(left, right):
        return left[0] * right[0] - left[1] * right[1], left[0] * right[1] + left[1] * right[0]

    def conj_times(left, right):
        return left[0] * right[0] + left[1] * right[1], left[0] * right[1] - left[1] * right[0]

    def scale(factor, value):
        return factor * value[0], factor * value[1]

    def plus(*values):
        return sum(v[0] for v in values), sum(v[1] for v in values)

    def size(value):
        return value[0] * value[0] + value[1] * value[1]

    rz, rq, zq = (rz_real, rz_imag), (rq_real, rq_imag), (zq_real, zq_imag)
    beta = jnp.sqrt(rr + EPSILON)
    inv = 1.0 / beta
    norm_one = rr * inv * inv
    product = scale(inv * inv, rz)
    h_first = (0.5 * norm_one + product[0], product[1])
    shift = (h_first[0] - 0.5, h_first[1])
    residue = zz * inv * inv - 2.0 * conj_times(shift, product)[0] + size(shift) * norm_one
    residue = jnp.maximum(residue, 0.0)
    h_sub = jnp.sqrt(residue + EPSILON)
    alpha = inv / h_sub
    gamma = scale(-alpha, shift)
    h_upper = scale(
        inv,
        plus(
            scale(0.5, plus(scale(alpha, rz), scale(rr, gamma))), scale(alpha, rq), times(gamma, rz)
        ),
    )
    second = plus(
        scale(alpha * alpha, zq),
        scale(alpha * zz, gamma),
        scale(alpha, conj_times(gamma, rq)),
        scale(size(gamma), rz),
    )
    h_middle = (0.5 * residue / (h_sub * h_sub) + second[0], second[1])
    keep = (h_middle[0] - 0.5, h_middle[1])
    on_z = plus(gamma, scale(-alpha, keep))
    on_r = plus(scale(-inv, h_upper), scale(-1.0, times(keep, gamma)))
    last = (
        alpha * alpha * qq
        + size(on_z) * zz
        + size(on_r) * rr
        + 2.0
        * (
            conj_times(on_r, times(on_z, rz))[0]
            + alpha * conj_times(on_r, rq)[0]
            + alpha * conj_times(on_z, zq)[0]
        )
    )
    h_last = jnp.sqrt(jnp.maximum(last, 0.0) + EPSILON)
    radius = jnp.sqrt(size(h_first) + h_sub * h_sub)
    cosine = scale(1.0 / radius, h_first)
    sine = h_sub / radius
    upper = plus(conj_times(cosine, h_upper), scale(sine, h_middle))
    lower = plus(times(cosine, h_middle), scale(-sine, h_upper))
    radius_two = jnp.sqrt(size(lower) + h_last * h_last)
    cosine_two = scale(1.0 / radius_two, lower)
    weight_two = scale(-sine * beta / radius_two, (cosine_two[0], -cosine_two[1]))
    goal = scale(beta, (cosine[0], -cosine[1]))
    weight_one = scale(1.0 / radius, plus(goal, scale(-1.0, times(upper, weight_two))))
    on_right = plus(scale(inv, weight_one), times(weight_two, gamma))
    on_image = scale(alpha, weight_two)
    return on_right[0], on_right[1], on_image[0], on_image[1]


def solution(mesh):
    return jax.shard_map(
        local,
        mesh=mesh,
        in_specs=(
            P(None, None, "row"),
            P(None, ("grp", "row", "col"), None, None),
            P(("grp", "row", "col")),
            P(("grp", "row", "col")),
            P(None, "row", None),
            P("row", None),
            P(),
            P("row", None),
            P("row", None),
            P(),
        ),
        out_specs=P(None, None, "row"),
        check_vma=False,
    )
```

```python
import functools

import jax
import jax.numpy as jnp
from jax import lax
from jax.experimental import pallas as pl
from jax.experimental.pallas import tpu as pltpu
from jax.sharding import PartitionSpec as P

REACH = 2
SPAN = 2 * REACH + 1
LANES = 128
EPSILON = 1e-06
GROUP = ("grp", "col")
CODES = 0
PER_ITEM = 5
ITEM_REST = LANES
PIECES = 4
EVERY = ("grp", "row", "col")

F32 = jnp.float32
BF16 = jnp.bfloat16
SMEM = pl.BlockSpec(memory_space=pltpu.SMEM)
VMEM = pl.BlockSpec(memory_space=pltpu.VMEM)
HBM = pl.BlockSpec(memory_space=pltpu.HBM)
ANY = pl.BlockSpec(memory_space=pl.ANY)


def dot_nn(left, right):
    return lax.dot_general(left, right, (((1,), (0,)), ((), ())), preferred_element_type=F32)


def dot_nt(left, right):
    return lax.dot_general(left, right, (((1,), (1,)), ((), ())), preferred_element_type=F32)


def halves(rows):
    if rows.dtype != F32:
        return rows
    high = rows.astype(BF16)
    return jnp.concatenate([high, (rows - high.astype(F32)).astype(BF16)], axis=0)


def joined(sums, count):
    return sums if sums.shape[0] == count else sums[:count] + sums[count:]


def odd_lanes(shape):
    return lax.rem(lax.broadcasted_iota(jnp.int32, shape, 1), 2) == 1


def twice(value, width):
    rows = value.shape[0]
    parts = []
    for k in range(width // LANES):
        first = (k // 2) * LANES
        part = value[:, first : first + LANES]
        if part.shape[1] < LANES:
            part = jnp.concatenate([part, jnp.zeros((rows, LANES - part.shape[1]), part.dtype)], axis=-1)
        lane = lax.broadcasted_iota(jnp.int32, (rows, LANES), 1)
        parts.append(jnp.take_along_axis(part, lax.div(lane, 2) + (k % 2) * (LANES // 2), axis=1))
    return jnp.concatenate(parts, axis=-1)


def from_left(value):
    return pltpu.roll(value, 1, 1)


def from_right(value):
    return pltpu.roll(value, value.shape[1] - 1, 1)


def item_place(slots, item):
    return CODES + slots + PER_ITEM * item


def window_start(leaf_ref, leaf, width):
    units = leaf_ref.shape[1] // LANES
    before = jnp.int32(0)
    for k in range(units):
        before = before + (leaf_ref[0, k * LANES] < leaf).astype(jnp.int32)
    return jnp.clip(before - 1, 0, units - width)


def window_mask(leaves_ref, leaf, unit, rows, width):
    leaves = jnp.concatenate([leaves_ref[unit + k] for k in range(width)], axis=-1)
    return jnp.broadcast_to(leaves, (rows, width * LANES)) == leaf


def window_copies(exp_ref, unit, window_ref, sem, width):
    coefs = exp_ref.shape[0]
    step = -(-coefs // PIECES)
    copies = []
    for p in range(PIECES):
        part = pl.ds(p * step, min(step, coefs - p * step))
        copies.append(
            pltpu.make_async_copy(exp_ref.at[part, pl.ds(unit, width)], window_ref.at[part], sem.at[p])
        )
    return copies


def clear_rest(window_ref, coefs):
    rest = window_ref.shape[0] - coefs
    window_ref[pl.ds(coefs, rest)] = jnp.zeros((rest, *window_ref.shape[1:]), BF16)


def window_rows(window_ref):
    coefs, width = window_ref.shape[:2]
    return jnp.concatenate([window_ref[:, k].reshape(2 * coefs, LANES) for k in range(width)], axis=-1)


def multi_rows(fields, width, leaf, unit, leaves_ref, low_ref, window_ref):
    if len(low_ref.shape) == 2:
        first = pl.multiple_of(unit * LANES, LANES)
        rows = low_ref[:, pl.ds(first, width * LANES)]
    else:
        rows = jnp.concatenate([low_ref[unit + k] for k in range(width)], axis=-1)
    mask = window_mask(leaves_ref, leaf, unit, 2 * fields, width)
    rows = halves(jnp.where(mask, rows.astype(F32), 0.0).astype(rows.dtype))
    total = joined(dot_nt(rows, window_rows(window_ref)), 2 * fields)
    on_real, on_imag = total[:fields], total[fields:]
    odd = odd_lanes(on_real.shape)
    other = jnp.where(odd, from_left(on_imag), from_right(on_imag))
    return jnp.where(odd, -on_real, on_real) - other


def edge_kernel(row_ref, image_ref, one_ref, two_ref):
    edge_of(row_ref, image_ref, one_ref, True)
    edge_of(row_ref, image_ref, two_ref, False)


def one_edge_kernel(early, row_ref, image_ref, out_ref):
    edge_of(row_ref, image_ref, out_ref, early)


def edge_of(row_ref, image_ref, out_ref, early):
    first_edge = (lax.rem(row_ref[0], 2) == 0) if early else (lax.rem(row_ref[0], 2) == 1)
    if len(image_ref.shape) == 2:
        edge = out_ref.shape[1]
        first, last = image_ref[:, :edge], image_ref[:, image_ref.shape[1] - edge :]
    else:
        edge = out_ref.shape[0]
        first, last = image_ref[:edge], image_ref[image_ref.shape[0] - edge :]

    @pl.when(first_edge)
    def _():
        out_ref[...] = first.astype(out_ref.dtype)

    @pl.when(jnp.logical_not(first_edge))
    def _():
        out_ref[...] = last.astype(out_ref.dtype)


def begin_kernel(
    fields, items, width, send, rows, row_ref, own_ref, pick_hbm, leaf_hbm, leaves_hbm,
    target_hbm, offset_hbm, pairs_hbm, right_hbm, exp_ref,
    plan_ref, out_ref, window_ref, leaves_ref, right_ref,
    pick_ref, leaf_ref, target_ref, offset_ref, pairs_ref, sem, window_sem,
):
    loads = [
        pltpu.make_async_copy(source, place, sem.at[k])
        for k, (source, place) in enumerate(
            (
                (leaf_hbm, leaf_ref),
                (pick_hbm, pick_ref),
                (target_hbm, target_ref),
                (offset_hbm, offset_ref),
                (pairs_hbm, pairs_ref),
                (leaves_hbm, leaves_ref),
                (right_hbm, right_ref),
            )
        )
    ]
    for load in loads:
        load.start()
    for i in range(items):
        clear_rest(window_ref.at[i], exp_ref.shape[0])
    slots = pairs_ref.shape[0]
    own = own_ref[0]
    loads[0].wait()
    loads[1].wait()
    row = row_ref[0]

    def partner(i, coming):
        number = own * items + i
        pair, number = lax.div(number, send), lax.rem(number, send)
        other = source_row(row, pair, rows) if coming else target_row(row, pair, rows)
        if coming and own_items_change_cores(rows, items, send):
            number = jnp.where(other == row, 1 - number, number)
        return other, number

    for i in range(items):
        other, number = partner(i, False)
        leaf = pick_ref[other, number, row]
        unit = window_start(leaf_ref, leaf, width)
        place = item_place(slots, i)
        plan_ref[place], plan_ref[place + 1] = leaf, unit
        for copy in window_copies(exp_ref, unit, window_ref.at[i], window_sem.at[i], width):
            copy.start()
    for load in loads[2:]:
        load.wait()
    for s in range(slots):
        plan_ref[CODES + s] = pairs_ref[s]
    for i in range(items):
        place = item_place(slots, i)
        other, number = partner(i, True)
        leaf = target_ref[0, other * send + number]
        plan_ref[place + 2], plan_ref[place + 3] = leaf, window_start(leaf_ref, leaf, width)
        plan_ref[place + 4] = offset_ref[0, other * send + number]
    for i in range(items):
        place = item_place(slots, i)
        leaf, unit = plan_ref[place], plan_ref[place + 1]
        for copy in window_copies(exp_ref, unit, window_ref.at[i], window_sem.at[i], width):
            copy.wait()
        out_ref[i] = multi_rows(fields, width, leaf, unit, leaves_ref, right_ref, window_ref.at[i]).astype(BF16)


def fetch_kernel(items, width, slots, plan_ref, exp_ref, trans_ref, window_ref, moved_ref, trans_buf, sem, trans_sem):
    coefs = trans_ref.shape[3]
    for i in range(items):
        clear_rest(window_ref.at[i], coefs)

    def trans_copy(i):
        offset = plan_ref[item_place(slots, i) + 4]
        return pltpu.make_async_copy(trans_ref.at[offset], trans_buf.at[i], trans_sem.at[i])

    def exp_copies(i):
        unit = plan_ref[item_place(slots, i) + 3]
        return window_copies(exp_ref, unit, window_ref.at[i], sem.at[i], width)

    for i in range(items):
        trans_copy(i).start()
        for copy in exp_copies(i):
            copy.start()
    rest = moved_ref.shape[1] - 2 * coefs
    for i in range(items):
        trans_copy(i).wait()
        moved_ref[i, pl.ds(0, 2 * coefs)] = trans_buf[i].reshape(2 * coefs, coefs)
        moved_ref[i, pl.ds(2 * coefs, rest)] = jnp.zeros((rest, coefs), BF16)
        for copy in exp_copies(i):
            copy.wait()


def edge_places(row_ref, edge, units):
    even = lax.rem(row_ref[0], 2) == 0
    return jnp.where(even, 0, edge + units), jnp.where(even, edge + units, 0)


def part(total, core, keep_ref, give_ref):
    for k in range(keep_ref.shape[0]):
        keep_ref[k] = total[2 * k + core].astype(keep_ref.dtype)
        give_ref[k] = total[2 * k + 1 - core].astype(give_ref.dtype)


def near_kernel(fields, row_ref, count_ref, plan_ref, one_ref, two_ref, here_ref, tiles_ref, out_ref, ext):
    units = out_ref.shape[0]
    edge = (ext.shape[0] - units) // 2
    one_at, two_at = edge_places(row_ref, edge, units)
    for k in range(edge):
        lanes = slice(k * LANES, (k + 1) * LANES)
        ext[one_at + k] = one_ref[:, lanes].astype(ext.dtype)
        ext[two_at + k] = two_ref[:, lanes].astype(ext.dtype)
    for k in range(units):
        ext[edge + k] = here_ref[:, k * LANES : (k + 1) * LANES]
    out_ref[...] = jnp.zeros_like(out_ref)
    near_slots(fields, count_ref, plan_ref, tiles_ref, out_ref, ext)


def last_near_kernel(
    fields, core_ref, row_ref, count_ref, plan_ref, one_ref, other_one_ref, two_ref, here_ref, tiles_ref, image_ref,
    keep_ref, give_ref, ext, total,
):
    units = total.shape[0]
    edge = (ext.shape[0] - units) // 2
    core = core_ref[0]
    one_at, two_at = edge_places(row_ref, edge, units)
    for k in range(edge // 2):
        ext[one_at + 2 * k + core] = one_ref[k]
        ext[one_at + 2 * k + 1 - core] = other_one_ref[k]
    ext[pl.ds(two_at, edge)] = two_ref[...]
    ext[edge : edge + units] = here_ref[...]
    total[...] = jnp.zeros_like(total)
    items, width = image_ref.shape[:2]
    for i in range(items):
        unit = plan_ref[item_place(tiles_ref.shape[1], i) + 3]
        for k in range(width):
            total[unit + k] += image_ref[i, k]
    near_slots(fields, count_ref, plan_ref, tiles_ref, total, ext)
    part(total, core_ref[0], keep_ref, give_ref)


def near_slots(fields, count_ref, plan_ref, tiles_ref, out_ref, ext):
    slots, tile = tiles_ref.shape[1], tiles_ref.shape[2]
    per = tile // LANES
    for s in range(slots):
        code = plan_ref[CODES + s]
        target = lax.div(code, SPAN)
        source = target + lax.rem(code, SPAN)
        rows = halves(jnp.concatenate([ext[source * per + k] for k in range(per)], axis=-1))
        on_real = joined(dot_nt(rows, tiles_ref[0, s]), 2 * fields)
        on_imag = joined(dot_nt(rows, tiles_ref[1, s]), 2 * fields)
        value = jnp.concatenate(
            [on_real[:fields] - on_imag[fields:], on_real[fields:] + on_imag[:fields]], axis=0
        )
        value = jnp.where(s < count_ref[0], value, 0.0)
        for k in range(per):
            out_ref[target * per + k] += value[:, k * LANES : (k + 1) * LANES]


def far_kernel(
    fields, items, width, slots, core_ref, plan_ref, leaves_ref, partial_ref, item_ref, trans_ref, window_ref,
    keep_ref, give_ref, total,
):
    total[...] = partial_ref[...]

    def add(i, unit, image):
        for k in range(width):
            total[unit + k] += image[:, k * LANES : (k + 1) * LANES]

    far_images(fields, items, width, slots, plan_ref, leaves_ref, item_ref, trans_ref, window_ref, add)
    part(total, core_ref[0], keep_ref, give_ref)


def first_far_kernel(
    fields, items, width, slots, plan_ref, leaves_ref, item_ref, trans_ref, window_ref, image_ref
):
    def store(i, unit, image):
        for k in range(width):
            image_ref[i, k] = image[:, k * LANES : (k + 1) * LANES]

    far_images(fields, items, width, slots, plan_ref, leaves_ref, item_ref, trans_ref, window_ref, store)


def far_images(fields, items, width, slots, plan_ref, leaves_ref, item_ref, trans_ref, window_ref, give):
    for i in range(items):
        plain = item_ref[i, :, : trans_ref.shape[1]].astype(F32)
        odd = odd_lanes(plain.shape)
        turned = jnp.where(odd, from_left(plain), -from_right(plain))
        rows = jnp.concatenate([plain, turned], axis=0).astype(BF16)
        local_field = dot_nn(rows, trans_ref[i]).astype(BF16).astype(F32)
        local_field = twice(local_field, plain.shape[1])
        local_real, local_imag = local_field[:fields], local_field[fields:]
        rows = jnp.concatenate(
            [jnp.where(odd, -local_imag, local_real), jnp.where(odd, local_real, local_imag)], axis=0
        ).astype(BF16)
        expansions = window_rows(window_ref.at[i])
        place = item_place(slots, i)
        leaf, unit = plan_ref[place + 2], plan_ref[place + 3]
        mask = window_mask(leaves_ref, leaf, unit, 2 * fields, width)
        image = jnp.where(mask, dot_nn(rows, expansions), 0.0)
        give(i, unit, image)


def pair_kernel(keep_ref, got_ref, out_ref):
    out_ref[...] = (keep_ref[...].astype(F32) + got_ref[...].astype(F32)).astype(out_ref.dtype)


def tree_sum(values):
    while len(values) > 1:
        values = [values[k] + values[k + 1] for k in range(0, len(values), 2)]
    return values[0]


def swap_order(chips):
    return list(range(chips - 1, 0, -1))


def by_step(parts):
    arrived = dict(zip(swap_order(len(parts)), parts[1:]))
    return [parts[0]] + [arrived[step] for step in range(1, len(parts))]


def close_kernel(*refs):
    refs[-1][...] = tree_sum([ref[...].astype(F32) for ref in by_step(refs[:-1])])


def assemble_kernel(
    fields, items, width, slots, core_ref, plan_ref, leaves_ref, mine_ref, theirs_ref, window_ref,
    out_ref, low_ref, made_ref,
):
    core = core_ref[0]
    for k in range(mine_ref.shape[0]):
        for ref, unit in ((mine_ref, 2 * k + core), (theirs_ref, 2 * k + 1 - core)):
            out_ref[unit] = ref[k]
            low_ref[unit] = ref[k].astype(BF16)
    for i in range(items):
        place = item_place(slots, i)
        made = multi_rows(
            fields, width, plan_ref[place], plan_ref[place + 1], leaves_ref, low_ref, window_ref.at[i]
        )
        made_ref[i, :, : made.shape[1]] = made.astype(BF16)


def flat_lines(totals, fields):
    per = LANES // fields
    lane = lax.broadcasted_iota(jnp.int32, (fields, LANES), 1)
    field = lax.broadcasted_iota(jnp.int32, (fields, LANES), 0)
    lines = []
    for first in range(0, len(totals), per):
        line = jnp.zeros((fields, LANES), F32)
        for k, total in enumerate(totals[first : first + per]):
            line = jnp.where(lane == field + k * fields, jnp.sum(total, axis=1, keepdims=True), line)
        lines.append(jnp.sum(line, axis=0, keepdims=True))
    return jnp.concatenate(lines, axis=0)


def columns_of(lines, count, fields):
    per = LANES // fields
    columns = []
    for k in range(lines.shape[0]):
        square = jnp.transpose(jnp.broadcast_to(lines[k : k + 1], (LANES, LANES)))
        columns += [square[j * fields : (j + 1) * fields] for j in range(per)]
    return columns[:count]


def gram_kernel(fields, core_ref, right_ref, image_ref, *refs):
    *parts, out_ref = refs
    totals = None
    for k in range(parts[0].shape[0]):
        unit = 2 * k + core_ref[0]
        r = right_ref[:, pl.ds(pl.multiple_of(unit * LANES, LANES), LANES)]
        z = image_ref[unit]
        q = tree_sum([part[k].astype(F32) for part in by_step(parts)])
        (rr, ri), (zr, zi), (qr, qi) = [(v[:fields], v[fields:]) for v in (r, z, q)]
        products = [
            rr * rr + ri * ri,
            rr * zr + ri * zi,
            rr * zi - ri * zr,
            zr * zr + zi * zi,
            rr * qr + ri * qi,
            rr * qi - ri * qr,
            zr * qr + zi * qi,
            zr * qi - zi * qr,
            qr * qr + qi * qi,
        ]
        totals = products if totals is None else [t + p for t, p in zip(totals, products)]
    out_ref[...] = jnp.broadcast_to(flat_lines(totals, fields)[None], out_ref.shape)


def final_kernel(fields, sums_ref, right_ref, image_ref, out_ref):
    units = image_ref.shape[0]
    sums = columns_of(jnp.sum(sums_ref[...], axis=0), 9, fields)
    a_real, a_imag, b_real, b_imag = krylov_coefficients(sums)
    for k in range(units):
        lanes = slice(k * LANES, (k + 1) * LANES)
        r_real, r_imag = right_ref[:fields, lanes], right_ref[fields:, lanes]
        z_real, z_imag = image_ref[k, :fields], image_ref[k, fields:]
        out_ref[:fields, lanes] = a_real * r_real - a_imag * r_imag + b_real * z_real - b_imag * z_imag
        out_ref[fields:, lanes] = a_real * r_imag + a_imag * r_real + b_real * z_imag + b_imag * z_real


def params(mebibytes=16):
    return pltpu.CompilerParams(vmem_limit_bytes=mebibytes * 1024 * 1024)


def is_power(count):
    return count & (count - 1) == 0


def reversed_bits(value, count):
    bits = count.bit_length() - 1
    return sum(((value >> k) & 1) << (bits - 1 - k) for k in range(bits))


def target_row(row, pair, rows):
    if not is_power(rows):
        return (pair - row + rows) % rows
    return pair ^ reversed_bits(row, rows)


def source_row(row, pair, rows):
    if not is_power(rows):
        return (pair - row + rows) % rows
    return reversed_bits(pair ^ row, rows)


def own_items_change_cores(rows, items, send):
    return items == 1 and send == 2


def item_route(rows, group, columns, send):
    items = rows * send // group

    def flat(r, g):
        return (g // columns * rows + r) * columns + g % columns

    def target(r, g, pair):
        d = target_row(r, pair, rows)
        return flat(d, g ^ 1 if d == r and own_items_change_cores(rows, items, send) else g)

    assert items * group == rows * send and (items % send == 0 or send % items == 0)
    routes = []
    for first in range(0, items, send):
        pairs = [(g * items + first) // send for g in range(group)]
        routes.append([(flat(r, g), target(r, g, pairs[g])) for r in range(rows) for g in range(group)])
    return items, routes


def local(
    right_side,
    near_tiles,
    tile_pairs,
    tile_count,
    panel_expansions,
    leaf_of_panel,
    far_pick,
    far_target,
    far_offset,
    translations,
):
    fields, panels = right_side.shape[1:]
    coefs = panel_expansions.shape[2]
    tile = near_tiles.shape[2]
    send = far_pick.shape[2]
    rows = lax.axis_size("row")
    group = lax.axis_size("grp") * lax.axis_size("col")
    row_here = lax.axis_index("row")
    own = lax.axis_index("grp") * lax.axis_size("col") + lax.axis_index("col")
    both = 2 * fields
    units = panels // LANES
    edge = REACH * tile
    edge_units = edge // LANES
    width = tile // LANES + 1
    items, routes = item_route(rows, group, lax.axis_size("col"), send)

    assert rows % 2 == 0
    neighbours = [[(r - 1 + 2 * (r % 2)) % rows for r in range(rows)], [r + 1 - 2 * (r % 2) for r in range(rows)]]
    own_place, row_place = own.reshape(1), row_here.reshape(1)
    core_place = lax.rem(own, 2).reshape(1)
    slots = near_tiles.shape[1]
    pad_coefs = -(-coefs // 8) * 8
    chips = group // 2
    assert group == 2 * chips and chips & (chips - 1) == 0 and LANES % fields == 0
    window_shape = jax.ShapeDtypeStruct((items, pad_coefs, width, 2, LANES), BF16)
    item_shape = jax.ShapeDtypeStruct((items, fields, 2 * pad_coefs), BF16)
    half_units = (units // 2, both, LANES)
    assert units % 2 == 0 and edge_units % 2 == 0

    def in_hbm(value):
        return pltpu.with_memory_space_constraint(value, pltpu.HBM)

    leaves = leaf_of_panel.reshape(units, 1, LANES)
    expansions = panel_expansions.transpose(2, 0, 1).reshape(coefs, 2, units, LANES).transpose(0, 2, 1, 3)
    expansions = in_hbm(expansions)
    moves = in_hbm(translations.transpose(0, 2, 1, 3))
    picks = far_pick.transpose(0, 2, 1)

    plan, made, windows, leaves, right = pl.pallas_call(
        functools.partial(begin_kernel, fields, items, width, send, rows),
        out_shape=(
            pltpu.SMEM((item_place(slots, items),), jnp.int32),
            item_shape,
            pltpu.VMEM(window_shape.shape, BF16),
            jax.ShapeDtypeStruct(leaves.shape, jnp.int32),
            jax.ShapeDtypeStruct((both, panels), F32),
        ),
        in_specs=[SMEM] * 2 + [HBM] * 8,
        out_specs=(SMEM,) + (VMEM,) * 4,
        scratch_shapes=[
            pltpu.SMEM(value.shape, jnp.int32)
            for value in (picks, leaf_of_panel, far_target, far_offset, tile_pairs)
        ]
        + [
            pltpu.SemaphoreType.DMA((7,)),
            pltpu.SemaphoreType.DMA((items, PIECES)),
        ],
        compiler_params=params(),
        name="begin",
    )(
        row_place,
        own_place,
        in_hbm(picks),
        in_hbm(leaf_of_panel),
        in_hbm(leaves),
        in_hbm(far_target),
        in_hbm(far_offset),
        in_hbm(tile_pairs),
        in_hbm(right_side.reshape(both, panels)),
        expansions,
    )

    def exchanged(made):
        parts = [
            lax.ppermute(made[k * send : k * send + min(send, items)], EVERY, route) for k, route in enumerate(routes)
        ]
        return parts[0] if len(parts) == 1 else jnp.concatenate(parts)

    def along_row(value, which):
        return lax.ppermute(value, "row", list(enumerate(neighbours[which])))

    def from_neighbours(image):
        one, two = pl.pallas_call(
            edge_kernel,
            out_shape=(jax.ShapeDtypeStruct((both, edge), BF16),) * 2,
            in_specs=[SMEM, VMEM],
            out_specs=(VMEM, VMEM),
            compiler_params=params(),
            name="edges",
        )(row_place, image)
        return along_row(one, 0), along_row(two, 1)

    def one_edge(image, edge_units, early):
        return pl.pallas_call(
            functools.partial(one_edge_kernel, early),
            out_shape=jax.ShapeDtypeStruct((edge_units, both, LANES), BF16),
            in_specs=[SMEM, VMEM],
            out_specs=VMEM,
            compiler_params=params(),
            name="edge",
        )(row_place, image)

    image_shape = jax.ShapeDtypeStruct((units, both, LANES), F32)
    target_windows, moved = pl.pallas_call(
        functools.partial(fetch_kernel, items, width, slots),
        out_shape=(
            pltpu.VMEM(window_shape.shape, BF16),
            pltpu.VMEM((items, 2 * pad_coefs, coefs), BF16),
        ),
        in_specs=[SMEM, HBM, HBM],
        out_specs=(VMEM, VMEM),
        scratch_shapes=[
            pltpu.VMEM((items, coefs, 2, coefs), BF16),
            pltpu.SemaphoreType.DMA((items, PIECES)),
            pltpu.SemaphoreType.DMA((items,)),
        ],
        compiler_params=params(24),
        cost_estimate=pl.CostEstimate(flops=0, bytes_accessed=6 * window_shape.size, transcendentals=0),
        name="fetch",
    )(plan, expansions, moves)

    def swapped(value, step):
        return lax.ppermute(value, GROUP, [(g, g ^ step) for g in range(group)])

    def near(one, two, low):
        return pl.pallas_call(
            functools.partial(near_kernel, fields),
            out_shape=image_shape,
            in_specs=[SMEM] * 3 + [VMEM] * 4,
            out_specs=VMEM,
            scratch_shapes=[pltpu.VMEM((units + 2 * edge_units, both, LANES), low.dtype)],
            compiler_params=params(),
            cost_estimate=pl.CostEstimate(
                flops=8 * fields * near_tiles.size // 2, bytes_accessed=2 * near_tiles.size, transcendentals=0
            ),
            name="near",
        )(row_place, tile_count, plan, one, two, low, near_tiles)

    def core_parts(partial, taken):
        half_shape = jax.ShapeDtypeStruct(half_units, F32)
        keep, give = pl.pallas_call(
            functools.partial(far_kernel, fields, items, width, slots),
            out_shape=(half_shape, half_shape),
            in_specs=[SMEM, SMEM] + [VMEM] * 5,
            out_specs=(VMEM, VMEM),
            scratch_shapes=[pltpu.VMEM(image_shape.shape, F32)],
            compiler_params=params(),
            name="far",
        )(core_place, plan, leaves, partial, taken, moved, target_windows)
        return keep, swapped(give, 1)

    def first_far(taken):
        return pl.pallas_call(
            functools.partial(first_far_kernel, fields, items, width, slots),
            out_shape=jax.ShapeDtypeStruct((items, width, both, LANES), F32),
            in_specs=[SMEM] + [VMEM] * 4,
            out_specs=VMEM,
            compiler_params=params(),
            name="first_far",
        )(plan, leaves, taken, moved, target_windows)

    def last_core_parts(one, other_one, two, low, image):
        half_shape = jax.ShapeDtypeStruct(half_units, BF16)
        keep, give = pl.pallas_call(
            functools.partial(last_near_kernel, fields),
            out_shape=(half_shape, half_shape),
            in_specs=[SMEM] * 4 + [VMEM] * 6,
            out_specs=(VMEM, VMEM),
            scratch_shapes=[
                pltpu.VMEM((units + 2 * edge_units, both, LANES), low.dtype),
                pltpu.VMEM(image_shape.shape, F32),
            ],
            compiler_params=params(),
            name="last_near",
        )(core_place, row_place, tile_count, plan, one, other_one, two, low, near_tiles, image)
        return keep, swapped(give, 1)

    def pair_sums(keep, got):
        pair = pl.pallas_call(
            pair_kernel,
            out_shape=jax.ShapeDtypeStruct(keep.shape, BF16),
            in_specs=[VMEM, VMEM],
            out_specs=VMEM,
            compiler_params=params(),
            name="pair",
        )(keep, got)
        arrived = {step: swapped(pair, 2 * step) for step in swap_order(chips)}
        return [pair] + list(arrived.values())

    def half_sum(parts):
        return pl.pallas_call(
            close_kernel,
            out_shape=jax.ShapeDtypeStruct(half_units, F32),
            in_specs=[VMEM] * chips,
            out_specs=VMEM,
            compiler_params=params(),
            name="close",
        )(*parts)

    def whole(mine, theirs):
        return pl.pallas_call(
            functools.partial(assemble_kernel, fields, items, width, slots),
            out_shape=(
                image_shape,
                jax.ShapeDtypeStruct(image_shape.shape, BF16),
                jax.ShapeDtypeStruct((items, fields, 2 * pad_coefs + ITEM_REST), BF16),
            ),
            in_specs=[SMEM, SMEM] + [VMEM] * 4,
            out_specs=(VMEM,) * 3,
            compiler_params=params(),
            name="assemble",
        )(core_place, plan, leaves, mine, theirs, windows)

    partial = near(*from_neighbours(right), right)
    mine = half_sum(pair_sums(*core_parts(partial, exchanged(made))))
    theirs = swapped(mine, 1)
    one = along_row(one_edge(mine, edge_units // 2, True), 0)
    z_all, z_low, made = whole(mine, theirs)
    image = first_far(exchanged(made))
    two = along_row(one_edge(z_low, edge_units, False), 1)
    parts = pair_sums(*last_core_parts(one, swapped(one, 1), two, z_low, image))

    lines = pl.pallas_call(
        functools.partial(gram_kernel, fields),
        out_shape=jax.ShapeDtypeStruct((2 * rows, -(-9 * fields // LANES), LANES), F32),
        in_specs=[SMEM] + [VMEM] * (2 + chips),
        out_specs=VMEM,
        compiler_params=params(),
        name="gram",
    )(core_place, right, z_all, *parts)
    columns = lax.axis_size("col")
    same_chip = [
        [((g + k) // columns * rows + r) * columns + (g + k) % columns for r in range(rows) for k in range(2)]
        for g in range(0, group, 2)
    ]
    sums = lax.all_to_all(lines, EVERY, 0, 0, axis_index_groups=same_chip, tiled=True)
    out = pl.pallas_call(
        functools.partial(final_kernel, fields),
        out_shape=jax.ShapeDtypeStruct((both, panels), F32),
        in_specs=[VMEM] * 3,
        out_specs=VMEM,
        compiler_params=params(),
        name="combine",
    )(sums, right, z_all)
    return out.reshape(right_side.shape)


def krylov_coefficients(sums):
    rr, rz_real, rz_imag, zz, rq_real, rq_imag, zq_real, zq_imag, qq = sums

    def times(left, right):
        return left[0] * right[0] - left[1] * right[1], left[0] * right[1] + left[1] * right[0]

    def conj_times(left, right):
        return left[0] * right[0] + left[1] * right[1], left[0] * right[1] - left[1] * right[0]

    def scale(factor, value):
        return factor * value[0], factor * value[1]

    def plus(*values):
        return sum(v[0] for v in values), sum(v[1] for v in values)

    def size(value):
        return value[0] * value[0] + value[1] * value[1]

    rz, rq, zq = (rz_real, rz_imag), (rq_real, rq_imag), (zq_real, zq_imag)
    beta = jnp.sqrt(rr + EPSILON)
    inv = 1.0 / beta
    norm_one = rr * inv * inv
    product = scale(inv * inv, rz)
    h_first = (0.5 * norm_one + product[0], product[1])
    shift = (h_first[0] - 0.5, h_first[1])
    residue = zz * inv * inv - 2.0 * conj_times(shift, product)[0] + size(shift) * norm_one
    residue = jnp.maximum(residue, 0.0)
    h_sub = jnp.sqrt(residue + EPSILON)
    alpha = inv / h_sub
    gamma = scale(-alpha, shift)
    h_upper = scale(
        inv,
        plus(
            scale(0.5, plus(scale(alpha, rz), scale(rr, gamma))), scale(alpha, rq), times(gamma, rz)
        ),
    )
    second = plus(
        scale(alpha * alpha, zq),
        scale(alpha * zz, gamma),
        scale(alpha, conj_times(gamma, rq)),
        scale(size(gamma), rz),
    )
    h_middle = (0.5 * residue / (h_sub * h_sub) + second[0], second[1])
    keep = (h_middle[0] - 0.5, h_middle[1])
    on_z = plus(gamma, scale(-alpha, keep))
    on_r = plus(scale(-inv, h_upper), scale(-1.0, times(keep, gamma)))
    last = (
        alpha * alpha * qq
        + size(on_z) * zz
        + size(on_r) * rr
        + 2.0
        * (
            conj_times(on_r, times(on_z, rz))[0]
            + alpha * conj_times(on_r, rq)[0]
            + alpha * conj_times(on_z, zq)[0]
        )
    )
    h_last = jnp.sqrt(jnp.maximum(last, 0.0) + EPSILON)
    radius = jnp.sqrt(size(h_first) + h_sub * h_sub)
    cosine = scale(1.0 / radius, h_first)
    sine = h_sub / radius
    upper = plus(conj_times(cosine, h_upper), scale(sine, h_middle))
    lower = plus(times(cosine, h_middle), scale(-sine, h_upper))
    radius_two = jnp.sqrt(size(lower) + h_last * h_last)
    cosine_two = scale(1.0 / radius_two, lower)
    weight_two = scale(-sine * beta / radius_two, (cosine_two[0], -cosine_two[1]))
    goal = scale(beta, (cosine[0], -cosine[1]))
    weight_one = scale(1.0 / radius, plus(goal, scale(-1.0, times(upper, weight_two))))
    on_right = plus(scale(inv, weight_one), times(weight_two, gamma))
    on_image = scale(alpha, weight_two)
    return on_right[0], on_right[1], on_image[0], on_image[1]


def solution(mesh):
    return jax.shard_map(
        local,
        mesh=mesh,
        in_specs=(
            P(None, None, "row"),
            P(None, ("grp", "row", "col"), None, None),
            P(("grp", "row", "col")),
            P(("grp", "row", "col")),
            P(None, "row", None),
            P("row", None),
            P(),
            P("row", None),
            P("row", None),
            P(),
        ),
        out_specs=P(None, None, "row"),
        check_vma=False,
    )
```

```python
import functools

import jax
import jax.numpy as jnp
from jax import lax
from jax.experimental import pallas as pl
from jax.experimental.pallas import tpu as pltpu
from jax.sharding import PartitionSpec as P

REACH = 2
SPAN = 2 * REACH + 1
LANES = 128
EPSILON = 1e-06
GROUP = ("grp", "col")
CODES = 0
PER_ITEM = 5
ITEM_REST = LANES
PIECES = 4
EVERY = ("grp", "row", "col")

F32 = jnp.float32
BF16 = jnp.bfloat16
SMEM = pl.BlockSpec(memory_space=pltpu.SMEM)
VMEM = pl.BlockSpec(memory_space=pltpu.VMEM)
HBM = pl.BlockSpec(memory_space=pltpu.HBM)
ANY = pl.BlockSpec(memory_space=pl.ANY)


def dot_nn(left, right):
    return lax.dot_general(left, right, (((1,), (0,)), ((), ())), preferred_element_type=F32)


def dot_nt(left, right):
    return lax.dot_general(left, right, (((1,), (1,)), ((), ())), preferred_element_type=F32)


def halves(rows):
    if rows.dtype != F32:
        return rows
    high = rows.astype(BF16)
    return jnp.concatenate([high, (rows - high.astype(F32)).astype(BF16)], axis=0)


def joined(sums, count):
    return sums if sums.shape[0] == count else sums[:count] + sums[count:]


def odd_lanes(shape):
    return lax.rem(lax.broadcasted_iota(jnp.int32, shape, 1), 2) == 1


def twice(value, width):
    rows = value.shape[0]
    parts = []
    for k in range(width // LANES):
        first = (k // 2) * LANES
        part = value[:, first : first + LANES]
        if part.shape[1] < LANES:
            part = jnp.concatenate([part, jnp.zeros((rows, LANES - part.shape[1]), part.dtype)], axis=-1)
        lane = lax.broadcasted_iota(jnp.int32, (rows, LANES), 1)
        parts.append(jnp.take_along_axis(part, lax.div(lane, 2) + (k % 2) * (LANES // 2), axis=1))
    return jnp.concatenate(parts, axis=-1)


def from_left(value):
    return pltpu.roll(value, 1, 1)


def from_right(value):
    return pltpu.roll(value, value.shape[1] - 1, 1)


def item_place(slots, item):
    return CODES + slots + PER_ITEM * item


def window_start(leaf_ref, leaf, width):
    units = leaf_ref.shape[1] // LANES
    before = jnp.int32(0)
    for k in range(units):
        before = before + (leaf_ref[0, k * LANES] < leaf).astype(jnp.int32)
    return jnp.clip(before - 1, 0, units - width)


def window_mask(leaves_ref, leaf, unit, rows, width):
    leaves = jnp.concatenate([leaves_ref[unit + k] for k in range(width)], axis=-1)
    return jnp.broadcast_to(leaves, (rows, width * LANES)) == leaf


def window_copies(exp_ref, unit, window_ref, sem, width):
    coefs = exp_ref.shape[0]
    step = -(-coefs // PIECES)
    copies = []
    for p in range(PIECES):
        part = pl.ds(p * step, min(step, coefs - p * step))
        copies.append(
            pltpu.make_async_copy(exp_ref.at[part, pl.ds(unit, width)], window_ref.at[part], sem.at[p])
        )
    return copies


def clear_rest(window_ref, coefs):
    rest = window_ref.shape[0] - coefs
    window_ref[pl.ds(coefs, rest)] = jnp.zeros((rest, *window_ref.shape[1:]), BF16)


def window_rows(window_ref):
    coefs, width = window_ref.shape[:2]
    return jnp.concatenate([window_ref[:, k].reshape(2 * coefs, LANES) for k in range(width)], axis=-1)


def multi_rows(fields, width, leaf, unit, leaves_ref, low_ref, window_ref):
    if len(low_ref.shape) == 2:
        first = pl.multiple_of(unit * LANES, LANES)
        rows = low_ref[:, pl.ds(first, width * LANES)]
    else:
        rows = jnp.concatenate([low_ref[unit + k] for k in range(width)], axis=-1)
    mask = window_mask(leaves_ref, leaf, unit, 2 * fields, width)
    rows = halves(jnp.where(mask, rows.astype(F32), 0.0).astype(rows.dtype))
    total = joined(dot_nt(rows, window_rows(window_ref)), 2 * fields)
    on_real, on_imag = total[:fields], total[fields:]
    odd = odd_lanes(on_real.shape)
    other = jnp.where(odd, from_left(on_imag), from_right(on_imag))
    return jnp.where(odd, -on_real, on_real) - other


def edge_kernel(row_ref, image_ref, one_ref, two_ref):
    edge_of(row_ref, image_ref, one_ref, True)
    edge_of(row_ref, image_ref, two_ref, False)


def one_edge_kernel(early, row_ref, image_ref, out_ref):
    edge_of(row_ref, image_ref, out_ref, early)


def edge_of(row_ref, image_ref, out_ref, early):
    first_edge = (lax.rem(row_ref[0], 2) == 0) if early else (lax.rem(row_ref[0], 2) == 1)
    if len(image_ref.shape) == 2:
        edge = out_ref.shape[1]
        first, last = image_ref[:, :edge], image_ref[:, image_ref.shape[1] - edge :]
    else:
        edge = out_ref.shape[0]
        first, last = image_ref[:edge], image_ref[image_ref.shape[0] - edge :]

    @pl.when(first_edge)
    def _():
        out_ref[...] = first.astype(out_ref.dtype)

    @pl.when(jnp.logical_not(first_edge))
    def _():
        out_ref[...] = last.astype(out_ref.dtype)


def begin_kernel(
    fields, items, width, send, rows, row_ref, own_ref, pick_hbm, leaf_hbm, leaves_hbm,
    target_hbm, offset_hbm, pairs_hbm, right_hbm, exp_ref,
    plan_ref, out_ref, window_ref, leaves_ref, right_ref,
    pick_ref, leaf_ref, target_ref, offset_ref, pairs_ref, sem, window_sem,
):
    loads = [
        pltpu.make_async_copy(source, place, sem.at[k])
        for k, (source, place) in enumerate(
            (
                (leaf_hbm, leaf_ref),
                (pick_hbm, pick_ref),
                (target_hbm, target_ref),
                (offset_hbm, offset_ref),
                (pairs_hbm, pairs_ref),
                (leaves_hbm, leaves_ref),
                (right_hbm, right_ref),
            )
        )
    ]
    for load in loads:
        load.start()
    for i in range(items):
        clear_rest(window_ref.at[i], exp_ref.shape[0])
    slots = pairs_ref.shape[0]
    own = own_ref[0]
    loads[0].wait()
    loads[1].wait()
    row = row_ref[0]

    def partner(i, coming):
        number = own * items + i
        pair, number = lax.div(number, send), lax.rem(number, send)
        other = source_row(row, pair, rows) if coming else target_row(row, pair, rows)
        if coming and own_items_change_cores(rows, items, send):
            number = jnp.where(other == row, 1 - number, number)
        return other, number

    for i in range(items):
        other, number = partner(i, False)
        leaf = pick_ref[other, number, row]
        unit = window_start(leaf_ref, leaf, width)
        place = item_place(slots, i)
        plan_ref[place], plan_ref[place + 1] = leaf, unit
        for copy in window_copies(exp_ref, unit, window_ref.at[i], window_sem.at[i], width):
            copy.start()
    for load in loads[2:]:
        load.wait()
    for s in range(slots):
        plan_ref[CODES + s] = pairs_ref[s]
    for i in range(items):
        place = item_place(slots, i)
        other, number = partner(i, True)
        leaf = target_ref[0, other * send + number]
        plan_ref[place + 2], plan_ref[place + 3] = leaf, window_start(leaf_ref, leaf, width)
        plan_ref[place + 4] = offset_ref[0, other * send + number]
    for i in range(items):
        place = item_place(slots, i)
        leaf, unit = plan_ref[place], plan_ref[place + 1]
        for copy in window_copies(exp_ref, unit, window_ref.at[i], window_sem.at[i], width):
            copy.wait()
        out_ref[i] = multi_rows(fields, width, leaf, unit, leaves_ref, right_ref, window_ref.at[i]).astype(BF16)


def fetch_kernel(items, width, slots, plan_ref, exp_ref, trans_ref, window_ref, moved_ref, trans_buf, sem, trans_sem):
    coefs = trans_ref.shape[3]
    for i in range(items):
        clear_rest(window_ref.at[i], coefs)

    def trans_copy(i):
        offset = plan_ref[item_place(slots, i) + 4]
        return pltpu.make_async_copy(trans_ref.at[offset], trans_buf.at[i], trans_sem.at[i])

    def exp_copies(i):
        unit = plan_ref[item_place(slots, i) + 3]
        return window_copies(exp_ref, unit, window_ref.at[i], sem.at[i], width)

    for i in range(items):
        trans_copy(i).start()
        for copy in exp_copies(i):
            copy.start()
    rest = moved_ref.shape[1] - 2 * coefs
    for i in range(items):
        trans_copy(i).wait()
        moved_ref[i, pl.ds(0, 2 * coefs)] = trans_buf[i].reshape(2 * coefs, coefs)
        moved_ref[i, pl.ds(2 * coefs, rest)] = jnp.zeros((rest, coefs), BF16)
        for copy in exp_copies(i):
            copy.wait()


def edge_places(row_ref, edge, units):
    even = lax.rem(row_ref[0], 2) == 0
    return jnp.where(even, 0, edge + units), jnp.where(even, edge + units, 0)


def part(total, core, keep_ref, give_ref):
    for k in range(keep_ref.shape[0]):
        keep_ref[k] = total[2 * k + core].astype(keep_ref.dtype)
        give_ref[k] = total[2 * k + 1 - core].astype(give_ref.dtype)


def near_kernel(fields, row_ref, count_ref, plan_ref, one_ref, two_ref, here_ref, tiles_ref, out_ref, ext):
    units = out_ref.shape[0]
    edge = (ext.shape[0] - units) // 2
    one_at, two_at = edge_places(row_ref, edge, units)
    for k in range(edge):
        lanes = slice(k * LANES, (k + 1) * LANES)
        ext[one_at + k] = one_ref[:, lanes].astype(ext.dtype)
        ext[two_at + k] = two_ref[:, lanes].astype(ext.dtype)
    for k in range(units):
        ext[edge + k] = here_ref[:, k * LANES : (k + 1) * LANES]
    out_ref[...] = jnp.zeros_like(out_ref)
    near_slots(fields, count_ref, plan_ref, tiles_ref, out_ref, ext)


def last_near_kernel(
    fields, core_ref, row_ref, count_ref, plan_ref, one_ref, other_one_ref, two_ref, here_ref, tiles_ref, image_ref,
    keep_ref, give_ref, ext, total,
):
    units = total.shape[0]
    edge = (ext.shape[0] - units) // 2
    core = core_ref[0]
    one_at, two_at = edge_places(row_ref, edge, units)
    for k in range(edge // 2):
        ext[one_at + 2 * k + core] = one_ref[k]
        ext[one_at + 2 * k + 1 - core] = other_one_ref[k]
    ext[pl.ds(two_at, edge)] = two_ref[...]
    ext[edge : edge + units] = here_ref[...]
    total[...] = jnp.zeros_like(total)
    items, width = image_ref.shape[:2]
    for i in range(items):
        unit = plan_ref[item_place(tiles_ref.shape[1], i) + 3]
        for k in range(width):
            total[unit + k] += image_ref[i, k]
    near_slots(fields, count_ref, plan_ref, tiles_ref, total, ext)
    part(total, core_ref[0], keep_ref, give_ref)


def near_slots(fields, count_ref, plan_ref, tiles_ref, out_ref, ext):
    slots, tile = tiles_ref.shape[1], tiles_ref.shape[2]
    per = tile // LANES
    for s in range(slots):
        code = plan_ref[CODES + s]
        target = lax.div(code, SPAN)
        source = target + lax.rem(code, SPAN)
        rows = halves(jnp.concatenate([ext[source * per + k] for k in range(per)], axis=-1))
        on_real = joined(dot_nt(rows, tiles_ref[0, s]), 2 * fields)
        on_imag = joined(dot_nt(rows, tiles_ref[1, s]), 2 * fields)
        value = jnp.concatenate(
            [on_real[:fields] - on_imag[fields:], on_real[fields:] + on_imag[:fields]], axis=0
        )
        value = jnp.where(s < count_ref[0], value, 0.0)
        for k in range(per):
            out_ref[target * per + k] += value[:, k * LANES : (k + 1) * LANES]


def far_kernel(
    fields, items, width, slots, core_ref, plan_ref, leaves_ref, partial_ref, item_ref, trans_ref, window_ref,
    keep_ref, give_ref, total,
):
    total[...] = partial_ref[...]

    def add(i, unit, image):
        for k in range(width):
            total[unit + k] += image[:, k * LANES : (k + 1) * LANES]

    far_images(fields, items, width, slots, plan_ref, leaves_ref, item_ref, trans_ref, window_ref, add)
    part(total, core_ref[0], keep_ref, give_ref)


def first_far_kernel(
    fields, items, width, slots, plan_ref, leaves_ref, item_ref, trans_ref, window_ref, image_ref
):
    def store(i, unit, image):
        for k in range(width):
            image_ref[i, k] = image[:, k * LANES : (k + 1) * LANES]

    far_images(fields, items, width, slots, plan_ref, leaves_ref, item_ref, trans_ref, window_ref, store)


def far_images(fields, items, width, slots, plan_ref, leaves_ref, item_ref, trans_ref, window_ref, give):
    for i in range(items):
        plain = item_ref[i, :, : trans_ref.shape[1]].astype(F32)
        odd = odd_lanes(plain.shape)
        turned = jnp.where(odd, from_left(plain), -from_right(plain))
        rows = jnp.concatenate([plain, turned], axis=0).astype(BF16)
        local_field = dot_nn(rows, trans_ref[i]).astype(BF16).astype(F32)
        local_field = twice(local_field, plain.shape[1])
        local_real, local_imag = local_field[:fields], local_field[fields:]
        rows = jnp.concatenate(
            [jnp.where(odd, -local_imag, local_real), jnp.where(odd, local_real, local_imag)], axis=0
        ).astype(BF16)
        expansions = window_rows(window_ref.at[i])
        place = item_place(slots, i)
        leaf, unit = plan_ref[place + 2], plan_ref[place + 3]
        mask = window_mask(leaves_ref, leaf, unit, 2 * fields, width)
        image = jnp.where(mask, dot_nn(rows, expansions), 0.0)
        give(i, unit, image)


def fold_kernel(chip_ref, keep_ref, got_ref, own_ref, *out_refs):
    share = own_ref.shape[0]
    steps = [0] + swap_order(1 + len(out_refs))
    for step, out_ref in zip(steps, (own_ref,) + out_refs):
        for k in range(share):
            unit = lax.bitwise_xor(chip_ref[0], step) * share + k
            out_ref[k] = (keep_ref[unit].astype(F32) + got_ref[unit].astype(F32)).astype(out_ref.dtype)


def pair_kernel(keep_ref, got_ref, out_ref):
    out_ref[...] = (keep_ref[...].astype(F32) + got_ref[...].astype(F32)).astype(out_ref.dtype)


def tree_sum(values):
    while len(values) > 1:
        values = [values[k] + values[k + 1] for k in range(0, len(values), 2)]
    return values[0]


def swap_order(chips):
    return list(range(chips - 1, 0, -1))


def by_step(parts):
    arrived = dict(zip(swap_order(len(parts)), parts[1:]))
    return [parts[0]] + [arrived[step] for step in range(1, len(parts))]


def close_kernel(*refs):
    refs[-1][...] = tree_sum([ref[...].astype(F32) for ref in by_step(refs[:-1])])


def assemble_kernel(
    fields, items, width, slots, core_ref, plan_ref, leaves_ref, mine_ref, theirs_ref, window_ref,
    out_ref, low_ref, made_ref,
):
    core = core_ref[0]
    for k in range(mine_ref.shape[0]):
        for ref, unit in ((mine_ref, 2 * k + core), (theirs_ref, 2 * k + 1 - core)):
            out_ref[unit] = ref[k]
            low_ref[unit] = ref[k].astype(BF16)
    for i in range(items):
        place = item_place(slots, i)
        made = multi_rows(
            fields, width, plan_ref[place], plan_ref[place + 1], leaves_ref, low_ref, window_ref.at[i]
        )
        made_ref[i, :, : made.shape[1]] = made.astype(BF16)


def flat_lines(totals, fields):
    per = LANES // fields
    lane = lax.broadcasted_iota(jnp.int32, (fields, LANES), 1)
    field = lax.broadcasted_iota(jnp.int32, (fields, LANES), 0)
    lines = []
    for first in range(0, len(totals), per):
        line = jnp.zeros((fields, LANES), F32)
        for k, total in enumerate(totals[first : first + per]):
            line = jnp.where(lane == field + k * fields, jnp.sum(total, axis=1, keepdims=True), line)
        lines.append(jnp.sum(line, axis=0, keepdims=True))
    return jnp.concatenate(lines, axis=0)


def columns_of(lines, count, fields):
    per = LANES // fields
    columns = []
    for k in range(lines.shape[0]):
        square = jnp.transpose(jnp.broadcast_to(lines[k : k + 1], (LANES, LANES)))
        columns += [square[j * fields : (j + 1) * fields] for j in range(per)]
    return columns[:count]


def gram_kernel(fields, core_ref, first_ref, right_ref, image_ref, *refs):
    *parts, out_ref = refs
    totals = None
    for k in range(parts[0].shape[0]):
        unit = 2 * (first_ref[0] + k) + core_ref[0]
        r = right_ref[:, pl.ds(pl.multiple_of(unit * LANES, LANES), LANES)]
        z = image_ref[unit]
        q = tree_sum([part[k].astype(F32) for part in by_step(parts)])
        (rr, ri), (zr, zi), (qr, qi) = [(v[:fields], v[fields:]) for v in (r, z, q)]
        products = [
            rr * rr + ri * ri,
            rr * zr + ri * zi,
            rr * zi - ri * zr,
            zr * zr + zi * zi,
            rr * qr + ri * qi,
            rr * qi - ri * qr,
            zr * qr + zi * qi,
            zr * qi - zi * qr,
            qr * qr + qi * qi,
        ]
        totals = products if totals is None else [t + p for t, p in zip(totals, products)]
    out_ref[...] = jnp.broadcast_to(flat_lines(totals, fields)[None], out_ref.shape)


def final_kernel(fields, sums_ref, right_ref, image_ref, out_ref):
    units = image_ref.shape[0]
    sums = columns_of(jnp.sum(sums_ref[...], axis=0), 9, fields)
    a_real, a_imag, b_real, b_imag = krylov_coefficients(sums)
    for k in range(units):
        lanes = slice(k * LANES, (k + 1) * LANES)
        r_real, r_imag = right_ref[:fields, lanes], right_ref[fields:, lanes]
        z_real, z_imag = image_ref[k, :fields], image_ref[k, fields:]
        out_ref[:fields, lanes] = a_real * r_real - a_imag * r_imag + b_real * z_real - b_imag * z_imag
        out_ref[fields:, lanes] = a_real * r_imag + a_imag * r_real + b_real * z_imag + b_imag * z_real


def params(mebibytes=16):
    return pltpu.CompilerParams(vmem_limit_bytes=mebibytes * 1024 * 1024)


def is_power(count):
    return count & (count - 1) == 0


def reversed_bits(value, count):
    bits = count.bit_length() - 1
    return sum(((value >> k) & 1) << (bits - 1 - k) for k in range(bits))


def target_row(row, pair, rows):
    if not is_power(rows):
        return (pair - row + rows) % rows
    return pair ^ reversed_bits(row, rows)


def source_row(row, pair, rows):
    if not is_power(rows):
        return (pair - row + rows) % rows
    return reversed_bits(pair ^ row, rows)


def own_items_change_cores(rows, items, send):
    return items == 1 and send == 2


def item_route(rows, group, columns, send):
    items = rows * send // group

    def flat(r, g):
        return (g // columns * rows + r) * columns + g % columns

    def target(r, g, pair):
        d = target_row(r, pair, rows)
        return flat(d, g ^ 1 if d == r and own_items_change_cores(rows, items, send) else g)

    assert items * group == rows * send and (items % send == 0 or send % items == 0)
    routes = []
    for first in range(0, items, send):
        pairs = [(g * items + first) // send for g in range(group)]
        routes.append([(flat(r, g), target(r, g, pairs[g])) for r in range(rows) for g in range(group)])
    return items, routes


def local(
    right_side,
    near_tiles,
    tile_pairs,
    tile_count,
    panel_expansions,
    leaf_of_panel,
    far_pick,
    far_target,
    far_offset,
    translations,
):
    fields, panels = right_side.shape[1:]
    coefs = panel_expansions.shape[2]
    tile = near_tiles.shape[2]
    send = far_pick.shape[2]
    rows = lax.axis_size("row")
    group = lax.axis_size("grp") * lax.axis_size("col")
    row_here = lax.axis_index("row")
    own = lax.axis_index("grp") * lax.axis_size("col") + lax.axis_index("col")
    both = 2 * fields
    units = panels // LANES
    edge = REACH * tile
    edge_units = edge // LANES
    width = tile // LANES + 1
    items, routes = item_route(rows, group, lax.axis_size("col"), send)

    assert rows % 2 == 0
    neighbours = [[(r - 1 + 2 * (r % 2)) % rows for r in range(rows)], [r + 1 - 2 * (r % 2) for r in range(rows)]]
    own_place, row_place = own.reshape(1), row_here.reshape(1)
    core_place, chip_place = lax.rem(own, 2).reshape(1), lax.div(own, 2).reshape(1)
    slots = near_tiles.shape[1]
    pad_coefs = -(-coefs // 8) * 8
    chips = group // 2
    assert group == 2 * chips and chips & (chips - 1) == 0 and LANES % fields == 0
    window_shape = jax.ShapeDtypeStruct((items, pad_coefs, width, 2, LANES), BF16)
    item_shape = jax.ShapeDtypeStruct((items, fields, 2 * pad_coefs), BF16)
    half_units = (units // 2, both, LANES)
    assert units % 2 == 0 and edge_units % 2 == 0

    def in_hbm(value):
        return pltpu.with_memory_space_constraint(value, pltpu.HBM)

    leaves = leaf_of_panel.reshape(units, 1, LANES)
    expansions = panel_expansions.transpose(2, 0, 1).reshape(coefs, 2, units, LANES).transpose(0, 2, 1, 3)
    expansions = in_hbm(expansions)
    moves = in_hbm(translations.transpose(0, 2, 1, 3))
    picks = far_pick.transpose(0, 2, 1)

    plan, made, windows, leaves, right = pl.pallas_call(
        functools.partial(begin_kernel, fields, items, width, send, rows),
        out_shape=(
            pltpu.SMEM((item_place(slots, items),), jnp.int32),
            item_shape,
            pltpu.VMEM(window_shape.shape, BF16),
            jax.ShapeDtypeStruct(leaves.shape, jnp.int32),
            jax.ShapeDtypeStruct((both, panels), F32),
        ),
        in_specs=[SMEM] * 2 + [HBM] * 8,
        out_specs=(SMEM,) + (VMEM,) * 4,
        scratch_shapes=[
            pltpu.SMEM(value.shape, jnp.int32)
            for value in (picks, leaf_of_panel, far_target, far_offset, tile_pairs)
        ]
        + [
            pltpu.SemaphoreType.DMA((7,)),
            pltpu.SemaphoreType.DMA((items, PIECES)),
        ],
        compiler_params=params(),
        name="begin",
    )(
        row_place,
        own_place,
        in_hbm(picks),
        in_hbm(leaf_of_panel),
        in_hbm(leaves),
        in_hbm(far_target),
        in_hbm(far_offset),
        in_hbm(tile_pairs),
        in_hbm(right_side.reshape(both, panels)),
        expansions,
    )

    def exchanged(made):
        parts = [
            lax.ppermute(made[k * send : k * send + min(send, items)], EVERY, route) for k, route in enumerate(routes)
        ]
        return parts[0] if len(parts) == 1 else jnp.concatenate(parts)

    def along_row(value, which):
        return lax.ppermute(value, "row", list(enumerate(neighbours[which])))

    def from_neighbours(image):
        one, two = pl.pallas_call(
            edge_kernel,
            out_shape=(jax.ShapeDtypeStruct((both, edge), BF16),) * 2,
            in_specs=[SMEM, VMEM],
            out_specs=(VMEM, VMEM),
            compiler_params=params(),
            name="edges",
        )(row_place, image)
        return along_row(one, 0), along_row(two, 1)

    def one_edge(image, edge_units, early):
        return pl.pallas_call(
            functools.partial(one_edge_kernel, early),
            out_shape=jax.ShapeDtypeStruct((edge_units, both, LANES), BF16),
            in_specs=[SMEM, VMEM],
            out_specs=VMEM,
            compiler_params=params(),
            name="edge",
        )(row_place, image)

    image_shape = jax.ShapeDtypeStruct((units, both, LANES), F32)
    target_windows, moved = pl.pallas_call(
        functools.partial(fetch_kernel, items, width, slots),
        out_shape=(
            pltpu.VMEM(window_shape.shape, BF16),
            pltpu.VMEM((items, 2 * pad_coefs, coefs), BF16),
        ),
        in_specs=[SMEM, HBM, HBM],
        out_specs=(VMEM, VMEM),
        scratch_shapes=[
            pltpu.VMEM((items, coefs, 2, coefs), BF16),
            pltpu.SemaphoreType.DMA((items, PIECES)),
            pltpu.SemaphoreType.DMA((items,)),
        ],
        compiler_params=params(24),
        cost_estimate=pl.CostEstimate(flops=0, bytes_accessed=6 * window_shape.size, transcendentals=0),
        name="fetch",
    )(plan, expansions, moves)

    def swapped(value, step):
        return lax.ppermute(value, GROUP, [(g, g ^ step) for g in range(group)])

    def near(one, two, low):
        return pl.pallas_call(
            functools.partial(near_kernel, fields),
            out_shape=image_shape,
            in_specs=[SMEM] * 3 + [VMEM] * 4,
            out_specs=VMEM,
            scratch_shapes=[pltpu.VMEM((units + 2 * edge_units, both, LANES), low.dtype)],
            compiler_params=params(),
            cost_estimate=pl.CostEstimate(
                flops=8 * fields * near_tiles.size // 2, bytes_accessed=2 * near_tiles.size, transcendentals=0
            ),
            name="near",
        )(row_place, tile_count, plan, one, two, low, near_tiles)

    def core_parts(partial, taken):
        half_shape = jax.ShapeDtypeStruct(half_units, F32)
        keep, give = pl.pallas_call(
            functools.partial(far_kernel, fields, items, width, slots),
            out_shape=(half_shape, half_shape),
            in_specs=[SMEM, SMEM] + [VMEM] * 5,
            out_specs=(VMEM, VMEM),
            scratch_shapes=[pltpu.VMEM(image_shape.shape, F32)],
            compiler_params=params(),
            name="far",
        )(core_place, plan, leaves, partial, taken, moved, target_windows)
        return keep, swapped(give, 1)

    def first_far(taken):
        return pl.pallas_call(
            functools.partial(first_far_kernel, fields, items, width, slots),
            out_shape=jax.ShapeDtypeStruct((items, width, both, LANES), F32),
            in_specs=[SMEM] + [VMEM] * 4,
            out_specs=VMEM,
            compiler_params=params(),
            name="first_far",
        )(plan, leaves, taken, moved, target_windows)

    def last_core_parts(one, other_one, two, low, image):
        half_shape = jax.ShapeDtypeStruct(half_units, BF16)
        keep, give = pl.pallas_call(
            functools.partial(last_near_kernel, fields),
            out_shape=(half_shape, half_shape),
            in_specs=[SMEM] * 4 + [VMEM] * 6,
            out_specs=(VMEM, VMEM),
            scratch_shapes=[
                pltpu.VMEM((units + 2 * edge_units, both, LANES), low.dtype),
                pltpu.VMEM(image_shape.shape, F32),
            ],
            compiler_params=params(),
            name="last_near",
        )(core_place, row_place, tile_count, plan, one, other_one, two, low, near_tiles, image)
        return keep, swapped(give, 1)

    def pair_sums(keep, got):
        pair = pl.pallas_call(
            pair_kernel,
            out_shape=jax.ShapeDtypeStruct(keep.shape, BF16),
            in_specs=[VMEM, VMEM],
            out_specs=VMEM,
            compiler_params=params(),
            name="pair",
        )(keep, got)
        arrived = {step: swapped(pair, 2 * step) for step in swap_order(chips)}
        return [pair] + list(arrived.values())

    def own_pieces(keep, got):
        share = (units // 2 // chips, both, LANES)
        pieces = pl.pallas_call(
            fold_kernel,
            out_shape=(jax.ShapeDtypeStruct(share, F32),) + (jax.ShapeDtypeStruct(share, BF16),) * (chips - 1),
            in_specs=[SMEM, VMEM, VMEM],
            out_specs=(VMEM,) * chips,
            compiler_params=params(),
            name="fold",
        )(chip_place, keep, got)
        return [pieces[0]] + [swapped(piece, 2 * step) for piece, step in zip(pieces[1:], swap_order(chips))]

    def half_sum(parts):
        return pl.pallas_call(
            close_kernel,
            out_shape=jax.ShapeDtypeStruct(half_units, F32),
            in_specs=[VMEM] * chips,
            out_specs=VMEM,
            compiler_params=params(),
            name="close",
        )(*parts)

    def whole(mine, theirs):
        return pl.pallas_call(
            functools.partial(assemble_kernel, fields, items, width, slots),
            out_shape=(
                image_shape,
                jax.ShapeDtypeStruct(image_shape.shape, BF16),
                jax.ShapeDtypeStruct((items, fields, 2 * pad_coefs + ITEM_REST), BF16),
            ),
            in_specs=[SMEM, SMEM] + [VMEM] * 4,
            out_specs=(VMEM,) * 3,
            compiler_params=params(),
            name="assemble",
        )(core_place, plan, leaves, mine, theirs, windows)

    partial = near(*from_neighbours(right), right)
    mine = half_sum(pair_sums(*core_parts(partial, exchanged(made))))
    theirs = swapped(mine, 1)
    one = along_row(one_edge(mine, edge_units // 2, True), 0)
    z_all, z_low, made = whole(mine, theirs)
    image = first_far(exchanged(made))
    two = along_row(one_edge(z_low, edge_units, False), 1)
    last_parts = last_core_parts(one, swapped(one, 1), two, z_low, image)
    columns = lax.axis_size("col")
    half = units // 2
    if half % chips == 0:
        first_unit = lax.div(own, 2) * (half // chips)
        parts = own_pieces(*last_parts)
        members = [list(range(group * rows))]
    else:
        first_unit = jnp.zeros_like(own)
        parts = pair_sums(*last_parts)
        members = [
            [((g + k) // columns * rows + r) * columns + (g + k) % columns for r in range(rows) for k in range(2)]
            for g in range(0, group, 2)
        ]

    lines = pl.pallas_call(
        functools.partial(gram_kernel, fields),
        out_shape=jax.ShapeDtypeStruct((len(members[0]), -(-9 * fields // LANES), LANES), F32),
        in_specs=[SMEM, SMEM] + [VMEM] * (2 + chips),
        out_specs=VMEM,
        compiler_params=params(),
        name="gram",
    )(core_place, first_unit.reshape(1), right, z_all, *parts)
    sums = lax.all_to_all(
        lines, EVERY, 0, 0, axis_index_groups=members if len(members) > 1 else None, tiled=True
    )
    out = pl.pallas_call(
        functools.partial(final_kernel, fields),
        out_shape=jax.ShapeDtypeStruct((both, panels), F32),
        in_specs=[VMEM] * 3,
        out_specs=VMEM,
        compiler_params=params(),
        name="combine",
    )(sums, right, z_all)
    return out.reshape(right_side.shape)


def krylov_coefficients(sums):
    rr, rz_real, rz_imag, zz, rq_real, rq_imag, zq_real, zq_imag, qq = sums

    def times(left, right):
        return left[0] * right[0] - left[1] * right[1], left[0] * right[1] + left[1] * right[0]

    def conj_times(left, right):
        return left[0] * right[0] + left[1] * right[1], left[0] * right[1] - left[1] * right[0]

    def scale(factor, value):
        return factor * value[0], factor * value[1]

    def plus(*values):
        return sum(v[0] for v in values), sum(v[1] for v in values)

    def size(value):
        return value[0] * value[0] + value[1] * value[1]

    rz, rq, zq = (rz_real, rz_imag), (rq_real, rq_imag), (zq_real, zq_imag)
    beta = jnp.sqrt(rr + EPSILON)
    inv = 1.0 / beta
    norm_one = rr * inv * inv
    product = scale(inv * inv, rz)
    h_first = (0.5 * norm_one + product[0], product[1])
    shift = (h_first[0] - 0.5, h_first[1])
    residue = zz * inv * inv - 2.0 * conj_times(shift, product)[0] + size(shift) * norm_one
    residue = jnp.maximum(residue, 0.0)
    h_sub = jnp.sqrt(residue + EPSILON)
    alpha = inv / h_sub
    gamma = scale(-alpha, shift)
    h_upper = scale(
        inv,
        plus(
            scale(0.5, plus(scale(alpha, rz), scale(rr, gamma))), scale(alpha, rq), times(gamma, rz)
        ),
    )
    second = plus(
        scale(alpha * alpha, zq),
        scale(alpha * zz, gamma),
        scale(alpha, conj_times(gamma, rq)),
        scale(size(gamma), rz),
    )
    h_middle = (0.5 * residue / (h_sub * h_sub) + second[0], second[1])
    keep = (h_middle[0] - 0.5, h_middle[1])
    on_z = plus(gamma, scale(-alpha, keep))
    on_r = plus(scale(-inv, h_upper), scale(-1.0, times(keep, gamma)))
    last = (
        alpha * alpha * qq
        + size(on_z) * zz
        + size(on_r) * rr
        + 2.0
        * (
            conj_times(on_r, times(on_z, rz))[0]
            + alpha * conj_times(on_r, rq)[0]
            + alpha * conj_times(on_z, zq)[0]
        )
    )
    h_last = jnp.sqrt(jnp.maximum(last, 0.0) + EPSILON)
    radius = jnp.sqrt(size(h_first) + h_sub * h_sub)
    cosine = scale(1.0 / radius, h_first)
    sine = h_sub / radius
    upper = plus(conj_times(cosine, h_upper), scale(sine, h_middle))
    lower = plus(times(cosine, h_middle), scale(-sine, h_upper))
    radius_two = jnp.sqrt(size(lower) + h_last * h_last)
    cosine_two = scale(1.0 / radius_two, lower)
    weight_two = scale(-sine * beta / radius_two, (cosine_two[0], -cosine_two[1]))
    goal = scale(beta, (cosine[0], -cosine[1]))
    weight_one = scale(1.0 / radius, plus(goal, scale(-1.0, times(upper, weight_two))))
    on_right = plus(scale(inv, weight_one), times(weight_two, gamma))
    on_image = scale(alpha, weight_two)
    return on_right[0], on_right[1], on_image[0], on_image[1]


def solution(mesh):
    return jax.shard_map(
        local,
        mesh=mesh,
        in_specs=(
            P(None, None, "row"),
            P(None, ("grp", "row", "col"), None, None),
            P(("grp", "row", "col")),
            P(("grp", "row", "col")),
            P(None, "row", None),
            P("row", None),
            P(),
            P("row", None),
            P("row", None),
            P(),
        ),
        out_specs=P(None, None, "row"),
        check_vma=False,
    )
```

```python
import functools

import jax
import jax.numpy as jnp
from jax import lax
from jax.experimental import pallas as pl
from jax.experimental.pallas import tpu as pltpu
from jax.sharding import PartitionSpec as P

REACH = 2
SPAN = 2 * REACH + 1
LANES = 128
EPSILON = 1e-06
GROUP = ("grp", "col")
CODES = 0
PER_ITEM = 5
ITEM_REST = LANES
PIECES = 4
EVERY = ("grp", "row", "col")

F32 = jnp.float32
BF16 = jnp.bfloat16
SMEM = pl.BlockSpec(memory_space=pltpu.SMEM)
VMEM = pl.BlockSpec(memory_space=pltpu.VMEM)
HBM = pl.BlockSpec(memory_space=pltpu.HBM)
ANY = pl.BlockSpec(memory_space=pl.ANY)


def dot_nn(left, right):
    return lax.dot_general(left, right, (((1,), (0,)), ((), ())), preferred_element_type=F32)


def dot_nt(left, right):
    return lax.dot_general(left, right, (((1,), (1,)), ((), ())), preferred_element_type=F32)


def halves(rows):
    if rows.dtype != F32:
        return rows
    high = rows.astype(BF16)
    return jnp.concatenate([high, (rows - high.astype(F32)).astype(BF16)], axis=0)


def joined(sums, count):
    return sums if sums.shape[0] == count else sums[:count] + sums[count:]


def odd_lanes(shape):
    return lax.rem(lax.broadcasted_iota(jnp.int32, shape, 1), 2) == 1


def twice(value, width):
    rows = value.shape[0]
    parts = []
    for k in range(width // LANES):
        first = (k // 2) * LANES
        part = value[:, first : first + LANES]
        if part.shape[1] < LANES:
            part = jnp.concatenate([part, jnp.zeros((rows, LANES - part.shape[1]), part.dtype)], axis=-1)
        lane = lax.broadcasted_iota(jnp.int32, (rows, LANES), 1)
        parts.append(jnp.take_along_axis(part, lax.div(lane, 2) + (k % 2) * (LANES // 2), axis=1))
    return jnp.concatenate(parts, axis=-1)


def from_left(value):
    return pltpu.roll(value, 1, 1)


def from_right(value):
    return pltpu.roll(value, value.shape[1] - 1, 1)


def item_place(slots, item):
    return CODES + slots + PER_ITEM * item


def window_start(leaves_ref, leaf, width):
    leaves = leaves_ref[...]
    first = lax.broadcasted_iota(jnp.int32, leaves.shape, 2) == 0
    before = jnp.sum(jnp.where(jnp.logical_and(first, leaves < leaf), 1.0, 0.0)).astype(jnp.int32)
    return jnp.clip(before - 1, 0, leaves.shape[0] - width)


def window_mask(leaves_ref, leaf, unit, rows, width):
    leaves = jnp.concatenate([leaves_ref[unit + k] for k in range(width)], axis=-1)
    return jnp.broadcast_to(leaves, (rows, width * LANES)) == leaf


def window_copies(exp_ref, unit, window_ref, sem, width):
    coefs = exp_ref.shape[0]
    step = -(-coefs // PIECES)
    copies = []
    for p in range(PIECES):
        part = pl.ds(p * step, min(step, coefs - p * step))
        copies.append(
            pltpu.make_async_copy(exp_ref.at[part, pl.ds(unit, width)], window_ref.at[part], sem.at[p])
        )
    return copies


def clear_rest(window_ref, coefs):
    rest = window_ref.shape[0] - coefs
    window_ref[pl.ds(coefs, rest)] = jnp.zeros((rest, *window_ref.shape[1:]), BF16)


def window_rows(window_ref):
    coefs, width = window_ref.shape[:2]
    return jnp.concatenate([window_ref[:, k].reshape(2 * coefs, LANES) for k in range(width)], axis=-1)


def multi_rows(fields, width, leaf, unit, leaves_ref, low_ref, window_ref):
    if len(low_ref.shape) == 2:
        first = pl.multiple_of(unit * LANES, LANES)
        rows = low_ref[:, pl.ds(first, width * LANES)]
    else:
        rows = jnp.concatenate([low_ref[unit + k] for k in range(width)], axis=-1)
    mask = window_mask(leaves_ref, leaf, unit, 2 * fields, width)
    rows = halves(jnp.where(mask, rows.astype(F32), 0.0).astype(rows.dtype))
    total = joined(dot_nt(rows, window_rows(window_ref)), 2 * fields)
    on_real, on_imag = total[:fields], total[fields:]
    odd = odd_lanes(on_real.shape)
    other = jnp.where(odd, from_left(on_imag), from_right(on_imag))
    return jnp.where(odd, -on_real, on_real) - other


def edge_kernel(row_ref, image_ref, one_ref, two_ref):
    edge_of(row_ref, image_ref, one_ref, True)
    edge_of(row_ref, image_ref, two_ref, False)


def one_edge_kernel(early, row_ref, image_ref, out_ref):
    edge_of(row_ref, image_ref, out_ref, early)


def edge_of(row_ref, image_ref, out_ref, early):
    first_edge = (lax.rem(row_ref[0], 2) == 0) if early else (lax.rem(row_ref[0], 2) == 1)
    if len(image_ref.shape) == 2:
        edge = out_ref.shape[1]
        first, last = image_ref[:, :edge], image_ref[:, image_ref.shape[1] - edge :]
    else:
        edge = out_ref.shape[0]
        first, last = image_ref[:edge], image_ref[image_ref.shape[0] - edge :]

    @pl.when(first_edge)
    def _():
        out_ref[...] = first.astype(out_ref.dtype)

    @pl.when(jnp.logical_not(first_edge))
    def _():
        out_ref[...] = last.astype(out_ref.dtype)


def begin_kernel(
    fields, items, width, send, rows, row_ref, own_ref, pick_hbm, leaves_hbm,
    target_hbm, offset_hbm, pairs_hbm, right_hbm, exp_ref,
    plan_ref, out_ref, window_ref, leaves_ref, right_ref,
    pick_ref, target_ref, offset_ref, pairs_ref, sem, window_sem,
):
    loads = [
        pltpu.make_async_copy(source, place, sem.at[k])
        for k, (source, place) in enumerate(
            (
                (leaves_hbm, leaves_ref),
                (pick_hbm, pick_ref),
                (target_hbm, target_ref),
                (offset_hbm, offset_ref),
                (pairs_hbm, pairs_ref),
                (right_hbm, right_ref),
            )
        )
    ]
    for load in loads:
        load.start()
    for i in range(items):
        clear_rest(window_ref.at[i], exp_ref.shape[0])
    slots = pairs_ref.shape[0]
    own = own_ref[0]
    loads[0].wait()
    loads[1].wait()
    row = row_ref[0]

    def partner(i, coming):
        number = own * items + i
        pair, number = lax.div(number, send), lax.rem(number, send)
        other = source_row(row, pair, rows) if coming else target_row(row, pair, rows)
        if coming and own_items_change_cores(rows, items, send):
            number = jnp.where(other == row, 1 - number, number)
        return other, number

    for i in range(items):
        other, number = partner(i, False)
        leaf = pick_ref[other, number, row]
        unit = window_start(leaves_ref, leaf, width)
        place = item_place(slots, i)
        plan_ref[place], plan_ref[place + 1] = leaf, unit
        for copy in window_copies(exp_ref, unit, window_ref.at[i], window_sem.at[i], width):
            copy.start()
    for load in loads[2:]:
        load.wait()
    for s in range(slots):
        plan_ref[CODES + s] = pairs_ref[s]
    for i in range(items):
        place = item_place(slots, i)
        other, number = partner(i, True)
        leaf = target_ref[0, other * send + number]
        plan_ref[place + 2], plan_ref[place + 3] = leaf, window_start(leaves_ref, leaf, width)
        plan_ref[place + 4] = offset_ref[0, other * send + number]
    for i in range(items):
        place = item_place(slots, i)
        leaf, unit = plan_ref[place], plan_ref[place + 1]
        for copy in window_copies(exp_ref, unit, window_ref.at[i], window_sem.at[i], width):
            copy.wait()
        made = multi_rows(fields, width, leaf, unit, leaves_ref, right_ref, window_ref.at[i])
        out_ref[i, :, : made.shape[1]] = made.astype(BF16)


def fetch_kernel(items, width, slots, plan_ref, exp_ref, trans_ref, window_ref, moved_ref, trans_buf, sem, trans_sem):
    coefs = trans_ref.shape[3]
    for i in range(items):
        clear_rest(window_ref.at[i], coefs)

    def trans_copy(i):
        offset = plan_ref[item_place(slots, i) + 4]
        return pltpu.make_async_copy(trans_ref.at[offset], trans_buf.at[i], trans_sem.at[i])

    def exp_copies(i):
        unit = plan_ref[item_place(slots, i) + 3]
        return window_copies(exp_ref, unit, window_ref.at[i], sem.at[i], width)

    for i in range(items):
        trans_copy(i).start()
        for copy in exp_copies(i):
            copy.start()
    rest = moved_ref.shape[1] - 2 * coefs
    for i in range(items):
        trans_copy(i).wait()
        moved_ref[i, pl.ds(0, 2 * coefs)] = trans_buf[i].reshape(2 * coefs, coefs)
        moved_ref[i, pl.ds(2 * coefs, rest)] = jnp.zeros((rest, coefs), BF16)
        for copy in exp_copies(i):
            copy.wait()


def edge_places(row_ref, edge, units):
    even = lax.rem(row_ref[0], 2) == 0
    return jnp.where(even, 0, edge + units), jnp.where(even, edge + units, 0)


def part(total, core, keep_ref, give_ref):
    for k in range(keep_ref.shape[0]):
        keep_ref[k] = total[2 * k + core].astype(keep_ref.dtype)
        give_ref[k] = total[2 * k + 1 - core].astype(give_ref.dtype)


def near_kernel(
    fields, core_ref, row_ref, count_ref, plan_ref, *refs
):
    *edge_refs, here_ref, tiles_ref, image_ref, keep_ref, give_ref, ext, total = refs
    units = total.shape[0]
    edge = (ext.shape[0] - units) // 2
    core = core_ref[0]
    one_at, two_at = edge_places(row_ref, edge, units)
    if len(here_ref.shape) == 2:
        one_ref, two_ref = edge_refs
        for k in range(edge):
            lanes = slice(k * LANES, (k + 1) * LANES)
            ext[one_at + k] = one_ref[:, lanes].astype(ext.dtype)
            ext[two_at + k] = two_ref[:, lanes].astype(ext.dtype)
        for k in range(units):
            ext[edge + k] = here_ref[:, k * LANES : (k + 1) * LANES]
    else:
        one_ref, other_one_ref, two_ref = edge_refs
        for k in range(edge // 2):
            ext[one_at + 2 * k + core] = one_ref[k]
            ext[one_at + 2 * k + 1 - core] = other_one_ref[k]
        ext[pl.ds(two_at, edge)] = two_ref[...]
        ext[edge : edge + units] = here_ref[...]
    total[...] = jnp.zeros_like(total)
    items, width = image_ref.shape[:2]
    for i in range(items):
        unit = plan_ref[item_place(tiles_ref.shape[1], i) + 3]
        for k in range(width):
            total[unit + k] += image_ref[i, k]
    near_slots(fields, count_ref, plan_ref, tiles_ref, total, ext)
    part(total, core, keep_ref, give_ref)


def near_slots(fields, count_ref, plan_ref, tiles_ref, out_ref, ext):
    slots, tile = tiles_ref.shape[1], tiles_ref.shape[2]
    per = tile // LANES
    for s in range(slots):
        code = plan_ref[CODES + s]
        target = lax.div(code, SPAN)
        source = target + lax.rem(code, SPAN)
        rows = halves(jnp.concatenate([ext[source * per + k] for k in range(per)], axis=-1))
        on_real = joined(dot_nt(rows, tiles_ref[0, s]), 2 * fields)
        on_imag = joined(dot_nt(rows, tiles_ref[1, s]), 2 * fields)
        value = jnp.concatenate(
            [on_real[:fields] - on_imag[fields:], on_real[fields:] + on_imag[:fields]], axis=0
        )
        value = jnp.where(s < count_ref[0], value, 0.0)
        for k in range(per):
            out_ref[target * per + k] += value[:, k * LANES : (k + 1) * LANES]


def far_kernel(
    fields, items, width, slots, plan_ref, leaves_ref, item_ref, trans_ref, window_ref, image_ref
):
    for i in range(items):
        plain = item_ref[i, :, : trans_ref.shape[1]].astype(F32)
        odd = odd_lanes(plain.shape)
        turned = jnp.where(odd, from_left(plain), -from_right(plain))
        rows = jnp.concatenate([plain, turned], axis=0).astype(BF16)
        local_field = dot_nn(rows, trans_ref[i]).astype(BF16).astype(F32)
        local_field = twice(local_field, plain.shape[1])
        local_real, local_imag = local_field[:fields], local_field[fields:]
        rows = jnp.concatenate(
            [jnp.where(odd, -local_imag, local_real), jnp.where(odd, local_real, local_imag)], axis=0
        ).astype(BF16)
        expansions = window_rows(window_ref.at[i])
        place = item_place(slots, i)
        leaf, unit = plan_ref[place + 2], plan_ref[place + 3]
        mask = window_mask(leaves_ref, leaf, unit, 2 * fields, width)
        image = jnp.where(mask, dot_nn(rows, expansions), 0.0)
        for k in range(width):
            image_ref[i, k] = image[:, k * LANES : (k + 1) * LANES]


def pair_kernel(keep_ref, got_ref, out_ref):
    out_ref[...] = (keep_ref[...].astype(F32) + got_ref[...].astype(F32)).astype(out_ref.dtype)


def tree_sum(values):
    while len(values) > 1:
        values = [values[k] + values[k + 1] for k in range(0, len(values), 2)]
    return values[0]


def swap_order(chips):
    return list(range(chips - 1, 0, -1))


def by_step(parts):
    arrived = dict(zip(swap_order(len(parts)), parts[1:]))
    return [parts[0]] + [arrived[step] for step in range(1, len(parts))]


def close_kernel(*refs):
    refs[-1][...] = tree_sum([ref[...].astype(F32) for ref in by_step(refs[:-1])])


def assemble_kernel(
    fields, items, width, slots, core_ref, plan_ref, leaves_ref, mine_ref, theirs_ref, window_ref,
    out_ref, low_ref, made_ref,
):
    core = core_ref[0]
    for k in range(mine_ref.shape[0]):
        for ref, unit in ((mine_ref, 2 * k + core), (theirs_ref, 2 * k + 1 - core)):
            out_ref[unit] = ref[k]
            low_ref[unit] = ref[k].astype(BF16)
    for i in range(items):
        place = item_place(slots, i)
        made = multi_rows(
            fields, width, plan_ref[place], plan_ref[place + 1], leaves_ref, low_ref, window_ref.at[i]
        )
        made_ref[i, :, : made.shape[1]] = made.astype(BF16)


def flat_lines(totals, fields):
    per = LANES // fields
    lane = lax.broadcasted_iota(jnp.int32, (fields, LANES), 1)
    field = lax.broadcasted_iota(jnp.int32, (fields, LANES), 0)
    lines = []
    for first in range(0, len(totals), per):
        line = jnp.zeros((fields, LANES), F32)
        for k, total in enumerate(totals[first : first + per]):
            line = jnp.where(lane == field + k * fields, jnp.sum(total, axis=1, keepdims=True), line)
        lines.append(jnp.sum(line, axis=0, keepdims=True))
    return jnp.concatenate(lines, axis=0)


def columns_of(lines, count, fields):
    per = LANES // fields
    columns = []
    for k in range(lines.shape[0]):
        square = jnp.transpose(jnp.broadcast_to(lines[k : k + 1], (LANES, LANES)))
        columns += [square[j * fields : (j + 1) * fields] for j in range(per)]
    return columns[:count]


def gram_kernel(fields, core_ref, right_ref, image_ref, *refs):
    *parts, out_ref = refs
    totals = None
    for k in range(parts[0].shape[0]):
        unit = 2 * k + core_ref[0]
        r = right_ref[:, pl.ds(pl.multiple_of(unit * LANES, LANES), LANES)]
        z = image_ref[unit]
        q = tree_sum([part[k].astype(F32) for part in by_step(parts)])
        (rr, ri), (zr, zi), (qr, qi) = [(v[:fields], v[fields:]) for v in (r, z, q)]
        products = [
            rr * rr + ri * ri,
            rr * zr + ri * zi,
            rr * zi - ri * zr,
            zr * zr + zi * zi,
            rr * qr + ri * qi,
            rr * qi - ri * qr,
            zr * qr + zi * qi,
            zr * qi - zi * qr,
            qr * qr + qi * qi,
        ]
        totals = products if totals is None else [t + p for t, p in zip(totals, products)]
    out_ref[...] = jnp.broadcast_to(flat_lines(totals, fields)[None], out_ref.shape)


def final_kernel(fields, sums_ref, right_ref, image_ref, out_ref):
    units = image_ref.shape[0]
    sums = columns_of(jnp.sum(sums_ref[...], axis=0), 9, fields)
    a_real, a_imag, b_real, b_imag = krylov_coefficients(sums)
    for k in range(units):
        lanes = slice(k * LANES, (k + 1) * LANES)
        r_real, r_imag = right_ref[:fields, lanes], right_ref[fields:, lanes]
        z_real, z_imag = image_ref[k, :fields], image_ref[k, fields:]
        out_ref[:fields, lanes] = a_real * r_real - a_imag * r_imag + b_real * z_real - b_imag * z_imag
        out_ref[fields:, lanes] = a_real * r_imag + a_imag * r_real + b_real * z_imag + b_imag * z_real


def params(mebibytes=16):
    return pltpu.CompilerParams(vmem_limit_bytes=mebibytes * 1024 * 1024)


def is_power(count):
    return count & (count - 1) == 0


def reversed_bits(value, count):
    bits = count.bit_length() - 1
    return sum(((value >> k) & 1) << (bits - 1 - k) for k in range(bits))


def target_row(row, pair, rows):
    if not is_power(rows):
        return (pair - row + rows) % rows
    return pair ^ reversed_bits(row, rows)


def source_row(row, pair, rows):
    if not is_power(rows):
        return (pair - row + rows) % rows
    return reversed_bits(pair ^ row, rows)


def own_items_change_cores(rows, items, send):
    return items == 1 and send == 2


def item_route(rows, group, columns, send):
    items = rows * send // group

    def flat(r, g):
        return (g // columns * rows + r) * columns + g % columns

    def target(r, g, pair):
        d = target_row(r, pair, rows)
        return flat(d, g ^ 1 if d == r and own_items_change_cores(rows, items, send) else g)

    assert items * group == rows * send and (items % send == 0 or send % items == 0)
    routes = []
    for first in range(0, items, send):
        pairs = [(g * items + first) // send for g in range(group)]
        routes.append([(flat(r, g), target(r, g, pairs[g])) for r in range(rows) for g in range(group)])
    return items, routes


def local(
    right_side,
    near_tiles,
    tile_pairs,
    tile_count,
    panel_expansions,
    leaf_of_panel,
    far_pick,
    far_target,
    far_offset,
    translations,
):
    fields, panels = right_side.shape[1:]
    coefs = panel_expansions.shape[2]
    tile = near_tiles.shape[2]
    send = far_pick.shape[2]
    rows = lax.axis_size("row")
    group = lax.axis_size("grp") * lax.axis_size("col")
    row_here = lax.axis_index("row")
    own = lax.axis_index("grp") * lax.axis_size("col") + lax.axis_index("col")
    both = 2 * fields
    units = panels // LANES
    edge = REACH * tile
    edge_units = edge // LANES
    width = tile // LANES + 1
    items, routes = item_route(rows, group, lax.axis_size("col"), send)

    assert rows % 2 == 0
    neighbours = [[(r - 1 + 2 * (r % 2)) % rows for r in range(rows)], [r + 1 - 2 * (r % 2) for r in range(rows)]]
    own_place, row_place = own.reshape(1), row_here.reshape(1)
    core_place = lax.rem(own, 2).reshape(1)
    slots = near_tiles.shape[1]
    pad_coefs = -(-coefs // 8) * 8
    chips = group // 2
    assert group == 2 * chips and chips & (chips - 1) == 0 and LANES % fields == 0
    window_shape = jax.ShapeDtypeStruct((items, pad_coefs, width, 2, LANES), BF16)
    item_shape = jax.ShapeDtypeStruct((items, fields, 2 * pad_coefs + ITEM_REST), BF16)
    half_units = (units // 2, both, LANES)
    assert units % 2 == 0 and edge_units % 2 == 0

    def in_hbm(value):
        return pltpu.with_memory_space_constraint(value, pltpu.HBM)

    leaves = leaf_of_panel.reshape(units, 1, LANES)
    expansions = panel_expansions.transpose(2, 0, 1).reshape(coefs, 2, units, LANES).transpose(0, 2, 1, 3)
    expansions = in_hbm(expansions)
    moves = in_hbm(translations.transpose(0, 2, 1, 3))
    picks = far_pick.transpose(0, 2, 1)

    plan, made, windows, leaves, right = pl.pallas_call(
        functools.partial(begin_kernel, fields, items, width, send, rows),
        out_shape=(
            pltpu.SMEM((item_place(slots, items),), jnp.int32),
            item_shape,
            pltpu.VMEM(window_shape.shape, BF16),
            jax.ShapeDtypeStruct(leaves.shape, jnp.int32),
            jax.ShapeDtypeStruct((both, panels), F32),
        ),
        in_specs=[SMEM] * 2 + [HBM] * 7,
        out_specs=(SMEM,) + (VMEM,) * 4,
        scratch_shapes=[
            pltpu.SMEM(value.shape, jnp.int32)
            for value in (picks, far_target, far_offset, tile_pairs)
        ]
        + [
            pltpu.SemaphoreType.DMA((6,)),
            pltpu.SemaphoreType.DMA((items, PIECES)),
        ],
        compiler_params=params(),
        name="begin",
    )(
        row_place,
        own_place,
        in_hbm(picks),
        in_hbm(leaves),
        in_hbm(far_target),
        in_hbm(far_offset),
        in_hbm(tile_pairs),
        in_hbm(right_side.reshape(both, panels)),
        expansions,
    )

    def exchanged(made):
        parts = [
            lax.ppermute(made[k * send : k * send + min(send, items)], EVERY, route) for k, route in enumerate(routes)
        ]
        return parts[0] if len(parts) == 1 else jnp.concatenate(parts)

    def along_row(value, which):
        return lax.ppermute(value, "row", list(enumerate(neighbours[which])))

    def from_neighbours(image):
        one, two = pl.pallas_call(
            edge_kernel,
            out_shape=(jax.ShapeDtypeStruct((both, edge), BF16),) * 2,
            in_specs=[SMEM, VMEM],
            out_specs=(VMEM, VMEM),
            compiler_params=params(),
            name="edges",
        )(row_place, image)
        return along_row(one, 0), along_row(two, 1)

    def one_edge(image, edge_units, early):
        return pl.pallas_call(
            functools.partial(one_edge_kernel, early),
            out_shape=jax.ShapeDtypeStruct((edge_units, both, LANES), BF16),
            in_specs=[SMEM, VMEM],
            out_specs=VMEM,
            compiler_params=params(),
            name="edge",
        )(row_place, image)

    image_shape = jax.ShapeDtypeStruct((units, both, LANES), F32)
    target_windows, moved = pl.pallas_call(
        functools.partial(fetch_kernel, items, width, slots),
        out_shape=(
            pltpu.VMEM(window_shape.shape, BF16),
            pltpu.VMEM((items, 2 * pad_coefs, coefs), BF16),
        ),
        in_specs=[SMEM, HBM, HBM],
        out_specs=(VMEM, VMEM),
        scratch_shapes=[
            pltpu.VMEM((items, coefs, 2, coefs), BF16),
            pltpu.SemaphoreType.DMA((items, PIECES)),
            pltpu.SemaphoreType.DMA((items,)),
        ],
        compiler_params=params(24),
        cost_estimate=pl.CostEstimate(flops=0, bytes_accessed=6 * window_shape.size, transcendentals=0),
        name="fetch",
    )(plan, expansions, moves)

    def swapped(value, step):
        return lax.ppermute(value, GROUP, [(g, g ^ step) for g in range(group)])

    def far(taken):
        return pl.pallas_call(
            functools.partial(far_kernel, fields, items, width, slots),
            out_shape=jax.ShapeDtypeStruct((items, width, both, LANES), F32),
            in_specs=[SMEM] + [VMEM] * 4,
            out_specs=VMEM,
            compiler_params=params(),
            name="far",
        )(plan, leaves, taken, moved, target_windows)

    def core_parts(edges, low, image, dtype):
        half_shape = jax.ShapeDtypeStruct(half_units, dtype)
        keep, give = pl.pallas_call(
            functools.partial(near_kernel, fields),
            out_shape=(half_shape, half_shape),
            in_specs=[SMEM] * 4 + [VMEM] * (3 + len(edges)),
            out_specs=(VMEM, VMEM),
            scratch_shapes=[
                pltpu.VMEM((units + 2 * edge_units, both, LANES), low.dtype),
                pltpu.VMEM(image_shape.shape, F32),
            ],
            compiler_params=params(),
            name="near",
        )(core_place, row_place, tile_count, plan, *edges, low, near_tiles, image)
        return keep, swapped(give, 1)

    def pair_sums(keep, got):
        pair = pl.pallas_call(
            pair_kernel,
            out_shape=jax.ShapeDtypeStruct(keep.shape, BF16),
            in_specs=[VMEM, VMEM],
            out_specs=VMEM,
            compiler_params=params(),
            name="pair",
        )(keep, got)
        arrived = {step: swapped(pair, 2 * step) for step in swap_order(chips)}
        return [pair] + list(arrived.values())

    def half_sum(parts):
        return pl.pallas_call(
            close_kernel,
            out_shape=jax.ShapeDtypeStruct(half_units, F32),
            in_specs=[VMEM] * chips,
            out_specs=VMEM,
            compiler_params=params(),
            name="close",
        )(*parts)

    def whole(mine, theirs):
        return pl.pallas_call(
            functools.partial(assemble_kernel, fields, items, width, slots),
            out_shape=(
                image_shape,
                jax.ShapeDtypeStruct(image_shape.shape, BF16),
                item_shape,
            ),
            in_specs=[SMEM, SMEM] + [VMEM] * 4,
            out_specs=(VMEM,) * 3,
            compiler_params=params(),
            name="assemble",
        )(core_place, plan, leaves, mine, theirs, windows)

    image = far(exchanged(made))
    mine = half_sum(pair_sums(*core_parts(from_neighbours(right), right, image, F32)))
    theirs = swapped(mine, 1)
    one = along_row(one_edge(mine, edge_units // 2, True), 0)
    z_all, z_low, made = whole(mine, theirs)
    image = far(exchanged(made))
    two = along_row(one_edge(z_low, edge_units, False), 1)
    parts = pair_sums(*core_parts((one, swapped(one, 1), two), z_low, image, BF16))

    lines = pl.pallas_call(
        functools.partial(gram_kernel, fields),
        out_shape=jax.ShapeDtypeStruct((2 * rows, -(-9 * fields // LANES), LANES), F32),
        in_specs=[SMEM] + [VMEM] * (2 + chips),
        out_specs=VMEM,
        compiler_params=params(),
        name="gram",
    )(core_place, right, z_all, *parts)
    columns = lax.axis_size("col")
    same_chip = [
        [((g + k) // columns * rows + r) * columns + (g + k) % columns for r in range(rows) for k in range(2)]
        for g in range(0, group, 2)
    ]
    sums = lax.all_to_all(lines, EVERY, 0, 0, axis_index_groups=same_chip, tiled=True)
    out = pl.pallas_call(
        functools.partial(final_kernel, fields),
        out_shape=jax.ShapeDtypeStruct((both, panels), F32),
        in_specs=[VMEM] * 3,
        out_specs=VMEM,
        compiler_params=params(),
        name="combine",
    )(sums, right, z_all)
    return out.reshape(right_side.shape)


def krylov_coefficients(sums):
    rr, rz_real, rz_imag, zz, rq_real, rq_imag, zq_real, zq_imag, qq = sums

    def times(left, right):
        return left[0] * right[0] - left[1] * right[1], left[0] * right[1] + left[1] * right[0]

    def conj_times(left, right):
        return left[0] * right[0] + left[1] * right[1], left[0] * right[1] - left[1] * right[0]

    def scale(factor, value):
        return factor * value[0], factor * value[1]

    def plus(*values):
        return sum(v[0] for v in values), sum(v[1] for v in values)

    def size(value):
        return value[0] * value[0] + value[1] * value[1]

    rz, rq, zq = (rz_real, rz_imag), (rq_real, rq_imag), (zq_real, zq_imag)
    beta = jnp.sqrt(rr + EPSILON)
    inv = 1.0 / beta
    norm_one = rr * inv * inv
    product = scale(inv * inv, rz)
    h_first = (0.5 * norm_one + product[0], product[1])
    shift = (h_first[0] - 0.5, h_first[1])
    residue = zz * inv * inv - 2.0 * conj_times(shift, product)[0] + size(shift) * norm_one
    residue = jnp.maximum(residue, 0.0)
    h_sub = jnp.sqrt(residue + EPSILON)
    alpha = inv / h_sub
    gamma = scale(-alpha, shift)
    h_upper = scale(
        inv,
        plus(
            scale(0.5, plus(scale(alpha, rz), scale(rr, gamma))), scale(alpha, rq), times(gamma, rz)
        ),
    )
    second = plus(
        scale(alpha * alpha, zq),
        scale(alpha * zz, gamma),
        scale(alpha, conj_times(gamma, rq)),
        scale(size(gamma), rz),
    )
    h_middle = (0.5 * residue / (h_sub * h_sub) + second[0], second[1])
    keep = (h_middle[0] - 0.5, h_middle[1])
    on_z = plus(gamma, scale(-alpha, keep))
    on_r = plus(scale(-inv, h_upper), scale(-1.0, times(keep, gamma)))
    last = (
        alpha * alpha * qq
        + size(on_z) * zz
        + size(on_r) * rr
        + 2.0
        * (
            conj_times(on_r, times(on_z, rz))[0]
            + alpha * conj_times(on_r, rq)[0]
            + alpha * conj_times(on_z, zq)[0]
        )
    )
    h_last = jnp.sqrt(jnp.maximum(last, 0.0) + EPSILON)
    radius = jnp.sqrt(size(h_first) + h_sub * h_sub)
    cosine = scale(1.0 / radius, h_first)
    sine = h_sub / radius
    upper = plus(conj_times(cosine, h_upper), scale(sine, h_middle))
    lower = plus(times(cosine, h_middle), scale(-sine, h_upper))
    radius_two = jnp.sqrt(size(lower) + h_last * h_last)
    cosine_two = scale(1.0 / radius_two, lower)
    weight_two = scale(-sine * beta / radius_two, (cosine_two[0], -cosine_two[1]))
    goal = scale(beta, (cosine[0], -cosine[1]))
    weight_one = scale(1.0 / radius, plus(goal, scale(-1.0, times(upper, weight_two))))
    on_right = plus(scale(inv, weight_one), times(weight_two, gamma))
    on_image = scale(alpha, weight_two)
    return on_right[0], on_right[1], on_image[0], on_image[1]


def solution(mesh):
    return jax.shard_map(
        local,
        mesh=mesh,
        in_specs=(
            P(None, None, "row"),
            P(None, ("grp", "row", "col"), None, None),
            P(("grp", "row", "col")),
            P(("grp", "row", "col")),
            P(None, "row", None),
            P("row", None),
            P(),
            P("row", None),
            P("row", None),
            P(),
        ),
        out_specs=P(None, None, "row"),
        check_vma=False,
    )
```

```python
import functools

import jax
import jax.numpy as jnp
from jax import lax
from jax.experimental import pallas as pl
from jax.experimental.pallas import tpu as pltpu
from jax.sharding import PartitionSpec as P

REACH = 2
SPAN = 2 * REACH + 1
LANES = 128
EPSILON = 1e-06
GROUP = ("grp", "col")
COUNT, CODES = range(2)
PER_ITEM = 4
ITEM_REST = LANES
PIECES = 4
EVERY = ("grp", "row", "col")

F32 = jnp.float32
BF16 = jnp.bfloat16
SMEM = pl.BlockSpec(memory_space=pltpu.SMEM)
VMEM = pl.BlockSpec(memory_space=pltpu.VMEM)
HBM = pl.BlockSpec(memory_space=pltpu.HBM)
ANY = pl.BlockSpec(memory_space=pl.ANY)


def dot_nn(left, right):
    return lax.dot_general(left, right, (((1,), (0,)), ((), ())), preferred_element_type=F32)


def dot_nt(left, right):
    return lax.dot_general(left, right, (((1,), (1,)), ((), ())), preferred_element_type=F32)


def halves(rows):
    if rows.dtype != F32:
        return rows
    high = rows.astype(BF16)
    return jnp.concatenate([high, (rows - high.astype(F32)).astype(BF16)], axis=0)


def joined(sums, count):
    return sums if sums.shape[0] == count else sums[:count] + sums[count:]


def odd_lanes(shape):
    return lax.rem(lax.broadcasted_iota(jnp.int32, shape, 1), 2) == 1


def twice(value, width):
    rows = value.shape[0]
    parts = []
    for k in range(width // LANES):
        first = (k // 2) * LANES
        part = value[:, first : first + LANES]
        if part.shape[1] < LANES:
            part = jnp.concatenate([part, jnp.zeros((rows, LANES - part.shape[1]), part.dtype)], axis=-1)
        lane = lax.broadcasted_iota(jnp.int32, (rows, LANES), 1)
        parts.append(jnp.take_along_axis(part, lax.div(lane, 2) + (k % 2) * (LANES // 2), axis=1))
    return jnp.concatenate(parts, axis=-1)


def from_left(value):
    return pltpu.roll(value, 1, 1)


def from_right(value):
    return pltpu.roll(value, value.shape[1] - 1, 1)


def item_place(slots, item):
    return CODES + slots + PER_ITEM * item


def window_start(leaves_ref, leaf, width):
    leaves = leaves_ref[...]
    first = lax.broadcasted_iota(jnp.int32, leaves.shape, 2) == 0
    before = jnp.sum(jnp.where(jnp.logical_and(first, leaves < leaf), 1.0, 0.0)).astype(jnp.int32)
    return jnp.clip(before - 1, 0, leaves.shape[0] - width)


def window_mask(leaves_ref, leaf, unit, rows, width):
    leaves = jnp.concatenate([leaves_ref[unit + k] for k in range(width)], axis=-1)
    return jnp.broadcast_to(leaves, (rows, width * LANES)) == leaf


def window_copies(exp_ref, unit, window_ref, sem, width):
    coefs = exp_ref.shape[0]
    step = -(-coefs // PIECES)
    copies = []
    for p in range(PIECES):
        part = pl.ds(p * step, min(step, coefs - p * step))
        copies.append(
            pltpu.make_async_copy(exp_ref.at[part, pl.ds(unit, width)], window_ref.at[part], sem.at[p])
        )
    return copies


def clear_rest(window_ref, coefs):
    rest = window_ref.shape[0] - coefs
    window_ref[pl.ds(coefs, rest)] = jnp.zeros((rest, *window_ref.shape[1:]), BF16)


def window_rows(window_ref):
    coefs, width = window_ref.shape[:2]
    return jnp.concatenate([window_ref[:, k].reshape(2 * coefs, LANES) for k in range(width)], axis=-1)


def multi_rows(fields, width, leaf, unit, leaves_ref, low_ref, window_ref):
    if len(low_ref.shape) == 2:
        first = pl.multiple_of(unit * LANES, LANES)
        rows = low_ref[:, pl.ds(first, width * LANES)]
    else:
        rows = jnp.concatenate([low_ref[unit + k] for k in range(width)], axis=-1)
    mask = window_mask(leaves_ref, leaf, unit, 2 * fields, width)
    rows = halves(jnp.where(mask, rows.astype(F32), 0.0).astype(rows.dtype))
    total = joined(dot_nt(rows, window_rows(window_ref)), 2 * fields)
    on_real, on_imag = total[:fields], total[fields:]
    odd = odd_lanes(on_real.shape)
    other = jnp.where(odd, from_left(on_imag), from_right(on_imag))
    return jnp.where(odd, -on_real, on_real) - other


def edge_kernel(row_ref, image_ref, one_ref, two_ref):
    edge_of(row_ref, image_ref, one_ref, True)
    edge_of(row_ref, image_ref, two_ref, False)


def one_edge_kernel(early, row_ref, image_ref, out_ref):
    edge_of(row_ref, image_ref, out_ref, early)


def edge_of(row_ref, image_ref, out_ref, early):
    first_edge = (lax.rem(row_ref[0], 2) == 0) if early else (lax.rem(row_ref[0], 2) == 1)
    if len(image_ref.shape) == 2:
        edge = out_ref.shape[1]
        first, last = image_ref[:, :edge], image_ref[:, image_ref.shape[1] - edge :]
    else:
        edge = out_ref.shape[0]
        first, last = image_ref[:edge], image_ref[image_ref.shape[0] - edge :]

    @pl.when(first_edge)
    def _():
        out_ref[...] = first.astype(out_ref.dtype)

    @pl.when(jnp.logical_not(first_edge))
    def _():
        out_ref[...] = last.astype(out_ref.dtype)


def begin_kernel(
    fields, items, width, send, rows, row_ref, own_ref, core_ref, count_ref, pick_hbm, leaves_hbm,
    target_hbm, offset_hbm, pairs_hbm, right_hbm, exp_ref, trans_ref,
    plan_ref, out_ref, window_ref, target_window_ref, moved_ref, leaves_ref, right_ref,
    pick_ref, target_ref, offset_ref, pairs_ref, trans_buf, sem, window_sem, target_sem, trans_sem,
):
    loads = [
        pltpu.make_async_copy(source, place, sem.at[k])
        for k, (source, place) in enumerate(
            (
                (leaves_hbm, leaves_ref),
                (pick_hbm, pick_ref),
                (target_hbm, target_ref),
                (offset_hbm, offset_ref),
                (pairs_hbm, pairs_ref),
                (right_hbm, right_ref),
            )
        )
    ]
    for load in loads:
        load.start()
    for i in range(items):
        clear_rest(window_ref.at[i], exp_ref.shape[0])
    slots = pairs_ref.shape[0]
    own = own_ref[0]
    loads[0].wait()
    loads[1].wait()
    row = row_ref[0]

    def partner(i, coming):
        number = own * items + i
        pair, number = lax.div(number, send), lax.rem(number, send)
        other = source_row(row, pair, rows) if coming else target_row(row, pair, rows)
        if coming and own_items_change_cores(rows, items, send):
            number = jnp.where(other == row, 1 - number, number)
        return other, number

    for i in range(items):
        other, number = partner(i, False)
        leaf = pick_ref[other, number, row]
        unit = window_start(leaves_ref, leaf, width)
        place = item_place(slots, i)
        plan_ref[place], plan_ref[place + 1] = leaf, unit
        for copy in window_copies(exp_ref, unit, window_ref.at[i], window_sem.at[i], width):
            copy.start()
    for load in loads[2:]:
        load.wait()
    coefs = trans_ref.shape[3]
    later = []
    del core_ref
    plan_ref[COUNT] = count_ref[0]
    for s in range(slots):
        plan_ref[CODES + s] = pairs_ref[s]
    for i in range(items):
        place = item_place(slots, i)
        other, number = partner(i, True)
        leaf = target_ref[0, other * send + number]
        plan_ref[place + 2], plan_ref[place + 3] = leaf, window_start(leaves_ref, leaf, width)
        offset = offset_ref[0, other * send + number]
        later.append(pltpu.make_async_copy(trans_ref.at[offset], trans_buf.at[i], trans_sem.at[i]))
        later += window_copies(exp_ref, plan_ref[place + 3], target_window_ref.at[i], target_sem.at[i], width)
    for copy in later:
        copy.start()
    for i in range(items):
        clear_rest(target_window_ref.at[i], coefs)
    for i in range(items):
        place = item_place(slots, i)
        leaf, unit = plan_ref[place], plan_ref[place + 1]
        for copy in window_copies(exp_ref, unit, window_ref.at[i], window_sem.at[i], width):
            copy.wait()
        made = multi_rows(fields, width, leaf, unit, leaves_ref, right_ref, window_ref.at[i])
        out_ref[i, :, : made.shape[1]] = made.astype(BF16)
    for copy in later:
        copy.wait()
    rest = moved_ref.shape[1] - 2 * coefs
    for i in range(items):
        moved_ref[i, pl.ds(0, 2 * coefs)] = trans_buf[i].reshape(2 * coefs, coefs)
        moved_ref[i, pl.ds(2 * coefs, rest)] = jnp.zeros((rest, coefs), BF16)


def edge_places(row_ref, edge, units):
    even = lax.rem(row_ref[0], 2) == 0
    return jnp.where(even, 0, edge + units), jnp.where(even, edge + units, 0)


def part(total, core, keep_ref, give_ref):
    for k in range(keep_ref.shape[0]):
        keep_ref[k] = total[2 * k + core].astype(keep_ref.dtype)
        give_ref[k] = total[2 * k + 1 - core].astype(give_ref.dtype)


def near_kernel(
    fields, core_ref, row_ref, plan_ref, *refs
):
    *edge_refs, here_ref, tiles_ref, image_ref, keep_ref, give_ref, ext, total = refs
    units = total.shape[0]
    edge = (ext.shape[0] - units) // 2
    core = core_ref[0]
    one_at, two_at = edge_places(row_ref, edge, units)
    if len(here_ref.shape) == 2:
        one_ref, two_ref = edge_refs
        for k in range(edge):
            lanes = slice(k * LANES, (k + 1) * LANES)
            ext[one_at + k] = one_ref[:, lanes].astype(ext.dtype)
            ext[two_at + k] = two_ref[:, lanes].astype(ext.dtype)
        for k in range(units):
            ext[edge + k] = here_ref[:, k * LANES : (k + 1) * LANES]
    else:
        one_ref, other_one_ref, two_ref = edge_refs
        for k in range(edge // 2):
            ext[one_at + 2 * k + core] = one_ref[k]
            ext[one_at + 2 * k + 1 - core] = other_one_ref[k]
        ext[pl.ds(two_at, edge)] = two_ref[...]
        ext[edge : edge + units] = here_ref[...]
    total[...] = jnp.zeros_like(total)
    items, width = image_ref.shape[:2]
    for i in range(items):
        unit = plan_ref[item_place(tiles_ref.shape[1], i) + 3]
        for k in range(width):
            total[unit + k] += image_ref[i, k]
    near_slots(fields, plan_ref, tiles_ref, total, ext)
    part(total, core, keep_ref, give_ref)


def near_slots(fields, plan_ref, tiles_ref, out_ref, ext):
    slots, tile = tiles_ref.shape[1], tiles_ref.shape[2]
    per = tile // LANES
    for s in range(slots):
        code = plan_ref[CODES + s]
        target = lax.div(code, SPAN)
        source = target + lax.rem(code, SPAN)
        rows = halves(jnp.concatenate([ext[source * per + k] for k in range(per)], axis=-1))
        on_real = joined(dot_nt(rows, tiles_ref[0, s]), 2 * fields)
        on_imag = joined(dot_nt(rows, tiles_ref[1, s]), 2 * fields)
        value = jnp.concatenate(
            [on_real[:fields] - on_imag[fields:], on_real[fields:] + on_imag[:fields]], axis=0
        )
        value = jnp.where(s < plan_ref[COUNT], value, 0.0)
        for k in range(per):
            out_ref[target * per + k] += value[:, k * LANES : (k + 1) * LANES]


def far_kernel(
    fields, items, width, slots, plan_ref, leaves_ref, item_ref, trans_ref, window_ref, image_ref
):
    for i in range(items):
        plain = item_ref[i, :, : trans_ref.shape[1]].astype(F32)
        odd = odd_lanes(plain.shape)
        turned = jnp.where(odd, from_left(plain), -from_right(plain))
        rows = jnp.concatenate([plain, turned], axis=0).astype(BF16)
        local_field = dot_nn(rows, trans_ref[i]).astype(BF16).astype(F32)
        local_field = twice(local_field, plain.shape[1])
        local_real, local_imag = local_field[:fields], local_field[fields:]
        rows = jnp.concatenate(
            [jnp.where(odd, -local_imag, local_real), jnp.where(odd, local_real, local_imag)], axis=0
        ).astype(BF16)
        expansions = window_rows(window_ref.at[i])
        place = item_place(slots, i)
        leaf, unit = plan_ref[place + 2], plan_ref[place + 3]
        mask = window_mask(leaves_ref, leaf, unit, 2 * fields, width)
        image = jnp.where(mask, dot_nn(rows, expansions), 0.0)
        for k in range(width):
            image_ref[i, k] = image[:, k * LANES : (k + 1) * LANES]


def pair_kernel(keep_ref, got_ref, out_ref):
    out_ref[...] = (keep_ref[...].astype(F32) + got_ref[...].astype(F32)).astype(out_ref.dtype)


def tree_sum(values):
    while len(values) > 1:
        values = [values[k] + values[k + 1] for k in range(0, len(values), 2)]
    return values[0]


def swap_order(chips):
    return list(range(chips - 1, 0, -1))


def by_step(parts):
    arrived = dict(zip(swap_order(len(parts)), parts[1:]))
    return [parts[0]] + [arrived[step] for step in range(1, len(parts))]


def close_kernel(*refs):
    refs[-1][...] = tree_sum([ref[...].astype(F32) for ref in by_step(refs[:-1])])


def assemble_kernel(
    fields, items, width, slots, core_ref, plan_ref, leaves_ref, mine_ref, theirs_ref, window_ref,
    out_ref, low_ref, made_ref,
):
    core = core_ref[0]
    for k in range(mine_ref.shape[0]):
        for ref, unit in ((mine_ref, 2 * k + core), (theirs_ref, 2 * k + 1 - core)):
            out_ref[unit] = ref[k]
            low_ref[unit] = ref[k].astype(BF16)
    for i in range(items):
        place = item_place(slots, i)
        made = multi_rows(
            fields, width, plan_ref[place], plan_ref[place + 1], leaves_ref, low_ref, window_ref.at[i]
        )
        made_ref[i, :, : made.shape[1]] = made.astype(BF16)


def flat_lines(totals, fields):
    per = LANES // fields
    lane = lax.broadcasted_iota(jnp.int32, (fields, LANES), 1)
    field = lax.broadcasted_iota(jnp.int32, (fields, LANES), 0)
    lines = []
    for first in range(0, len(totals), per):
        line = jnp.zeros((fields, LANES), F32)
        for k, total in enumerate(totals[first : first + per]):
            line = jnp.where(lane == field + k * fields, jnp.sum(total, axis=1, keepdims=True), line)
        lines.append(jnp.sum(line, axis=0, keepdims=True))
    return jnp.concatenate(lines, axis=0)


def columns_of(lines, count, fields):
    per = LANES // fields
    columns = []
    for k in range(lines.shape[0]):
        square = jnp.transpose(jnp.broadcast_to(lines[k : k + 1], (LANES, LANES)))
        columns += [square[j * fields : (j + 1) * fields] for j in range(per)]
    return columns[:count]


def gram_kernel(fields, core_ref, right_ref, image_ref, *refs):
    *parts, out_ref = refs
    totals = None
    for k in range(parts[0].shape[0]):
        unit = 2 * k + core_ref[0]
        r = right_ref[:, pl.ds(pl.multiple_of(unit * LANES, LANES), LANES)]
        z = image_ref[unit]
        q = tree_sum([part[k].astype(F32) for part in by_step(parts)])
        (rr, ri), (zr, zi), (qr, qi) = [(v[:fields], v[fields:]) for v in (r, z, q)]
        products = [
            rr * rr + ri * ri,
            rr * zr + ri * zi,
            rr * zi - ri * zr,
            zr * zr + zi * zi,
            rr * qr + ri * qi,
            rr * qi - ri * qr,
            zr * qr + zi * qi,
            zr * qi - zi * qr,
            qr * qr + qi * qi,
        ]
        totals = products if totals is None else [t + p for t, p in zip(totals, products)]
    out_ref[...] = jnp.broadcast_to(flat_lines(totals, fields)[None], out_ref.shape)


def final_kernel(fields, sums_ref, right_ref, image_ref, out_ref):
    units = image_ref.shape[0]
    sums = columns_of(jnp.sum(sums_ref[...], axis=0), 9, fields)
    a_real, a_imag, b_real, b_imag = krylov_coefficients(sums)
    for k in range(units):
        lanes = slice(k * LANES, (k + 1) * LANES)
        r_real, r_imag = right_ref[:fields, lanes], right_ref[fields:, lanes]
        z_real, z_imag = image_ref[k, :fields], image_ref[k, fields:]
        out_ref[:fields, lanes] = a_real * r_real - a_imag * r_imag + b_real * z_real - b_imag * z_imag
        out_ref[fields:, lanes] = a_real * r_imag + a_imag * r_real + b_real * z_imag + b_imag * z_real


def params(mebibytes=16):
    return pltpu.CompilerParams(vmem_limit_bytes=mebibytes * 1024 * 1024)


def is_power(count):
    return count & (count - 1) == 0


def reversed_bits(value, count):
    bits = count.bit_length() - 1
    return sum(((value >> k) & 1) << (bits - 1 - k) for k in range(bits))


def target_row(row, pair, rows):
    if not is_power(rows):
        return (pair - row + rows) % rows
    return pair ^ reversed_bits(row, rows)


def source_row(row, pair, rows):
    if not is_power(rows):
        return (pair - row + rows) % rows
    return reversed_bits(pair ^ row, rows)


def own_items_change_cores(rows, items, send):
    return items == 1 and send == 2


def item_route(rows, group, columns, send):
    items = rows * send // group

    def flat(r, g):
        return (g // columns * rows + r) * columns + g % columns

    def target(r, g, pair):
        d = target_row(r, pair, rows)
        return flat(d, g ^ 1 if d == r and own_items_change_cores(rows, items, send) else g)

    assert items * group == rows * send and (items % send == 0 or send % items == 0)
    routes = []
    for first in range(0, items, send):
        pairs = [(g * items + first) // send for g in range(group)]
        routes.append([(flat(r, g), target(r, g, pairs[g])) for r in range(rows) for g in range(group)])
    return items, routes


def local(
    right_side,
    near_tiles,
    tile_pairs,
    tile_count,
    panel_expansions,
    leaf_of_panel,
    far_pick,
    far_target,
    far_offset,
    translations,
):
    fields, panels = right_side.shape[1:]
    coefs = panel_expansions.shape[2]
    tile = near_tiles.shape[2]
    send = far_pick.shape[2]
    rows = lax.axis_size("row")
    group = lax.axis_size("grp") * lax.axis_size("col")
    row_here = lax.axis_index("row")
    own = lax.axis_index("grp") * lax.axis_size("col") + lax.axis_index("col")
    both = 2 * fields
    units = panels // LANES
    edge = REACH * tile
    edge_units = edge // LANES
    width = tile // LANES + 1
    items, routes = item_route(rows, group, lax.axis_size("col"), send)

    assert rows % 2 == 0
    neighbours = [[(r - 1 + 2 * (r % 2)) % rows for r in range(rows)], [r + 1 - 2 * (r % 2) for r in range(rows)]]
    own_place, row_place = own.reshape(1), row_here.reshape(1)
    core_place = lax.rem(own, 2).reshape(1)
    slots = near_tiles.shape[1]
    pad_coefs = -(-coefs // 8) * 8
    chips = group // 2
    assert group == 2 * chips and chips & (chips - 1) == 0 and LANES % fields == 0
    window_shape = jax.ShapeDtypeStruct((items, pad_coefs, width, 2, LANES), BF16)
    item_shape = jax.ShapeDtypeStruct((items, fields, 2 * pad_coefs + ITEM_REST), BF16)
    half_units = (units // 2, both, LANES)
    assert units % 2 == 0 and edge_units % 2 == 0

    def in_hbm(value):
        return pltpu.with_memory_space_constraint(value, pltpu.HBM)

    leaves = leaf_of_panel.reshape(units, 1, LANES)
    expansions = panel_expansions.transpose(2, 0, 1).reshape(coefs, 2, units, LANES).transpose(0, 2, 1, 3)
    expansions = in_hbm(expansions)
    moves = in_hbm(translations.transpose(0, 2, 1, 3))
    picks = far_pick.transpose(0, 2, 1)

    plan, made, windows, target_windows, moved, leaves, right = pl.pallas_call(
        functools.partial(begin_kernel, fields, items, width, send, rows),
        out_shape=(
            pltpu.SMEM((item_place(slots, items),), jnp.int32),
            item_shape,
            pltpu.VMEM(window_shape.shape, BF16),
            pltpu.VMEM(window_shape.shape, BF16),
            pltpu.VMEM((items, 2 * pad_coefs, coefs), BF16),
            jax.ShapeDtypeStruct(leaves.shape, jnp.int32),
            jax.ShapeDtypeStruct((both, panels), F32),
        ),
        in_specs=[SMEM] * 4 + [HBM] * 8,
        out_specs=(SMEM,) + (VMEM,) * 6,
        scratch_shapes=[
            pltpu.SMEM(value.shape, jnp.int32)
            for value in (picks, far_target, far_offset, tile_pairs)
        ]
        + [
            pltpu.VMEM((items, coefs, 2, coefs), BF16),
            pltpu.SemaphoreType.DMA((6,)),
            pltpu.SemaphoreType.DMA((items, PIECES)),
            pltpu.SemaphoreType.DMA((items, PIECES)),
            pltpu.SemaphoreType.DMA((items,)),
        ],
        compiler_params=params(24),
        name="begin",
    )(
        row_place,
        own_place,
        core_place,
        tile_count,
        in_hbm(picks),
        in_hbm(leaves),
        in_hbm(far_target),
        in_hbm(far_offset),
        in_hbm(tile_pairs),
        in_hbm(right_side.reshape(both, panels)),
        expansions,
        moves,
    )

    def exchanged(made):
        parts = [
            lax.ppermute(made[k * send : k * send + min(send, items)], EVERY, route) for k, route in enumerate(routes)
        ]
        return parts[0] if len(parts) == 1 else jnp.concatenate(parts)

    def along_row(value, which):
        return lax.ppermute(value, "row", list(enumerate(neighbours[which])))

    def from_neighbours(image):
        one, two = pl.pallas_call(
            edge_kernel,
            out_shape=(jax.ShapeDtypeStruct((both, edge), BF16),) * 2,
            in_specs=[SMEM, VMEM],
            out_specs=(VMEM, VMEM),
            compiler_params=params(),
            name="edges",
        )(row_place, image)
        return along_row(one, 0), along_row(two, 1)

    def one_edge(image, edge_units, early):
        return pl.pallas_call(
            functools.partial(one_edge_kernel, early),
            out_shape=jax.ShapeDtypeStruct((edge_units, both, LANES), BF16),
            in_specs=[SMEM, VMEM],
            out_specs=VMEM,
            compiler_params=params(),
            name="edge",
        )(row_place, image)

    image_shape = jax.ShapeDtypeStruct((units, both, LANES), F32)
    def swapped(value, step):
        return lax.ppermute(value, GROUP, [(g, g ^ step) for g in range(group)])

    def far(taken):
        return pl.pallas_call(
            functools.partial(far_kernel, fields, items, width, slots),
            out_shape=jax.ShapeDtypeStruct((items, width, both, LANES), F32),
            in_specs=[SMEM] + [VMEM] * 4,
            out_specs=VMEM,
            compiler_params=params(),
            name="far",
        )(plan, leaves, taken, moved, target_windows)

    def core_parts(edges, low, image, dtype):
        half_shape = jax.ShapeDtypeStruct(half_units, dtype)
        keep, give = pl.pallas_call(
            functools.partial(near_kernel, fields),
            out_shape=(half_shape, half_shape),
            in_specs=[SMEM] * 3 + [VMEM] * (3 + len(edges)),
            out_specs=(VMEM, VMEM),
            scratch_shapes=[
                pltpu.VMEM((units + 2 * edge_units, both, LANES), low.dtype),
                pltpu.VMEM(image_shape.shape, F32),
            ],
            compiler_params=params(),
            name="near",
        )(core_place, row_place, plan, *edges, low, near_tiles, image)
        return keep, swapped(give, 1)

    def pair_sums(keep, got):
        pair = pl.pallas_call(
            pair_kernel,
            out_shape=jax.ShapeDtypeStruct(keep.shape, BF16),
            in_specs=[VMEM, VMEM],
            out_specs=VMEM,
            compiler_params=params(),
            name="pair",
        )(keep, got)
        arrived = {step: swapped(pair, 2 * step) for step in swap_order(chips)}
        return [pair] + list(arrived.values())

    def half_sum(parts):
        return pl.pallas_call(
            close_kernel,
            out_shape=jax.ShapeDtypeStruct(half_units, F32),
            in_specs=[VMEM] * chips,
            out_specs=VMEM,
            compiler_params=params(),
            name="close",
        )(*parts)

    def whole(mine, theirs):
        return pl.pallas_call(
            functools.partial(assemble_kernel, fields, items, width, slots),
            out_shape=(
                image_shape,
                jax.ShapeDtypeStruct(image_shape.shape, BF16),
                item_shape,
            ),
            in_specs=[SMEM, SMEM] + [VMEM] * 4,
            out_specs=(VMEM,) * 3,
            compiler_params=params(),
            name="assemble",
        )(core_place, plan, leaves, mine, theirs, windows)

    image = far(exchanged(made))
    mine = half_sum(pair_sums(*core_parts(from_neighbours(right), right, image, F32)))
    theirs = swapped(mine, 1)
    one = along_row(one_edge(mine, edge_units // 2, True), 0)
    z_all, z_low, made = whole(mine, theirs)
    image = far(exchanged(made))
    two = along_row(one_edge(z_low, edge_units, False), 1)
    parts = pair_sums(*core_parts((one, swapped(one, 1), two), z_low, image, BF16))

    lines = pl.pallas_call(
        functools.partial(gram_kernel, fields),
        out_shape=jax.ShapeDtypeStruct((2 * rows, -(-9 * fields // LANES), LANES), F32),
        in_specs=[SMEM] + [VMEM] * (2 + chips),
        out_specs=VMEM,
        compiler_params=params(),
        name="gram",
    )(core_place, right, z_all, *parts)
    columns = lax.axis_size("col")
    same_chip = [
        [((g + k) // columns * rows + r) * columns + (g + k) % columns for r in range(rows) for k in range(2)]
        for g in range(0, group, 2)
    ]
    sums = lax.all_to_all(lines, EVERY, 0, 0, axis_index_groups=same_chip, tiled=True)
    out = pl.pallas_call(
        functools.partial(final_kernel, fields),
        out_shape=jax.ShapeDtypeStruct((both, panels), F32),
        in_specs=[VMEM] * 3,
        out_specs=VMEM,
        compiler_params=params(),
        name="combine",
    )(sums, right, z_all)
    return out.reshape(right_side.shape)


def krylov_coefficients(sums):
    rr, rz_real, rz_imag, zz, rq_real, rq_imag, zq_real, zq_imag, qq = sums

    def times(left, right):
        return left[0] * right[0] - left[1] * right[1], left[0] * right[1] + left[1] * right[0]

    def conj_times(left, right):
        return left[0] * right[0] + left[1] * right[1], left[0] * right[1] - left[1] * right[0]

    def scale(factor, value):
        return factor * value[0], factor * value[1]

    def plus(*values):
        return sum(v[0] for v in values), sum(v[1] for v in values)

    def size(value):
        return value[0] * value[0] + value[1] * value[1]

    rz, rq, zq = (rz_real, rz_imag), (rq_real, rq_imag), (zq_real, zq_imag)
    beta = jnp.sqrt(rr + EPSILON)
    inv = 1.0 / beta
    norm_one = rr * inv * inv
    product = scale(inv * inv, rz)
    h_first = (0.5 * norm_one + product[0], product[1])
    shift = (h_first[0] - 0.5, h_first[1])
    residue = zz * inv * inv - 2.0 * conj_times(shift, product)[0] + size(shift) * norm_one
    residue = jnp.maximum(residue, 0.0)
    h_sub = jnp.sqrt(residue + EPSILON)
    alpha = inv / h_sub
    gamma = scale(-alpha, shift)
    h_upper = scale(
        inv,
        plus(
            scale(0.5, plus(scale(alpha, rz), scale(rr, gamma))), scale(alpha, rq), times(gamma, rz)
        ),
    )
    second = plus(
        scale(alpha * alpha, zq),
        scale(alpha * zz, gamma),
        scale(alpha, conj_times(gamma, rq)),
        scale(size(gamma), rz),
    )
    h_middle = (0.5 * residue / (h_sub * h_sub) + second[0], second[1])
    keep = (h_middle[0] - 0.5, h_middle[1])
    on_z = plus(gamma, scale(-alpha, keep))
    on_r = plus(scale(-inv, h_upper), scale(-1.0, times(keep, gamma)))
    last = (
        alpha * alpha * qq
        + size(on_z) * zz
        + size(on_r) * rr
        + 2.0
        * (
            conj_times(on_r, times(on_z, rz))[0]
            + alpha * conj_times(on_r, rq)[0]
            + alpha * conj_times(on_z, zq)[0]
        )
    )
    h_last = jnp.sqrt(jnp.maximum(last, 0.0) + EPSILON)
    radius = jnp.sqrt(size(h_first) + h_sub * h_sub)
    cosine = scale(1.0 / radius, h_first)
    sine = h_sub / radius
    upper = plus(conj_times(cosine, h_upper), scale(sine, h_middle))
    lower = plus(times(cosine, h_middle), scale(-sine, h_upper))
    radius_two = jnp.sqrt(size(lower) + h_last * h_last)
    cosine_two = scale(1.0 / radius_two, lower)
    weight_two = scale(-sine * beta / radius_two, (cosine_two[0], -cosine_two[1]))
    goal = scale(beta, (cosine[0], -cosine[1]))
    weight_one = scale(1.0 / radius, plus(goal, scale(-1.0, times(upper, weight_two))))
    on_right = plus(scale(inv, weight_one), times(weight_two, gamma))
    on_image = scale(alpha, weight_two)
    return on_right[0], on_right[1], on_image[0], on_image[1]


def solution(mesh):
    return jax.shard_map(
        local,
        mesh=mesh,
        in_specs=(
            P(None, None, "row"),
            P(None, ("grp", "row", "col"), None, None),
            P(("grp", "row", "col")),
            P(("grp", "row", "col")),
            P(None, "row", None),
            P("row", None),
            P(),
            P("row", None),
            P("row", None),
            P(),
        ),
        out_specs=P(None, None, "row"),
        check_vma=False,
    )
```

```python
import functools

import jax
import jax.numpy as jnp
from jax import lax
from jax.experimental import pallas as pl
from jax.experimental.pallas import tpu as pltpu
from jax.sharding import PartitionSpec as P

REACH = 2
SPAN = 2 * REACH + 1
LANES = 128
EPSILON = 1e-06
GROUP = ("grp", "col")
CODES = 0
PER_ITEM = 5
ITEM_REST = LANES
PIECES = 4
EVERY = ("grp", "row", "col")

F32 = jnp.float32
BF16 = jnp.bfloat16
SMEM = pl.BlockSpec(memory_space=pltpu.SMEM)
VMEM = pl.BlockSpec(memory_space=pltpu.VMEM)
HBM = pl.BlockSpec(memory_space=pltpu.HBM)
ANY = pl.BlockSpec(memory_space=pl.ANY)


def dot_nn(left, right):
    return lax.dot_general(left, right, (((1,), (0,)), ((), ())), preferred_element_type=F32)


def dot_nt(left, right):
    return lax.dot_general(left, right, (((1,), (1,)), ((), ())), preferred_element_type=F32)


def halves(rows):
    if rows.dtype != F32:
        return rows
    high = rows.astype(BF16)
    return jnp.concatenate([high, (rows - high.astype(F32)).astype(BF16)], axis=0)


def joined(sums, count):
    return sums if sums.shape[0] == count else sums[:count] + sums[count:]


def odd_lanes(shape):
    return lax.rem(lax.broadcasted_iota(jnp.int32, shape, 1), 2) == 1


def twice(value, width):
    rows = value.shape[0]
    parts = []
    for k in range(width // LANES):
        first = (k // 2) * LANES
        part = value[:, first : first + LANES]
        if part.shape[1] < LANES:
            part = jnp.concatenate([part, jnp.zeros((rows, LANES - part.shape[1]), part.dtype)], axis=-1)
        lane = lax.broadcasted_iota(jnp.int32, (rows, LANES), 1)
        parts.append(jnp.take_along_axis(part, lax.div(lane, 2) + (k % 2) * (LANES // 2), axis=1))
    return jnp.concatenate(parts, axis=-1)


def from_left(value):
    return pltpu.roll(value, 1, 1)


def from_right(value):
    return pltpu.roll(value, value.shape[1] - 1, 1)


def item_place(slots, item):
    return CODES + slots + PER_ITEM * item


def window_start(leaf_ref, leaf, width):
    units = leaf_ref.shape[1] // LANES
    before = jnp.int32(0)
    for k in range(units):
        before = before + (leaf_ref[0, k * LANES] < leaf).astype(jnp.int32)
    return jnp.clip(before - 1, 0, units - width)


def window_mask(leaves_ref, leaf, unit, rows, width):
    leaves = jnp.concatenate([leaves_ref[unit + k] for k in range(width)], axis=-1)
    return jnp.broadcast_to(leaves, (rows, width * LANES)) == leaf


def window_copies(exp_ref, unit, window_ref, sem, width):
    coefs = exp_ref.shape[0]
    step = -(-coefs // PIECES)
    copies = []
    for p in range(PIECES):
        part = pl.ds(p * step, min(step, coefs - p * step))
        copies.append(
            pltpu.make_async_copy(exp_ref.at[part, pl.ds(unit, width)], window_ref.at[part], sem.at[p])
        )
    return copies


def clear_rest(window_ref, coefs):
    rest = window_ref.shape[0] - coefs
    window_ref[pl.ds(coefs, rest)] = jnp.zeros((rest, *window_ref.shape[1:]), BF16)


def window_rows(window_ref):
    coefs, width = window_ref.shape[:2]
    return jnp.concatenate([window_ref[:, k].reshape(2 * coefs, LANES) for k in range(width)], axis=-1)


def multi_rows(fields, width, leaf, unit, leaves_ref, low_ref, window_ref):
    if len(low_ref.shape) == 2:
        first = pl.multiple_of(unit * LANES, LANES)
        rows = low_ref[:, pl.ds(first, width * LANES)]
    else:
        rows = jnp.concatenate([low_ref[unit + k] for k in range(width)], axis=-1)
    mask = window_mask(leaves_ref, leaf, unit, 2 * fields, width)
    rows = halves(jnp.where(mask, rows.astype(F32), 0.0).astype(rows.dtype))
    total = joined(dot_nt(rows, window_rows(window_ref)), 2 * fields)
    on_real, on_imag = total[:fields], total[fields:]
    odd = odd_lanes(on_real.shape)
    other = jnp.where(odd, from_left(on_imag), from_right(on_imag))
    return jnp.where(odd, -on_real, on_real) - other


def edge_kernel(row_ref, image_ref, one_ref, two_ref):
    edge_of(row_ref, image_ref, one_ref, True)
    edge_of(row_ref, image_ref, two_ref, False)


def one_edge_kernel(early, row_ref, image_ref, out_ref):
    edge_of(row_ref, image_ref, out_ref, early)


def edge_of(row_ref, image_ref, out_ref, early):
    first_edge = (lax.rem(row_ref[0], 2) == 0) if early else (lax.rem(row_ref[0], 2) == 1)
    if len(image_ref.shape) == 2:
        edge = out_ref.shape[1]
        first, last = image_ref[:, :edge], image_ref[:, image_ref.shape[1] - edge :]
    else:
        edge = out_ref.shape[0]
        first, last = image_ref[:edge], image_ref[image_ref.shape[0] - edge :]

    @pl.when(first_edge)
    def _():
        out_ref[...] = first.astype(out_ref.dtype)

    @pl.when(jnp.logical_not(first_edge))
    def _():
        out_ref[...] = last.astype(out_ref.dtype)


def begin_kernel(
    fields, items, width, send, rows, row_ref, own_ref, pick_hbm, leaf_hbm, leaves_hbm,
    target_hbm, offset_hbm, pairs_hbm, right_hbm, exp_ref,
    plan_ref, out_ref, window_ref, leaves_ref, right_ref,
    pick_ref, leaf_ref, target_ref, offset_ref, pairs_ref, sem, window_sem,
):
    loads = [
        pltpu.make_async_copy(source, place, sem.at[k])
        for k, (source, place) in enumerate(
            (
                (leaf_hbm, leaf_ref),
                (pick_hbm, pick_ref),
                (target_hbm, target_ref),
                (offset_hbm, offset_ref),
                (pairs_hbm, pairs_ref),
                (leaves_hbm, leaves_ref),
                (right_hbm, right_ref),
            )
        )
    ]
    for load in loads:
        load.start()
    for i in range(items):
        clear_rest(window_ref.at[i], exp_ref.shape[0])
    slots = pairs_ref.shape[0]
    own = own_ref[0]
    loads[0].wait()
    loads[1].wait()
    row = row_ref[0]

    def partner(i, coming):
        number = own * items + i
        pair, number = lax.div(number, send), lax.rem(number, send)
        other = source_row(row, pair, rows) if coming else target_row(row, pair, rows)
        if coming and own_items_change_cores(rows, items, send):
            number = jnp.where(other == row, 1 - number, number)
        return other, number

    for i in range(items):
        other, number = partner(i, False)
        leaf = pick_ref[other, number, row]
        unit = window_start(leaf_ref, leaf, width)
        place = item_place(slots, i)
        plan_ref[place], plan_ref[place + 1] = leaf, unit
        for copy in window_copies(exp_ref, unit, window_ref.at[i], window_sem.at[i], width):
            copy.start()
    for load in loads[2:]:
        load.wait()
    for s in range(slots):
        plan_ref[CODES + s] = pairs_ref[s]
    for i in range(items):
        place = item_place(slots, i)
        other, number = partner(i, True)
        leaf = target_ref[0, other * send + number]
        plan_ref[place + 2], plan_ref[place + 3] = leaf, window_start(leaf_ref, leaf, width)
        plan_ref[place + 4] = offset_ref[0, other * send + number]
    for i in range(items):
        place = item_place(slots, i)
        leaf, unit = plan_ref[place], plan_ref[place + 1]
        for copy in window_copies(exp_ref, unit, window_ref.at[i], window_sem.at[i], width):
            copy.wait()
        out_ref[i] = multi_rows(fields, width, leaf, unit, leaves_ref, right_ref, window_ref.at[i]).astype(BF16)


def fetch_kernel(items, width, slots, plan_ref, exp_ref, trans_ref, window_ref, moved_ref, trans_buf, sem, trans_sem):
    coefs = trans_ref.shape[3]
    for i in range(items):
        clear_rest(window_ref.at[i], coefs)

    def trans_copy(i):
        offset = plan_ref[item_place(slots, i) + 4]
        return pltpu.make_async_copy(trans_ref.at[offset], trans_buf.at[i], trans_sem.at[i])

    def exp_copies(i):
        unit = plan_ref[item_place(slots, i) + 3]
        return window_copies(exp_ref, unit, window_ref.at[i], sem.at[i], width)

    for i in range(items):
        trans_copy(i).start()
        for copy in exp_copies(i):
            copy.start()
    rest = moved_ref.shape[1] - 2 * coefs
    for i in range(items):
        trans_copy(i).wait()
        moved_ref[i, pl.ds(0, 2 * coefs)] = trans_buf[i].reshape(2 * coefs, coefs)
        moved_ref[i, pl.ds(2 * coefs, rest)] = jnp.zeros((rest, coefs), BF16)
        for copy in exp_copies(i):
            copy.wait()


def edge_places(row_ref, edge, units):
    even = lax.rem(row_ref[0], 2) == 0
    return jnp.where(even, 0, edge + units), jnp.where(even, edge + units, 0)


def part(total, core, keep_ref, give_ref):
    for k in range(keep_ref.shape[0]):
        keep_ref[k] = total[2 * k + core].astype(keep_ref.dtype)
        give_ref[k] = total[2 * k + 1 - core].astype(give_ref.dtype)


def near_kernel(fields, row_ref, count_ref, plan_ref, one_ref, two_ref, here_ref, tiles_ref, out_ref, ext):
    units = out_ref.shape[0]
    edge = (ext.shape[0] - units) // 2
    one_at, two_at = edge_places(row_ref, edge, units)
    for k in range(edge):
        lanes = slice(k * LANES, (k + 1) * LANES)
        ext[one_at + k] = one_ref[:, lanes].astype(ext.dtype)
        ext[two_at + k] = two_ref[:, lanes].astype(ext.dtype)
    for k in range(units):
        ext[edge + k] = here_ref[:, k * LANES : (k + 1) * LANES]
    out_ref[...] = jnp.zeros_like(out_ref)
    near_slots(fields, count_ref, plan_ref, tiles_ref, out_ref, ext)


def last_near_kernel(
    fields, core_ref, row_ref, count_ref, plan_ref, one_ref, other_one_ref, two_ref, here_ref, tiles_ref, image_ref,
    keep_ref, give_ref, ext, total,
):
    units = total.shape[0]
    edge = (ext.shape[0] - units) // 2
    core = core_ref[0]
    one_at, two_at = edge_places(row_ref, edge, units)
    for k in range(edge // 2):
        ext[one_at + 2 * k + core] = one_ref[k]
        ext[one_at + 2 * k + 1 - core] = other_one_ref[k]
    ext[pl.ds(two_at, edge)] = two_ref[...]
    ext[edge : edge + units] = here_ref[...]
    total[...] = jnp.zeros_like(total)
    items, width = image_ref.shape[:2]
    for i in range(items):
        unit = plan_ref[item_place(tiles_ref.shape[1], i) + 3]
        for k in range(width):
            total[unit + k] += image_ref[i, k]
    near_slots(fields, count_ref, plan_ref, tiles_ref, total, ext)
    part(total, core_ref[0], keep_ref, give_ref)


def near_slots(fields, count_ref, plan_ref, tiles_ref, out_ref, ext):
    slots, tile = tiles_ref.shape[1], tiles_ref.shape[2]
    per = tile // LANES
    for s in range(slots):
        code = plan_ref[CODES + s]
        target = lax.div(code, SPAN)
        source = target + lax.rem(code, SPAN)
        rows = halves(jnp.concatenate([ext[source * per + k] for k in range(per)], axis=-1))
        on_real = joined(dot_nt(rows, tiles_ref[0, s]), 2 * fields)
        on_imag = joined(dot_nt(rows, tiles_ref[1, s]), 2 * fields)
        value = jnp.concatenate(
            [on_real[:fields] - on_imag[fields:], on_real[fields:] + on_imag[:fields]], axis=0
        )
        value = jnp.where(s < count_ref[0], value, 0.0)
        for k in range(per):
            out_ref[target * per + k] += value[:, k * LANES : (k + 1) * LANES]


def far_kernel(
    fields, items, width, slots, core_ref, plan_ref, leaves_ref, partial_ref, item_ref, trans_ref, window_ref,
    keep_ref, give_ref, total,
):
    total[...] = partial_ref[...]

    def add(i, unit, image):
        for k in range(width):
            total[unit + k] += image[:, k * LANES : (k + 1) * LANES]

    far_images(fields, items, width, slots, plan_ref, leaves_ref, item_ref, trans_ref, window_ref, add)
    part(total, core_ref[0], keep_ref, give_ref)


def first_far_kernel(
    fields, items, width, slots, plan_ref, leaves_ref, item_ref, trans_ref, window_ref, image_ref
):
    def store(i, unit, image):
        for k in range(width):
            image_ref[i, k] = image[:, k * LANES : (k + 1) * LANES]

    far_images(fields, items, width, slots, plan_ref, leaves_ref, item_ref, trans_ref, window_ref, store)


def far_images(fields, items, width, slots, plan_ref, leaves_ref, item_ref, trans_ref, window_ref, give):
    for i in range(items):
        plain = item_ref[i, :, : trans_ref.shape[1]].astype(F32)
        odd = odd_lanes(plain.shape)
        turned = jnp.where(odd, from_left(plain), -from_right(plain))
        rows = jnp.concatenate([plain, turned], axis=0).astype(BF16)
        local_field = dot_nn(rows, trans_ref[i]).astype(BF16).astype(F32)
        local_field = twice(local_field, plain.shape[1])
        local_real, local_imag = local_field[:fields], local_field[fields:]
        rows = jnp.concatenate(
            [jnp.where(odd, -local_imag, local_real), jnp.where(odd, local_real, local_imag)], axis=0
        ).astype(BF16)
        expansions = window_rows(window_ref.at[i])
        place = item_place(slots, i)
        leaf, unit = plan_ref[place + 2], plan_ref[place + 3]
        mask = window_mask(leaves_ref, leaf, unit, 2 * fields, width)
        image = jnp.where(mask, dot_nn(rows, expansions), 0.0)
        give(i, unit, image)


def pair_kernel(keep_ref, got_ref, out_ref):
    out_ref[...] = (keep_ref[...].astype(F32) + got_ref[...].astype(F32)).astype(out_ref.dtype)


def tree_sum(values):
    while len(values) > 1:
        values = [values[k] + values[k + 1] for k in range(0, len(values), 2)]
    return values[0]


def swap_order(chips):
    return list(range(chips - 1, 0, -1))


def by_step(parts):
    arrived = dict(zip(swap_order(len(parts)), parts[1:]))
    return [parts[0]] + [arrived[step] for step in range(1, len(parts))]


def close_kernel(*refs):
    refs[-1][...] = tree_sum([ref[...].astype(F32) for ref in by_step(refs[:-1])])


def assemble_kernel(
    fields, items, width, slots, core_ref, plan_ref, leaves_ref, mine_ref, theirs_ref, window_ref,
    out_ref, low_ref, made_ref,
):
    core = core_ref[0]
    for k in range(mine_ref.shape[0]):
        for ref, unit in ((mine_ref, 2 * k + core), (theirs_ref, 2 * k + 1 - core)):
            out_ref[unit] = ref[k]
            low_ref[unit] = ref[k].astype(BF16)
    for i in range(items):
        place = item_place(slots, i)
        made = multi_rows(
            fields, width, plan_ref[place], plan_ref[place + 1], leaves_ref, low_ref, window_ref.at[i]
        )
        made_ref[i, :, : made.shape[1]] = made.astype(BF16)


def flat_lines(totals, fields):
    per = LANES // fields
    lane = lax.broadcasted_iota(jnp.int32, (fields, LANES), 1)
    field = lax.broadcasted_iota(jnp.int32, (fields, LANES), 0)
    lines = []
    for first in range(0, len(totals), per):
        line = jnp.zeros((fields, LANES), F32)
        for k, total in enumerate(totals[first : first + per]):
            line = jnp.where(lane == field + k * fields, jnp.sum(total, axis=1, keepdims=True), line)
        lines.append(jnp.sum(line, axis=0, keepdims=True))
    return jnp.concatenate(lines, axis=0)


def columns_of(lines, count, fields):
    per = LANES // fields
    columns = []
    for k in range(lines.shape[0]):
        square = jnp.transpose(jnp.broadcast_to(lines[k : k + 1], (LANES, LANES)))
        columns += [square[j * fields : (j + 1) * fields] for j in range(per)]
    return columns[:count]


def gram_kernel(fields, core_ref, right_ref, image_ref, *refs):
    *parts, out_ref = refs
    totals = None
    for k in range(parts[0].shape[0]):
        unit = 2 * k + core_ref[0]
        r = right_ref[:, pl.ds(pl.multiple_of(unit * LANES, LANES), LANES)]
        z = image_ref[unit]
        q = tree_sum([part[k].astype(F32) for part in by_step(parts)])
        (rr, ri), (zr, zi), (qr, qi) = [(v[:fields], v[fields:]) for v in (r, z, q)]
        products = [
            rr * rr + ri * ri,
            rr * zr + ri * zi,
            rr * zi - ri * zr,
            zr * zr + zi * zi,
            rr * qr + ri * qi,
            rr * qi - ri * qr,
            zr * qr + zi * qi,
            zr * qi - zi * qr,
            qr * qr + qi * qi,
        ]
        totals = products if totals is None else [t + p for t, p in zip(totals, products)]
    out_ref[...] = jnp.broadcast_to(flat_lines(totals, fields)[None], out_ref.shape)


def final_kernel(fields, sums_ref, right_ref, image_ref, out_ref):
    units = image_ref.shape[0]
    sums = columns_of(jnp.sum(sums_ref[...], axis=0), 9, fields)
    a_real, a_imag, b_real, b_imag = krylov_coefficients(sums)
    for k in range(units):
        lanes = slice(k * LANES, (k + 1) * LANES)
        r_real, r_imag = right_ref[:fields, lanes], right_ref[fields:, lanes]
        z_real, z_imag = image_ref[k, :fields], image_ref[k, fields:]
        out_ref[:fields, lanes] = a_real * r_real - a_imag * r_imag + b_real * z_real - b_imag * z_imag
        out_ref[fields:, lanes] = a_real * r_imag + a_imag * r_real + b_real * z_imag + b_imag * z_real


def params(mebibytes=16):
    return pltpu.CompilerParams(vmem_limit_bytes=mebibytes * 1024 * 1024)


def is_power(count):
    return count & (count - 1) == 0


def reversed_bits(value, count):
    bits = count.bit_length() - 1
    return sum(((value >> k) & 1) << (bits - 1 - k) for k in range(bits))


def target_row(row, pair, rows):
    if not is_power(rows):
        return (pair - row + rows) % rows
    return pair ^ reversed_bits(row, rows)


def source_row(row, pair, rows):
    if not is_power(rows):
        return (pair - row + rows) % rows
    return reversed_bits(pair ^ row, rows)


def own_items_change_cores(rows, items, send):
    return items == 1 and send == 2


def item_route(rows, group, columns, send):
    items = rows * send // group

    def flat(r, g):
        return (g // columns * rows + r) * columns + g % columns

    def target(r, g, pair):
        d = target_row(r, pair, rows)
        return flat(d, g ^ 1 if d == r and own_items_change_cores(rows, items, send) else g)

    assert items * group == rows * send and (items % send == 0 or send % items == 0)
    routes = []
    for first in range(0, items, send):
        pairs = [(g * items + first) // send for g in range(group)]
        routes.append([(flat(r, g), target(r, g, pairs[g])) for r in range(rows) for g in range(group)])
    return items, routes


def local(
    right_side,
    near_tiles,
    tile_pairs,
    tile_count,
    panel_expansions,
    leaf_of_panel,
    far_pick,
    far_target,
    far_offset,
    translations,
):
    fields, panels = right_side.shape[1:]
    coefs = panel_expansions.shape[2]
    tile = near_tiles.shape[2]
    send = far_pick.shape[2]
    rows = lax.axis_size("row")
    group = lax.axis_size("grp") * lax.axis_size("col")
    row_here = lax.axis_index("row")
    own = lax.axis_index("grp") * lax.axis_size("col") + lax.axis_index("col")
    both = 2 * fields
    units = panels // LANES
    edge = REACH * tile
    edge_units = edge // LANES
    width = tile // LANES + 1
    items, routes = item_route(rows, group, lax.axis_size("col"), send)

    assert rows % 2 == 0
    neighbours = [[(r - 1 + 2 * (r % 2)) % rows for r in range(rows)], [r + 1 - 2 * (r % 2) for r in range(rows)]]
    own_place, row_place = own.reshape(1), row_here.reshape(1)
    core_place = lax.rem(own, 2).reshape(1)
    slots = near_tiles.shape[1]
    pad_coefs = -(-coefs // 8) * 8
    chips = group // 2
    assert group == 2 * chips and chips & (chips - 1) == 0 and LANES % fields == 0
    window_shape = jax.ShapeDtypeStruct((items, pad_coefs, width, 2, LANES), BF16)
    item_shape = jax.ShapeDtypeStruct((items, fields, 2 * pad_coefs), BF16)
    half_units = (units // 2, both, LANES)
    assert units % 2 == 0 and edge_units % 2 == 0

    def in_hbm(value):
        return pltpu.with_memory_space_constraint(value, pltpu.HBM)

    leaves = leaf_of_panel.reshape(units, 1, LANES)
    expansions = panel_expansions.transpose(2, 0, 1).reshape(coefs, 2, units, LANES).transpose(0, 2, 1, 3)
    expansions = in_hbm(expansions)
    moves = in_hbm(translations.transpose(0, 2, 1, 3))
    picks = far_pick.transpose(0, 2, 1)

    plan, made, windows, leaves, right = pl.pallas_call(
        functools.partial(begin_kernel, fields, items, width, send, rows),
        out_shape=(
            pltpu.SMEM((item_place(slots, items),), jnp.int32),
            item_shape,
            pltpu.VMEM(window_shape.shape, BF16),
            jax.ShapeDtypeStruct(leaves.shape, jnp.int32),
            jax.ShapeDtypeStruct((both, panels), F32),
        ),
        in_specs=[SMEM] * 2 + [HBM] * 8,
        out_specs=(SMEM,) + (VMEM,) * 4,
        scratch_shapes=[
            pltpu.SMEM(value.shape, jnp.int32)
            for value in (picks, leaf_of_panel, far_target, far_offset, tile_pairs)
        ]
        + [
            pltpu.SemaphoreType.DMA((7,)),
            pltpu.SemaphoreType.DMA((items, PIECES)),
        ],
        compiler_params=params(),
        name="begin",
    )(
        row_place,
        own_place,
        in_hbm(picks),
        in_hbm(leaf_of_panel),
        in_hbm(leaves),
        in_hbm(far_target),
        in_hbm(far_offset),
        in_hbm(tile_pairs),
        in_hbm(right_side.reshape(both, panels)),
        expansions,
    )

    def exchanged(made):
        parts = [
            lax.ppermute(made[k * send : k * send + min(send, items)], EVERY, route) for k, route in enumerate(routes)
        ]
        return parts[0] if len(parts) == 1 else jnp.concatenate(parts)

    def along_row(value, which):
        return lax.ppermute(value, "row", list(enumerate(neighbours[which])))

    def from_neighbours(image):
        one, two = pl.pallas_call(
            edge_kernel,
            out_shape=(jax.ShapeDtypeStruct((both, edge), BF16),) * 2,
            in_specs=[SMEM, VMEM],
            out_specs=(VMEM, VMEM),
            compiler_params=params(),
            name="edges",
        )(row_place, image)
        return along_row(one, 0), along_row(two, 1)

    def one_edge(image, edge_units, early):
        return pl.pallas_call(
            functools.partial(one_edge_kernel, early),
            out_shape=jax.ShapeDtypeStruct((edge_units, both, LANES), BF16),
            in_specs=[SMEM, VMEM],
            out_specs=VMEM,
            compiler_params=params(),
            name="edge",
        )(row_place, image)

    image_shape = jax.ShapeDtypeStruct((units, both, LANES), F32)
    target_windows, moved = pl.pallas_call(
        functools.partial(fetch_kernel, items, width, slots),
        out_shape=(
            pltpu.VMEM(window_shape.shape, BF16),
            pltpu.VMEM((items, 2 * pad_coefs, coefs), BF16),
        ),
        in_specs=[SMEM, HBM, HBM],
        out_specs=(VMEM, VMEM),
        scratch_shapes=[
            pltpu.VMEM((items, coefs, 2, coefs), BF16),
            pltpu.SemaphoreType.DMA((items, PIECES)),
            pltpu.SemaphoreType.DMA((items,)),
        ],
        compiler_params=params(24),
        cost_estimate=pl.CostEstimate(flops=0, bytes_accessed=6 * window_shape.size, transcendentals=0),
        name="fetch",
    )(plan, expansions, moves)

    def swapped(value, step):
        return lax.ppermute(value, GROUP, [(g, g ^ step) for g in range(group)])

    def near(one, two, low):
        return pl.pallas_call(
            functools.partial(near_kernel, fields),
            out_shape=image_shape,
            in_specs=[SMEM] * 3 + [VMEM] * 4,
            out_specs=VMEM,
            scratch_shapes=[pltpu.VMEM((units + 2 * edge_units, both, LANES), low.dtype)],
            compiler_params=params(),
            cost_estimate=pl.CostEstimate(
                flops=8 * fields * near_tiles.size // 2, bytes_accessed=2 * near_tiles.size, transcendentals=0
            ),
            name="near",
        )(row_place, tile_count, plan, one, two, low, near_tiles)

    def core_parts(partial, taken):
        keep, give = pl.pallas_call(
            functools.partial(far_kernel, fields, items, width, slots),
            out_shape=(jax.ShapeDtypeStruct(half_units, F32), jax.ShapeDtypeStruct(half_units, BF16)),
            in_specs=[SMEM, SMEM] + [VMEM] * 5,
            out_specs=(VMEM, VMEM),
            scratch_shapes=[pltpu.VMEM(image_shape.shape, F32)],
            compiler_params=params(),
            name="far",
        )(core_place, plan, leaves, partial, taken, moved, target_windows)
        return keep, swapped(give, 1)

    def first_far(taken):
        return pl.pallas_call(
            functools.partial(first_far_kernel, fields, items, width, slots),
            out_shape=jax.ShapeDtypeStruct((items, width, both, LANES), F32),
            in_specs=[SMEM] + [VMEM] * 4,
            out_specs=VMEM,
            compiler_params=params(),
            name="first_far",
        )(plan, leaves, taken, moved, target_windows)

    def last_core_parts(one, other_one, two, low, image):
        half_shape = jax.ShapeDtypeStruct(half_units, BF16)
        keep, give = pl.pallas_call(
            functools.partial(last_near_kernel, fields),
            out_shape=(half_shape, half_shape),
            in_specs=[SMEM] * 4 + [VMEM] * 6,
            out_specs=(VMEM, VMEM),
            scratch_shapes=[
                pltpu.VMEM((units + 2 * edge_units, both, LANES), low.dtype),
                pltpu.VMEM(image_shape.shape, F32),
            ],
            compiler_params=params(),
            name="last_near",
        )(core_place, row_place, tile_count, plan, one, other_one, two, low, near_tiles, image)
        return keep, swapped(give, 1)

    def pair_sums(keep, got):
        pair = pl.pallas_call(
            pair_kernel,
            out_shape=jax.ShapeDtypeStruct(keep.shape, BF16),
            in_specs=[VMEM, VMEM],
            out_specs=VMEM,
            compiler_params=params(),
            name="pair",
        )(keep, got)
        arrived = {step: swapped(pair, 2 * step) for step in swap_order(chips)}
        return [pair] + list(arrived.values())

    def half_sum(parts):
        return pl.pallas_call(
            close_kernel,
            out_shape=jax.ShapeDtypeStruct(half_units, F32),
            in_specs=[VMEM] * chips,
            out_specs=VMEM,
            compiler_params=params(),
            name="close",
        )(*parts)

    def whole(mine, theirs):
        return pl.pallas_call(
            functools.partial(assemble_kernel, fields, items, width, slots),
            out_shape=(
                image_shape,
                jax.ShapeDtypeStruct(image_shape.shape, BF16),
                jax.ShapeDtypeStruct((items, fields, 2 * pad_coefs + ITEM_REST), BF16),
            ),
            in_specs=[SMEM, SMEM] + [VMEM] * 4,
            out_specs=(VMEM,) * 3,
            compiler_params=params(),
            name="assemble",
        )(core_place, plan, leaves, mine, theirs, windows)

    partial = near(*from_neighbours(right), right)
    mine = half_sum(pair_sums(*core_parts(partial, exchanged(made))))
    theirs = swapped(mine, 1)
    one = along_row(one_edge(mine, edge_units // 2, True), 0)
    z_all, z_low, made = whole(mine, theirs)
    image = first_far(exchanged(made))
    two = along_row(one_edge(z_low, edge_units, False), 1)
    parts = pair_sums(*last_core_parts(one, swapped(one, 1), two, z_low, image))

    lines = pl.pallas_call(
        functools.partial(gram_kernel, fields),
        out_shape=jax.ShapeDtypeStruct((2 * rows, -(-9 * fields // LANES), LANES), F32),
        in_specs=[SMEM] + [VMEM] * (2 + chips),
        out_specs=VMEM,
        compiler_params=params(),
        name="gram",
    )(core_place, right, z_all, *parts)
    columns = lax.axis_size("col")
    same_chip = [
        [((g + k) // columns * rows + r) * columns + (g + k) % columns for r in range(rows) for k in range(2)]
        for g in range(0, group, 2)
    ]
    sums = lax.all_to_all(lines, EVERY, 0, 0, axis_index_groups=same_chip, tiled=True)
    out = pl.pallas_call(
        functools.partial(final_kernel, fields),
        out_shape=jax.ShapeDtypeStruct((both, panels), F32),
        in_specs=[VMEM] * 3,
        out_specs=VMEM,
        compiler_params=params(),
        name="combine",
    )(sums, right, z_all)
    return out.reshape(right_side.shape)


def krylov_coefficients(sums):
    rr, rz_real, rz_imag, zz, rq_real, rq_imag, zq_real, zq_imag, qq = sums

    def times(left, right):
        return left[0] * right[0] - left[1] * right[1], left[0] * right[1] + left[1] * right[0]

    def conj_times(left, right):
        return left[0] * right[0] + left[1] * right[1], left[0] * right[1] - left[1] * right[0]

    def scale(factor, value):
        return factor * value[0], factor * value[1]

    def plus(*values):
        return sum(v[0] for v in values), sum(v[1] for v in values)

    def size(value):
        return value[0] * value[0] + value[1] * value[1]

    rz, rq, zq = (rz_real, rz_imag), (rq_real, rq_imag), (zq_real, zq_imag)
    beta = jnp.sqrt(rr + EPSILON)
    inv = 1.0 / beta
    norm_one = rr * inv * inv
    product = scale(inv * inv, rz)
    h_first = (0.5 * norm_one + product[0], product[1])
    shift = (h_first[0] - 0.5, h_first[1])
    residue = zz * inv * inv - 2.0 * conj_times(shift, product)[0] + size(shift) * norm_one
    residue = jnp.maximum(residue, 0.0)
    h_sub = jnp.sqrt(residue + EPSILON)
    alpha = inv / h_sub
    gamma = scale(-alpha, shift)
    h_upper = scale(
        inv,
        plus(
            scale(0.5, plus(scale(alpha, rz), scale(rr, gamma))), scale(alpha, rq), times(gamma, rz)
        ),
    )
    second = plus(
        scale(alpha * alpha, zq),
        scale(alpha * zz, gamma),
        scale(alpha, conj_times(gamma, rq)),
        scale(size(gamma), rz),
    )
    h_middle = (0.5 * residue / (h_sub * h_sub) + second[0], second[1])
    keep = (h_middle[0] - 0.5, h_middle[1])
    on_z = plus(gamma, scale(-alpha, keep))
    on_r = plus(scale(-inv, h_upper), scale(-1.0, times(keep, gamma)))
    last = (
        alpha * alpha * qq
        + size(on_z) * zz
        + size(on_r) * rr
        + 2.0
        * (
            conj_times(on_r, times(on_z, rz))[0]
            + alpha * conj_times(on_r, rq)[0]
            + alpha * conj_times(on_z, zq)[0]
        )
    )
    h_last = jnp.sqrt(jnp.maximum(last, 0.0) + EPSILON)
    radius = jnp.sqrt(size(h_first) + h_sub * h_sub)
    cosine = scale(1.0 / radius, h_first)
    sine = h_sub / radius
    upper = plus(conj_times(cosine, h_upper), scale(sine, h_middle))
    lower = plus(times(cosine, h_middle), scale(-sine, h_upper))
    radius_two = jnp.sqrt(size(lower) + h_last * h_last)
    cosine_two = scale(1.0 / radius_two, lower)
    weight_two = scale(-sine * beta / radius_two, (cosine_two[0], -cosine_two[1]))
    goal = scale(beta, (cosine[0], -cosine[1]))
    weight_one = scale(1.0 / radius, plus(goal, scale(-1.0, times(upper, weight_two))))
    on_right = plus(scale(inv, weight_one), times(weight_two, gamma))
    on_image = scale(alpha, weight_two)
    return on_right[0], on_right[1], on_image[0], on_image[1]


def solution(mesh):
    return jax.shard_map(
        local,
        mesh=mesh,
        in_specs=(
            P(None, None, "row"),
            P(None, ("grp", "row", "col"), None, None),
            P(("grp", "row", "col")),
            P(("grp", "row", "col")),
            P(None, "row", None),
            P("row", None),
            P(),
            P("row", None),
            P("row", None),
            P(),
        ),
        out_specs=P(None, None, "row"),
        check_vma=False,
    )
```

```python
import functools

import jax
import jax.numpy as jnp
from jax import lax
from jax.experimental import pallas as pl
from jax.experimental.pallas import tpu as pltpu
from jax.sharding import PartitionSpec as P

REACH = 2
SPAN = 2 * REACH + 1
LANES = 128
EPSILON = 1e-06
GROUP = ("grp", "col")
CODES = 0
PER_ITEM = 5
ITEM_REST = LANES
PIECES = 4
EVERY = ("grp", "row", "col")

F32 = jnp.float32
BF16 = jnp.bfloat16
SMEM = pl.BlockSpec(memory_space=pltpu.SMEM)
VMEM = pl.BlockSpec(memory_space=pltpu.VMEM)
HBM = pl.BlockSpec(memory_space=pltpu.HBM)
ANY = pl.BlockSpec(memory_space=pl.ANY)


def dot_nn(left, right):
    return lax.dot_general(left, right, (((1,), (0,)), ((), ())), preferred_element_type=F32)


def dot_nt(left, right):
    return lax.dot_general(left, right, (((1,), (1,)), ((), ())), preferred_element_type=F32)


def halves(rows):
    if rows.dtype != F32:
        return rows
    high = rows.astype(BF16)
    return jnp.concatenate([high, (rows - high.astype(F32)).astype(BF16)], axis=0)


def joined(sums, count):
    return sums if sums.shape[0] == count else sums[:count] + sums[count:]


def odd_lanes(shape):
    return lax.rem(lax.broadcasted_iota(jnp.int32, shape, 1), 2) == 1


def twice(value, width):
    rows = value.shape[0]
    parts = []
    for k in range(width // LANES):
        first = (k // 2) * LANES
        part = value[:, first : first + LANES]
        if part.shape[1] < LANES:
            part = jnp.concatenate([part, jnp.zeros((rows, LANES - part.shape[1]), part.dtype)], axis=-1)
        lane = lax.broadcasted_iota(jnp.int32, (rows, LANES), 1)
        parts.append(jnp.take_along_axis(part, lax.div(lane, 2) + (k % 2) * (LANES // 2), axis=1))
    return jnp.concatenate(parts, axis=-1)


def from_left(value):
    return pltpu.roll(value, 1, 1)


def from_right(value):
    return pltpu.roll(value, value.shape[1] - 1, 1)


def item_place(slots, item):
    return CODES + slots + PER_ITEM * item


def window_start(leaf_ref, leaf, width):
    units = leaf_ref.shape[1] // LANES
    before = jnp.int32(0)
    for k in range(units):
        before = before + (leaf_ref[0, k * LANES] < leaf).astype(jnp.int32)
    return jnp.clip(before - 1, 0, units - width)


def window_mask(leaves_ref, leaf, unit, rows, width):
    leaves = jnp.concatenate([leaves_ref[unit + k] for k in range(width)], axis=-1)
    return jnp.broadcast_to(leaves, (rows, width * LANES)) == leaf


def window_copies(exp_ref, unit, window_ref, sem, width):
    coefs = exp_ref.shape[0]
    step = -(-coefs // PIECES)
    copies = []
    for p in range(PIECES):
        part = pl.ds(p * step, min(step, coefs - p * step))
        copies.append(
            pltpu.make_async_copy(exp_ref.at[part, pl.ds(unit, width)], window_ref.at[part], sem.at[p])
        )
    return copies


def clear_rest(window_ref, coefs):
    rest = window_ref.shape[0] - coefs
    window_ref[pl.ds(coefs, rest)] = jnp.zeros((rest, *window_ref.shape[1:]), BF16)


def window_rows(window_ref):
    coefs, width = window_ref.shape[:2]
    return jnp.concatenate([window_ref[:, k].reshape(2 * coefs, LANES) for k in range(width)], axis=-1)


def multi_rows(fields, width, leaf, unit, leaves_ref, low_ref, window_ref):
    if len(low_ref.shape) == 2:
        first = pl.multiple_of(unit * LANES, LANES)
        rows = low_ref[:, pl.ds(first, width * LANES)]
    else:
        rows = jnp.concatenate([low_ref[unit + k] for k in range(width)], axis=-1)
    mask = window_mask(leaves_ref, leaf, unit, 2 * fields, width)
    rows = halves(jnp.where(mask, rows.astype(F32), 0.0).astype(rows.dtype))
    total = joined(dot_nt(rows, window_rows(window_ref)), 2 * fields)
    on_real, on_imag = total[:fields], total[fields:]
    odd = odd_lanes(on_real.shape)
    other = jnp.where(odd, from_left(on_imag), from_right(on_imag))
    return jnp.where(odd, -on_real, on_real) - other


def edge_kernel(row_ref, image_ref, one_ref, two_ref):
    edge_of(row_ref, image_ref, one_ref, True)
    edge_of(row_ref, image_ref, two_ref, False)


def one_edge_kernel(early, row_ref, image_ref, out_ref):
    edge_of(row_ref, image_ref, out_ref, early)


def edge_of(row_ref, image_ref, out_ref, early):
    first_edge = (lax.rem(row_ref[0], 2) == 0) if early else (lax.rem(row_ref[0], 2) == 1)
    if len(image_ref.shape) == 2:
        edge = out_ref.shape[1]
        first, last = image_ref[:, :edge], image_ref[:, image_ref.shape[1] - edge :]
    else:
        edge = out_ref.shape[0]
        first, last = image_ref[:edge], image_ref[image_ref.shape[0] - edge :]

    @pl.when(first_edge)
    def _():
        out_ref[...] = first.astype(out_ref.dtype)

    @pl.when(jnp.logical_not(first_edge))
    def _():
        out_ref[...] = last.astype(out_ref.dtype)


def begin_kernel(
    fields, items, width, send, rows, row_ref, own_ref, pick_hbm, leaf_hbm, leaves_hbm,
    target_hbm, offset_hbm, pairs_hbm, right_hbm, exp_ref,
    plan_ref, out_ref, window_ref, leaves_ref, right_ref,
    pick_ref, leaf_ref, target_ref, offset_ref, pairs_ref, sem, window_sem,
):
    loads = [
        pltpu.make_async_copy(source, place, sem.at[k])
        for k, (source, place) in enumerate(
            (
                (leaf_hbm, leaf_ref),
                (pick_hbm, pick_ref),
                (target_hbm, target_ref),
                (offset_hbm, offset_ref),
                (pairs_hbm, pairs_ref),
                (leaves_hbm, leaves_ref),
                (right_hbm, right_ref),
            )
        )
    ]
    for load in loads:
        load.start()
    for i in range(items):
        clear_rest(window_ref.at[i], exp_ref.shape[0])
    slots = pairs_ref.shape[0]
    own = own_ref[0]
    loads[0].wait()
    loads[1].wait()
    row = row_ref[0]

    def partner(i, coming):
        number = own * items + i
        pair, number = lax.div(number, send), lax.rem(number, send)
        other = source_row(row, pair, rows) if coming else target_row(row, pair, rows)
        if coming and own_items_change_cores(rows, items, send):
            number = jnp.where(other == row, 1 - number, number)
        return other, number

    for i in range(items):
        other, number = partner(i, False)
        leaf = pick_ref[other, number, row]
        unit = window_start(leaf_ref, leaf, width)
        place = item_place(slots, i)
        plan_ref[place], plan_ref[place + 1] = leaf, unit
        for copy in window_copies(exp_ref, unit, window_ref.at[i], window_sem.at[i], width):
            copy.start()
    for load in loads[2:]:
        load.wait()
    for s in range(slots):
        plan_ref[CODES + s] = pairs_ref[s]
    for i in range(items):
        place = item_place(slots, i)
        other, number = partner(i, True)
        leaf = target_ref[0, other * send + number]
        plan_ref[place + 2], plan_ref[place + 3] = leaf, window_start(leaf_ref, leaf, width)
        plan_ref[place + 4] = offset_ref[0, other * send + number]
    for i in range(items):
        place = item_place(slots, i)
        leaf, unit = plan_ref[place], plan_ref[place + 1]
        for copy in window_copies(exp_ref, unit, window_ref.at[i], window_sem.at[i], width):
            copy.wait()
        out_ref[i] = multi_rows(fields, width, leaf, unit, leaves_ref, right_ref, window_ref.at[i]).astype(BF16)


def fetch_kernel(items, width, slots, plan_ref, exp_ref, trans_ref, window_ref, moved_ref, trans_buf, sem, trans_sem):
    coefs = trans_ref.shape[3]
    for i in range(items):
        clear_rest(window_ref.at[i], coefs)

    def trans_copy(i):
        offset = plan_ref[item_place(slots, i) + 4]
        return pltpu.make_async_copy(trans_ref.at[offset], trans_buf.at[i], trans_sem.at[i])

    def exp_copies(i):
        unit = plan_ref[item_place(slots, i) + 3]
        return window_copies(exp_ref, unit, window_ref.at[i], sem.at[i], width)

    for i in range(items):
        trans_copy(i).start()
        for copy in exp_copies(i):
            copy.start()
    rest = moved_ref.shape[1] - 2 * coefs
    for i in range(items):
        trans_copy(i).wait()
        moved_ref[i, pl.ds(0, 2 * coefs)] = trans_buf[i].reshape(2 * coefs, coefs)
        moved_ref[i, pl.ds(2 * coefs, rest)] = jnp.zeros((rest, coefs), BF16)
        for copy in exp_copies(i):
            copy.wait()


def edge_places(row_ref, edge, units):
    even = lax.rem(row_ref[0], 2) == 0
    return jnp.where(even, 0, edge + units), jnp.where(even, edge + units, 0)


def part(total, core, keep_ref, give_ref):
    for k in range(keep_ref.shape[0]):
        keep_ref[k] = total[2 * k + core].astype(keep_ref.dtype)
        give_ref[k] = total[2 * k + 1 - core].astype(give_ref.dtype)


def near_kernel(fields, row_ref, count_ref, plan_ref, one_ref, two_ref, here_ref, tiles_ref, out_ref, ext):
    units = out_ref.shape[0]
    edge = (ext.shape[0] - units) // 2
    one_at, two_at = edge_places(row_ref, edge, units)
    for k in range(edge):
        lanes = slice(k * LANES, (k + 1) * LANES)
        ext[one_at + k] = one_ref[:, lanes].astype(ext.dtype)
        ext[two_at + k] = two_ref[:, lanes].astype(ext.dtype)
    for k in range(units):
        ext[edge + k] = here_ref[:, k * LANES : (k + 1) * LANES]
    out_ref[...] = jnp.zeros_like(out_ref)
    near_slots(fields, count_ref, plan_ref, tiles_ref, out_ref, ext)


def last_near_kernel(
    fields, core_ref, row_ref, count_ref, plan_ref, one_ref, other_one_ref, two_ref, here_ref, tiles_ref, image_ref,
    keep_ref, give_ref, ext, total,
):
    units = total.shape[0]
    edge = (ext.shape[0] - units) // 2
    core = core_ref[0]
    one_at, two_at = edge_places(row_ref, edge, units)
    for k in range(edge // 2):
        ext[one_at + 2 * k + core] = one_ref[k]
        ext[one_at + 2 * k + 1 - core] = other_one_ref[k]
    ext[pl.ds(two_at, edge)] = two_ref[...]
    ext[edge : edge + units] = here_ref[...]
    total[...] = jnp.zeros_like(total)
    items, width = image_ref.shape[:2]
    for i in range(items):
        unit = plan_ref[item_place(tiles_ref.shape[1], i) + 3]
        for k in range(width):
            total[unit + k] += image_ref[i, k]
    near_slots(fields, count_ref, plan_ref, tiles_ref, total, ext)
    part(total, core_ref[0], keep_ref, give_ref)


def near_slots(fields, count_ref, plan_ref, tiles_ref, out_ref, ext):
    slots, tile = tiles_ref.shape[1], tiles_ref.shape[2]
    per = tile // LANES
    for s in range(slots):
        code = plan_ref[CODES + s]
        target = lax.div(code, SPAN)
        source = target + lax.rem(code, SPAN)
        rows = halves(jnp.concatenate([ext[source * per + k] for k in range(per)], axis=-1))
        on_real = joined(dot_nt(rows, tiles_ref[0, s]), 2 * fields)
        on_imag = joined(dot_nt(rows, tiles_ref[1, s]), 2 * fields)
        value = jnp.concatenate(
            [on_real[:fields] - on_imag[fields:], on_real[fields:] + on_imag[:fields]], axis=0
        )
        value = jnp.where(s < count_ref[0], value, 0.0)
        for k in range(per):
            out_ref[target * per + k] += value[:, k * LANES : (k + 1) * LANES]


def far_kernel(
    fields, items, width, slots, core_ref, plan_ref, leaves_ref, partial_ref, item_ref, trans_ref, window_ref,
    keep_ref, give_ref, total,
):
    total[...] = partial_ref[...]

    def add(i, unit, image):
        for k in range(width):
            total[unit + k] += image[:, k * LANES : (k + 1) * LANES]

    far_images(fields, items, width, slots, plan_ref, leaves_ref, item_ref, trans_ref, window_ref, add)
    part(total, core_ref[0], keep_ref, give_ref)


def first_far_kernel(
    fields, items, width, slots, plan_ref, leaves_ref, item_ref, trans_ref, window_ref, image_ref
):
    def store(i, unit, image):
        for k in range(width):
            image_ref[i, k] = image[:, k * LANES : (k + 1) * LANES]

    far_images(fields, items, width, slots, plan_ref, leaves_ref, item_ref, trans_ref, window_ref, store)


def far_images(fields, items, width, slots, plan_ref, leaves_ref, item_ref, trans_ref, window_ref, give):
    for i in range(items):
        plain = item_ref[i, :, : trans_ref.shape[1]].astype(F32)
        odd = odd_lanes(plain.shape)
        turned = jnp.where(odd, from_left(plain), -from_right(plain))
        rows = jnp.concatenate([plain, turned], axis=0).astype(BF16)
        local_field = dot_nn(rows, trans_ref[i]).astype(BF16).astype(F32)
        local_field = twice(local_field, plain.shape[1])
        local_real, local_imag = local_field[:fields], local_field[fields:]
        rows = jnp.concatenate(
            [jnp.where(odd, -local_imag, local_real), jnp.where(odd, local_real, local_imag)], axis=0
        ).astype(BF16)
        expansions = window_rows(window_ref.at[i])
        place = item_place(slots, i)
        leaf, unit = plan_ref[place + 2], plan_ref[place + 3]
        mask = window_mask(leaves_ref, leaf, unit, 2 * fields, width)
        image = jnp.where(mask, dot_nn(rows, expansions), 0.0)
        give(i, unit, image)


def pair_kernel(keep_ref, got_ref, out_ref):
    out_ref[...] = (keep_ref[...].astype(F32) + got_ref[...].astype(F32)).astype(out_ref.dtype)


def tree_sum(values):
    while len(values) > 1:
        values = [values[k] + values[k + 1] for k in range(0, len(values), 2)]
    return values[0]


def swap_order(chips):
    return [chips - 1] + list(range(1, chips - 1))


def by_step(parts):
    arrived = dict(zip(swap_order(len(parts)), parts[1:]))
    return [parts[0]] + [arrived[step] for step in range(1, len(parts))]


def close_kernel(*refs):
    refs[-1][...] = tree_sum([ref[...].astype(F32) for ref in by_step(refs[:-1])])


def assemble_kernel(
    fields, items, width, slots, core_ref, plan_ref, leaves_ref, mine_ref, theirs_ref, window_ref,
    out_ref, low_ref, made_ref,
):
    core = core_ref[0]
    for k in range(mine_ref.shape[0]):
        for ref, unit in ((mine_ref, 2 * k + core), (theirs_ref, 2 * k + 1 - core)):
            out_ref[unit] = ref[k]
            low_ref[unit] = ref[k].astype(BF16)
    for i in range(items):
        place = item_place(slots, i)
        made = multi_rows(
            fields, width, plan_ref[place], plan_ref[place + 1], leaves_ref, low_ref, window_ref.at[i]
        )
        made_ref[i, :, : made.shape[1]] = made.astype(BF16)


def flat_lines(totals, fields):
    per = LANES // fields
    lane = lax.broadcasted_iota(jnp.int32, (fields, LANES), 1)
    field = lax.broadcasted_iota(jnp.int32, (fields, LANES), 0)
    lines = []
    for first in range(0, len(totals), per):
        line = jnp.zeros((fields, LANES), F32)
        for k, total in enumerate(totals[first : first + per]):
            line = jnp.where(lane == field + k * fields, jnp.sum(total, axis=1, keepdims=True), line)
        lines.append(jnp.sum(line, axis=0, keepdims=True))
    return jnp.concatenate(lines, axis=0)


def columns_of(lines, count, fields):
    per = LANES // fields
    columns = []
    for k in range(lines.shape[0]):
        square = jnp.transpose(jnp.broadcast_to(lines[k : k + 1], (LANES, LANES)))
        columns += [square[j * fields : (j + 1) * fields] for j in range(per)]
    return columns[:count]


def gram_kernel(fields, core_ref, right_ref, image_ref, *refs):
    *parts, out_ref = refs
    totals = None
    for k in range(parts[0].shape[0]):
        unit = 2 * k + core_ref[0]
        r = right_ref[:, pl.ds(pl.multiple_of(unit * LANES, LANES), LANES)]
        z = image_ref[unit]
        q = tree_sum([part[k].astype(F32) for part in by_step(parts)])
        (rr, ri), (zr, zi), (qr, qi) = [(v[:fields], v[fields:]) for v in (r, z, q)]
        products = [
            rr * rr + ri * ri,
            rr * zr + ri * zi,
            rr * zi - ri * zr,
            zr * zr + zi * zi,
            rr * qr + ri * qi,
            rr * qi - ri * qr,
            zr * qr + zi * qi,
            zr * qi - zi * qr,
            qr * qr + qi * qi,
        ]
        totals = products if totals is None else [t + p for t, p in zip(totals, products)]
    out_ref[...] = jnp.broadcast_to(flat_lines(totals, fields)[None], out_ref.shape)


def final_kernel(fields, sums_ref, right_ref, image_ref, out_ref):
    units = image_ref.shape[0]
    sums = columns_of(jnp.sum(sums_ref[...], axis=0), 9, fields)
    a_real, a_imag, b_real, b_imag = krylov_coefficients(sums)
    for k in range(units):
        lanes = slice(k * LANES, (k + 1) * LANES)
        r_real, r_imag = right_ref[:fields, lanes], right_ref[fields:, lanes]
        z_real, z_imag = image_ref[k, :fields], image_ref[k, fields:]
        out_ref[:fields, lanes] = a_real * r_real - a_imag * r_imag + b_real * z_real - b_imag * z_imag
        out_ref[fields:, lanes] = a_real * r_imag + a_imag * r_real + b_real * z_imag + b_imag * z_real


def params(mebibytes=16):
    return pltpu.CompilerParams(vmem_limit_bytes=mebibytes * 1024 * 1024)


def is_power(count):
    return count & (count - 1) == 0


def reversed_bits(value, count):
    bits = count.bit_length() - 1
    return sum(((value >> k) & 1) << (bits - 1 - k) for k in range(bits))


def target_row(row, pair, rows):
    if not is_power(rows):
        return (pair - row + rows) % rows
    return pair ^ reversed_bits(row, rows)


def source_row(row, pair, rows):
    if not is_power(rows):
        return (pair - row + rows) % rows
    return reversed_bits(pair ^ row, rows)


def own_items_change_cores(rows, items, send):
    return items == 1 and send == 2


def item_route(rows, group, columns, send):
    items = rows * send // group

    def flat(r, g):
        return (g // columns * rows + r) * columns + g % columns

    def target(r, g, pair):
        d = target_row(r, pair, rows)
        return flat(d, g ^ 1 if d == r and own_items_change_cores(rows, items, send) else g)

    assert items * group == rows * send and (items % send == 0 or send % items == 0)
    routes = []
    for first in range(0, items, send):
        pairs = [(g * items + first) // send for g in range(group)]
        routes.append([(flat(r, g), target(r, g, pairs[g])) for r in range(rows) for g in range(group)])
    return items, routes


def local(
    right_side,
    near_tiles,
    tile_pairs,
    tile_count,
    panel_expansions,
    leaf_of_panel,
    far_pick,
    far_target,
    far_offset,
    translations,
):
    fields, panels = right_side.shape[1:]
    coefs = panel_expansions.shape[2]
    tile = near_tiles.shape[2]
    send = far_pick.shape[2]
    rows = lax.axis_size("row")
    group = lax.axis_size("grp") * lax.axis_size("col")
    row_here = lax.axis_index("row")
    own = lax.axis_index("grp") * lax.axis_size("col") + lax.axis_index("col")
    both = 2 * fields
    units = panels // LANES
    edge = REACH * tile
    edge_units = edge // LANES
    width = tile // LANES + 1
    items, routes = item_route(rows, group, lax.axis_size("col"), send)

    assert rows % 2 == 0
    neighbours = [[(r - 1 + 2 * (r % 2)) % rows for r in range(rows)], [r + 1 - 2 * (r % 2) for r in range(rows)]]
    own_place, row_place = own.reshape(1), row_here.reshape(1)
    core_place = lax.rem(own, 2).reshape(1)
    slots = near_tiles.shape[1]
    pad_coefs = -(-coefs // 8) * 8
    chips = group // 2
    assert group == 2 * chips and chips & (chips - 1) == 0 and LANES % fields == 0
    window_shape = jax.ShapeDtypeStruct((items, pad_coefs, width, 2, LANES), BF16)
    item_shape = jax.ShapeDtypeStruct((items, fields, 2 * pad_coefs), BF16)
    half_units = (units // 2, both, LANES)
    assert units % 2 == 0 and edge_units % 2 == 0

    def in_hbm(value):
        return pltpu.with_memory_space_constraint(value, pltpu.HBM)

    leaves = leaf_of_panel.reshape(units, 1, LANES)
    expansions = panel_expansions.transpose(2, 0, 1).reshape(coefs, 2, units, LANES).transpose(0, 2, 1, 3)
    expansions = in_hbm(expansions)
    moves = in_hbm(translations.transpose(0, 2, 1, 3))
    picks = far_pick.transpose(0, 2, 1)

    plan, made, windows, leaves, right = pl.pallas_call(
        functools.partial(begin_kernel, fields, items, width, send, rows),
        out_shape=(
            pltpu.SMEM((item_place(slots, items),), jnp.int32),
            item_shape,
            pltpu.VMEM(window_shape.shape, BF16),
            jax.ShapeDtypeStruct(leaves.shape, jnp.int32),
            jax.ShapeDtypeStruct((both, panels), F32),
        ),
        in_specs=[SMEM] * 2 + [HBM] * 8,
        out_specs=(SMEM,) + (VMEM,) * 4,
        scratch_shapes=[
            pltpu.SMEM(value.shape, jnp.int32)
            for value in (picks, leaf_of_panel, far_target, far_offset, tile_pairs)
        ]
        + [
            pltpu.SemaphoreType.DMA((7,)),
            pltpu.SemaphoreType.DMA((items, PIECES)),
        ],
        compiler_params=params(),
        name="begin",
    )(
        row_place,
        own_place,
        in_hbm(picks),
        in_hbm(leaf_of_panel),
        in_hbm(leaves),
        in_hbm(far_target),
        in_hbm(far_offset),
        in_hbm(tile_pairs),
        in_hbm(right_side.reshape(both, panels)),
        expansions,
    )

    def exchanged(made):
        parts = [
            lax.ppermute(made[k * send : k * send + min(send, items)], EVERY, route) for k, route in enumerate(routes)
        ]
        return parts[0] if len(parts) == 1 else jnp.concatenate(parts)

    def along_row(value, which):
        return lax.ppermute(value, "row", list(enumerate(neighbours[which])))

    def from_neighbours(image):
        one, two = pl.pallas_call(
            edge_kernel,
            out_shape=(jax.ShapeDtypeStruct((both, edge), BF16),) * 2,
            in_specs=[SMEM, VMEM],
            out_specs=(VMEM, VMEM),
            compiler_params=params(),
            name="edges",
        )(row_place, image)
        return along_row(one, 0), along_row(two, 1)

    def one_edge(image, edge_units, early):
        return pl.pallas_call(
            functools.partial(one_edge_kernel, early),
            out_shape=jax.ShapeDtypeStruct((edge_units, both, LANES), BF16),
            in_specs=[SMEM, VMEM],
            out_specs=VMEM,
            compiler_params=params(),
            name="edge",
        )(row_place, image)

    image_shape = jax.ShapeDtypeStruct((units, both, LANES), F32)
    target_windows, moved = pl.pallas_call(
        functools.partial(fetch_kernel, items, width, slots),
        out_shape=(
            pltpu.VMEM(window_shape.shape, BF16),
            pltpu.VMEM((items, 2 * pad_coefs, coefs), BF16),
        ),
        in_specs=[SMEM, HBM, HBM],
        out_specs=(VMEM, VMEM),
        scratch_shapes=[
            pltpu.VMEM((items, coefs, 2, coefs), BF16),
            pltpu.SemaphoreType.DMA((items, PIECES)),
            pltpu.SemaphoreType.DMA((items,)),
        ],
        compiler_params=params(24),
        cost_estimate=pl.CostEstimate(flops=0, bytes_accessed=6 * window_shape.size, transcendentals=0),
        name="fetch",
    )(plan, expansions, moves)

    def swapped(value, step):
        return lax.ppermute(value, GROUP, [(g, g ^ step) for g in range(group)])

    def near(one, two, low):
        return pl.pallas_call(
            functools.partial(near_kernel, fields),
            out_shape=image_shape,
            in_specs=[SMEM] * 3 + [VMEM] * 4,
            out_specs=VMEM,
            scratch_shapes=[pltpu.VMEM((units + 2 * edge_units, both, LANES), low.dtype)],
            compiler_params=params(),
            cost_estimate=pl.CostEstimate(
                flops=8 * fields * near_tiles.size // 2, bytes_accessed=2 * near_tiles.size, transcendentals=0
            ),
            name="near",
        )(row_place, tile_count, plan, one, two, low, near_tiles)

    def core_parts(partial, taken):
        keep, give = pl.pallas_call(
            functools.partial(far_kernel, fields, items, width, slots),
            out_shape=(jax.ShapeDtypeStruct(half_units, F32), jax.ShapeDtypeStruct(half_units, BF16)),
            in_specs=[SMEM, SMEM] + [VMEM] * 5,
            out_specs=(VMEM, VMEM),
            scratch_shapes=[pltpu.VMEM(image_shape.shape, F32)],
            compiler_params=params(),
            name="far",
        )(core_place, plan, leaves, partial, taken, moved, target_windows)
        return keep, swapped(give, 1)

    def first_far(taken):
        return pl.pallas_call(
            functools.partial(first_far_kernel, fields, items, width, slots),
            out_shape=jax.ShapeDtypeStruct((items, width, both, LANES), F32),
            in_specs=[SMEM] + [VMEM] * 4,
            out_specs=VMEM,
            compiler_params=params(),
            name="first_far",
        )(plan, leaves, taken, moved, target_windows)

    def last_core_parts(one, other_one, two, low, image):
        half_shape = jax.ShapeDtypeStruct(half_units, BF16)
        keep, give = pl.pallas_call(
            functools.partial(last_near_kernel, fields),
            out_shape=(half_shape, half_shape),
            in_specs=[SMEM] * 4 + [VMEM] * 6,
            out_specs=(VMEM, VMEM),
            scratch_shapes=[
                pltpu.VMEM((units + 2 * edge_units, both, LANES), low.dtype),
                pltpu.VMEM(image_shape.shape, F32),
            ],
            compiler_params=params(),
            name="last_near",
        )(core_place, row_place, tile_count, plan, one, other_one, two, low, near_tiles, image)
        return keep, swapped(give, 1)

    def pair_sums(keep, got):
        pair = pl.pallas_call(
            pair_kernel,
            out_shape=jax.ShapeDtypeStruct(keep.shape, BF16),
            in_specs=[VMEM, VMEM],
            out_specs=VMEM,
            compiler_params=params(),
            name="pair",
        )(keep, got)
        arrived = {step: swapped(pair, 2 * step) for step in swap_order(chips)}
        return [pair] + list(arrived.values())

    def half_sum(parts):
        return pl.pallas_call(
            close_kernel,
            out_shape=jax.ShapeDtypeStruct(half_units, F32),
            in_specs=[VMEM] * chips,
            out_specs=VMEM,
            compiler_params=params(),
            name="close",
        )(*parts)

    def whole(mine, theirs):
        return pl.pallas_call(
            functools.partial(assemble_kernel, fields, items, width, slots),
            out_shape=(
                image_shape,
                jax.ShapeDtypeStruct(image_shape.shape, BF16),
                jax.ShapeDtypeStruct((items, fields, 2 * pad_coefs + ITEM_REST), BF16),
            ),
            in_specs=[SMEM, SMEM] + [VMEM] * 4,
            out_specs=(VMEM,) * 3,
            compiler_params=params(),
            name="assemble",
        )(core_place, plan, leaves, mine, theirs, windows)

    partial = near(*from_neighbours(right), right)
    mine = half_sum(pair_sums(*core_parts(partial, exchanged(made))))
    theirs = swapped(mine, 1)
    one = along_row(one_edge(mine, edge_units // 2, True), 0)
    z_all, z_low, made = whole(mine, theirs)
    image = first_far(exchanged(made))
    two = along_row(one_edge(z_low, edge_units, False), 1)
    parts = pair_sums(*last_core_parts(one, swapped(one, 1), two, z_low, image))

    lines = pl.pallas_call(
        functools.partial(gram_kernel, fields),
        out_shape=jax.ShapeDtypeStruct((2 * rows, -(-9 * fields // LANES), LANES), F32),
        in_specs=[SMEM] + [VMEM] * (2 + chips),
        out_specs=VMEM,
        compiler_params=params(),
        name="gram",
    )(core_place, right, z_all, *parts)
    columns = lax.axis_size("col")
    same_chip = [
        [((g + k) // columns * rows + r) * columns + (g + k) % columns for r in range(rows) for k in range(2)]
        for g in range(0, group, 2)
    ]
    sums = lax.all_to_all(lines, EVERY, 0, 0, axis_index_groups=same_chip, tiled=True)
    out = pl.pallas_call(
        functools.partial(final_kernel, fields),
        out_shape=jax.ShapeDtypeStruct((both, panels), F32),
        in_specs=[VMEM] * 3,
        out_specs=VMEM,
        compiler_params=params(),
        name="combine",
    )(sums, right, z_all)
    return out.reshape(right_side.shape)


def krylov_coefficients(sums):
    rr, rz_real, rz_imag, zz, rq_real, rq_imag, zq_real, zq_imag, qq = sums

    def times(left, right):
        return left[0] * right[0] - left[1] * right[1], left[0] * right[1] + left[1] * right[0]

    def conj_times(left, right):
        return left[0] * right[0] + left[1] * right[1], left[0] * right[1] - left[1] * right[0]

    def scale(factor, value):
        return factor * value[0], factor * value[1]

    def plus(*values):
        return sum(v[0] for v in values), sum(v[1] for v in values)

    def size(value):
        return value[0] * value[0] + value[1] * value[1]

    rz, rq, zq = (rz_real, rz_imag), (rq_real, rq_imag), (zq_real, zq_imag)
    beta = jnp.sqrt(rr + EPSILON)
    inv = 1.0 / beta
    norm_one = rr * inv * inv
    product = scale(inv * inv, rz)
    h_first = (0.5 * norm_one + product[0], product[1])
    shift = (h_first[0] - 0.5, h_first[1])
    residue = zz * inv * inv - 2.0 * conj_times(shift, product)[0] + size(shift) * norm_one
    residue = jnp.maximum(residue, 0.0)
    h_sub = jnp.sqrt(residue + EPSILON)
    alpha = inv / h_sub
    gamma = scale(-alpha, shift)
    h_upper = scale(
        inv,
        plus(
            scale(0.5, plus(scale(alpha, rz), scale(rr, gamma))), scale(alpha, rq), times(gamma, rz)
        ),
    )
    second = plus(
        scale(alpha * alpha, zq),
        scale(alpha * zz, gamma),
        scale(alpha, conj_times(gamma, rq)),
        scale(size(gamma), rz),
    )
    h_middle = (0.5 * residue / (h_sub * h_sub) + second[0], second[1])
    keep = (h_middle[0] - 0.5, h_middle[1])
    on_z = plus(gamma, scale(-alpha, keep))
    on_r = plus(scale(-inv, h_upper), scale(-1.0, times(keep, gamma)))
    last = (
        alpha * alpha * qq
        + size(on_z) * zz
        + size(on_r) * rr
        + 2.0
        * (
            conj_times(on_r, times(on_z, rz))[0]
            + alpha * conj_times(on_r, rq)[0]
            + alpha * conj_times(on_z, zq)[0]
        )
    )
    h_last = jnp.sqrt(jnp.maximum(last, 0.0) + EPSILON)
    radius = jnp.sqrt(size(h_first) + h_sub * h_sub)
    cosine = scale(1.0 / radius, h_first)
    sine = h_sub / radius
    upper = plus(conj_times(cosine, h_upper), scale(sine, h_middle))
    lower = plus(times(cosine, h_middle), scale(-sine, h_upper))
    radius_two = jnp.sqrt(size(lower) + h_last * h_last)
    cosine_two = scale(1.0 / radius_two, lower)
    weight_two = scale(-sine * beta / radius_two, (cosine_two[0], -cosine_two[1]))
    goal = scale(beta, (cosine[0], -cosine[1]))
    weight_one = scale(1.0 / radius, plus(goal, scale(-1.0, times(upper, weight_two))))
    on_right = plus(scale(inv, weight_one), times(weight_two, gamma))
    on_image = scale(alpha, weight_two)
    return on_right[0], on_right[1], on_image[0], on_image[1]


def solution(mesh):
    return jax.shard_map(
        local,
        mesh=mesh,
        in_specs=(
            P(None, None, "row"),
            P(None, ("grp", "row", "col"), None, None),
            P(("grp", "row", "col")),
            P(("grp", "row", "col")),
            P(None, "row", None),
            P("row", None),
            P(),
            P("row", None),
            P("row", None),
            P(),
        ),
        out_specs=P(None, None, "row"),
        check_vma=False,
    )
```
